32 devices in a mesh: section: 2 (over core), ctx: 4 (over z), fsdp: 4 (over y, x).
Axes of the slice: x: 2, y: 2, z: 4, core: 2. Of those that a mesh axis runs over, the one named last changes fastest.
Arguments:
- tokens: bfloat16 [2, 4, 512, 1024], P(None, 'fsdp', 'ctx'), may hold values from -6 to 6
- lengths: int32 [2, 4, 2], P(None, 'fsdp'), may hold values from 0 to 512, as said below
- cotangent: bfloat16 [2, 4, 512, 1024], P(None, 'fsdp', 'ctx'), may hold values from -6 to 6
- norm_one: bfloat16 [2, 1024], P('section', 'fsdp'), may hold values from 0.5 to 1.5
- qkv_weight: bfloat16 [2, 1024, 3072], P('section', 'fsdp'), may hold values from -0.1875 to 0.1875
- decay_weight: bfloat16 [2, 1024, 8], P('section', 'fsdp'), may hold values from -0.08984375 to 0.08984375
- decay_bias: bfloat16 [2, 8], P('section', 'fsdp'), may hold values from 3 to 9
- persistent: bfloat16 [2, 16, 2048], P('section', None, 'fsdp'), may hold values from -6 to 6
- out_weight: bfloat16 [2, 1024, 1024], P('section', 'fsdp'), may hold values from -0.375 to 0.375
- norm_two: bfloat16 [2, 1024], P('section', 'fsdp'), may hold values from 0.5 to 1.5
- gate_up: bfloat16 [2, 1024, 5632], P('section', 'fsdp'), may hold values from -0.1875 to 0.1875
- down_weight: bfloat16 [2, 2816, 1024], P('section', 'fsdp'), may hold values from -0.109375 to 0.109375
Outputs:
- output: bfloat16 [2, 4, 512, 1024], P('section', 'fsdp', 'ctx')
- input_grad: bfloat16 [2, 4, 512, 1024], P('section', 'fsdp', 'ctx')
- grad_norm_one: float32 [2, 1024], P('section', 'fsdp')
- grad_qkv_weight: float32 [2, 1024, 3072], P('section', 'fsdp')
- grad_decay_weight: float32 [2, 1024, 8], P('section', 'fsdp')
- grad_decay_bias: float32 [2, 8], P('section', 'fsdp')
- grad_persistent: float32 [2, 16, 2048], P('section', None, 'fsdp')
- grad_out_weight: float32 [2, 1024, 1024], P('section', 'fsdp')
- grad_norm_two: float32 [2, 1024], P('section', 'fsdp')
- grad_gate_up: float32 [2, 1024, 5632], P('section', 'fsdp')
- grad_down_weight: float32 [2, 2816, 1024], P('section', 'fsdp')
The draws below stay inside these ranges and needn't reach their ends.
Inputs may be any that keep to these rules, and one draw needn't show every extreme that they name: `lengths`: each group's two entries sum to 512; the first is at least 128, the second is 0 or at least 128; in every group one micro-batch holds a single sequence of all 512 positions.
All inputs are finite; a program needn't handle non-finite values.
Results may differ from the reference program's by a relative error of at most 0.025.
Values may be sent and summed in bfloat16 or wider, within the bound.
No kernel may reach another device: no remote copies, remote signals or barrier semaphores. Data moves between devices by JAX's collectives and lax.ppermute only.
A program may use at most 384 MiB of HBM per device.

```python
import jax
import jax.numpy as jnp
from jax import lax

D = 1024
HEADS = 8
FF = 2816
PERSIST = 16
SPAN = 64
MB = 2
HD = 128
GROUPS = 4
GTOK = 512
MIN_LEN = 128


def draw_lengths(key, part):
    key = jax.random.fold_in(key, 5)
    first_key, pick_key = jax.random.split(key)
    first_length = jax.random.randint(first_key, (MB, GROUPS), MIN_LEN, GTOK - MIN_LEN + 1)
    chosen = jax.random.randint(pick_key, (GROUPS,), 0, MB)
    single = jnp.arange(MB)[:, None] == chosen[None, :]
    first_length = jnp.where(single, GTOK, first_length)
    return jnp.stack([first_length, GTOK - first_length], axis=-1).astype(jnp.int32)


def block_scale(key, dims, cuts, low, high):
    loudness, own = 1.0, jax.random.fold_in(key, 6)
    for dim, shards_of in cuts:
        heights = jnp.exp(jax.random.uniform(jax.random.fold_in(own, dim), (shards_of,), jnp.float32, low / len(cuts), high / len(cuts)))
        loudness = loudness * jnp.repeat(heights, dims[dim] // shards_of).reshape([-1 if axis == dim else 1 for axis in range(len(dims))])
    return loudness


def gaussian(own_key, shape, width, bound, cuts=(), kind=jnp.bfloat16):
    entries = width * jax.random.normal(own_key, shape, jnp.float32)
    if cuts:
        entries = entries * block_scale(own_key, shape, cuts, -0.22, 0.18)
    return jnp.clip(entries, -bound, bound).astype(kind)


def setup_inputs(seed: int = 0) -> dict:
    arg_keys = jax.random.split(jax.random.key(seed), 13)
    tokens = gaussian(arg_keys[0], (MB, GROUPS, GTOK, D), 1.0, 6.0, ((1, 4), (2, 4)))
    lengths = draw_lengths(jax.random.fold_in(arg_keys[12], 71), 0)
    cotangent = gaussian(arg_keys[2], (MB, GROUPS, GTOK, D), 1.0, 6.0, ((1, 4), (2, 4)))
    norm_one = jnp.clip(1.0 + 0.1 * jax.random.normal(arg_keys[3], (2, D), jnp.float32), 0.5, 1.5).astype(jnp.bfloat16)
    qkv_weight = gaussian(arg_keys[4], (2, D, 3 * D), D ** -0.5, 0.1875, ((0, 2), (1, 4)))
    decay_weight = gaussian(arg_keys[5], (2, D, HEADS), 0.015, 0.08984375, ((0, 2), (1, 4)))
    decay_bias = jnp.clip(3.0 + 6.0 * jax.random.uniform(arg_keys[6], (2, HEADS), jnp.float32) ** block_scale(arg_keys[6], (2, HEADS), ((0, 2), (1, 4)), -0.2, 0.2), 3.0, 9.0).astype(jnp.bfloat16)
    persistent = gaussian(arg_keys[7], (2, PERSIST, 2 * D), 1.0, 6.0, ((0, 2), (2, 4)))
    out_weight = gaussian(arg_keys[8], (2, D, D), (D // 4) ** -0.5, 0.375, ((0, 2), (1, 4)))
    norm_two = jnp.clip(1.0 + 0.1 * jax.random.normal(arg_keys[9], (2, D), jnp.float32), 0.5, 1.5).astype(jnp.bfloat16)
    gate_up = gaussian(arg_keys[10], (2, D, 2 * FF), D ** -0.5, 0.1875, ((0, 2), (1, 4)))
    down_weight = gaussian(arg_keys[11], (2, FF, D), FF ** -0.5, 0.109375, ((0, 2), (1, 4)))
    return {"tokens": tokens, "lengths": lengths, "cotangent": cotangent, "norm_one": norm_one, "qkv_weight": qkv_weight, "decay_weight": decay_weight, "decay_bias": decay_bias, "persistent": persistent, "out_weight": out_weight, "norm_two": norm_two, "gate_up": gate_up, "down_weight": down_weight}


epsilon = 1e-05
highest = lax.Precision.HIGHEST
negative = -1e+30

@jax.custom_vjp
def low(v):
    return lax.optimization_barrier(v.astype(jnp.bfloat16)).astype(jnp.float32)

@jax.custom_vjp
def low_back(v):
    return v

def low_keep(v):
    return (low(v), None)

def low_pass(kept, grad):
    return (grad,)

def back_keep(v):
    return (v, None)

def back_low(kept, grad):
    return (low(grad),)
low.defvjp(low_keep, low_pass)
low_back.defvjp(back_keep, back_low)

def rms_norm(values, gain):
    return values * lax.rsqrt(lax.optimization_barrier(jnp.mean(values * values, axis=-1, keepdims=True)) + epsilon) * gain

def product(left_side, right_side):
    return jnp.dot(left_side, right_side, precision=highest)

def layer_pack(pack_rows, lengths, weights):
    norm_one, qkv_weight, decay_weight, decay_bias, persistent, out_weight, norm_two, gate_up, down_weight = weights
    score_scale = HD ** (-0.5)
    positions = jnp.arange(GTOK, dtype=jnp.int32)
    documents = (positions >= lengths[0]).astype(jnp.int32)
    starts = (positions == 0) | (positions == lengths[0])
    normed = low(rms_norm(pack_rows, norm_one))
    projected = low_back(low(product(normed, qkv_weight)))
    decay_logits = product(normed, decay_weight) + decay_bias
    retention_log = jax.nn.log_sigmoid(decay_logits)
    retention = jnp.where(starts[:, None], 0.0, jax.nn.sigmoid(decay_logits))
    inflow = jnp.sqrt(1.0 - retention * retention)
    queries = projected[:, :D].reshape(GTOK, HEADS, HD)
    key_heads = projected[:, D:2 * D].reshape(GTOK, HEADS, HD)
    value_heads = projected[:, 2 * D:].reshape(GTOK, HEADS, HD)
    fixed_keys = persistent[:, :D].reshape(PERSIST, HEADS, HD)
    fixed_values = persistent[:, D:].reshape(PERSIST, HEADS, HD)
    all_values = jnp.concatenate([fixed_values, value_heads], axis=0)
    query_block = min(512, GTOK)

    def attend(block_index):
        row_queries = lax.dynamic_slice_in_dim(queries, block_index * query_block, query_block, 0)
        row_positions = block_index * query_block + jnp.arange(query_block, dtype=jnp.int32)
        row_documents = (row_positions >= lengths[0]).astype(jnp.int32)
        allowed = (positions[None, :] <= row_positions[:, None]) & (documents[None, :] == row_documents[:, None])
        full_mask = jnp.concatenate([jnp.ones((query_block, PERSIST), bool), allowed], axis=1)
        fixed_scores = jnp.einsum('thd,phd->htp', row_queries, fixed_keys, precision=highest) * score_scale
        local_scores = jnp.einsum('thd,khd->htk', row_queries, key_heads, precision=highest) * score_scale
        scores = low_back(jnp.concatenate([fixed_scores, local_scores], axis=2))
        weights_soft = low(jax.nn.softmax(jnp.where(full_mask[None], scores, negative), axis=2))
        return jnp.einsum('htk,khd->thd', weights_soft, all_values, precision=highest)
    attended = lax.map(jax.checkpoint(attend), jnp.arange(GTOK // query_block)).reshape(GTOK, HEADS, HD)

    def remember(state, block_index):
        begin = block_index * SPAN
        block_queries = lax.dynamic_slice_in_dim(queries, begin, SPAN, 0)
        block_keys = lax.dynamic_slice_in_dim(key_heads, begin, SPAN, 0)
        block_values = lax.dynamic_slice_in_dim(value_heads, begin, SPAN, 0)
        block_log = lax.dynamic_slice_in_dim(retention_log, begin, SPAN, 0)
        inflow_heads = lax.dynamic_slice_in_dim(inflow, begin, SPAN, 0).T
        block_documents = lax.dynamic_slice_in_dim(documents, begin, SPAN, 0)
        prior_document = (begin - 1 >= lengths[0]).astype(jnp.int32)
        cumulative = jnp.cumsum(block_log, axis=0).T
        row_order = jnp.arange(SPAN)
        same_document = (block_documents[:, None] == block_documents[None, :]) & (row_order[None, :] <= row_order[:, None])
        spread = jnp.where(same_document[None], cumulative[:, :, None] - cumulative[:, None, :], 0.0)
        decay_matrix = jnp.where(same_document[None], jnp.exp(spread), 0.0)
        scores = low_back(jnp.einsum('thd,shd->hts', block_queries, block_keys, precision=highest) * score_scale)
        mixing = low(scores * decay_matrix * inflow_heads[:, None, :])
        reading = jnp.einsum('hts,shd->thd', mixing, block_values, precision=highest)
        carried = jnp.where(block_documents == prior_document, 1.0, 0.0)[None, :] * jnp.exp(cumulative)
        from_state = jnp.einsum('thd,hde->the', block_queries, state, precision=highest) * score_scale
        reading = reading + carried.T[:, :, None] * from_state
        last_document = block_documents[SPAN - 1]
        tail_weight = jnp.where(block_documents == last_document, 1.0, 0.0)[None, :] * jnp.exp(cumulative[:, -1:] - cumulative) * inflow_heads
        sent_keys = low(block_keys * tail_weight.T[:, :, None])
        local_state = jnp.einsum('shd,she->hde', sent_keys, block_values, precision=highest)
        through = jnp.exp(cumulative[:, -1]) * jnp.where(last_document == prior_document, 1.0, 0.0)
        return (through[:, None, None] * state + local_state, reading)
    initial = jnp.zeros((HEADS, HD, HD), jnp.float32)
    final_state, readings = lax.scan(jax.checkpoint(remember), initial, jnp.arange(GTOK // SPAN))
    reading = readings.reshape(GTOK, HEADS, HD)
    combined = low_back(low((attended + reading).reshape(GTOK, D)))
    middle = pack_rows + low_back(product(combined, out_weight))
    normed_two = low(rms_norm(middle, norm_two))
    gate_up_rows = low_back(product(normed_two, gate_up))
    activated = low(jax.nn.silu(gate_up_rows[:, :FF]) * gate_up_rows[:, FF:])
    return middle + low_back(product(activated, down_weight))

def section_layer(activations, lengths, weights):
    flat_rows = activations.reshape(MB * GROUPS, GTOK, D)
    flat_lengths = lengths.reshape(MB * GROUPS, 2)

    def one_pack(paired):
        return layer_pack(paired[0], paired[1], weights)
    return lax.map(jax.checkpoint(one_pack), (flat_rows, flat_lengths)).reshape(activations.shape)

def reference(tokens, lengths, cotangent, norm_one, qkv_weight, decay_weight, decay_bias, persistent, out_weight, norm_two, gate_up, down_weight):
    stacked = tuple((weight.astype(jnp.float32) for weight in (norm_one, qkv_weight, decay_weight, decay_bias, persistent, out_weight, norm_two, gate_up, down_weight)))

    def forward(inputs, parameters):
        first_weights = tuple((parameter[0] for parameter in parameters))
        second_weights = tuple((parameter[1] for parameter in parameters))
        between = low_back(low(section_layer(inputs, lengths, first_weights)))
        return section_layer(between, lengths, second_weights)
    result, pullback = jax.vjp(forward, tokens.astype(jnp.float32), stacked)
    input_grad, weight_grads = pullback(cotangent.astype(jnp.float32))
    return (result.astype(jnp.bfloat16), input_grad.astype(jnp.bfloat16), weight_grads[0], weight_grads[1], weight_grads[2], weight_grads[3], weight_grads[4], weight_grads[5], weight_grads[6], weight_grads[7], weight_grads[8])
```

```python
import jax
import jax.numpy as jnp
from jax import lax
from jax.sharding import PartitionSpec as P

epsilon = 1e-05
negative = -1e30
wide = jnp.float32
half = jnp.bfloat16


def exchange(value, axis, distance):
    count = lax.axis_size(axis)
    return lax.ppermute(value, axis, [(i, i ^ distance) for i in range(count)])


def gather_parts(block, axis):
    count = lax.axis_size(axis)
    return [block] + [exchange(block, axis, r) for r in range(1, count)]


def scatter_sum(blocks, axis):
    total = blocks[0].astype(wide)
    for r in range(1, len(blocks)):
        total = total + exchange(blocks[r].astype(half), axis, r).astype(wide)
    return total


def in_order(parts, index, dim):
    count = len(parts)
    shape = list(parts[0].shape)
    size = shape[dim]
    shape[dim] = size * count
    whole = jnp.zeros(shape, parts[0].dtype)
    for r, part in enumerate(parts):
        whole = lax.dynamic_update_slice_in_dim(whole, part, (index ^ r) * size, dim)
    return whole


def columns_here(shard, kinds, axis):
    count, index = lax.axis_size(axis), lax.axis_index(axis)
    rows, width = shard.shape[0], shard.shape[1] // (kinds * count)
    blocks = shard.reshape(rows, kinds, count, width)
    parts = []
    for r in range(count):
        block = lax.dynamic_index_in_dim(blocks, index ^ r, 2, False).reshape(rows, kinds * width)
        parts.append(block if r == 0 else exchange(block, axis, r))
    return in_order(parts, index, 0)


def rows_here(columns, kinds, axis):
    count, index = lax.axis_size(axis), lax.axis_index(axis)
    rows, width = columns.shape[0] // count, columns.shape[1] // kinds
    parts = []
    for r in range(count):
        block = lax.dynamic_slice_in_dim(columns, (index ^ r) * rows, rows, 0)
        block = block if r == 0 else exchange(block, axis, r)
        parts.append(block.reshape(rows, kinds, 1, width))
    return in_order(parts, index, 2).reshape(rows, kinds * count * width)


def line_sum(value, axis):
    count, index = lax.axis_size(axis), lax.axis_index(axis)
    if count != 4:
        return lax.psum(value, axis)

    def plus(a, b):
        return (a.astype(wide) + b.astype(wide)).astype(value.dtype)

    pair = plus(value, lax.ppermute(value, axis, [(0, 1), (3, 2)]))
    total = plus(pair, lax.ppermute(pair, axis, [(1, 2), (2, 1)]))
    outer = lax.ppermute(total, axis, [(1, 0), (2, 3)])
    return jnp.where((index == 0) | (index == 3), outer, total)


def dot(a, b, contract=(1, 0)):
    return lax.dot_general(a, b, (((contract[0],), (contract[1],)), ((), ())), preferred_element_type=wide)


def normalise(values, gain):
    scale = lax.rsqrt(jnp.mean(values * values, axis=-1, keepdims=True) + epsilon)
    return (values * scale * gain).astype(half)


def normalise_back(values, gain, grad):
    scale = lax.rsqrt(jnp.mean(values * values, axis=-1, keepdims=True) + epsilon)
    unit = values * scale
    grad_gain = jnp.sum(grad * unit, axis=0)
    scaled = grad * gain
    return scale * (scaled - unit * jnp.mean(scaled * unit, axis=-1, keepdims=True)), grad_gain


def heads_first(rows, size):
    return rows.reshape(rows.shape[0], rows.shape[1] // size, size).transpose(1, 0, 2)


def rows_first(heads):
    return heads.transpose(1, 0, 2).reshape(heads.shape[1], heads.shape[0] * heads.shape[2])


def batched(a, b, contract):
    return lax.dot_general(a, b, (((contract[0],), (contract[1],)), ((0,), (0,))), preferred_element_type=wide)


def cumulative(values, positions):
    earlier = (positions[None, :] <= positions[:, None]).astype(wide)
    return jnp.dot(earlier, values, precision=lax.Precision.HIGHEST)


def mixer_parts(projected, logits, fixed, length, positions, size):
    width = projected.shape[1] // 3
    q, k, v = (heads_first(projected[:, i * width : (i + 1) * width], size) for i in range(3))
    fixed_k, fixed_v = (heads_first(fixed[:, i * width : (i + 1) * width], size) for i in range(2))
    scale = size ** (-0.5)
    documents = positions >= length
    starts = (positions == 0) | (positions == length)
    allowed = ((positions[None, :] <= positions[:, None]) & (documents[:, None] == documents[None, :]))[None]
    log_keep = jax.nn.log_sigmoid(logits)
    total_log = cumulative(log_keep, positions).T
    keep = jnp.where(starts[:, None], 0.0, jax.nn.sigmoid(logits)).T
    lose = jnp.where(starts[:, None], 1.0, jax.nn.sigmoid(-logits)).T
    inflow = jnp.sqrt(lose * (1.0 + keep))
    scores = batched(q, k, (2, 2)) * scale
    fixed_scores = batched(q, fixed_k, (2, 2)) * scale
    masked = jnp.where(allowed, scores, negative)
    top = jnp.maximum(jnp.max(masked, axis=2), jnp.max(fixed_scores, axis=2))[:, :, None]
    weights, fixed_weights = jnp.exp(masked - top), jnp.exp(fixed_scores - top)
    mass = 1.0 / (jnp.sum(weights, axis=2) + jnp.sum(fixed_weights, axis=2))[:, :, None]
    weights, fixed_weights = weights * mass, fixed_weights * mass
    fall = jnp.exp(jnp.where(allowed, total_log[:, :, None] - total_log[:, None, :], negative))
    reach = scores * fall
    both = (weights + reach * inflow[:, None, :]).astype(half)
    return q, k, v, fixed_k, fixed_v, weights, fixed_weights, fall, reach, both, keep, lose, inflow


def mixer(projected, logits, fixed, length, positions, size):
    parts = mixer_parts(projected, logits, fixed, length, positions, size)
    q, k, v, fixed_k, fixed_v, weights, fixed_weights, fall, reach, both, keep, lose, inflow = parts
    mixed = batched(both, v, (2, 1)) + batched(fixed_weights.astype(half), fixed_v, (2, 1))
    return rows_first(mixed.astype(half))


def mixer_back(projected, logits, fixed, length, positions, size, grad):
    parts = mixer_parts(projected, logits, fixed, length, positions, size)
    q, k, v, fixed_k, fixed_v, weights, fixed_weights, fall, reach, both, keep, lose, inflow = parts
    scale = size ** (-0.5)
    grad = heads_first(grad, size)
    grad_both = batched(grad, v, (2, 2))
    grad_fixed = batched(grad, fixed_v, (2, 2))
    delta = (jnp.sum(weights * grad_both, axis=2) + jnp.sum(fixed_weights * grad_fixed, axis=2))[:, :, None]
    grad_scores = (weights * (grad_both - delta) + grad_both * fall * inflow[:, None, :]).astype(half)
    grad_fixed_scores = (fixed_weights * (grad_fixed - delta)).astype(half)
    grad_q = (batched(grad_scores, k, (2, 1)) + batched(grad_fixed_scores, fixed_k, (2, 1))) * scale
    grad_k = batched(grad_scores, q, (1, 1)) * scale
    grad_v = batched(both, grad, (1, 1))
    grad_fixed_k = batched(grad_fixed_scores, q, (1, 1)) * scale
    grad_fixed_v = batched(fixed_weights.astype(half), grad, (1, 1))
    pull = grad_both * reach
    grad_inflow = jnp.sum(pull, axis=1)
    grad_total = jnp.sum(pull * inflow[:, None, :], axis=2) - inflow * grad_inflow
    later = (positions[None, :] >= positions[:, None]).astype(wide)
    grad_log = jnp.dot(grad_total, later.T, precision=lax.Precision.HIGHEST)
    lose_all = jax.nn.sigmoid(-logits).T
    grad_logits = grad_log * lose_all - grad_inflow * keep * keep * lose / inflow
    grad_projected = jnp.concatenate([rows_first(grad_q), rows_first(grad_k), rows_first(grad_v)], axis=1)
    grad_persistent = jnp.concatenate([rows_first(grad_fixed_k), rows_first(grad_fixed_v)], axis=1)
    return grad_projected.astype(half), grad_logits.T, grad_persistent


def per_device(
    tokens,
    lengths,
    cotangent,
    norm_one,
    qkv_weight,
    decay_weight,
    decay_bias,
    persistent,
    out_weight,
    norm_two,
    gate_up,
    down_weight,
):
    sections, ctx_count, fsdp_count = (lax.axis_size(a) for a in ("section", "ctx", "fsdp"))
    section, ctx, fsdp = (lax.axis_index(a) for a in ("section", "ctx", "fsdp"))
    spread = ctx_count // fsdp_count
    rows, width = tokens.shape[2:]
    heads_here = decay_bias.shape[1]
    size = width // (heads_here * fsdp_count)
    inner = heads_here * size
    first = section == 0

    def own_batch(value):
        return lax.dynamic_index_in_dim(value, section, 0, False)[0]

    pairs = [(c * fsdp_count + f, f * ctx_count + c) for c in range(ctx_count) for f in range(fsdp_count)]

    def to_plane(value):
        return lax.ppermute(value, ("ctx", "fsdp"), pairs)

    def from_plane(value):
        return lax.ppermute(value, ("ctx", "fsdp"), [(b, a) for a, b in pairs])

    x_in = to_plane(own_batch(tokens))
    g_in = to_plane(own_batch(cotangent))
    length = to_plane(own_batch(lengths))[0]

    def both_layers(own):
        other = exchange(own, "section", 1)
        return jnp.where(first, own, other), jnp.where(first, other, own)

    small = jnp.concatenate(
        [
            norm_one[0],
            norm_two[0],
            decay_weight[0].reshape(-1),
            persistent[0].reshape(-1),
        ]
    )
    small = jnp.stack(both_layers(in_order([p[None] for p in gather_parts(small, "fsdp")], fsdp, 0)))
    cut = width // fsdp_count
    sizes = [cut, cut, decay_weight[0].size, persistent[0].size]
    edges = [0]
    for piece in sizes:
        edges.append(edges[-1] + piece)
    gains_one, gains_two, decays, fixeds = (small[:, :, a:b] for a, b in zip(edges[:-1], edges[1:]))
    gains_one = gains_one.reshape(2, width).astype(wide)
    gains_two = gains_two.reshape(2, width).astype(wide)
    head_count = heads_here * fsdp_count
    decays = lax.dynamic_slice_in_dim(decays.reshape(2, width, head_count), fsdp * heads_here, heads_here, 2)
    slots = persistent.shape[1]
    fixeds = fixeds.reshape(2, fsdp_count, slots, 2 * cut).transpose(0, 2, 1, 3).reshape(2, slots, 2, fsdp_count, inner)
    fixeds = lax.dynamic_index_in_dim(fixeds, fsdp, 3, False).reshape(2, slots, 2 * inner)
    biases = jnp.stack(both_layers(decay_bias[0])).astype(wide)
    qkvs = both_layers(columns_here(qkv_weight[0], 3, "fsdp"))
    outs = both_layers(out_weight[0])
    gate_ups = both_layers(columns_here(gate_up[0], 2, "fsdp"))
    downs = both_layers(down_weight[0])
    hidden = downs[0].shape[0]

    pieces = [(k * fsdp_count + (fsdp ^ r)) * rows + jnp.arange(rows) for k in range(spread) for r in range(fsdp_count)]
    all_positions = jnp.concatenate(pieces)
    groups = [[g * spread + k for k in range(spread)] for g in range(ctx_count // spread)]

    def whole(value):
        if spread == 1:
            return value
        return lax.all_gather(value, "ctx", axis_index_groups=groups, axis=0, tiled=True)

    def own_rows(value):
        if spread == 1:
            return value
        count = value.shape[0] // spread
        return lax.dynamic_slice_in_dim(value, (ctx % spread) * count, count, 0)

    def blocks_of(value):
        return list(value.reshape(fsdp_count, rows, value.shape[1]))

    def forward(layer, x, last):
        normed = jnp.concatenate(gather_parts(normalise(x, gains_one[layer]), "fsdp"))
        projected = dot(normed, qkvs[layer]).astype(half)
        logits = dot(normed, decays[layer]) + biases[layer]
        seen, seen_logits = whole(projected), whole(logits)
        combined = own_rows(mixer(seen, seen_logits, fixeds[layer], length, all_positions, size))
        middle = x + scatter_sum(blocks_of(dot(combined, outs[layer])), "fsdp")
        normed_two = jnp.concatenate(gather_parts(normalise(middle, gains_two[layer]), "fsdp"))
        gates = dot(normed_two, gate_ups[layer])
        activated = (jax.nn.silu(gates[:, :hidden]) * gates[:, hidden:]).astype(half)
        out = middle + scatter_sum(blocks_of(dot(activated, downs[layer])), "fsdp")
        return out.astype(half), (x, normed, seen, seen_logits, combined, middle, normed_two, gates, activated)

    def backward(layer, g_out, saved):
        x, normed, seen, seen_logits, combined, middle, normed_two, gates, activated = saved
        g_rows = jnp.concatenate(gather_parts(g_out, "fsdp"))
        grad_down = dot(activated, g_rows, (0, 0))
        g_activated = dot(g_rows, downs[layer], (1, 1))
        gate, up = gates[:, :hidden], gates[:, hidden:]
        sig = jax.nn.sigmoid(gate)
        g_up = g_activated * gate * sig
        g_gate = g_activated * up * sig * (1.0 + gate * (1.0 - sig))
        g_gates = jnp.concatenate([g_gate, g_up], axis=1).astype(half)
        grad_gate_up = dot(normed_two, g_gates, (0, 0))
        g_normed_two = scatter_sum(blocks_of(dot(g_gates, gate_ups[layer], (1, 1))), "fsdp")
        g_middle, grad_norm_two = normalise_back(middle, gains_two[layer], g_normed_two)
        g_middle = g_middle + g_out.astype(wide)
        g_branch = jnp.concatenate(gather_parts(g_middle.astype(half), "fsdp"))
        grad_out = dot(combined, g_branch, (0, 0))
        g_combined = whole(dot(g_branch, outs[layer], (1, 1)).astype(half))
        g_projected, g_logits, grad_fixed = mixer_back(
            seen, seen_logits, fixeds[layer], length, all_positions, size, g_combined
        )
        g_projected, g_logits = own_rows(g_projected), own_rows(g_logits)
        grad_fixed = jnp.where(ctx % spread == 0, grad_fixed, 0.0)
        grad_qkv = dot(normed, g_projected, (0, 0))
        grad_decay = dot(normed.astype(wide), g_logits, (0, 0))
        grad_bias = jnp.sum(g_logits, axis=0)
        g_normed = dot(g_projected, qkvs[layer], (1, 1)) + dot(g_logits, decays[layer].astype(wide), (1, 1))
        g_normed = scatter_sum(blocks_of(g_normed), "fsdp")
        g_x, grad_norm_one = normalise_back(x, gains_one[layer], g_normed)
        g_x = (g_x + g_middle).astype(half)
        large = (grad_qkv, grad_out, grad_gate_up, grad_down)
        return g_x, tuple(g.astype(half) for g in large), (grad_norm_one, grad_norm_two, grad_decay, grad_bias, grad_fixed)

    between, saved_first = forward(0, x_in.astype(wide), False)
    out, saved_second = forward(1, between.astype(wide), True)
    g_between, large_second, small_second = backward(1, g_in, saved_second)
    g_input, large_first, small_first = backward(0, g_between, saved_first)

    def reduced(from_first, from_second):
        received = exchange(jnp.where(first, from_second, from_first), "section", 1)
        own = jnp.where(first, from_first, from_second)
        own = (own.astype(wide) + received.astype(wide)).astype(half)
        return line_sum(own, "ctx")

    grad_qkv, grad_out, grad_gate_up, grad_down = (reduced(a, b) for a, b in zip(large_first, large_second))
    grad_qkv = rows_here(grad_qkv, 3, "fsdp")
    grad_gate_up = rows_here(grad_gate_up, 2, "fsdp")

    def small_whole(pieces):
        n_one, n_two, decay, bias, fixed = pieces
        decay_all = lax.dynamic_update_slice_in_dim(jnp.zeros((width, head_count), wide), decay, fsdp * heads_here, 1)
        bias_all = lax.dynamic_update_slice_in_dim(jnp.zeros((head_count,), wide), bias, fsdp * heads_here, 0)
        fixed_all = jnp.zeros((slots, 2, fsdp_count, inner), wide)
        fixed_all = lax.dynamic_update_slice_in_dim(fixed_all, fixed.reshape(slots, 2, 1, inner), fsdp, 2)
        return jnp.concatenate([n_one, n_two, decay_all.reshape(-1), fixed_all.reshape(-1), bias_all])

    tiny_first, tiny_second = small_whole(small_first), small_whole(small_second)
    tiny = lax.psum(jnp.stack([tiny_first, tiny_second]), ("section", "ctx", "fsdp"))
    tiny = lax.dynamic_index_in_dim(tiny, section, 0, False)
    grad_norm_one = lax.dynamic_slice_in_dim(tiny[:width], fsdp * cut, cut, 0)
    grad_norm_two = lax.dynamic_slice_in_dim(tiny[width : 2 * width], fsdp * cut, cut, 0)
    at = 2 * width
    grad_decay = lax.dynamic_slice_in_dim(tiny[at : at + width * head_count].reshape(width, head_count), fsdp * cut, cut, 0)
    at += width * head_count
    grad_fixed = tiny[at : at + slots * 2 * width].reshape(slots, 2 * width)
    grad_fixed = lax.dynamic_slice_in_dim(grad_fixed, fsdp * 2 * cut, 2 * cut, 1)
    at += slots * 2 * width
    grad_bias = lax.dynamic_slice_in_dim(tiny[at:], fsdp * heads_here, heads_here, 0)

    return (
        from_plane(out)[None, None],
        from_plane(g_input)[None, None],
        grad_norm_one[None],
        grad_qkv.astype(wide)[None],
        grad_decay[None],
        grad_bias[None],
        grad_fixed[None],
        grad_out.astype(wide)[None],
        grad_norm_two[None],
        grad_gate_up.astype(wide)[None],
        grad_down.astype(wide)[None],
    )


def solution(mesh):
    by_row = P("section", "fsdp", None)
    by_gain = P("section", "fsdp")
    by_token = P(None, "fsdp", "ctx", None)
    by_output = P("section", "fsdp", "ctx", None)
    by_slot = P("section", None, "fsdp")
    return jax.shard_map(
        per_device,
        mesh=mesh,
        in_specs=(
            by_token,
            P(None, "fsdp", None),
            by_token,
            by_gain,
            by_row,
            by_row,
            by_gain,
            by_slot,
            by_row,
            by_gain,
            by_row,
            by_row,
        ),
        out_specs=(
            by_output,
            by_output,
            by_gain,
            by_row,
            by_row,
            by_gain,
            by_slot,
            by_row,
            by_gain,
            by_row,
            by_row,
        ),
        check_vma=False,
    )
```

```python
import jax
import jax.numpy as jnp
from jax import lax
from jax.experimental import pallas as pl
from jax.experimental.pallas import tpu as pltpu
from jax.sharding import PartitionSpec as P

epsilon = 1e-05
negative = -1e30
wide = jnp.float32
half = jnp.bfloat16
LANES = 128
PAIR = 64
vmem = pl.BlockSpec(memory_space=pltpu.VMEM)
smem = pl.BlockSpec(memory_space=pltpu.SMEM)
anywhere = pl.BlockSpec(memory_space=pltpu.HBM)


def outside(*arrays):
    return [pltpu.with_memory_space_constraint(array, pltpu.HBM) for array in arrays]


def mm(a, b):
    return lax.dot_general(a, b, (((1,), (0,)), ((), ())), preferred_element_type=wide)


def mm_nt(a, b):
    return lax.dot_general(a, b, (((1,), (1,)), ((), ())), preferred_element_type=wide)


def mm_tn(a, b):
    return lax.dot_general(a, b, (((0,), (0,)), ((), ())), preferred_element_type=wide)


def sig(v):
    return 1.0 / (1.0 + jnp.exp(-v))


def call(body, out_shape, in_specs, scratch, flops, moved, name):
    return pl.pallas_call(
        body,
        out_shape=out_shape,
        in_specs=in_specs,
        out_specs=jax.tree.map(lambda _: vmem, out_shape),
        scratch_shapes=scratch,
        compiler_params=pltpu.CompilerParams(vmem_limit_bytes=26 * 1024 * 1024),
        cost_estimate=pl.CostEstimate(flops=flops, bytes_accessed=moved, transcendentals=0),
        name=name,
    )


def shape(dims, kind=half):
    return jax.ShapeDtypeStruct(tuple(dims), kind)


def pack_heads(count, shard, place):
    rows, columns = shard.shape
    inner = columns // (3 * count)

    def body(place_ref, shard_ref, *outs):
        for r in range(count):
            target = place_ref[0] ^ r
            for kind in range(3):
                at = pl.multiple_of(kind * count * inner + target * inner, inner)
                outs[r][:, kind * inner : (kind + 1) * inner] = shard_ref[:, pl.ds(at, inner)]

    outs = [shape((rows, 3 * inner))] * count
    return call(body, outs, [smem, vmem], [], 0, 2 * shard.size * 2, "pack_heads")(place, shard)


def pack_gates(count, shard, place):
    rows, columns = shard.shape
    hidden = columns // 2
    mine = columns // count

    def body(place_ref, shard_ref, *rest):
        outs, mixed = rest[:count], rest[count]
        low = lax.broadcasted_iota(jnp.int32, (rows, LANES), 1) < PAIR
        for m in range(hidden // LANES):
            gate = shard_ref[:, m * LANES : (m + 1) * LANES].astype(wide)
            up = shard_ref[:, hidden + m * LANES : hidden + (m + 1) * LANES].astype(wide)
            even = jnp.where(low, gate, pltpu.roll(up, PAIR, 1))
            odd = jnp.where(low, pltpu.roll(gate, PAIR, 1), up)
            mixed[:, 2 * m * LANES : (2 * m + 1) * LANES] = even.astype(half)
            mixed[:, (2 * m + 1) * LANES : (2 * m + 2) * LANES] = odd.astype(half)
        for r in range(count):
            at = pl.multiple_of((place_ref[0] ^ r) * mine, LANES)
            outs[r][...] = mixed[:, pl.ds(at, mine)]

    outs = [shape((rows, mine))] * count
    scratch = [pltpu.VMEM((rows, columns), half)]
    return call(body, outs, [smem, vmem], scratch, 0, 2 * shard.size * 2, "pack_gates")(place, shard)


class Loader:
    def __init__(self, place_ref, layer, sems):
        self.place, self.layer, self.sems, self.used, self.waits = place_ref, layer, sems, 0, []

    def start(self, mine, other, target, relative=False):
        handles = []
        rows = mine[0].shape[0]
        for r in range(len(mine)):
            at = r * rows if relative else pl.multiple_of((self.place[0] ^ r) * rows, rows)
            where = target.at[pl.ds(at, rows)]
            sem = self.sems.at[self.used]
            self.used += 1

            @pl.when(self.place[1] == self.layer)
            def _(r=r, where=where, sem=sem):
                pltpu.make_async_copy(mine[r], where, sem).start()

            @pl.when(self.place[1] != self.layer)
            def _(r=r, where=where, sem=sem):
                pltpu.make_async_copy(other[r], where, sem).start()

            handles.append(pltpu.make_async_copy(mine[r], where, sem))
        return handles


def finish(handles):
    for handle in handles:
        handle.wait()


def put_rows(parts, target, place_ref):
    rows = parts[0].shape[0]
    for r, part in enumerate(parts):
        target[pl.ds(pl.multiple_of((place_ref[0] ^ r) * rows, rows), rows), :] = part[...]


def take_rows(source, outs, place_ref):
    rows = outs[0].shape[0]
    for r, out in enumerate(outs):
        out[...] = source[pl.ds(pl.multiple_of((place_ref[0] ^ r) * rows, rows), rows), :].astype(out.dtype)


def three_way(v):
    high = v.astype(half)
    rest = v - high.astype(wide)
    middle = rest.astype(half)
    return high, middle, (rest - middle.astype(wide)).astype(half)


def exact_sum(mask, values):
    return sum(mm(mask, piece) for piece in three_way(values))


def gate_rows(logits, length, rows):
    at = lax.broadcasted_iota(jnp.int32, (rows, LANES), 0)
    starts = (at == 0) | (at == length)
    spill = jnp.log(1.0 + jnp.exp(-jnp.abs(logits)))
    log_keep = jnp.minimum(logits, 0.0) - spill
    keep = jnp.where(starts, 0.0, sig(logits))
    lose = jnp.where(starts, 1.0, sig(-logits))
    return log_keep, keep, lose


def totals(log_keep, rows):
    below = lax.broadcasted_iota(jnp.int32, (rows, rows), 1) <= lax.broadcasted_iota(jnp.int32, (rows, rows), 0)
    return exact_sum(below.astype(wide).astype(half), log_keep)


def block_scores(i, block, head, size, inner, projected, fixed, total, total_t, inflow_t, length, scale):
    n = (i + 1) * block
    rows = slice(i * block, n)
    lanes = slice(head * size, (head + 1) * size)
    q = projected[rows, lanes]
    k = projected[0:n, inner + head * size : inner + (head + 1) * size]
    v = projected[0:n, 2 * inner + head * size : 2 * inner + (head + 1) * size]
    fixed_k = fixed[:, lanes]
    fixed_v = fixed[:, inner + head * size : inner + (head + 1) * size]
    scores = mm_nt(q, k) * scale
    fixed_scores = mm_nt(q, fixed_k) * scale
    at = i * block + lax.broadcasted_iota(jnp.int32, (block, 1), 0)
    begin = jnp.where(at >= length, length, 0)
    column = lax.broadcasted_iota(jnp.int32, (block, n), 1)
    allowed = (column <= at) & (column >= begin)
    masked = jnp.where(allowed, scores, negative)
    top = jnp.maximum(jnp.max(masked, axis=1, keepdims=True), jnp.max(fixed_scores, axis=1, keepdims=True))
    weights, fixed_weights = jnp.exp(masked - top), jnp.exp(fixed_scores - top)
    mass = 1.0 / (jnp.sum(weights, axis=1, keepdims=True) + jnp.sum(fixed_weights, axis=1, keepdims=True))
    weights, fixed_weights = weights * mass, fixed_weights * mass
    fall = jnp.exp(jnp.where(allowed, total[rows, head : head + 1] - total_t[head : head + 1, 0:n], negative))
    reach = scores * fall
    both = (weights + reach * inflow_t[head : head + 1, 0:n]).astype(half)
    return q, k, v, fixed_k, fixed_v, weights, fixed_weights, fall, reach, both


def mix_forward(layer, heads, size, place, parts, qkv_mine, qkv_other, out_mine, out_other, decay, bias, fixed):
    count = len(parts)
    rows, width = parts[0].shape
    total_rows, inner = rows * count, heads * size
    scale = size ** (-0.5)
    block = rows

    def body(place_ref, *refs):
        parts_in, mine, other = refs[:count], refs[count : 2 * count], refs[2 * count : 3 * count]
        o_mine, o_other, refs = refs[3 * count : 3 * count + 1], refs[3 * count + 1 : 3 * count + 2], refs[3 * count + 2 :]
        decay_ref, bias_ref, fixed_ref, refs = refs[0], refs[1], refs[2], refs[3:]
        terms, refs = refs[:count], refs[count:]
        combined, normed, projected, logits_out, weight, out_weight, whole, sems = refs
        loader = Loader(place_ref, layer, sems)
        handles = loader.start(mine, other, weight)
        out_handles = loader.start(o_mine, o_other, out_weight, relative=True)
        put_rows(parts_in, normed, place_ref)
        length = place_ref[2]
        logits = mm(normed[...], decay_ref[...]) + bias_ref[...]
        logits_out[...] = logits
        log_keep, keep, lose = gate_rows(logits, length, total_rows)
        total = totals(log_keep, total_rows)
        total_t = total.T
        inflow_t = jnp.sqrt(lose * (1.0 + keep)).T
        finish(handles)
        for kind in range(3):
            lanes = slice(kind * inner, (kind + 1) * inner)
            projected[:, lanes] = mm(normed[...], weight[:, lanes]).astype(half)
        for head in range(heads):
            for i in range(count):
                q, k, v, fixed_k, fixed_v, weights, fixed_weights, fall, reach, both = block_scores(
                    i, block, head, size, inner, projected, fixed_ref, total, total_t, inflow_t, length, scale
                )
                mixed = mm(both, v) + mm(fixed_weights.astype(half), fixed_v)
                combined[i * block : (i + 1) * block, head * size : (head + 1) * size] = mixed.astype(half)
        finish(out_handles)
        whole[...] = mm(combined[...], out_weight[...])
        take_rows(whole, terms, place_ref)

    outs = [shape((rows, width), wide if r == 0 else half) for r in range(count)] + [
        shape((total_rows, inner)),
        shape((total_rows, width)),
        shape((total_rows, 3 * inner)),
        shape((total_rows, LANES), wide),
    ]
    scratch = [
        pltpu.VMEM((width, 3 * inner), half),
        pltpu.VMEM((inner, width), half),
        pltpu.VMEM((total_rows, width), wide),
        pltpu.SemaphoreType.DMA((count + 1,)),
    ]
    specs = [smem] + [vmem] * count + [anywhere] * (2 * count + 2) + [vmem] * 3
    flops = 2 * total_rows * (width * 4 * inner + inner * total_rows * 2)
    moved = 2 * (width * 3 * inner + total_rows * (2 * width + 4 * inner))
    return call(body, outs, specs, scratch, flops, moved, "mix_forward")(
        place, *parts, *outside(*qkv_mine, *qkv_other, out_mine, out_other), decay, bias, fixed
    )


def mix_backward(layer, heads, size, place, parts, out_mine, out_other, qkv_mine, qkv_other, decay, fixed, projected, logits, normed, gain):
    count = len(parts)
    rows, width = parts[0].shape
    total_rows, inner = rows * count, heads * size
    scale = size ** (-0.5)
    block = rows

    def body(place_ref, *refs):
        parts_in, refs = refs[:count], refs[count:]
        o_mine, o_other, refs = refs[:1], refs[1:2], refs[2:]
        mine, other, refs = refs[:count], refs[count : 2 * count], refs[2 * count :]
        decay_ref, fixed_ref, projected, logits_ref, normed_ref, gain_ref = refs[:6]
        refs = refs[6:]
        terms, refs = refs[:count], refs[count:]
        branch, g_projected, g_logits_out, g_fixed, g_gain, refs = refs[0], refs[1], refs[2], refs[3], refs[4], refs[5:]
        weight, out_weight, combined, g_k, g_v, pulled, pushed, whole, sems = refs
        loader = Loader(place_ref, layer, sems)
        out_handles = loader.start(o_mine, o_other, out_weight, relative=True)
        handles = loader.start(mine, other, weight)
        put_rows(parts_in, branch, place_ref)
        length = place_ref[2]
        logits = logits_ref[...]
        log_keep, keep, lose = gate_rows(logits, length, total_rows)
        total = totals(log_keep, total_rows)
        total_t = total.T
        inflow = jnp.sqrt(lose * (1.0 + keep))
        inflow_t = inflow.T
        finish(out_handles)
        combined[...] = mm_nt(branch[...], out_weight[...]).astype(half)
        g_k[...] = jnp.zeros_like(g_k)
        g_v[...] = jnp.zeros_like(g_v)
        pulled[...] = jnp.zeros_like(pulled)
        pushed[...] = jnp.zeros_like(pushed)
        g_fixed[...] = jnp.zeros_like(g_fixed)
        for head in range(heads):
            lanes = slice(head * size, (head + 1) * size)
            for i in range(count):
                n = (i + 1) * block
                here = slice(i * block, n)
                q, k, v, fixed_k, fixed_v, weights, fixed_weights, fall, reach, both = block_scores(
                    i, block, head, size, inner, projected, fixed_ref, total, total_t, inflow_t, length, scale
                )
                grad = combined[here, lanes]
                g_both = mm_nt(grad, v)
                g_few = mm_nt(grad, fixed_v)
                delta = jnp.sum(weights * g_both, axis=1, keepdims=True) + jnp.sum(
                    fixed_weights * g_few, axis=1, keepdims=True
                )
                inflow_row = inflow_t[head : head + 1, 0:n]
                g_scores = (weights * (g_both - delta) + g_both * fall * inflow_row).astype(half)
                g_few_scores = (fixed_weights * (g_few - delta)).astype(half)
                g_projected[here, lanes] = ((mm(g_scores, k) + mm(g_few_scores, fixed_k)) * scale).astype(half)
                g_k[0:n, lanes] += mm_tn(g_scores, q)
                g_v[0:n, lanes] += mm_tn(both, grad)
                g_fixed[:, lanes] += mm_tn(g_few_scores, q) * scale
                g_fixed[:, inner + head * size : inner + (head + 1) * size] += mm_tn(fixed_weights.astype(half), grad)
                pull = g_both * reach
                pulled[head : head + 1, 0:n] += jnp.sum(pull, axis=0, keepdims=True)
                pushed[here, head : head + 1] = jnp.sum(pull * inflow_row, axis=1, keepdims=True)
        g_projected[:, inner : 2 * inner] = (g_k[...] * scale).astype(half)
        g_projected[:, 2 * inner : 3 * inner] = g_v[...].astype(half)
        g_inflow = jnp.concatenate([pulled[...], jnp.zeros((LANES - 8, total_rows), wide)], axis=0).T
        g_total = pushed[...] - inflow * g_inflow
        above = lax.broadcasted_iota(jnp.int32, (total_rows, total_rows), 1) >= lax.broadcasted_iota(
            jnp.int32, (total_rows, total_rows), 0
        )
        g_log = exact_sum(above.astype(wide).astype(half), g_total)
        g_logits = g_log * sig(-logits) - g_inflow * keep * keep * lose / inflow
        lane = lax.broadcasted_iota(jnp.int32, (total_rows, LANES), 1)
        g_logits = jnp.where(lane < heads, g_logits, 0.0)
        g_logits_out[...] = g_logits
        finish(handles)
        high, middle, low = three_way(g_logits)
        whole[...] = (
            mm_nt(g_projected[...], weight[...]) + mm_nt(high, decay_ref[...]) + mm_nt(middle, decay_ref[...])
        )
        pulls = jnp.sum(whole[...] * normed_ref[...].astype(wide), axis=0, keepdims=True) / gain_ref[...]
        g_gain[...] = jnp.broadcast_to(pulls, g_gain.shape)
        take_rows(whole, terms, place_ref)

    outs = [shape((rows, width), wide if r == 0 else half) for r in range(count)] + [
        shape((total_rows, width)),
        shape((total_rows, 3 * inner)),
        shape((total_rows, LANES), wide),
        shape((fixed.shape[0], 2 * inner), wide),
        shape((8, width), wide),
    ]
    scratch = [
        pltpu.VMEM((width, 3 * inner), half),
        pltpu.VMEM((inner, width), half),
        pltpu.VMEM((total_rows, inner), half),
        pltpu.VMEM((total_rows, inner), wide),
        pltpu.VMEM((total_rows, inner), wide),
        pltpu.VMEM((8, total_rows), wide),
        pltpu.VMEM((total_rows, LANES), wide),
        pltpu.VMEM((total_rows, width), wide),
        pltpu.SemaphoreType.DMA((count + 1,)),
    ]
    specs = [smem] + [vmem] * count + [anywhere] * 2 + [anywhere] * (2 * count) + [vmem] * 6
    flops = 2 * total_rows * (width * 4 * inner + inner * total_rows * 5)
    moved = 2 * (width * 4 * inner + total_rows * (5 * width + 6 * inner))
    return call(body, outs, specs, scratch, flops, moved, "mix_backward")(
        place, *parts, *outside(out_mine, out_other, *qkv_mine, *qkv_other), decay, fixed, projected, logits, normed, gain
    )


def gates_of(tile_pair):
    rows, columns = tile_pair.shape
    if columns == LANES:
        return tile_pair[:, :PAIR], pltpu.roll(tile_pair, PAIR, 1)[:, :PAIR]
    first, second = tile_pair[:, :LANES], tile_pair[:, LANES:]
    low = lax.broadcasted_iota(jnp.int32, (rows, LANES), 1) < PAIR
    gate = jnp.where(low, first, pltpu.roll(second, PAIR, 1))
    up = jnp.where(low, pltpu.roll(first, PAIR, 1), second)
    return gate, up


def tiles_of(gate, up):
    rows, columns = gate.shape
    if columns == PAIR:
        return jnp.concatenate([gate, up], axis=1)
    low = lax.broadcasted_iota(jnp.int32, (rows, LANES), 1) < PAIR
    first = jnp.where(low, gate, pltpu.roll(up, PAIR, 1))
    second = jnp.where(low, pltpu.roll(gate, PAIR, 1), up)
    return jnp.concatenate([first, second], axis=1)


def tile_ranges(columns):
    return [(at, min(2 * LANES, columns - at)) for at in range(0, columns, 2 * LANES)]


def feed_forward(layer, place, parts, gu_mine, gu_other, down_mine, down_other):
    count = len(parts)
    rows, width = parts[0].shape
    total_rows = rows * count
    columns, hidden = gu_mine[0].shape[1], down_mine.shape[0]
    padded = -(-hidden // LANES) * LANES

    def body(place_ref, *refs):
        parts_in, refs = refs[:count], refs[count:]
        mine, other, refs = refs[:count], refs[count : 2 * count], refs[2 * count :]
        d_mine, d_other, refs = refs[:1], refs[1:2], refs[2:]
        terms, normed, refs = refs[:count], refs[count], refs[count + 1 :]
        weight, down, active, whole, sems = refs
        loader = Loader(place_ref, layer, sems)
        handles = loader.start(mine, other, weight)
        down_handles = loader.start(d_mine, d_other, down, relative=True)
        put_rows(parts_in, normed, place_ref)
        if padded != hidden:
            down[hidden:, :] = jnp.zeros((padded - hidden, width), half)
            active[:, padded - LANES :] = jnp.zeros((total_rows, LANES), half)
        finish(handles)
        for at, size in tile_ranges(columns):
            gate, up = gates_of(mm(normed[...], weight[:, at : at + size]))
            active[:, at // 2 : (at + size) // 2] = (gate * sig(gate) * up).astype(half)
        finish(down_handles)
        whole[...] = mm(active[...], down[...])
        take_rows(whole, terms, place_ref)

    outs = [shape((rows, width), wide if r == 0 else half) for r in range(count)] + [shape((total_rows, width))]
    scratch = [
        pltpu.VMEM((width, columns), half),
        pltpu.VMEM((padded, width), half),
        pltpu.VMEM((total_rows, padded), half),
        pltpu.VMEM((total_rows, width), wide),
        pltpu.SemaphoreType.DMA((count + 1,)),
    ]
    specs = [smem] + [vmem] * count + [anywhere] * (2 * count + 2)
    flops = 2 * total_rows * width * (columns + hidden)
    moved = 2 * (width * (columns + hidden) + total_rows * 4 * width)
    return call(body, outs, specs, scratch, flops, moved, "feed_forward")(
        place, *parts, *outside(*gu_mine, *gu_other, down_mine, down_other)
    )


def feed_backward(layer, place, parts, normed_two, gain, gu_mine, gu_other, down_mine, down_other):
    count = len(parts)
    rows, width = parts[0].shape
    total_rows = rows * count
    columns, hidden = gu_mine[0].shape[1], down_mine.shape[0]
    padded = -(-hidden // LANES) * LANES

    def body(place_ref, *refs):
        parts_in, refs = refs[:count], refs[count:]
        normed, gain_ref, refs = refs[0], refs[1], refs[2:]
        mine, other, refs = refs[:count], refs[count : 2 * count], refs[2 * count :]
        d_mine, d_other, refs = refs[:1], refs[1:2], refs[2:]
        terms, refs = refs[:count], refs[count:]
        g_out, g_gates, active, g_gain, refs = refs[0], refs[1], refs[2], refs[3], refs[4:]
        weight, down, whole, sems = refs
        loader = Loader(place_ref, layer, sems)
        handles = loader.start(mine, other, weight)
        down_handles = loader.start(d_mine, d_other, down, relative=True)
        put_rows(parts_in, g_out, place_ref)
        finish(handles)
        finish(down_handles)
        for at, size in tile_ranges(columns):
            inside = slice(at // 2, (at + size) // 2)
            gate, up = gates_of(mm(normed[...], weight[:, at : at + size]))
            g_active = mm_nt(g_out[...], down[inside, :])
            open_ = sig(gate)
            lit = gate * open_
            active[:, inside] = (lit * up).astype(half)
            g_up = g_active * lit
            g_gate = g_active * up * (open_ * (1.0 + gate - lit))
            g_gates[:, at : at + size] = tiles_of(g_gate, g_up).astype(half)
        whole[...] = mm_nt(g_gates[...], weight[...])
        pulls = jnp.sum(whole[...] * normed[...].astype(wide), axis=0, keepdims=True) / gain_ref[...]
        g_gain[...] = jnp.broadcast_to(pulls, g_gain.shape)
        take_rows(whole, terms, place_ref)

    outs = [shape((rows, width), wide if r == 0 else half) for r in range(count)] + [
        shape((total_rows, width)),
        shape((total_rows, columns)),
        shape((total_rows, hidden)),
        shape((8, width), wide),
    ]
    scratch = [
        pltpu.VMEM((width, columns), half),
        pltpu.VMEM((hidden, width), half),
        pltpu.VMEM((total_rows, width), wide),
        pltpu.SemaphoreType.DMA((count + 1,)),
    ]
    specs = [smem] + [vmem] * (count + 2) + [anywhere] * (2 * count + 2)
    flops = 2 * total_rows * width * (2 * columns + hidden)
    moved = 2 * (width * (columns + hidden) + total_rows * (6 * width + columns + hidden))
    return call(body, outs, specs, scratch, flops, moved, "feed_backward")(
        place, *parts, normed_two, gain, *outside(*gu_mine, *gu_other, down_mine, down_other)
    )


def pack_small(norm_one, norm_two, decay, bias, persistent, lengths):
    cut, heads_all = decay.shape
    slots, columns = persistent.shape
    heads = bias.shape[1]
    lanes = cut // LANES
    total = 16 * (1 + lanes + columns // LANES)

    batches = lengths.shape[0]

    def body(lengths_ref, one_ref, two_ref, decay_ref, bias_ref, fixed_ref, out):
        rows = [ref[0:1, b * LANES : (b + 1) * LANES].astype(wide) for ref in (one_ref, two_ref) for b in range(lanes)]
        rows.append(jnp.concatenate([bias_ref[...].astype(wide), jnp.zeros((1, LANES - heads), wide)], axis=1))
        for m in range(batches):
            for part in (lengths_ref[m] // 64, lengths_ref[m] % 64):
                rows.append(jnp.full((1, LANES), part.astype(wide)))
        rows.append(jnp.zeros((16 - len(rows), LANES), wide))
        out[0:16, :] = jnp.concatenate(rows, axis=0).astype(half)
        padded = jnp.concatenate([decay_ref[...].astype(wide), jnp.zeros((cut, LANES - heads_all), wide)], axis=1).T
        for b in range(lanes):
            out[16 * (1 + b) : 16 * (2 + b), :] = padded[0:16, b * LANES : (b + 1) * LANES].astype(half)
        for c in range(columns // LANES):
            at = 16 * (1 + lanes + c)
            out[at : at + slots, :] = fixed_ref[:, c * LANES : (c + 1) * LANES]

    return call(body, [shape((total, LANES))], [smem] + [vmem] * 5, [], 0, 1 << 17, "pack_small")(
        lengths, norm_one, norm_two, decay, bias, persistent
    )[0]


def unpack_small(heads, slots, width, place, parts):
    count = len(parts)
    rows = parts[0].shape[0] // 2
    cut = width // count
    lanes = cut // LANES
    inner = heads * LANES

    def body(place_ref, *refs):
        ins, outs, length, held = refs[:count], refs[count:-2], refs[-2], refs[-1]
        f = place_ref[0]
        for r, part in enumerate(ins):
            for k in range(2):
                layer = place_ref[1] if k == 0 else 1 - place_ref[1]
                held[layer, f ^ r] = part[k * rows : (k + 1) * rows, :].astype(wide)
        at = 2 * lanes + 1 + 2 * place_ref[1]
        found = held[place_ref[1], place_ref[2], pl.ds(at, 2), :]
        length[...] = jnp.broadcast_to(found[0:1] * 64.0 + found[1:2], length.shape).astype(jnp.int32)
        for layer in range(2):
            one, two, decay, bias, fixed = outs[5 * layer : 5 * layer + 5]
            for t in range(count):
                for b in range(lanes):
                    at = t * cut + b * LANES
                    one[0:1, at : at + LANES] = held[layer, t, b : b + 1, :]
                    two[0:1, at : at + LANES] = held[layer, t, lanes + b : lanes + b + 1, :]
                    group = held[layer, t, 16 * (1 + b) : 16 * (2 + b), :]
                    row = lax.broadcasted_iota(jnp.int32, (16, LANES), 0)
                    mine = [
                        jnp.sum(jnp.where(row == f * heads + h, group, 0.0), axis=0, keepdims=True) for h in range(heads)
                    ]
                    mine.append(jnp.zeros((LANES - heads, LANES), wide))
                    decay[at : at + LANES, :] = jnp.concatenate(mine, axis=0).T.astype(half)
            bias[...] = held[layer, f, 2 * lanes : 2 * lanes + 1, :]
            for kind in range(2):
                source = kind * (count // 2) + f // 2
                for h in range(heads):
                    at = pl.multiple_of(16 * (1 + lanes + (f % 2) * heads + h), 16)
                    lane = kind * inner + h * LANES
                    fixed[:, lane : lane + LANES] = held[layer, source, pl.ds(at, slots), :].astype(half)

    outs = [
        shape((1, width), wide),
        shape((1, width), wide),
        shape((width, LANES)),
        shape((1, LANES), wide),
        shape((slots, 2 * inner)),
    ] * 2 + [shape((8, LANES), jnp.int32)]
    scratch = [pltpu.VMEM((2, count, rows, LANES), wide)]
    made = call(body, outs, [smem] + [vmem] * count, scratch, 0, 1 << 20, "unpack_small")(place, *parts)
    return [list(pair) for pair in zip(made[:5], made[5:10])], made[10][0, 0]


def join_forward(rounded, terms, residual, gain):
    dims = terms[0].shape

    def body(*refs):
        count = len(terms)
        residual_ref, refs_in = refs[count], refs[:count]
        total = residual_ref[...].astype(wide)
        for ref in refs_in:
            total = total + ref[...].astype(wide)
        if gain is None:
            refs[count + 1][...] = total.astype(half)
            return
        gain_ref, out, normed = refs[count + 1 :]
        if rounded:
            total = total.astype(half).astype(wide)
        out[...] = total.astype(out.dtype)
        scale = lax.rsqrt(jnp.mean(total * total, axis=1, keepdims=True) + epsilon)
        normed[...] = (total * scale * gain_ref[...]).astype(half)

    outs = [shape(dims, half if rounded else wide), shape(dims)]
    inputs = [*terms, residual, gain]
    if gain is None:
        outs, inputs = [shape(dims)], inputs[:-1]
    return call(body, outs, [vmem] * len(inputs), [], 0, dims[0] * dims[1] * 20, "join_forward")(*inputs)


def norm_rows(values, gain):
    def body(values_ref, gain_ref, normed):
        total = values_ref[...].astype(wide)
        scale = lax.rsqrt(jnp.mean(total * total, axis=1, keepdims=True) + epsilon)
        normed[...] = (total * scale * gain_ref[...]).astype(half)

    return call(body, [shape(values.shape)], [vmem, vmem], [], 0, values.size * 4, "norm_rows")(values, gain)[0]


def join_backward(terms, values, gain, onward):
    dims = terms[0].shape

    def body(*refs):
        count = len(terms)
        values_ref, gain_ref, onward_ref, out, rounded = refs[count:]
        grad = refs[0][...].astype(wide)
        for ref in refs[1:count]:
            grad = grad + ref[...].astype(wide)
        v = values_ref[...].astype(wide)
        scale = lax.rsqrt(jnp.mean(v * v, axis=1, keepdims=True) + epsilon)
        unit = v * scale
        scaled = grad * gain_ref[...]
        through = scale * (scaled - unit * jnp.mean(scaled * unit, axis=1, keepdims=True))
        total = onward_ref[...].astype(wide) + through
        out[...] = total
        rounded[...] = total.astype(half)

    outs = [shape(dims, wide), shape(dims)]
    inputs = [*terms, values, gain, onward]
    return call(body, outs, [vmem] * len(inputs), [], 0, dims[0] * dims[1] * 24, "join_backward")(*inputs)


SMALL = 16


def lane_half(source, target, which, count):
    for t in range(count):
        at = pl.multiple_of(t * 2 * LANES + which * LANES, LANES)
        target[:, t * LANES : (t + 1) * LANES] = source[:, pl.ds(at, LANES)]


def packer(packed, received):
    def put(at, value):
        rows = value.shape[0]
        if received is not None:
            value = value + received[at : at + rows, :].astype(wide)
        packed[at : at + rows, :] = value.astype(half)

    return put


def small_rows(rows):
    found = jnp.concatenate(rows, axis=0)
    return jnp.concatenate([found, jnp.zeros((SMALL - found.shape[0], LANES), wide)], axis=0)


def grad_call(body, chunks, total, inputs, received, scratch, flops, name):
    outs = [shape((b - a, LANES)) for a, b in split_rows(total, chunks)]
    if received is not None:
        inputs = inputs + [received]
    scratch = scratch + [pltpu.VMEM((total, LANES), half)]
    moved = sum(v.size * v.dtype.itemsize for v in inputs) + total * LANES * 2
    return call(body, outs, [smem] + [vmem] * (len(inputs) - 1), scratch, flops, moved, name)(*inputs)


def grad_feed(chunks, count, place, normed, g_gates, active, g_out, g_gain, received=None):
    total_rows, width = normed.shape
    columns, hidden = g_gates.shape[1], active.shape[1]
    tiles = columns // LANES
    block = columns + SMALL
    side = width // 2

    def body(place_ref, normed_ref, gates_ref, active_ref, g_out_ref, gain_ref, *refs):
        left, packed = refs[-2:]
        got, outs = (None, refs[:-2]) if received is None else (refs[0], refs[1:-2])
        which = 1 - place_ref[1] if received is None else place_ref[1]
        put = packer(packed, got)
        lane_half(normed_ref, left, which, count)
        turned = left[...].T
        for at in range(0, columns, 2 * LANES):
            size = min(2 * LANES, columns - at)
            tile = mm(turned, gates_ref[:, at : at + size])
            for t in range(count):
                for c in range(size // LANES):
                    put(t * block + at + c * LANES, tile[t * LANES : (t + 1) * LANES, c * LANES : (c + 1) * LANES])
        for t in range(count):
            at = pl.multiple_of(t * 2 * LANES + which * LANES, LANES)
            put(t * block + columns, small_rows([gain_ref[0:1, pl.ds(at, LANES)]]))
        active_t = active_ref[...].T
        for c in range(0, side // LANES, 2):
            at = pl.multiple_of(which * side + c * LANES, LANES)
            tile = mm(active_t, g_out_ref[:, pl.ds(at, 2 * LANES)])
            put(count * block + c * hidden, tile[:, :LANES])
            put(count * block + (c + 1) * hidden, tile[:, LANES:])
        chunk_out(packed, outs)

    local = (side // LANES) * hidden
    inputs = [place, normed, g_gates, active, g_out, g_gain]
    scratch = [pltpu.VMEM((total_rows, side), half)]
    flops = total_rows * width * (columns + hidden)
    return grad_call(body, chunks, count * block + local, inputs, received, scratch, flops, "grad_feed")


def grad_mix(chunks, count, place, normed, g_projected, combined, branch, g_logits, g_gain, g_fixed, received=None):
    total_rows, width = normed.shape
    columns, inner = g_projected.shape[1], combined.shape[1]
    heads = inner // LANES
    slots = g_fixed.shape[0]
    block = columns + SMALL + slots
    side = width // 2

    def body(place_ref, normed_ref, proj_ref, comb_ref, branch_ref, logits_ref, gain_ref, fixed_ref, *refs):
        left, packed = refs[-2:]
        got, outs = (None, refs[:-2]) if received is None else (refs[0], refs[1:-2])
        which = 1 - place_ref[1] if received is None else place_ref[1]
        put = packer(packed, got)
        lane_half(normed_ref, left, which, count)
        turned = left[...].T
        for at in range(0, columns, 2 * LANES):
            tile = mm(turned, proj_ref[:, at : at + 2 * LANES])
            for t in range(count):
                for c in range(2):
                    put(t * block + at + c * LANES, tile[t * LANES : (t + 1) * LANES, c * LANES : (c + 1) * LANES])
        logits = logits_ref[...]
        logits_t = logits.T
        decay = sum(mm(piece, left[...]) for piece in three_way(logits_t)[:2])
        near = pl.multiple_of(which * LANES, LANES)
        for t in range(count):
            at = pl.multiple_of(t * 2 * LANES + which * LANES, LANES)
            rows = [decay[0:heads, t * LANES : (t + 1) * LANES], gain_ref[0:1, pl.ds(at, LANES)]]
            put(t * block + columns, small_rows(rows))
            keys_here = (place_ref[0] // 2 == t).astype(wide)
            values_here = (place_ref[0] // 2 + 2 == t).astype(wide)
            fixed = fixed_ref[:, pl.ds(near, LANES)] * keys_here
            fixed = fixed + fixed_ref[:, pl.ds(pl.multiple_of(inner + near, LANES), LANES)] * values_here
            put(t * block + columns + SMALL, fixed)
        comb_t = comb_ref[:, pl.ds(near, LANES)].T
        for c in range(0, width // LANES, 2):
            tile = mm(comb_t, branch_ref[:, c * LANES : (c + 2) * LANES])
            put(count * block + c * LANES, tile[:, :LANES])
            put(count * block + (c + 1) * LANES, tile[:, LANES:])
        put(count * block + width, small_rows([jnp.sum(logits, axis=0, keepdims=True)]))
        packed[count * block + width + SMALL :, :] = jnp.zeros((SMALL, LANES), half)
        chunk_out(packed, outs)

    local = width + 2 * SMALL
    inputs = [place, normed, g_projected, combined, branch, g_logits, g_gain, g_fixed]
    scratch = [pltpu.VMEM((total_rows, side), half)]
    flops = total_rows * width * (columns + inner)
    return grad_call(body, chunks, count * block + local, inputs, received, scratch, flops, "grad_mix")


def split_rows(total, chunks):
    units = total // SMALL
    edges = [SMALL * (units * k // chunks) for k in range(chunks)] + [total]
    return list(zip(edges[:-1], edges[1:]))


def chunk_out(whole, outs):
    at = 0
    for out in outs:
        out[...] = whole[at : at + out.shape[0], :]
        at += out.shape[0]


def spread(count, block, place, chunks):
    total = sum(chunk.shape[0] for chunk, _ in chunks)

    def body(place_ref, *refs):
        ins, outs, whole = refs[: 2 * len(chunks)], refs[2 * len(chunks) : -1], refs[-1]
        for inner in range(2):

            @pl.when(place_ref[3] == inner)
            def _(inner=inner):
                at = 0
                for chunk in ins[1 - inner :: 2]:
                    whole[at : at + chunk.shape[0], :] = chunk[...]
                    at += chunk.shape[0]

        take_rows(whole, outs[:count], place_ref)
        outs[count][...] = whole[count * block :, :]

    outs = [shape((block, LANES))] * count + [shape((total - count * block, LANES))]
    scratch = [pltpu.VMEM((total, LANES), half)]
    flat = [piece for pair in chunks for piece in pair]
    return call(body, outs, [smem] + [vmem] * len(flat), scratch, 0, total * 768, "spread")(place, *flat)


def collect_feed(chunks, place, parts, local):
    count = len(parts)
    columns = parts[0].shape[0] - SMALL
    total = count * columns + SMALL + local.shape[0]

    def body(place_ref, *refs):
        parts_in, local_ref, outs, whole = refs[:count], refs[count], refs[count + 1 : -1], refs[-1]
        for r, part in enumerate(parts_in):
            at = pl.multiple_of((place_ref[0] ^ r) * columns, columns)
            whole[pl.ds(at, columns), :] = part[0:columns, :]
        small = sum(part[columns:, :].astype(wide) for part in parts_in)
        whole[count * columns : count * columns + SMALL, :] = small.astype(half)
        whole[count * columns + SMALL :, :] = local_ref[...]
        chunk_out(whole, outs)

    outs = [shape((b - a, LANES)) for a, b in split_rows(total, chunks)]
    return call(body, outs, [smem] + [vmem] * (count + 1), [pltpu.VMEM((total, LANES), half)], 0, total * 512, "collect_feed")(
        place, *parts, local
    )


def collect_mix(chunks, heads, place, parts, local):
    count = len(parts)
    slots = parts[0].shape[0] % (3 * heads * LANES) - SMALL
    columns = parts[0].shape[0] - SMALL - slots
    total = count * columns + SMALL + 2 * slots + local.shape[0]

    def body(place_ref, *refs):
        parts_in, local_ref, outs, whole, few = refs[:count], refs[count], refs[count + 1 : -2], refs[-2], refs[-1]
        for r, part in enumerate(parts_in):
            source = place_ref[0] ^ r
            at = pl.multiple_of(source * columns, columns)
            whole[pl.ds(at, columns), :] = part[0:columns, :]
            few[pl.ds(source, 1)] = part[columns:, :].astype(wide)[None]
        base = count * columns
        decay = [few[t, 0:heads, :] for t in range(count)]
        gain = sum(few[t, heads : heads + 1, :] for t in range(count))
        whole[base : base + SMALL, :] = small_rows(decay + [gain]).astype(half)
        near = (place_ref[0] % 2) * 2
        for k in range(2):
            at = base + SMALL + k * slots
            whole[at : at + slots, :] = few[near + k, SMALL:, :].astype(half)
        whole[base + SMALL + 2 * slots :, :] = local_ref[...]
        chunk_out(whole, outs)

    outs = [shape((b - a, LANES)) for a, b in split_rows(total, chunks)]
    scratch = [pltpu.VMEM((total, LANES), half), pltpu.VMEM((count, SMALL + slots, LANES), wide)]
    return call(body, outs, [smem] + [vmem] * (count + 1), scratch, 0, total * 512, "collect_mix")(place, *parts, local)


def unpack(body, totals, out_shape, place, name):
    chunks = len(totals[0][0])
    edges = [0]
    for chunk in totals[0][0]:
        edges.append(edges[-1] + chunk.shape[0])

    def whole_body(place_ref, *refs):
        ins, outs, halves, sems = refs[: 4 * chunks], refs[4 * chunks : -2], refs[-2], refs[-1]
        handles = []
        for side in range(2):
            for c in range(chunks):
                spot = place_ref[1] if side == 0 else 1 - place_ref[1]
                where = halves.at[spot, pl.ds(edges[c], edges[c + 1] - edges[c])]
                sem = sems.at[side * chunks + c]
                for layer in range(2):
                    source = ins[layer * 2 * chunks + side * chunks + c]

                    @pl.when(place_ref[1] == layer)
                    def _(source=source, where=where, sem=sem):
                        pltpu.make_async_copy(source, where, sem).start()

                handles.append(pltpu.make_async_copy(ins[side * chunks + c], where, sem))
        finish(handles)
        body(place_ref, halves, *outs)

    inputs = [piece for layer in totals for side in layer for piece in side]
    scratch = [pltpu.VMEM((2, edges[-1], LANES), half), pltpu.SemaphoreType.DMA((2 * chunks,))]
    moved = sum(o.size * 4 for o in out_shape) + 4 * edges[-1] * LANES
    return call(whole_body, out_shape, [smem] + [anywhere] * len(inputs), scratch, 0, moved, name)(place, *inputs)


def unpack_feed(count, columns, hidden, width, totals, place):
    part = width // count
    side = width // 2
    tiles = columns // LANES

    def body(place_ref, halves, gate_up, down, gain):
        low = lax.broadcasted_iota(jnp.int32, (LANES, LANES), 1) < PAIR
        middle = gate_up.shape[1] // 2
        for h in range(2):
            rows = slice(h * LANES, (h + 1) * LANES)
            for m in range(middle // LANES):
                even = halves[h, 2 * m * LANES : (2 * m + 1) * LANES, :].astype(wide)
                odd = halves[h, (2 * m + 1) * LANES : (2 * m + 2) * LANES, :].astype(wide)
                gate_up[rows, m * LANES : (m + 1) * LANES] = jnp.where(low, even, pltpu.roll(odd, PAIR, 1))
                gate_up[rows, middle + m * LANES : middle + (m + 1) * LANES] = jnp.where(low, pltpu.roll(even, PAIR, 1), odd)
            base = count * columns
            gain[0:1, h * LANES : (h + 1) * LANES] = halves[h, base : base + SMALL, :].astype(wide)[0:1]
            base += SMALL
            for c in range(side // LANES):
                at = h * side + c * LANES
                down[:, at : at + LANES] = halves[h, base + c * hidden : base + (c + 1) * hidden, :].astype(wide)

    outs = [shape((part, count * columns), wide), shape((hidden, width), wide), shape((1, part), wide)]
    return unpack(body, totals, outs, place, "unpack_feed")


def unpack_mix(count, heads, slots, width, totals, place):
    part = width // count
    inner = heads * LANES
    columns = 3 * inner

    def body(place_ref, halves, qkv, out, gain, decay, bias, fixed):
        for h in range(2):
            rows = slice(h * LANES, (h + 1) * LANES)
            for t in range(count):
                for kind in range(3):
                    for head in range(heads):
                        source = t * columns + kind * inner + head * LANES
                        at = kind * count * inner + t * inner + head * LANES
                        qkv[rows, at : at + LANES] = halves[h, source : source + LANES, :].astype(wide)
            base = count * columns
            small = halves[h, base : base + SMALL, :].astype(wide)
            padded = jnp.concatenate([small, jnp.zeros((LANES - SMALL, LANES), wide)], axis=0).T
            decay[rows, :] = padded[:, 0 : count * heads]
            gain[0:1, rows] = small[count * heads : count * heads + 1]
            for k in range(2):
                at = base + SMALL + k * slots
                lanes = slice(k * inner + h * LANES, k * inner + (h + 1) * LANES)
                fixed[:, lanes] = halves[h, at : at + slots, :].astype(wide)
            base += SMALL + 2 * slots
            for c in range(width // LANES):
                source = base + c * LANES
                out[rows, c * LANES : (c + 1) * LANES] = halves[h, source : source + LANES, :].astype(wide)
            if h == 0:
                bias[...] = halves[h, base + width : base + width + SMALL, :].astype(wide)[0:1, 0:heads]

    outs = [
        shape((part, count * columns), wide),
        shape((inner, width), wide),
        shape((1, part), wide),
        shape((part, count * heads), wide),
        shape((1, heads), wide),
        shape((slots, 2 * inner), wide),
    ]
    return unpack(body, totals, outs, place, "unpack_mix")


def tie(*values):
    return lax.optimization_barrier(values)


def exchange(value, axis, distance):
    count = lax.axis_size(axis)
    return lax.ppermute(value, axis, [(i, i ^ distance) for i in range(count)])


def gather_parts(block, axis):
    count = lax.axis_size(axis)
    far = {r: exchange(block, axis, r) for r in reversed(range(1, count))}
    return [block] + [far[r] for r in range(1, count)]


def trade_parts(blocks, axis):
    far = {r: exchange(blocks[r], axis, r) for r in reversed(range(1, len(blocks)))}
    return [blocks[0]] + [far[r] for r in range(1, len(blocks))]


def plane_device(
    tokens,
    lengths,
    cotangent,
    norm_one,
    qkv_weight,
    decay_weight,
    decay_bias,
    persistent,
    out_weight,
    norm_two,
    gate_up,
    down_weight,
):
    ctx_count, count = lax.axis_size("ctx"), lax.axis_size("fsdp")
    section, ctx, fsdp = (lax.axis_index(a) for a in ("section", "ctx", "fsdp"))
    rows, width = tokens.shape[2:]
    heads = decay_bias.shape[1]
    size = width // (heads * count)
    inner = heads * size

    def own_batch(value):
        return lax.dynamic_index_in_dim(value, section, 0, False)[0]

    pairs = [(c * count + f, f * ctx_count + c) for c in range(ctx_count) for f in range(count)]

    def turn_plane(value):
        return lax.ppermute(value, ("ctx", "fsdp"), pairs)

    def swap(value):
        return exchange(value, "section", 1)

    slots = persistent.shape[1]
    spot = jnp.stack([fsdp, section, ctx]).astype(jnp.int32)
    x_own, qkv_shard = tie(own_batch(tokens), qkv_weight[0])
    x_in = turn_plane(x_own)
    qkv_packed = pack_heads(count, qkv_shard, spot)
    qkv_mine = trade_parts(qkv_packed, "fsdp")
    small = pack_small(norm_one, norm_two, decay_weight[0], decay_bias, persistent[0], lengths[:, 0, 0])
    small, qkv_packed = tie(small, qkv_packed)
    smalls = gather_parts(jnp.concatenate([small, swap(small)]), "fsdp")
    (gains_one, gains_two, decays, biases, fixeds), length = unpack_small(heads, slots, width, spot, smalls)
    place = jnp.stack([fsdp, section, length, (ctx == 1) | (ctx == 2)]).astype(jnp.int32)
    out_mine = out_weight[0]
    out_other = swap(out_mine)
    gu_packed = pack_gates(count, gate_up[0], spot)
    x_parts = gather_parts(norm_rows(x_in, gains_one[0]), "fsdp")
    qkv_mine, x_parts, gu_packed, g_own = tie(qkv_mine, x_parts, gu_packed, own_batch(cotangent))
    qkv_other = [swap(piece) for piece in qkv_mine]
    gu_mine = trade_parts(gu_packed, "fsdp")
    down_mine = down_weight[0]
    down_other = swap(down_mine)
    g_in = turn_plane(g_own)
    hidden = down_mine.shape[0]
    columns = gu_mine[0].shape[1]

    def mix_first_half(layer, parts):
        *terms, combined, seen, projected, logits = mix_forward(
            layer, heads, size, place, parts, qkv_mine, qkv_other, out_mine, out_other, decays[layer], biases[layer], fixeds[layer]
        )
        return terms, (seen, projected, logits, combined)

    def mix_second_half(layer, terms, x):
        middle, normed_two = join_forward(False, trade_parts(terms, "fsdp"), x, gains_two[layer])
        return middle, gather_parts(normed_two, "fsdp")

    def feed_step(layer, parts, saved):
        *terms, g_rows, g_gates, active, g_gain = feed_backward(
            layer, place, parts, saved[6], gains_two[layer], gu_mine, gu_other, down_mine, down_other
        )
        return terms, (saved[6], g_gates, active, g_rows, g_gain)

    def mix_step(layer, parts, saved):
        x, seen, projected, logits, combined, middle, seen_two = saved
        *terms, branch, g_projected, g_logits, g_fixed, g_gain = mix_backward(
            layer, heads, size, place, parts, out_mine, out_other, qkv_mine, qkv_other,
            decays[layer], fixeds[layer], projected, logits, seen, gains_one[layer],
        )
        return terms, (seen, g_projected, combined, branch, g_logits, g_gain, g_fixed)

    inside = (ctx == 1) | (ctx == 2)
    line = {"queue": [], "inward": None, "across": None, "total": None, "flight": (None, None), "sums": []}

    def begin():
        own = line["queue"].pop(0) if line["queue"] else None
        total = line["total"]
        if own is not None and total is not None:
            sent = jnp.where(inside, total, own)
            route = [(0, 1), (3, 2), (1, 0), (2, 3)]
        else:
            sent = own if total is None else total
            route = [(0, 1), (3, 2)] if total is None else [(1, 0), (2, 3)]
        pair = line["across"]
        line["sent"] = (sent, pair, own, total is not None)
        return [v for v in (sent, pair) if v is not None], route

    def go(values, route):
        values = list(values)
        sent, pair, own, closing = line["sent"]
        sent = values.pop(0) if sent is not None else None
        pair = values.pop(0) if pair is not None else None
        line["sent"] = (sent, pair, own, closing)
        flight = [None, None]
        if sent is not None:
            flight[0] = lax.ppermute(sent, "ctx", route)
        if pair is not None:
            flight[1] = lax.ppermute(pair, "ctx", [(1, 2), (2, 1)])
        line["flight"] = flight

    def plus(a, b):
        return (a.astype(wide) + b.astype(wide)).astype(half)

    def step(*held, more=()):
        landed, crossed = line["flight"]
        waiting = [v for v in (landed, crossed) if v is not None]
        held, waiting = tie(held, waiting)
        if landed is not None:
            landed = waiting.pop(0)
        if crossed is not None:
            crossed = waiting.pop(0)
        sent, pair, own, closing = line.get("sent", (None, None, None, False))
        line["total"] = None if pair is None else plus(pair, crossed)
        line["across"] = None if own is None else plus(own, landed)
        if closing:
            line["sums"].append((sent, landed))
        line["queue"].extend(more)
        ready, route = begin()
        held, ready = tie(held, ready)
        go(ready, route)
        return held

    def taken(number):
        found, line["sums"] = line["sums"][:number], line["sums"][number:]
        return found

    terms, kept = mix_first_half(0, x_parts)
    terms, gu_mine = tie(terms, gu_mine)
    gu_other = [swap(piece) for piece in gu_mine]
    middle, parts = mix_second_half(0, terms, x_in)
    *terms, seen_two = feed_forward(0, place, parts, gu_mine, gu_other, down_mine, down_other)
    saved_first = (x_in, *kept, middle, seen_two)
    between, normed = join_forward(True, trade_parts(terms, "fsdp"), middle, gains_one[1])
    terms, kept = mix_first_half(1, gather_parts(normed, "fsdp"))
    terms, g_parts = tie(terms, gather_parts(g_in, "fsdp"))
    middle, parts = mix_second_half(1, terms, between)
    *terms_out, seen_two = feed_forward(1, place, parts, gu_mine, gu_other, down_mine, down_other)
    saved_second = (between, *kept, middle, seen_two)
    terms, feed = feed_step(1, g_parts, saved_second)
    out = join_forward(True, trade_parts(terms_out, "fsdp"), middle, None)[0]
    terms, out = tie(terms, out)
    out = turn_plane(out)
    other = grad_feed(1, count, place, *feed)[0]
    terms, other, out = tie(trade_parts(terms, "fsdp"), other, out)
    g_middle, g_branch = join_backward(terms, saved_second[5], gains_two[1], g_in)
    parts = gather_parts(g_branch, "fsdp")
    f1 = grad_feed(4, count, place, *feed, received=swap(other))
    (parts,) = step(parts, more=f1)
    terms, mix = mix_step(1, parts, saved_second)
    (terms,) = step(terms)
    other = grad_mix(1, count, place, *mix)[0]
    terms, other = step(trade_parts(terms, "fsdp"), other)
    g_middle, g_branch = join_backward(terms, between, gains_one[1], g_middle)
    parts = gather_parts(g_branch, "fsdp")
    m1 = grad_mix(2, count, place, *mix, received=swap(other))
    (parts,) = step(parts, more=m1)
    terms, feed = feed_step(0, parts, saved_first)
    (terms,) = step(terms)
    other = grad_feed(1, count, place, *feed)[0]
    terms, other = step(trade_parts(terms, "fsdp"), other)
    g_middle, g_branch = join_backward(terms, saved_first[5], gains_two[0], g_branch)
    parts = gather_parts(g_branch, "fsdp")
    f0 = grad_feed(4, count, place, *feed, received=swap(other))
    (parts,) = step(parts, more=f0)
    terms, mix = mix_step(0, parts, saved_first)
    (terms,) = step(terms)
    other = grad_mix(1, count, place, *mix)[0]
    received = swap(other)
    terms, received = step(trade_parts(terms, "fsdp"), received)
    m0 = grad_mix(2, count, place, *mix, received=received)
    g_input = join_backward(terms, x_in, gains_one[0], g_middle)[1]

    def trade(block, chunks):
        *blocks, local = spread(count, block, place, chunks)
        return trade_parts(blocks, "fsdp"), local

    feed_block = columns + SMALL
    mix_block = 3 * inner + SMALL + slots
    f1 = trade(feed_block, taken(4))
    g_input, f1 = step(g_input, f1, more=m0)
    feed_second = collect_feed(1, place, *f1)
    m1 = trade(mix_block, taken(2))
    feed_second, m1 = step(feed_second, m1)
    mix_second = collect_mix(1, heads, place, *m1)
    (mix_second,) = step(mix_second)
    (mix_second,) = step(mix_second)
    (mix_second,) = step(mix_second)
    f0 = trade(feed_block, taken(4))
    g_input, f0 = step(g_input, f0)
    g_input = turn_plane(g_input)
    m0 = trade(mix_block, taken(2))
    feed_first = collect_feed(1, place, *f0)
    mix_first = collect_mix(1, heads, place, *m0)

    def owned(layer, chunks):
        return chunks, [lax.ppermute(chunk, "section", [(1 - layer, layer)]) for chunk in chunks]

    grad_gate_up, grad_down, grad_norm_two = unpack_feed(
        count, columns, hidden, width, (owned(0, feed_first), owned(1, feed_second)), place
    )
    grad_qkv, grad_out, grad_norm_one, grad_decay, grad_bias, grad_fixed = unpack_mix(
        count, heads, slots, width, (owned(0, mix_first), owned(1, mix_second)), place
    )
    return (
        out[None, None],
        g_input[None, None],
        grad_norm_one,
        grad_qkv[None],
        grad_decay[None],
        grad_bias,
        grad_fixed[None],
        grad_out[None],
        grad_norm_two,
        grad_gate_up[None],
        grad_down[None],
    )


def scatter_sum(blocks, axis):
    total = blocks[0].astype(wide)
    for r in range(1, len(blocks)):
        total = total + exchange(blocks[r].astype(half), axis, r).astype(wide)
    return total


def in_order(parts, index, dim):
    count = len(parts)
    shape = list(parts[0].shape)
    size = shape[dim]
    shape[dim] = size * count
    whole = jnp.zeros(shape, parts[0].dtype)
    for r, part in enumerate(parts):
        whole = lax.dynamic_update_slice_in_dim(whole, part, (index ^ r) * size, dim)
    return whole


def columns_here(shard, kinds, axis):
    count, index = lax.axis_size(axis), lax.axis_index(axis)
    rows, width = shard.shape[0], shard.shape[1] // (kinds * count)
    blocks = shard.reshape(rows, kinds, count, width)
    parts = []
    for r in range(count):
        block = lax.dynamic_index_in_dim(blocks, index ^ r, 2, False).reshape(rows, kinds * width)
        parts.append(block if r == 0 else exchange(block, axis, r))
    return in_order(parts, index, 0)


def rows_here(columns, kinds, axis):
    count, index = lax.axis_size(axis), lax.axis_index(axis)
    rows, width = columns.shape[0] // count, columns.shape[1] // kinds
    parts = []
    for r in range(count):
        block = lax.dynamic_slice_in_dim(columns, (index ^ r) * rows, rows, 0)
        block = block if r == 0 else exchange(block, axis, r)
        parts.append(block.reshape(rows, kinds, 1, width))
    return in_order(parts, index, 2).reshape(rows, kinds * count * width)


def line_sum(value, axis):
    count, index = lax.axis_size(axis), lax.axis_index(axis)
    if count != 4:
        return lax.psum(value, axis)

    def plus(a, b):
        return (a.astype(wide) + b.astype(wide)).astype(value.dtype)

    pair = plus(value, lax.ppermute(value, axis, [(0, 1), (3, 2)]))
    total = plus(pair, lax.ppermute(pair, axis, [(1, 2), (2, 1)]))
    outer = lax.ppermute(total, axis, [(1, 0), (2, 3)])
    return jnp.where((index == 0) | (index == 3), outer, total)


def dot(a, b, contract=(1, 0)):
    return lax.dot_general(a, b, (((contract[0],), (contract[1],)), ((), ())), preferred_element_type=wide)


def normalise(values, gain):
    scale = lax.rsqrt(jnp.mean(values * values, axis=-1, keepdims=True) + epsilon)
    return (values * scale * gain).astype(half)


def normalise_back(values, gain, grad):
    scale = lax.rsqrt(jnp.mean(values * values, axis=-1, keepdims=True) + epsilon)
    unit = values * scale
    grad_gain = jnp.sum(grad * unit, axis=0)
    scaled = grad * gain
    return scale * (scaled - unit * jnp.mean(scaled * unit, axis=-1, keepdims=True)), grad_gain


def heads_first(rows, size):
    return rows.reshape(rows.shape[0], rows.shape[1] // size, size).transpose(1, 0, 2)


def rows_first(heads):
    return heads.transpose(1, 0, 2).reshape(heads.shape[1], heads.shape[0] * heads.shape[2])


def batched(a, b, contract):
    return lax.dot_general(a, b, (((contract[0],), (contract[1],)), ((0,), (0,))), preferred_element_type=wide)


def cumulative(values, positions):
    earlier = (positions[None, :] <= positions[:, None]).astype(wide)
    return jnp.dot(earlier, values, precision=lax.Precision.HIGHEST)


def mixer_parts(projected, logits, fixed, length, positions, size):
    width = projected.shape[1] // 3
    q, k, v = (heads_first(projected[:, i * width : (i + 1) * width], size) for i in range(3))
    fixed_k, fixed_v = (heads_first(fixed[:, i * width : (i + 1) * width], size) for i in range(2))
    scale = size ** (-0.5)
    documents = positions >= length
    starts = (positions == 0) | (positions == length)
    allowed = ((positions[None, :] <= positions[:, None]) & (documents[:, None] == documents[None, :]))[None]
    log_keep = jax.nn.log_sigmoid(logits)
    total_log = cumulative(log_keep, positions).T
    keep = jnp.where(starts[:, None], 0.0, jax.nn.sigmoid(logits)).T
    lose = jnp.where(starts[:, None], 1.0, jax.nn.sigmoid(-logits)).T
    inflow = jnp.sqrt(lose * (1.0 + keep))
    scores = batched(q, k, (2, 2)) * scale
    fixed_scores = batched(q, fixed_k, (2, 2)) * scale
    masked = jnp.where(allowed, scores, negative)
    top = jnp.maximum(jnp.max(masked, axis=2), jnp.max(fixed_scores, axis=2))[:, :, None]
    weights, fixed_weights = jnp.exp(masked - top), jnp.exp(fixed_scores - top)
    mass = 1.0 / (jnp.sum(weights, axis=2) + jnp.sum(fixed_weights, axis=2))[:, :, None]
    weights, fixed_weights = weights * mass, fixed_weights * mass
    fall = jnp.exp(jnp.where(allowed, total_log[:, :, None] - total_log[:, None, :], negative))
    reach = scores * fall
    both = (weights + reach * inflow[:, None, :]).astype(half)
    return q, k, v, fixed_k, fixed_v, weights, fixed_weights, fall, reach, both, keep, lose, inflow


def mixer(projected, logits, fixed, length, positions, size):
    parts = mixer_parts(projected, logits, fixed, length, positions, size)
    q, k, v, fixed_k, fixed_v, weights, fixed_weights, fall, reach, both, keep, lose, inflow = parts
    mixed = batched(both, v, (2, 1)) + batched(fixed_weights.astype(half), fixed_v, (2, 1))
    return rows_first(mixed.astype(half))


def mixer_back(projected, logits, fixed, length, positions, size, grad):
    parts = mixer_parts(projected, logits, fixed, length, positions, size)
    q, k, v, fixed_k, fixed_v, weights, fixed_weights, fall, reach, both, keep, lose, inflow = parts
    scale = size ** (-0.5)
    grad = heads_first(grad, size)
    grad_both = batched(grad, v, (2, 2))
    grad_fixed = batched(grad, fixed_v, (2, 2))
    delta = (jnp.sum(weights * grad_both, axis=2) + jnp.sum(fixed_weights * grad_fixed, axis=2))[:, :, None]
    grad_scores = (weights * (grad_both - delta) + grad_both * fall * inflow[:, None, :]).astype(half)
    grad_fixed_scores = (fixed_weights * (grad_fixed - delta)).astype(half)
    grad_q = (batched(grad_scores, k, (2, 1)) + batched(grad_fixed_scores, fixed_k, (2, 1))) * scale
    grad_k = batched(grad_scores, q, (1, 1)) * scale
    grad_v = batched(both, grad, (1, 1))
    grad_fixed_k = batched(grad_fixed_scores, q, (1, 1)) * scale
    grad_fixed_v = batched(fixed_weights.astype(half), grad, (1, 1))
    pull = grad_both * reach
    grad_inflow = jnp.sum(pull, axis=1)
    grad_total = jnp.sum(pull * inflow[:, None, :], axis=2) - inflow * grad_inflow
    later = (positions[None, :] >= positions[:, None]).astype(wide)
    grad_log = jnp.dot(grad_total, later.T, precision=lax.Precision.HIGHEST)
    lose_all = jax.nn.sigmoid(-logits).T
    grad_logits = grad_log * lose_all - grad_inflow * keep * keep * lose / inflow
    grad_projected = jnp.concatenate([rows_first(grad_q), rows_first(grad_k), rows_first(grad_v)], axis=1)
    grad_persistent = jnp.concatenate([rows_first(grad_fixed_k), rows_first(grad_fixed_v)], axis=1)
    return grad_projected.astype(half), grad_logits.T, grad_persistent


def general_device(
    tokens,
    lengths,
    cotangent,
    norm_one,
    qkv_weight,
    decay_weight,
    decay_bias,
    persistent,
    out_weight,
    norm_two,
    gate_up,
    down_weight,
):
    sections, ctx_count, fsdp_count = (lax.axis_size(a) for a in ("section", "ctx", "fsdp"))
    section, ctx, fsdp = (lax.axis_index(a) for a in ("section", "ctx", "fsdp"))
    spread = ctx_count // fsdp_count
    rows, width = tokens.shape[2:]
    heads_here = decay_bias.shape[1]
    size = width // (heads_here * fsdp_count)
    inner = heads_here * size
    first = section == 0

    def own_batch(value):
        return lax.dynamic_index_in_dim(value, section, 0, False)[0]

    pairs = [(c * fsdp_count + f, f * ctx_count + c) for c in range(ctx_count) for f in range(fsdp_count)]

    def to_plane(value):
        return lax.ppermute(value, ("ctx", "fsdp"), pairs)

    def from_plane(value):
        return lax.ppermute(value, ("ctx", "fsdp"), [(b, a) for a, b in pairs])

    x_in = to_plane(own_batch(tokens))
    g_in = to_plane(own_batch(cotangent))
    length = to_plane(own_batch(lengths))[0]

    def both_layers(own):
        other = exchange(own, "section", 1)
        return jnp.where(first, own, other), jnp.where(first, other, own)

    small = jnp.concatenate(
        [
            norm_one[0],
            norm_two[0],
            decay_weight[0].reshape(-1),
            persistent[0].reshape(-1),
        ]
    )
    small = jnp.stack(both_layers(in_order([p[None] for p in gather_parts(small, "fsdp")], fsdp, 0)))
    cut = width // fsdp_count
    sizes = [cut, cut, decay_weight[0].size, persistent[0].size]
    edges = [0]
    for piece in sizes:
        edges.append(edges[-1] + piece)
    gains_one, gains_two, decays, fixeds = (small[:, :, a:b] for a, b in zip(edges[:-1], edges[1:]))
    gains_one = gains_one.reshape(2, width).astype(wide)
    gains_two = gains_two.reshape(2, width).astype(wide)
    head_count = heads_here * fsdp_count
    decays = lax.dynamic_slice_in_dim(decays.reshape(2, width, head_count), fsdp * heads_here, heads_here, 2)
    slots = persistent.shape[1]
    fixeds = fixeds.reshape(2, fsdp_count, slots, 2 * cut).transpose(0, 2, 1, 3).reshape(2, slots, 2, fsdp_count, inner)
    fixeds = lax.dynamic_index_in_dim(fixeds, fsdp, 3, False).reshape(2, slots, 2 * inner)
    biases = jnp.stack(both_layers(decay_bias[0])).astype(wide)
    qkvs = both_layers(columns_here(qkv_weight[0], 3, "fsdp"))
    outs = both_layers(out_weight[0])
    gate_ups = both_layers(columns_here(gate_up[0], 2, "fsdp"))
    downs = both_layers(down_weight[0])
    hidden = downs[0].shape[0]

    pieces = [(k * fsdp_count + (fsdp ^ r)) * rows + jnp.arange(rows) for k in range(spread) for r in range(fsdp_count)]
    all_positions = jnp.concatenate(pieces)
    groups = [[g * spread + k for k in range(spread)] for g in range(ctx_count // spread)]

    def whole(value):
        if spread == 1:
            return value
        return lax.all_gather(value, "ctx", axis_index_groups=groups, axis=0, tiled=True)

    def own_rows(value):
        if spread == 1:
            return value
        count = value.shape[0] // spread
        return lax.dynamic_slice_in_dim(value, (ctx % spread) * count, count, 0)

    def blocks_of(value):
        return list(value.reshape(fsdp_count, rows, value.shape[1]))

    def forward(layer, x, last):
        normed = jnp.concatenate(gather_parts(normalise(x, gains_one[layer]), "fsdp"))
        projected = dot(normed, qkvs[layer]).astype(half)
        logits = dot(normed, decays[layer]) + biases[layer]
        seen, seen_logits = whole(projected), whole(logits)
        combined = own_rows(mixer(seen, seen_logits, fixeds[layer], length, all_positions, size))
        middle = x + scatter_sum(blocks_of(dot(combined, outs[layer])), "fsdp")
        normed_two = jnp.concatenate(gather_parts(normalise(middle, gains_two[layer]), "fsdp"))
        gates = dot(normed_two, gate_ups[layer])
        activated = (jax.nn.silu(gates[:, :hidden]) * gates[:, hidden:]).astype(half)
        out = middle + scatter_sum(blocks_of(dot(activated, downs[layer])), "fsdp")
        return out.astype(half), (x, normed, seen, seen_logits, combined, middle, normed_two, gates, activated)

    def backward(layer, g_out, saved):
        x, normed, seen, seen_logits, combined, middle, normed_two, gates, activated = saved
        g_rows = jnp.concatenate(gather_parts(g_out, "fsdp"))
        grad_down = dot(activated, g_rows, (0, 0))
        g_activated = dot(g_rows, downs[layer], (1, 1))
        gate, up = gates[:, :hidden], gates[:, hidden:]
        sig = jax.nn.sigmoid(gate)
        g_up = g_activated * gate * sig
        g_gate = g_activated * up * sig * (1.0 + gate * (1.0 - sig))
        g_gates = jnp.concatenate([g_gate, g_up], axis=1).astype(half)
        grad_gate_up = dot(normed_two, g_gates, (0, 0))
        g_normed_two = scatter_sum(blocks_of(dot(g_gates, gate_ups[layer], (1, 1))), "fsdp")
        g_middle, grad_norm_two = normalise_back(middle, gains_two[layer], g_normed_two)
        g_middle = g_middle + g_out.astype(wide)
        g_branch = jnp.concatenate(gather_parts(g_middle.astype(half), "fsdp"))
        grad_out = dot(combined, g_branch, (0, 0))
        g_combined = whole(dot(g_branch, outs[layer], (1, 1)).astype(half))
        g_projected, g_logits, grad_fixed = mixer_back(
            seen, seen_logits, fixeds[layer], length, all_positions, size, g_combined
        )
        g_projected, g_logits = own_rows(g_projected), own_rows(g_logits)
        grad_fixed = jnp.where(ctx % spread == 0, grad_fixed, 0.0)
        grad_qkv = dot(normed, g_projected, (0, 0))
        grad_decay = dot(normed.astype(wide), g_logits, (0, 0))
        grad_bias = jnp.sum(g_logits, axis=0)
        g_normed = dot(g_projected, qkvs[layer], (1, 1)) + dot(g_logits, decays[layer].astype(wide), (1, 1))
        g_normed = scatter_sum(blocks_of(g_normed), "fsdp")
        g_x, grad_norm_one = normalise_back(x, gains_one[layer], g_normed)
        g_x = (g_x + g_middle).astype(half)
        large = (grad_qkv, grad_out, grad_gate_up, grad_down)
        return g_x, tuple(g.astype(half) for g in large), (grad_norm_one, grad_norm_two, grad_decay, grad_bias, grad_fixed)

    between, saved_first = forward(0, x_in.astype(wide), False)
    out, saved_second = forward(1, between.astype(wide), True)
    g_between, large_second, small_second = backward(1, g_in, saved_second)
    g_input, large_first, small_first = backward(0, g_between, saved_first)

    def reduced(from_first, from_second):
        received = exchange(jnp.where(first, from_second, from_first), "section", 1)
        own = jnp.where(first, from_first, from_second)
        own = (own.astype(wide) + received.astype(wide)).astype(half)
        return line_sum(own, "ctx")

    grad_qkv, grad_out, grad_gate_up, grad_down = (reduced(a, b) for a, b in zip(large_first, large_second))
    grad_qkv = rows_here(grad_qkv, 3, "fsdp")
    grad_gate_up = rows_here(grad_gate_up, 2, "fsdp")

    def small_whole(pieces):
        n_one, n_two, decay, bias, fixed = pieces
        decay_all = lax.dynamic_update_slice_in_dim(jnp.zeros((width, head_count), wide), decay, fsdp * heads_here, 1)
        bias_all = lax.dynamic_update_slice_in_dim(jnp.zeros((head_count,), wide), bias, fsdp * heads_here, 0)
        fixed_all = jnp.zeros((slots, 2, fsdp_count, inner), wide)
        fixed_all = lax.dynamic_update_slice_in_dim(fixed_all, fixed.reshape(slots, 2, 1, inner), fsdp, 2)
        return jnp.concatenate([n_one, n_two, decay_all.reshape(-1), fixed_all.reshape(-1), bias_all])

    tiny_first, tiny_second = small_whole(small_first), small_whole(small_second)
    tiny = lax.psum(jnp.stack([tiny_first, tiny_second]), ("section", "ctx", "fsdp"))
    tiny = lax.dynamic_index_in_dim(tiny, section, 0, False)
    grad_norm_one = lax.dynamic_slice_in_dim(tiny[:width], fsdp * cut, cut, 0)
    grad_norm_two = lax.dynamic_slice_in_dim(tiny[width : 2 * width], fsdp * cut, cut, 0)
    at = 2 * width
    grad_decay = lax.dynamic_slice_in_dim(tiny[at : at + width * head_count].reshape(width, head_count), fsdp * cut, cut, 0)
    at += width * head_count
    grad_fixed = tiny[at : at + slots * 2 * width].reshape(slots, 2 * width)
    grad_fixed = lax.dynamic_slice_in_dim(grad_fixed, fsdp * 2 * cut, 2 * cut, 1)
    at += slots * 2 * width
    grad_bias = lax.dynamic_slice_in_dim(tiny[at:], fsdp * heads_here, heads_here, 0)

    return (
        from_plane(out)[None, None],
        from_plane(g_input)[None, None],
        grad_norm_one[None],
        grad_qkv.astype(wide)[None],
        grad_decay[None],
        grad_bias[None],
        grad_fixed[None],
        grad_out.astype(wide)[None],
        grad_norm_two[None],
        grad_gate_up.astype(wide)[None],
        grad_down.astype(wide)[None],
    )


def solution(mesh):
    by_row = P("section", "fsdp", None)
    by_gain = P("section", "fsdp")
    by_token = P(None, "fsdp", "ctx", None)
    by_output = P("section", "fsdp", "ctx", None)
    by_slot = P("section", None, "fsdp")
    plane = mesh.shape["ctx"] == mesh.shape["fsdp"] == 4
    return jax.shard_map(
        plane_device if plane else general_device,
        mesh=mesh,
        in_specs=(
            by_token,
            P(None, "fsdp", None),
            by_token,
            by_gain,
            by_row,
            by_row,
            by_gain,
            by_slot,
            by_row,
            by_gain,
            by_row,
            by_row,
        ),
        out_specs=(
            by_output,
            by_output,
            by_gain,
            by_row,
            by_row,
            by_gain,
            by_slot,
            by_row,
            by_gain,
            by_row,
            by_row,
        ),
        check_vma=False,
    )
```

```python
import jax
import jax.numpy as jnp
from jax import lax
from jax.experimental import pallas as pl
from jax.experimental.pallas import tpu as pltpu
from jax.sharding import PartitionSpec as P

epsilon = 1e-05
negative = -1e30
wide = jnp.float32
half = jnp.bfloat16
LANES = 128
PAIR = 64
ROOM = {
    "mix_forward": 20,
    "mix_backward": 24,
    "feed_forward": 20,
    "feed_backward": 24,
    "grad_feed": 20,
    "grad_mix": 16,
    "assemble": 12,
    "pack_gates": 16,
    "spread": 12,
    "collect_feed": 12,
    "unpack_mix": 16,
}
vmem = pl.BlockSpec(memory_space=pltpu.VMEM)
smem = pl.BlockSpec(memory_space=pltpu.SMEM)
anywhere = pl.BlockSpec(memory_space=pl.ANY)


def mm(a, b):
    return lax.dot_general(a, b, (((1,), (0,)), ((), ())), preferred_element_type=wide)


def mm_nt(a, b):
    return lax.dot_general(a, b, (((1,), (1,)), ((), ())), preferred_element_type=wide)


def mm_tn(a, b):
    return lax.dot_general(a, b, (((0,), (0,)), ((), ())), preferred_element_type=wide)


def sig(v):
    return 1.0 / (1.0 + jnp.exp(-v))


def call(body, out_shape, in_specs, scratch, flops, moved, name):
    return pl.pallas_call(
        body,
        out_shape=out_shape,
        in_specs=in_specs,
        out_specs=jax.tree.map(lambda _: vmem, out_shape),
        scratch_shapes=scratch,
        compiler_params=pltpu.CompilerParams(vmem_limit_bytes=ROOM.get(name, 8) * 1024 * 1024),
        cost_estimate=pl.CostEstimate(flops=flops, bytes_accessed=moved, transcendentals=0),
        name=name,
    )


def shape(dims, kind=half):
    return jax.ShapeDtypeStruct(tuple(dims), kind)


def pack_heads(count, shard, place):
    rows, columns = shard.shape
    inner = columns // (3 * count)

    def body(place_ref, shard_ref, *outs):
        for r in range(count):
            target = place_ref[0] ^ r
            for kind in range(3):
                at = pl.multiple_of(kind * count * inner + target * inner, inner)
                outs[r][:, kind * inner : (kind + 1) * inner] = shard_ref[:, pl.ds(at, inner)]

    outs = [shape((rows, 3 * inner))] * count
    return call(body, outs, [smem, vmem], [], 0, 2 * shard.size * 2, "pack_heads")(place, shard)


def pack_gates(count, shard, place):
    rows, columns = shard.shape
    hidden = columns // 2
    mine = columns // count

    def body(place_ref, shard_ref, *rest):
        outs, mixed = rest[:count], rest[count]
        low = lax.broadcasted_iota(jnp.int32, (rows, LANES), 1) < PAIR
        for m in range(hidden // LANES):
            gate = shard_ref[:, m * LANES : (m + 1) * LANES].astype(wide)
            up = shard_ref[:, hidden + m * LANES : hidden + (m + 1) * LANES].astype(wide)
            even = jnp.where(low, gate, pltpu.roll(up, PAIR, 1))
            odd = jnp.where(low, pltpu.roll(gate, PAIR, 1), up)
            mixed[:, 2 * m * LANES : (2 * m + 1) * LANES] = even.astype(half)
            mixed[:, (2 * m + 1) * LANES : (2 * m + 2) * LANES] = odd.astype(half)
        for r in range(count):
            at = pl.multiple_of((place_ref[0] ^ r) * mine, LANES)
            outs[r][...] = mixed[:, pl.ds(at, mine)]

    outs = [shape((rows, mine))] * count
    scratch = [pltpu.VMEM((rows, columns), half)]
    return call(body, outs, [smem, vmem], scratch, 0, 2 * shard.size * 2, "pack_gates")(place, shard)


def assemble(place, parts):
    count = len(parts)
    rows, columns = parts[0].shape

    def body(place_ref, *refs):
        put_rows(refs[:count], refs[count], place_ref)

    outs = [shape((rows * count, columns))]
    moved = 4 * rows * count * columns
    return call(body, outs, [smem] + [vmem] * count, [], 0, moved, "assemble")(place, *parts)[0]


def fetch(place_ref, layer, mine, other, target, sems, span=None):
    rows, columns = mine.shape
    span = columns if span is None else span
    handles = []
    for k, at in enumerate(range(0, columns, span)):
        lanes = pl.ds(at, min(span, columns - at))
        where = target.at[pl.ds(0, rows), lanes]
        for own, source in ((True, mine), (False, other)):

            @pl.when((place_ref[1] == layer) == own)
            def _(source=source, lanes=lanes, where=where, k=k):
                pltpu.make_async_copy(source.at[pl.ds(0, rows), lanes], where, sems.at[k]).start()

        handles.append(pltpu.make_async_copy(mine.at[pl.ds(0, rows), lanes], where, sems.at[k]))
    return handles


def finish(handles):
    for handle in handles:
        handle.wait()


def put_rows(parts, target, place_ref):
    rows = parts[0].shape[0]
    for r, part in enumerate(parts):
        target[pl.ds(pl.multiple_of((place_ref[0] ^ r) * rows, rows), rows), :] = part[...]


def take_rows(source, outs, place_ref):
    rows = outs[0].shape[0]
    for r, out in enumerate(outs):
        out[...] = source[pl.ds(pl.multiple_of((place_ref[0] ^ r) * rows, rows), rows), :].astype(out.dtype)


def three_way(v):
    high = v.astype(half)
    rest = v - high.astype(wide)
    middle = rest.astype(half)
    return high, middle, (rest - middle.astype(wide)).astype(half)


def exact_sum(values, mask):
    return sum(mm(piece, mask) for piece in three_way(values))


def gate_lanes(logits, length):
    rows = logits.shape[1]
    at = lax.broadcasted_iota(jnp.int32, logits.shape, 1)
    starts = (at == 0) | (at == length)
    spill = jnp.log(1.0 + jnp.exp(-jnp.abs(logits)))
    log_keep = jnp.minimum(logits, 0.0) - spill
    keep = jnp.where(starts, 0.0, sig(logits))
    lose = jnp.where(starts, 1.0, sig(-logits))
    before = lax.broadcasted_iota(jnp.int32, (rows, rows), 0) <= lax.broadcasted_iota(jnp.int32, (rows, rows), 1)
    return log_keep, keep, lose, exact_sum(log_keep, before.astype(wide).astype(half))


def turned(values):
    return jnp.concatenate([values, jnp.zeros((LANES - values.shape[0], values.shape[1]), wide)], axis=0).T


def block_scores(i, block, head, size, inner, projected, fixed, total, total_t, inflow_t, length, scale):
    n = (i + 1) * block
    rows = slice(i * block, n)
    lanes = slice(head * size, (head + 1) * size)
    q = projected[rows, lanes]
    k = projected[0:n, inner + head * size : inner + (head + 1) * size]
    v = projected[0:n, 2 * inner + head * size : 2 * inner + (head + 1) * size]
    fixed_k = fixed[:, lanes]
    fixed_v = fixed[:, inner + head * size : inner + (head + 1) * size]
    scores = mm_nt(q, k) * scale
    fixed_scores = mm_nt(q, fixed_k) * scale
    at = i * block + lax.broadcasted_iota(jnp.int32, (block, 1), 0)
    begin = jnp.where(at >= length, length, 0)
    column = lax.broadcasted_iota(jnp.int32, (block, n), 1)
    allowed = (column <= at) & (column >= begin)
    masked = jnp.where(allowed, scores, negative)
    top = jnp.maximum(jnp.max(masked, axis=1, keepdims=True), jnp.max(fixed_scores, axis=1, keepdims=True))
    weights, fixed_weights = jnp.exp(masked - top), jnp.exp(fixed_scores - top)
    mass = 1.0 / (jnp.sum(weights, axis=1, keepdims=True) + jnp.sum(fixed_weights, axis=1, keepdims=True))
    weights, fixed_weights = weights * mass, fixed_weights * mass
    fall = jnp.exp(jnp.where(allowed, total[rows, head : head + 1] - total_t[head : head + 1, 0:n], negative))
    reach = scores * fall
    both = (weights + reach * inflow_t[head : head + 1, 0:n]).astype(half)
    return q, k, v, fixed_k, fixed_v, weights, fixed_weights, fall, reach, both


def mix_forward(layer, heads, size, place, parts, rows, gain, weights, decay, bias, fixed):
    count = len(parts)
    width = parts[0].shape[1]
    total_rows, inner = rows * count, heads * size
    scale = size ** (-0.5)
    block = rows

    def body(place_ref, *refs):
        parts_in, refs = refs[:count], refs[count:]
        (mine, other, o_mine, o_other), refs = refs[:4], refs[4:]
        (gain_ref, decay_ref, bias_ref, fixed_ref), refs = refs[:4], refs[4:]
        terms, refs = refs[:count], refs[count:]
        combined, normed, projected, logits_out, weight, out_weight, whole, sems = refs
        handles = fetch(place_ref, layer, mine, other, weight, sems, inner)
        out_handles = fetch(place_ref, layer, o_mine, o_other, out_weight, sems.at[pl.ds(3, 1)])
        for r, part in enumerate(parts_in):
            values = part[0:rows, :].astype(wide)
            root = lax.rsqrt(jnp.mean(values * values, axis=1, keepdims=True) + epsilon)
            here = pl.ds(pl.multiple_of((place_ref[0] ^ r) * rows, rows), rows)
            normed[here, :] = (values * root * gain_ref[...]).astype(half)
        length = place_ref[2]
        logits = mm_nt(decay_ref[...], normed[...]) + bias_ref[:, 0:1]
        logits_out[...] = logits
        log_keep, keep, lose, total_t = gate_lanes(logits, length)
        total = turned(total_t)
        inflow_t = jnp.sqrt(lose * (1.0 + keep))
        for kind in range(3):
            handles[kind].wait()
            lanes = slice(kind * inner, (kind + 1) * inner)
            projected[:, lanes] = mm(normed[...], weight[:, lanes]).astype(half)
        for head in range(heads):
            for i in range(count):
                q, k, v, fixed_k, fixed_v, soft, fixed_soft, fall, reach, both = block_scores(
                    i, block, head, size, inner, projected, fixed_ref, total, total_t, inflow_t, length, scale
                )
                mixed = mm(both, v) + mm(fixed_soft.astype(half), fixed_v)
                combined[i * block : (i + 1) * block, head * size : (head + 1) * size] = mixed.astype(half)
        finish(out_handles)
        whole[...] = mm(combined[...], out_weight[...])
        take_rows(whole, terms, place_ref)

    outs = [shape((rows, width), wide if r == 0 else half) for r in range(count)] + [
        shape((total_rows, inner)),
        shape((total_rows, width)),
        shape((total_rows, 3 * inner)),
        shape((16, total_rows), wide),
    ]
    scratch = [
        pltpu.VMEM((width, 3 * inner), half),
        pltpu.VMEM((inner, width), half),
        pltpu.VMEM((total_rows, width), wide),
        pltpu.SemaphoreType.DMA((4,)),
    ]
    specs = [smem] + [vmem] * count + [anywhere] * 4 + [vmem] * 4
    flops = 2 * total_rows * (width * 4 * inner + inner * total_rows * 2)
    moved = 2 * (width * 3 * inner + total_rows * (2 * width + 4 * inner))
    return call(body, outs, specs, scratch, flops, moved, "mix_forward")(
        place, *parts, *weights, gain, decay, bias, fixed
    )


def mix_backward(layer, heads, size, place, parts, weights, decay, fixed, projected, logits, normed, gain):
    count = len(parts)
    rows, width = parts[0].shape
    total_rows, inner = rows * count, heads * size
    scale = size ** (-0.5)
    block = rows

    def body(place_ref, *refs):
        parts_in, refs = refs[:count], refs[count:]
        (mine, other, o_mine, o_other), refs = refs[:4], refs[4:]
        decay_ref, fixed_ref, projected, logits_ref, normed_ref, gain_ref = refs[:6]
        refs = refs[6:]
        terms, refs = refs[:count], refs[count:]
        branch, g_projected, g_logits_out, g_fixed, g_gain, refs = refs[0], refs[1], refs[2], refs[3], refs[4], refs[5:]
        weight, out_weight, combined, g_k, g_v, pulled, pushed, whole, sems = refs
        out_handles = fetch(place_ref, layer, o_mine, o_other, out_weight, sems.at[pl.ds(1, 1)])
        handles = fetch(place_ref, layer, mine, other, weight, sems.at[pl.ds(0, 1)])
        put_rows(parts_in, branch, place_ref)
        length = place_ref[2]
        logits = logits_ref[...]
        log_keep, keep, lose, total_t = gate_lanes(logits, length)
        total = turned(total_t)
        inflow_t = jnp.sqrt(lose * (1.0 + keep))
        finish(out_handles)
        combined[...] = mm_nt(branch[...], out_weight[...]).astype(half)
        g_k[...] = jnp.zeros_like(g_k)
        g_v[...] = jnp.zeros_like(g_v)
        pulled[...] = jnp.zeros_like(pulled)
        pushed[...] = jnp.zeros_like(pushed)
        g_fixed[...] = jnp.zeros_like(g_fixed)
        for head in range(heads):
            lanes = slice(head * size, (head + 1) * size)
            for i in range(count):
                n = (i + 1) * block
                here = slice(i * block, n)
                q, k, v, fixed_k, fixed_v, weights, fixed_weights, fall, reach, both = block_scores(
                    i, block, head, size, inner, projected, fixed_ref, total, total_t, inflow_t, length, scale
                )
                grad = combined[here, lanes]
                g_both = mm_nt(grad, v)
                g_few = mm_nt(grad, fixed_v)
                delta = jnp.sum(weights * g_both, axis=1, keepdims=True) + jnp.sum(
                    fixed_weights * g_few, axis=1, keepdims=True
                )
                inflow_row = inflow_t[head : head + 1, 0:n]
                g_scores = (weights * (g_both - delta) + g_both * fall * inflow_row).astype(half)
                g_few_scores = (fixed_weights * (g_few - delta)).astype(half)
                g_projected[here, lanes] = ((mm(g_scores, k) + mm(g_few_scores, fixed_k)) * scale).astype(half)
                g_k[0:n, lanes] += mm_tn(g_scores, q)
                g_v[0:n, lanes] += mm_tn(both, grad)
                g_fixed[:, lanes] += mm_tn(g_few_scores, q) * scale
                g_fixed[:, inner + head * size : inner + (head + 1) * size] += mm_tn(fixed_weights.astype(half), grad)
                pull = g_both * reach
                pulled[head : head + 1, 0:n] += jnp.sum(pull, axis=0, keepdims=True)
                pushed[here, head : head + 1] = jnp.sum(pull * inflow_row, axis=1, keepdims=True)
        g_projected[:, inner : 2 * inner] = (g_k[...] * scale).astype(half)
        g_projected[:, 2 * inner : 3 * inner] = g_v[...].astype(half)
        g_inflow = pulled[...]
        g_total = pushed[...].T[0:16] - inflow_t * g_inflow
        after = lax.broadcasted_iota(jnp.int32, (total_rows, total_rows), 0) >= lax.broadcasted_iota(
            jnp.int32, (total_rows, total_rows), 1
        )
        g_log = exact_sum(g_total, after.astype(wide).astype(half))
        g_logits = g_log * sig(-logits) - g_inflow * keep * keep * lose / inflow_t
        row = lax.broadcasted_iota(jnp.int32, g_logits.shape, 0)
        g_logits = jnp.where(row < heads, g_logits, 0.0)
        g_logits_out[...] = g_logits
        finish(handles)
        high, middle, low = three_way(g_logits)
        whole[...] = (
            mm_nt(g_projected[...], weight[...]) + mm_tn(high, decay_ref[...]) + mm_tn(middle, decay_ref[...])
        )
        pulls = jnp.sum(whole[...] * normed_ref[...].astype(wide), axis=0, keepdims=True) / gain_ref[...]
        g_gain[...] = jnp.broadcast_to(pulls, g_gain.shape)
        take_rows(whole, terms, place_ref)

    outs = [shape((rows, width), wide if r == 0 else half) for r in range(count)] + [
        shape((total_rows, width)),
        shape((total_rows, 3 * inner)),
        shape((16, total_rows), wide),
        shape((fixed.shape[0], 2 * inner), wide),
        shape((8, width), wide),
    ]
    scratch = [
        pltpu.VMEM((width, 3 * inner), half),
        pltpu.VMEM((inner, width), half),
        pltpu.VMEM((total_rows, inner), half),
        pltpu.VMEM((total_rows, inner), wide),
        pltpu.VMEM((total_rows, inner), wide),
        pltpu.VMEM((16, total_rows), wide),
        pltpu.VMEM((total_rows, LANES), wide),
        pltpu.VMEM((total_rows, width), wide),
        pltpu.SemaphoreType.DMA((2,)),
    ]
    specs = [smem] + [vmem] * count + [anywhere] * 4 + [vmem] * 6
    flops = 2 * total_rows * (width * 4 * inner + inner * total_rows * 5)
    moved = 2 * (width * 4 * inner + total_rows * (5 * width + 6 * inner))
    return call(body, outs, specs, scratch, flops, moved, "mix_backward")(
        place, *parts, *weights, decay, fixed, projected, logits, normed, gain
    )


def gates_of(tile_pair):
    rows, columns = tile_pair.shape
    if columns == LANES:
        return tile_pair[:, :PAIR], pltpu.roll(tile_pair, PAIR, 1)[:, :PAIR]
    first, second = tile_pair[:, :LANES], tile_pair[:, LANES:]
    low = lax.broadcasted_iota(jnp.int32, (rows, LANES), 1) < PAIR
    gate = jnp.where(low, first, pltpu.roll(second, PAIR, 1))
    up = jnp.where(low, pltpu.roll(first, PAIR, 1), second)
    return gate, up


def tiles_of(gate, up):
    rows, columns = gate.shape
    if columns == PAIR:
        return jnp.concatenate([gate, up], axis=1)
    low = lax.broadcasted_iota(jnp.int32, (rows, LANES), 1) < PAIR
    first = jnp.where(low, gate, pltpu.roll(up, PAIR, 1))
    second = jnp.where(low, pltpu.roll(gate, PAIR, 1), up)
    return jnp.concatenate([first, second], axis=1)


def tile_ranges(columns):
    return [(at, min(2 * LANES, columns - at)) for at in range(0, columns, 2 * LANES)]


def feed_forward(layer, place, parts, weights):
    count = len(parts)
    rows, width = parts[0].shape
    total_rows = rows * count
    columns, hidden = weights[0].shape[1], weights[2].shape[0]
    padded = -(-hidden // LANES) * LANES

    def body(place_ref, *refs):
        parts_in, refs = refs[:count], refs[count:]
        (mine, other, d_mine, d_other), refs = refs[:4], refs[4:]
        terms, normed, refs = refs[:count], refs[count], refs[count + 1 :]
        weight, down, active, whole, sems = refs
        handles = fetch(place_ref, layer, mine, other, weight, sems.at[pl.ds(0, 1)])
        down_handles = fetch(place_ref, layer, d_mine, d_other, down, sems.at[pl.ds(1, 1)])
        put_rows(parts_in, normed, place_ref)
        if padded != hidden:
            down[hidden:, :] = jnp.zeros((padded - hidden, width), half)
            active[:, padded - LANES :] = jnp.zeros((total_rows, LANES), half)
        finish(handles)
        for at, size in tile_ranges(columns):
            gate, up = gates_of(mm(normed[...], weight[:, at : at + size]))
            active[:, at // 2 : (at + size) // 2] = (gate * sig(gate) * up).astype(half)
        finish(down_handles)
        whole[...] = mm(active[...], down[...])
        take_rows(whole, terms, place_ref)

    outs = [shape((rows, width), wide if r == 0 else half) for r in range(count)] + [shape((total_rows, width))]
    scratch = [
        pltpu.VMEM((width, columns), half),
        pltpu.VMEM((padded, width), half),
        pltpu.VMEM((total_rows, padded), half),
        pltpu.VMEM((total_rows, width), wide),
        pltpu.SemaphoreType.DMA((2,)),
    ]
    specs = [smem] + [vmem] * count + [anywhere] * 4
    flops = 2 * total_rows * width * (columns + hidden)
    moved = 2 * (width * (columns + hidden) + total_rows * 4 * width)
    return call(body, outs, specs, scratch, flops, moved, "feed_forward")(
        place, *parts, *weights
    )


def feed_backward(layer, place, parts, normed_two, gain, weights):
    count = len(parts)
    rows, width = parts[0].shape
    total_rows = rows * count
    columns, hidden = weights[0].shape[1], weights[2].shape[0]
    padded = -(-hidden // LANES) * LANES

    def body(place_ref, *refs):
        parts_in, refs = refs[:count], refs[count:]
        normed, gain_ref, refs = refs[0], refs[1], refs[2:]
        (mine, other, d_mine, d_other), refs = refs[:4], refs[4:]
        terms, refs = refs[:count], refs[count:]
        g_out, g_gates, active, g_gain, refs = refs[0], refs[1], refs[2], refs[3], refs[4:]
        weight, down, whole, sems = refs
        handles = fetch(place_ref, layer, mine, other, weight, sems.at[pl.ds(0, 1)])
        down_handles = fetch(place_ref, layer, d_mine, d_other, down, sems.at[pl.ds(1, 1)])
        put_rows(parts_in, g_out, place_ref)
        finish(handles)
        finish(down_handles)
        for at, size in tile_ranges(columns):
            inside = slice(at // 2, (at + size) // 2)
            gate, up = gates_of(mm(normed[...], weight[:, at : at + size]))
            g_active = mm_nt(g_out[...], down[inside, :])
            open_ = sig(gate)
            lit = gate * open_
            active[:, inside] = (lit * up).astype(half)
            g_up = g_active * lit
            g_gate = g_active * up * (open_ * (1.0 + gate - lit))
            g_gates[:, at : at + size] = tiles_of(g_gate, g_up).astype(half)
        whole[...] = mm_nt(g_gates[...], weight[...])
        pulls = jnp.sum(whole[...] * normed[...].astype(wide), axis=0, keepdims=True) / gain_ref[...]
        g_gain[...] = jnp.broadcast_to(pulls, g_gain.shape)
        take_rows(whole, terms, place_ref)

    outs = [shape((rows, width), wide if r == 0 else half) for r in range(count)] + [
        shape((total_rows, width)),
        shape((total_rows, columns)),
        shape((total_rows, hidden)),
        shape((8, width), wide),
    ]
    scratch = [
        pltpu.VMEM((width, columns), half),
        pltpu.VMEM((hidden, width), half),
        pltpu.VMEM((total_rows, width), wide),
        pltpu.SemaphoreType.DMA((2,)),
    ]
    specs = [smem] + [vmem] * (count + 2) + [anywhere] * 4
    flops = 2 * total_rows * width * (2 * columns + hidden)
    moved = 2 * (width * (columns + hidden) + total_rows * (6 * width + columns + hidden))
    return call(body, outs, specs, scratch, flops, moved, "feed_backward")(
        place, *parts, normed_two, gain, *weights
    )


def pack_small(norm_one, norm_two, decay, bias, persistent, lengths):
    cut, heads_all = decay.shape
    slots, columns = persistent.shape
    heads = bias.shape[1]
    lanes = cut // LANES
    total = 16 * (1 + lanes + columns // LANES)

    batches = lengths.shape[0]

    def body(lengths_ref, one_ref, two_ref, decay_ref, bias_ref, fixed_ref, out):
        rows = [ref[0:1, b * LANES : (b + 1) * LANES].astype(wide) for ref in (one_ref, two_ref) for b in range(lanes)]
        rows.append(jnp.concatenate([bias_ref[...].astype(wide), jnp.zeros((1, LANES - heads), wide)], axis=1))
        for m in range(batches):
            for part in (lengths_ref[m] // 64, lengths_ref[m] % 64):
                rows.append(jnp.full((1, LANES), part.astype(wide)))
        rows.append(jnp.zeros((16 - len(rows), LANES), wide))
        out[0:16, :] = jnp.concatenate(rows, axis=0).astype(half)
        padded = jnp.concatenate([decay_ref[...].astype(wide), jnp.zeros((cut, LANES - heads_all), wide)], axis=1).T
        for b in range(lanes):
            out[16 * (1 + b) : 16 * (2 + b), :] = padded[0:16, b * LANES : (b + 1) * LANES].astype(half)
        for c in range(columns // LANES):
            at = 16 * (1 + lanes + c)
            out[at : at + slots, :] = fixed_ref[:, c * LANES : (c + 1) * LANES]

    return call(body, [shape((total, LANES))], [smem] + [vmem] * 5, [], 0, 1 << 17, "pack_small")(
        lengths, norm_one, norm_two, decay, bias, persistent
    )[0]


def beside(rows, mine, other):
    height, width = rows.shape
    groups = 2 * mine.shape[0] // 16
    across = width // LANES
    below = 16 * -(-groups // across)

    def body(rows_ref, mine_ref, other_ref, out):
        out[0:height, :] = rows_ref[...]
        out[height:, :] = jnp.zeros((below, width), half)
        for g in range(groups):
            ref, at = (mine_ref, g) if g < groups // 2 else (other_ref, g - groups // 2)
            spot = (height + 16 * (g // across), LANES * (g % across))
            out[spot[0] : spot[0] + 16, spot[1] : spot[1] + LANES] = ref[16 * at : 16 * at + 16, :]

    outs = [shape((height + below, width))]
    return call(body, outs, [vmem] * 3, [], 0, 1 << 20, "beside")(rows, mine, other)[0]


def turn_bias(row):
    at = lax.broadcasted_iota(jnp.int32, (16, LANES), 0) == lax.broadcasted_iota(jnp.int32, (16, LANES), 1)
    return jnp.broadcast_to(jnp.sum(jnp.where(at, row, 0.0), axis=1, keepdims=True), (16, LANES))


def unpack_small(heads, slots, height, rows, place, parts):
    count = len(parts)
    width = parts[0].shape[1]
    cut = width // count
    lanes = cut // LANES
    across = width // LANES
    inner = heads * LANES

    def body(place_ref, *refs):
        ins, outs, length, held = refs[:count], refs[count:-2], refs[-2], refs[-1]
        f = place_ref[0]
        for r, part in enumerate(ins):
            for k in range(2):
                layer = place_ref[1] if k == 0 else 1 - place_ref[1]
                for g in range(rows // 16):
                    at = k * (rows // 16) + g
                    top, left = height + 16 * (at // across), LANES * (at % across)
                    held[layer, f ^ r, 16 * g : 16 * g + 16, :] = part[top : top + 16, left : left + LANES].astype(wide)
        at = 2 * lanes + 1 + 2 * place_ref[1]
        found = held[place_ref[1], place_ref[2], pl.ds(at, 2), :]
        length[...] = jnp.broadcast_to(found[0:1] * 64.0 + found[1:2], length.shape).astype(jnp.int32)
        for layer in range(2):
            one, two, decay, bias, fixed = outs[5 * layer : 5 * layer + 5]
            for t in range(count):
                for b in range(lanes):
                    at = t * cut + b * LANES
                    one[0:1, at : at + LANES] = held[layer, t, b : b + 1, :]
                    two[0:1, at : at + LANES] = held[layer, t, lanes + b : lanes + b + 1, :]
                    group = held[layer, t, 16 * (1 + b) : 16 * (2 + b), :]
                    row = lax.broadcasted_iota(jnp.int32, (16, LANES), 0)
                    mine = [
                        jnp.sum(jnp.where(row == f * heads + h, group, 0.0), axis=0, keepdims=True) for h in range(heads)
                    ]
                    mine.append(jnp.zeros((16 - heads, LANES), wide))
                    decay[:, at : at + LANES] = jnp.concatenate(mine, axis=0).astype(half)
            bias[...] = turn_bias(held[layer, f, 2 * lanes : 2 * lanes + 1, :])
            for kind in range(2):
                source = kind * (count // 2) + f // 2
                for h in range(heads):
                    at = pl.multiple_of(16 * (1 + lanes + (f % 2) * heads + h), 16)
                    lane = kind * inner + h * LANES
                    fixed[:, lane : lane + LANES] = held[layer, source, pl.ds(at, slots), :].astype(half)

    outs = [
        shape((1, width), wide),
        shape((1, width), wide),
        shape((16, width)),
        shape((16, LANES), wide),
        shape((slots, 2 * inner)),
    ] * 2 + [shape((8, LANES), jnp.int32)]
    scratch = [pltpu.VMEM((2, count, rows, LANES), wide)]
    made = call(body, outs, [smem] + [vmem] * count, scratch, 0, 1 << 20, "unpack_small")(place, *parts)
    return [list(pair) for pair in zip(made[:5], made[5:10])], made[10][0, 0]


def join_forward(rounded, terms, residual, gain):
    dims = terms[0].shape

    def body(*refs):
        count = len(terms)
        residual_ref, refs_in = refs[count], refs[:count]
        total = residual_ref[...].astype(wide)
        for ref in refs_in:
            total = total + ref[...].astype(wide)
        if gain is None:
            refs[count + 1][...] = total.astype(half)
            return
        gain_ref, out, normed = refs[count + 1 :]
        if rounded:
            total = total.astype(half).astype(wide)
        out[...] = total.astype(out.dtype)
        scale = lax.rsqrt(jnp.mean(total * total, axis=1, keepdims=True) + epsilon)
        normed[...] = (total * scale * gain_ref[...]).astype(half)

    outs = [shape(dims, half if rounded else wide), shape(dims)]
    inputs = [*terms, residual, gain]
    if gain is None:
        outs, inputs = [shape(dims)], inputs[:-1]
    return call(body, outs, [vmem] * len(inputs), [], 0, dims[0] * dims[1] * 20, "join_forward")(*inputs)


def join_backward(terms, values, gain, onward):
    dims = terms[0].shape

    def body(*refs):
        count = len(terms)
        values_ref, gain_ref, onward_ref, out, rounded = refs[count:]
        grad = refs[0][...].astype(wide)
        for ref in refs[1:count]:
            grad = grad + ref[...].astype(wide)
        v = values_ref[...].astype(wide)
        scale = lax.rsqrt(jnp.mean(v * v, axis=1, keepdims=True) + epsilon)
        unit = v * scale
        scaled = grad * gain_ref[...]
        through = scale * (scaled - unit * jnp.mean(scaled * unit, axis=1, keepdims=True))
        total = onward_ref[...].astype(wide) + through
        out[...] = total
        rounded[...] = total.astype(half)

    outs = [shape(dims, wide), shape(dims)]
    inputs = [*terms, values, gain, onward]
    return call(body, outs, [vmem] * len(inputs), [], 0, dims[0] * dims[1] * 24, "join_backward")(*inputs)


SMALL = 16


def lane_half(source, target, which, count):
    for t in range(count):
        at = pl.multiple_of(t * 2 * LANES + which * LANES, LANES)
        target[:, t * LANES : (t + 1) * LANES] = source[:, pl.ds(at, LANES)]


STRIPS = 4


def strip_of(columns):
    return SMALL * -(-(columns + SMALL) // (SMALL * STRIPS))


def packer(packed):
    def put(at, value):
        packed[at : at + value.shape[0], :] = value.astype(half)

    return put


def strip_packer(packed, strip, chunk):
    def put(t, at, value):
        done = 0
        while done < value.shape[0]:
            k, row = divmod(at + done, strip)
            size = min(value.shape[0] - done, strip - row)
            where = k * chunk + t * strip + row
            packed[where : where + size, :] = value[done : done + size].astype(half)
            done += size

    return put


def small_rows(rows):
    found = jnp.concatenate(rows, axis=0)
    return jnp.concatenate([found, jnp.zeros((SMALL - found.shape[0], LANES), wide)], axis=0)


def grad_call(body, chunks, total, inputs, scratch, flops, name):
    outs = [shape((total, LANES))] + [shape((b - a, LANES)) for a, b in split_rows(total, chunks)]
    scratch = scratch + [pltpu.VMEM((total, LANES), half)]
    moved = sum(v.size * v.dtype.itemsize for v in inputs) + total * LANES * 4
    return call(body, outs, [smem] + [vmem] * (len(inputs) - 1), scratch, flops, moved, name)(*inputs)


def grad_feed(chunks, count, place, normed, g_gates, active, g_out, g_gain):
    total_rows, width = normed.shape
    columns, hidden = g_gates.shape[1], active.shape[1]
    tiles = columns // LANES
    strip = strip_of(columns)
    chunk = count * strip + hidden
    side = width // 2

    def body(place_ref, normed_ref, gates_ref, active_ref, g_out_ref, gain_ref, *refs):
        sent, outs, left, packed = refs[0], refs[1:-2], refs[-2], refs[-1]
        for turn in range(2):
            which = 1 - place_ref[1] if turn == 0 else place_ref[1]
            packed_here = sent if turn == 0 else packed
            put, put_row = packer(packed_here), strip_packer(packed_here, strip, chunk)
            lane_half(normed_ref, left, which, count)
            turned = left[...].T
            for at in range(0, columns, 2 * LANES):
                size = min(2 * LANES, columns - at)
                tile = mm(turned, gates_ref[:, at : at + size])
                for t in range(count):
                    for c in range(size // LANES):
                        put_row(t, at + c * LANES, tile[t * LANES : (t + 1) * LANES, c * LANES : (c + 1) * LANES])
            for t in range(count):
                at = pl.multiple_of(t * 2 * LANES + which * LANES, LANES)
                rest = STRIPS * strip - columns - SMALL
                put_row(t, columns, small_rows([gain_ref[0:1, pl.ds(at, LANES)]]))
                put_row(t, columns + SMALL, jnp.zeros((rest, LANES), wide))
            active_t = active_ref[...].T
            for c in range(0, side // LANES, 2):
                at = pl.multiple_of(which * side + c * LANES, LANES)
                tile = mm(active_t, g_out_ref[:, pl.ds(at, 2 * LANES)])
                put(c * chunk + count * strip, tile[:, :LANES])
                put((c + 1) * chunk + count * strip, tile[:, LANES:])
        chunk_out(packed, outs)

    inputs = [place, normed, g_gates, active, g_out, g_gain]
    scratch = [pltpu.VMEM((total_rows, side), half)]
    flops = total_rows * width * (columns + hidden)
    return grad_call(body, chunks, STRIPS * chunk, inputs, scratch, flops, "grad_feed")


def grad_mix(chunks, total, count, place, normed, g_projected, combined, branch, g_logits, g_gain, g_fixed):
    total_rows, width = normed.shape
    columns, inner = g_projected.shape[1], combined.shape[1]
    heads = inner // LANES
    slots = g_fixed.shape[0]
    block = columns + SMALL + slots
    side = width // 2

    def body(place_ref, normed_ref, proj_ref, comb_ref, branch_ref, logits_ref, gain_ref, fixed_ref, *refs):
        sent, outs, left, packed = refs[0], refs[1:-2], refs[-2], refs[-1]
        for turn in range(2):
            which = 1 - place_ref[1] if turn == 0 else place_ref[1]
            put = packer(sent if turn == 0 else packed)
            lane_half(normed_ref, left, which, count)
            turned = left[...].T
            for at in range(0, columns, 2 * LANES):
                tile = mm(turned, proj_ref[:, at : at + 2 * LANES])
                for t in range(count):
                    for c in range(2):
                        put(t * block + at + c * LANES, tile[t * LANES : (t + 1) * LANES, c * LANES : (c + 1) * LANES])
            logits = logits_ref[...]
            decay = sum(mm(piece, left[...]) for piece in three_way(logits)[:2])
            near = pl.multiple_of(which * LANES, LANES)
            for t in range(count):
                at = pl.multiple_of(t * 2 * LANES + which * LANES, LANES)
                rows = [decay[0:heads, t * LANES : (t + 1) * LANES], gain_ref[0:1, pl.ds(at, LANES)]]
                put(t * block + columns, small_rows(rows))
                keys_here = (place_ref[0] // 2 == t).astype(wide)
                values_here = (place_ref[0] // 2 + 2 == t).astype(wide)
                fixed = fixed_ref[:, pl.ds(near, LANES)] * keys_here
                fixed = fixed + fixed_ref[:, pl.ds(pl.multiple_of(inner + near, LANES), LANES)] * values_here
                put(t * block + columns + SMALL, fixed)
            comb_t = comb_ref[:, pl.ds(near, LANES)].T
            for c in range(0, width // LANES, 2):
                tile = mm(comb_t, branch_ref[:, c * LANES : (c + 2) * LANES])
                put(count * block + c * LANES, tile[:, :LANES])
                put(count * block + (c + 1) * LANES, tile[:, LANES:])
            put(count * block + width, jnp.broadcast_to(jnp.sum(logits, axis=1, keepdims=True), (SMALL, LANES)))
            (sent if turn == 0 else packed)[count * block + width + SMALL :, :] = jnp.zeros(
                (total - count * block - width - SMALL, LANES), half
            )
        chunk_out(packed, outs)

    inputs = [place, normed, g_projected, combined, branch, g_logits, g_gain, g_fixed]
    scratch = [pltpu.VMEM((total_rows, side), half)]
    flops = total_rows * width * (columns + inner)
    return grad_call(body, chunks, total, inputs, scratch, flops, "grad_mix")


def split_rows(total, chunks):
    units = total // SMALL
    edges = [SMALL * (units * k // chunks) for k in range(chunks)] + [total]
    return list(zip(edges[:-1], edges[1:]))


def chunk_out(whole, outs):
    at = 0
    for out in outs:
        out[...] = whole[at : at + out.shape[0], :]
        at += out.shape[0]


def spread(count, block, place, chunks, add=False):
    total = sum(chunk.shape[0] for chunk, _ in chunks)

    def body(place_ref, *refs):
        ins, outs, whole = refs[: 2 * len(chunks)], refs[2 * len(chunks) : -1], refs[-1]
        at = 0
        if add:
            for one, two in zip(ins[0::2], ins[1::2]):
                whole[at : at + one.shape[0], :] = (one[...].astype(wide) + two[...].astype(wide)).astype(half)
                at += one.shape[0]
        for inner in range(0 if add else 2):

            @pl.when(place_ref[3] == inner)
            def _(inner=inner):
                at = 0
                for chunk in ins[1 - inner :: 2]:
                    whole[at : at + chunk.shape[0], :] = chunk[...]
                    at += chunk.shape[0]

        take_rows(whole, outs[:count], place_ref)
        outs[count][...] = whole[count * block :, :]

    outs = [shape((block, LANES))] * count + [shape((total - count * block, LANES))]
    scratch = [pltpu.VMEM((total, LANES), half)]
    flat = [piece for pair in chunks for piece in pair]
    return call(body, outs, [smem] + [vmem] * len(flat), scratch, 0, total * 768, "spread")(place, *flat)


def spread_strips(count, strip, place, chunks):
    chunk = chunks[0][0].shape[0]
    own = chunk - count * strip
    many = len(chunks)

    def body(place_ref, *refs):
        ins, outs = refs[: 2 * many], refs[2 * many :]
        for inner in range(2):

            @pl.when(place_ref[3] == inner)
            def _(inner=inner):
                for k, ref in enumerate(ins[1 - inner :: 2]):
                    for r in range(count):
                        at = pl.multiple_of((place_ref[0] ^ r) * strip, SMALL)
                        outs[r][k * strip : (k + 1) * strip, :] = ref[pl.ds(at, strip), :]
                    outs[count][k * own : (k + 1) * own, :] = ref[count * strip :, :]

    outs = [shape((many * strip, LANES))] * count + [shape((many * own, LANES))]
    flat = [piece for pair in chunks for piece in pair]
    return call(body, outs, [smem] + [vmem] * len(flat), [], 0, many * chunk * 768, "spread")(place, *flat)


def collect_feed(columns, place, sets):
    count = len(sets[0][0])
    strip = strip_of(columns)
    own = sum(local.shape[0] for _, local in sets)
    total = count * columns + SMALL + own
    flat = [piece for parts, local in sets for piece in (*parts, local)]

    def body(place_ref, *refs):
        ins, whole = refs[: len(flat)], refs[-1]
        first, below = 0, count * columns + SMALL
        small = jnp.zeros((SMALL, LANES), wide)
        for number, (parts, local) in enumerate(sets):
            here = ins[number * (count + 1) : (number + 1) * (count + 1)]
            many = parts[0].shape[0] // strip
            for k in range(many):
                row = (first + k) * strip
                size = min(strip, columns - row)
                for r in range(count):
                    at = pl.multiple_of((place_ref[0] ^ r) * columns + row, SMALL)
                    whole[pl.ds(at, size), :] = here[r][k * strip : k * strip + size, :]
                    if size < strip:
                        small = small + here[r][k * strip + size : k * strip + size + SMALL, :].astype(wide)
            first += many
            whole[below : below + local.shape[0], :] = here[count][...]
            below += local.shape[0]
        whole[count * columns : count * columns + SMALL, :] = small.astype(half)

    outs = [shape((total, LANES))]
    return call(body, outs, [smem] + [vmem] * len(flat), [], 0, total * 512, "collect_feed")(place, *flat)


def collect_mix(chunks, heads, total, place, parts, local):
    count = len(parts)
    slots = parts[0].shape[0] % (3 * heads * LANES) - SMALL
    columns = parts[0].shape[0] - SMALL - slots
    filled = count * columns + SMALL + 2 * slots + local.shape[0]

    def body(place_ref, *refs):
        parts_in, local_ref, outs, whole, few = refs[:count], refs[count], refs[count + 1 : -2], refs[-2], refs[-1]
        for r, part in enumerate(parts_in):
            source = place_ref[0] ^ r
            at = pl.multiple_of(source * columns, columns)
            whole[pl.ds(at, columns), :] = part[0:columns, :]
            few[pl.ds(source, 1)] = part[columns:, :].astype(wide)[None]
        base = count * columns
        decay = [few[t, 0:heads, :] for t in range(count)]
        gain = sum(few[t, heads : heads + 1, :] for t in range(count))
        whole[base : base + SMALL, :] = small_rows(decay + [gain]).astype(half)
        near = (place_ref[0] % 2) * 2
        for k in range(2):
            at = base + SMALL + k * slots
            whole[at : at + slots, :] = few[near + k, SMALL:, :].astype(half)
        whole[base + SMALL + 2 * slots : filled, :] = local_ref[...]
        whole[filled:, :] = jnp.zeros((total - filled, LANES), half)
        chunk_out(whole, outs)

    outs = [shape((b - a, LANES)) for a, b in split_rows(total, chunks)]
    scratch = [pltpu.VMEM((total, LANES), half), pltpu.VMEM((count, SMALL + slots, LANES), wide)]
    return call(body, outs, [smem] + [vmem] * (count + 1), scratch, 0, total * 512, "collect_mix")(place, *parts, local)


def gather_halves(place_ref, ins, halves, sems, edges):
    chunks = len(edges) - 1
    handles = []
    for side in range(2):
        for c in range(chunks):
            spot = place_ref[1] if side == 0 else 1 - place_ref[1]
            where = halves.at[spot, pl.ds(edges[c], edges[c + 1] - edges[c])]
            sem = sems.at[side * chunks + c]
            for layer in range(2):
                source = ins[layer * 2 * chunks + side * chunks + c]

                @pl.when(place_ref[1] == layer)
                def _(source=source, where=where, sem=sem):
                    pltpu.make_async_copy(source, where, sem).start()

            handles.append(pltpu.make_async_copy(ins[side * chunks + c], where, sem))
    finish(handles)


def unpack(body, totals, out_shape, place, name):
    chunks = len(totals[0][0])
    edges = [0]
    for chunk in totals[0][0]:
        edges.append(edges[-1] + chunk.shape[0])

    def whole_body(place_ref, *refs):
        ins, outs, halves, sems = refs[: 4 * chunks], refs[4 * chunks : -2], refs[-2], refs[-1]
        gather_halves(place_ref, ins, halves, sems, edges)
        body(place_ref, halves, *outs)

    inputs = [piece for layer in totals for side in layer for piece in side]
    scratch = [pltpu.VMEM((2, edges[-1], LANES), half), pltpu.SemaphoreType.DMA((2 * chunks,))]
    moved = sum(o.size * 4 for o in out_shape) + 4 * edges[-1] * LANES
    return call(whole_body, out_shape, [smem] + [anywhere] * len(inputs), scratch, 0, moved, name)(place, *inputs)


def unpack_feed(count, columns, hidden, width, totals, place):
    part = width // count
    side = width // 2
    chunks = len(totals[0][0])
    edges = [0]
    for chunk in totals[0][0]:
        edges.append(edges[-1] + chunk.shape[0])
    steps = 4
    span = count * columns // steps
    tiles = span // LANES

    def body(place_ref, *refs):
        ins, (gate_up, down, gain), halves, sems = refs[: 4 * chunks], refs[4 * chunks : -2], refs[-2], refs[-1]
        step = pl.program_id(0)

        @pl.when(step == 0)
        def _():
            gather_halves(place_ref, ins, halves, sems, edges)
            base = count * columns
            for h in range(2):
                gain[0:1, h * LANES : (h + 1) * LANES] = halves[h, base : base + SMALL, :].astype(wide)[0:1]

        low = lax.broadcasted_iota(jnp.int32, (LANES, LANES), 1) < PAIR
        for is_up in range(2):

            @pl.when(step // 2 == is_up)
            def _(is_up=is_up):
                for h in range(2):
                    for m in range(tiles):
                        at = pl.multiple_of((step % 2) * 2 * span + 2 * m * LANES, LANES)
                        even = halves[h, pl.ds(at, LANES), :].astype(wide)
                        odd = halves[h, pl.ds(at + LANES, LANES), :].astype(wide)
                        if is_up:
                            value = jnp.where(low, pltpu.roll(even, PAIR, 1), odd)
                        else:
                            value = jnp.where(low, even, pltpu.roll(odd, PAIR, 1))
                        gate_up[h * LANES : (h + 1) * LANES, m * LANES : (m + 1) * LANES] = value

        base = count * columns + SMALL
        for c in range(2):
            at = pl.multiple_of(base + ((step % 2) * 2 + c) * hidden, SMALL)
            down[:, c * LANES : (c + 1) * LANES] = halves[step // 2, pl.ds(at, hidden), :].astype(wide)

    outs = [shape((part, count * columns), wide), shape((hidden, width), wide), shape((1, part), wide)]
    inputs = [piece for layer in totals for half_side in layer for piece in half_side]
    moved = sum(o.size * 4 for o in outs) + 4 * edges[-1] * LANES
    return pl.pallas_call(
        body,
        grid=(steps,),
        out_shape=outs,
        in_specs=[smem] + [anywhere] * len(inputs),
        out_specs=[
            pl.BlockSpec((part, span), lambda i: (0, i)),
            pl.BlockSpec((hidden, width // steps), lambda i: (0, i)),
            pl.BlockSpec((1, part), lambda i: (0, 0)),
        ],
        scratch_shapes=[pltpu.VMEM((2, edges[-1], LANES), half), pltpu.SemaphoreType.DMA((2 * chunks,))],
        compiler_params=pltpu.CompilerParams(vmem_limit_bytes=16 * 1024 * 1024),
        cost_estimate=pl.CostEstimate(flops=0, bytes_accessed=moved, transcendentals=0),
        name="unpack_feed",
    )(place, *inputs)


def unpack_mix(count, heads, slots, width, totals, place):
    part = width // count
    inner = heads * LANES
    columns = 3 * inner

    def body(place_ref, halves, qkv, out, gain, decay, bias, fixed):
        for h in range(2):
            rows = slice(h * LANES, (h + 1) * LANES)
            for t in range(count):
                for kind in range(3):
                    for head in range(heads):
                        source = t * columns + kind * inner + head * LANES
                        at = kind * count * inner + t * inner + head * LANES
                        qkv[rows, at : at + LANES] = halves[h, source : source + LANES, :].astype(wide)
            base = count * columns
            small = halves[h, base : base + SMALL, :].astype(wide)
            padded = jnp.concatenate([small, jnp.zeros((LANES - SMALL, LANES), wide)], axis=0).T
            decay[rows, :] = padded[:, 0 : count * heads]
            gain[0:1, rows] = small[count * heads : count * heads + 1]
            for k in range(2):
                at = base + SMALL + k * slots
                lanes = slice(k * inner + h * LANES, k * inner + (h + 1) * LANES)
                fixed[:, lanes] = halves[h, at : at + slots, :].astype(wide)
            base += SMALL + 2 * slots
            for c in range(width // LANES):
                source = base + c * LANES
                out[rows, c * LANES : (c + 1) * LANES] = halves[h, source : source + LANES, :].astype(wide)
            if h == 0:
                found = halves[h, base + width : base + width + SMALL, :].astype(wide)
                bias[...] = jnp.concatenate([found[k : k + 1, 0:1] for k in range(heads)], axis=1)

    outs = [
        shape((part, count * columns), wide),
        shape((inner, width), wide),
        shape((1, part), wide),
        shape((part, count * heads), wide),
        shape((1, heads), wide),
        shape((slots, 2 * inner), wide),
    ]
    return unpack(body, totals, outs, place, "unpack_mix")


def tie(*values):
    return lax.optimization_barrier(values)


def exchange(value, axis, distance):
    count = lax.axis_size(axis)
    return lax.ppermute(value, axis, [(i, i ^ distance) for i in range(count)])


def gather_parts(block, axis):
    count = lax.axis_size(axis)
    far = {r: exchange(block, axis, r) for r in reversed(range(1, count))}
    return [block] + [far[r] for r in range(1, count)]


def trade_parts(blocks, axis):
    far = {r: exchange(blocks[r], axis, r) for r in reversed(range(1, len(blocks)))}
    return [blocks[0]] + [far[r] for r in range(1, len(blocks))]


def plane_device(
    tokens,
    lengths,
    cotangent,
    norm_one,
    qkv_weight,
    decay_weight,
    decay_bias,
    persistent,
    out_weight,
    norm_two,
    gate_up,
    down_weight,
):
    ctx_count, count = lax.axis_size("ctx"), lax.axis_size("fsdp")
    section, ctx, fsdp = (lax.axis_index(a) for a in ("section", "ctx", "fsdp"))
    rows, width = tokens.shape[2:]
    heads = decay_bias.shape[1]
    size = width // (heads * count)
    inner = heads * size

    def own_batch(value):
        return lax.dynamic_index_in_dim(value, section, 0, False)[0]

    pairs = []
    for s in range(2):
        flip = s * (count - 1)
        for c in range(ctx_count):
            for f in range(count):
                here, there = c * count + f, (f ^ flip) * count + (c ^ flip)
                pairs.append((s * ctx_count * count + here, s * ctx_count * count + there))

    def turn_plane(value):
        return lax.ppermute(value, ("section", "ctx", "fsdp"), pairs)

    def swap(value):
        return exchange(value, "section", 1)

    slots = persistent.shape[1]
    flip = section * (count - 1)
    spot = jnp.stack([fsdp, section, ctx ^ flip]).astype(jnp.int32)
    x_own, qkv_shard = tie(own_batch(tokens), qkv_weight[0])
    x_in = turn_plane(x_own)
    qkv_packed = pack_heads(count, qkv_shard, spot)
    qkv_parts = trade_parts(qkv_packed, "fsdp")
    small = pack_small(norm_one, norm_two, decay_weight[0], decay_bias, persistent[0], lengths[:, 0, 0])
    x_parts = gather_parts(beside(x_in, small, swap(small)), "fsdp")
    (gains_one, gains_two, decays, biases, fixeds), length = unpack_small(
        heads, slots, rows, small.shape[0], spot, x_parts
    )
    gu_packed = pack_gates(count, gate_up[0], spot)
    qkv_parts, gu_packed, _, g_own = tie(qkv_parts, gu_packed, x_parts, own_batch(cotangent))
    g_in = turn_plane(g_own)
    gu_parts = trade_parts(gu_packed, "fsdp")
    qkv_mine = assemble(spot, qkv_parts)
    qkv_other = swap(qkv_mine)
    out_mine = out_weight[0]
    out_other = swap(out_mine)
    mix_weights = (qkv_mine, qkv_other, out_mine, out_other)
    down_mine = down_weight[0]
    down_other = swap(down_mine)
    length, down_other = tie(length, down_other)
    place = jnp.stack([fsdp, section, length, (ctx == 1) | (ctx == 2)]).astype(jnp.int32)
    seat = jnp.stack([fsdp ^ flip, section, length]).astype(jnp.int32)
    hidden = down_mine.shape[0]
    columns = gu_packed[0].shape[1]

    def mix_first_half(layer, parts):
        *terms, combined, seen, projected, logits = mix_forward(
            layer, heads, size, seat, parts, rows, gains_one[layer], mix_weights, decays[layer], biases[layer], fixeds[layer]
        )
        return terms, (seen, projected, logits, combined)

    def mix_second_half(layer, terms, x):
        middle, normed_two = join_forward(False, trade_parts(terms, "fsdp"), x, gains_two[layer])
        return middle, gather_parts(normed_two, "fsdp")

    def feed_step(layer, parts, saved):
        *terms, g_rows, g_gates, active, g_gain = feed_backward(layer, seat, parts, saved[6], gains_two[layer], feed_weights)
        return terms, (saved[6], g_gates, active, g_rows, g_gain)

    def mix_step(layer, parts, saved):
        x, seen, projected, logits, combined, middle, seen_two = saved
        *terms, branch, g_projected, g_logits, g_fixed, g_gain = mix_backward(
            layer, heads, size, seat, parts, mix_weights, decays[layer], fixeds[layer], projected, logits, seen, gains_one[layer]
        )
        return terms, (seen, g_projected, combined, branch, g_logits, g_gain, g_fixed)

    inside = (ctx == 1) | (ctx == 2)
    line = {"queue": [], "inward": None, "across": None, "total": None, "flight": (None, None), "sums": []}

    def begin():
        own = line["queue"].pop(0) if line["queue"] else None
        total = line["total"]
        if own is not None and total is not None:
            sent = jnp.where(inside, total, own)
            route = [(0, 1), (3, 2), (1, 0), (2, 3)]
        else:
            sent = own if total is None else total
            route = [(0, 1), (3, 2)] if total is None else [(1, 0), (2, 3)]
        pair = line["across"]
        line["sent"] = (sent, pair, own, total is not None)
        return [v for v in (sent, pair) if v is not None], route

    def go(values, route):
        values = list(values)
        sent, pair, own, closing = line["sent"]
        sent = values.pop(0) if sent is not None else None
        pair = values.pop(0) if pair is not None else None
        line["sent"] = (sent, pair, own, closing)
        flight = [None, None]
        if sent is not None:
            flight[0] = lax.ppermute(sent, "ctx", route)
        if pair is not None:
            flight[1] = lax.ppermute(pair, "ctx", [(1, 2), (2, 1)])
        line["flight"] = flight

    def plus(a, b):
        return (a.astype(wide) + b.astype(wide)).astype(half)

    def step(*held, more=None):
        landed, crossed = line["flight"]
        waiting = [v for v in (landed, crossed) if v is not None]
        held, waiting = tie(held, waiting)
        if landed is not None:
            landed = waiting.pop(0)
        if crossed is not None:
            crossed = waiting.pop(0)
        sent, pair, own, closing = line.get("sent", (None, None, None, False))
        line["total"] = None if pair is None else plus(pair, crossed)
        line["across"] = None if own is None else plus(own, landed)
        if closing:
            line["sums"].append((sent, landed))
        if more is not None:
            line["queue"].extend(more(*held))
        ready, route = begin()
        held, ready = tie(held, ready)
        go(ready, route)
        return held

    def taken(number, skip=0):
        found = line["sums"][skip : skip + number]
        del line["sums"][skip : skip + number]
        return found

    terms, kept = mix_first_half(0, x_parts)
    terms, gu_parts[1], g_in = tie(terms, gu_parts[1], g_in)
    terms, gu_parts = tie(trade_parts(terms, "fsdp"), gu_parts)
    gu_mine = assemble(spot, gu_parts)
    feed_weights = (gu_mine, swap(gu_mine), down_mine, down_other)
    middle, normed_two = join_forward(False, terms, x_in, gains_two[0])
    parts = gather_parts(normed_two, "fsdp")
    *terms, seen_two = feed_forward(0, seat, parts, feed_weights)
    terms = trade_parts(terms, "fsdp")
    saved_first = (x_in, *kept, middle, seen_two)
    between = join_forward(True, terms, middle, None)[0]
    terms, kept = mix_first_half(1, gather_parts(between, "fsdp"))
    terms, g_three, g_two, g_one = tie(terms, *(exchange(g_in, "fsdp", r) for r in (3, 2, 1)))
    middle, parts = mix_second_half(1, terms, between)
    *terms_out, seen_two = feed_forward(1, seat, parts, feed_weights)
    saved_second = (between, *kept, middle, seen_two)
    terms, feed = feed_step(1, [g_in, g_one, g_two, g_three], saved_second)

    def to_owner(layer, chunks):
        return [lax.ppermute(chunk, "section", [(1 - layer, layer)]) for chunk in chunks]

    def trade(block, chunks, add=False):
        *blocks, local = spread(count, block, place, chunks, add)
        return trade_parts(blocks, "fsdp"), local

    def trade_strips(chunks):
        *blocks, local = spread_strips(count, strip, place, chunks)
        return trade_parts(blocks, "fsdp"), local

    strip = strip_of(columns)
    pad = 2 * (count * strip + hidden)
    mix_block = 3 * inner + SMALL + slots

    def summed(own, received):
        at, chunks = 0, []
        for chunk in own:
            chunks.append(plus(chunk, received[at : at + chunk.shape[0]]))
            at += chunk.shape[0]
        return chunks

    sent, *own = grad_feed(4, count, place, *feed)
    terms, sent = tie(trade_parts(terms, "fsdp"), sent)
    g_middle, g_branch = join_backward(terms, saved_second[5], gains_two[1], g_in)
    parts = gather_parts(g_branch, "fsdp")
    parts, received = tie(parts, swap(sent))
    (parts,) = step(parts, more=lambda _: summed(own, received))
    terms, mix = mix_step(1, parts, saved_second)
    terms, terms_out = step(terms, trade_parts(terms_out, "fsdp"))
    out = join_forward(True, terms_out, saved_second[5], None)[0]
    sent, *own = grad_mix(2, pad, count, place, *mix)
    terms, sent = step(trade_parts(terms, "fsdp"), sent)
    g_middle, g_branch = join_backward(terms, between, gains_one[1], g_middle)
    parts, sent = step(gather_parts(g_branch, "fsdp"), sent)
    terms, feed = feed_step(0, parts, saved_first)
    terms, _ = step(terms, swap(sent), more=lambda _, received: summed(own, received))
    sent, *own = grad_feed(4, count, place, *feed)
    terms, sent = step(trade_parts(terms, "fsdp"), sent)
    received = swap(sent)
    g_middle, g_branch = join_backward(terms, saved_first[5], gains_two[0], g_branch)
    g_branch, received = tie(g_branch, received)
    (parts,) = step(gather_parts(g_branch, "fsdp"), more=lambda _: summed(own, received))
    f1 = trade_strips(taken(4))
    terms, mix = mix_step(0, parts, saved_first)
    terms, f1 = step(terms, f1)
    feed_second = collect_feed(columns, place, [f1])
    sent, *own = grad_mix(1, pad, count, place, *mix)
    (terms,) = step(trade_parts(terms, "fsdp"))
    g_input = join_backward(terms, x_in, gains_one[0], g_middle)[1]
    received = swap(sent)
    g_input, received, feed_second = step(g_input, received, feed_second)
    m0 = trade(mix_block, [(own[0], received)], add=True)
    (m0,) = step(m0, more=lambda pieces: collect_mix(2, heads, pad, place, *pieces))
    f0 = trade_strips(taken(2, 2))
    (f0,) = step(f0)
    m1 = trade(mix_block, taken(2))
    (m1,) = step(m1)
    feed_second_other = to_owner(1, feed_second)
    f0_last = trade_strips(taken(2))
    mix_second = collect_mix(2, heads, pad, place, *m1)
    f0_last, mix_second, g_input = step(f0_last, mix_second, g_input)
    feed_first = collect_feed(columns, place, [f0, f0_last])
    feed_first_other = to_owner(0, feed_first)
    m0_first = [jnp.where(inside, *pair) for pair in taken(1)]
    m0_first_other = to_owner(0, m0_first)
    mix_second_other = to_owner(1, mix_second)
    feed_first_other, feed_second_other, m0_first_other, mix_second_other, g_input, out = step(
        feed_first_other, feed_second_other, m0_first_other, mix_second_other, g_input, out
    )
    m0_last = [jnp.where(inside, *pair) for pair in taken(1)]
    m0_last_other = to_owner(0, m0_last)
    out, g_turned = turn_plane(out), turn_plane(g_input)
    grad_gate_up, grad_down, grad_norm_two = unpack_feed(
        count,
        columns,
        hidden,
        width,
        ((feed_first, feed_first_other), (feed_second, feed_second_other)),
        place,
    )
    m0_last_other, grad_down = tie(m0_last_other, grad_down)
    grad_qkv, grad_out, grad_norm_one, grad_decay, grad_bias, grad_fixed = unpack_mix(
        count,
        heads,
        slots,
        width,
        ((m0_first + m0_last, m0_first_other + m0_last_other), (mix_second, mix_second_other)),
        place,
    )
    out, g_turned, grad_bias = tie(out, g_turned, grad_bias)
    return (
        out[None, None],
        g_turned[None, None],
        grad_norm_one,
        grad_qkv[None],
        grad_decay[None],
        grad_bias,
        grad_fixed[None],
        grad_out[None],
        grad_norm_two,
        grad_gate_up[None],
        grad_down[None],
    )


def scatter_sum(blocks, axis):
    total = blocks[0].astype(wide)
    for r in range(1, len(blocks)):
        total = total + exchange(blocks[r].astype(half), axis, r).astype(wide)
    return total


def in_order(parts, index, dim):
    count = len(parts)
    shape = list(parts[0].shape)
    size = shape[dim]
    shape[dim] = size * count
    whole = jnp.zeros(shape, parts[0].dtype)
    for r, part in enumerate(parts):
        whole = lax.dynamic_update_slice_in_dim(whole, part, (index ^ r) * size, dim)
    return whole


def columns_here(shard, kinds, axis):
    count, index = lax.axis_size(axis), lax.axis_index(axis)
    rows, width = shard.shape[0], shard.shape[1] // (kinds * count)
    blocks = shard.reshape(rows, kinds, count, width)
    parts = []
    for r in range(count):
        block = lax.dynamic_index_in_dim(blocks, index ^ r, 2, False).reshape(rows, kinds * width)
        parts.append(block if r == 0 else exchange(block, axis, r))
    return in_order(parts, index, 0)


def rows_here(columns, kinds, axis):
    count, index = lax.axis_size(axis), lax.axis_index(axis)
    rows, width = columns.shape[0] // count, columns.shape[1] // kinds
    parts = []
    for r in range(count):
        block = lax.dynamic_slice_in_dim(columns, (index ^ r) * rows, rows, 0)
        block = block if r == 0 else exchange(block, axis, r)
        parts.append(block.reshape(rows, kinds, 1, width))
    return in_order(parts, index, 2).reshape(rows, kinds * count * width)


def line_sum(value, axis):
    count, index = lax.axis_size(axis), lax.axis_index(axis)
    if count != 4:
        return lax.psum(value, axis)

    def plus(a, b):
        return (a.astype(wide) + b.astype(wide)).astype(value.dtype)

    pair = plus(value, lax.ppermute(value, axis, [(0, 1), (3, 2)]))
    total = plus(pair, lax.ppermute(pair, axis, [(1, 2), (2, 1)]))
    outer = lax.ppermute(total, axis, [(1, 0), (2, 3)])
    return jnp.where((index == 0) | (index == 3), outer, total)


def dot(a, b, contract=(1, 0)):
    return lax.dot_general(a, b, (((contract[0],), (contract[1],)), ((), ())), preferred_element_type=wide)


def normalise(values, gain):
    scale = lax.rsqrt(jnp.mean(values * values, axis=-1, keepdims=True) + epsilon)
    return (values * scale * gain).astype(half)


def normalise_back(values, gain, grad):
    scale = lax.rsqrt(jnp.mean(values * values, axis=-1, keepdims=True) + epsilon)
    unit = values * scale
    grad_gain = jnp.sum(grad * unit, axis=0)
    scaled = grad * gain
    return scale * (scaled - unit * jnp.mean(scaled * unit, axis=-1, keepdims=True)), grad_gain


def heads_first(rows, size):
    return rows.reshape(rows.shape[0], rows.shape[1] // size, size).transpose(1, 0, 2)


def rows_first(heads):
    return heads.transpose(1, 0, 2).reshape(heads.shape[1], heads.shape[0] * heads.shape[2])


def batched(a, b, contract):
    return lax.dot_general(a, b, (((contract[0],), (contract[1],)), ((0,), (0,))), preferred_element_type=wide)


def cumulative(values, positions):
    earlier = (positions[None, :] <= positions[:, None]).astype(wide)
    return jnp.dot(earlier, values, precision=lax.Precision.HIGHEST)


def mixer_parts(projected, logits, fixed, length, positions, size):
    width = projected.shape[1] // 3
    q, k, v = (heads_first(projected[:, i * width : (i + 1) * width], size) for i in range(3))
    fixed_k, fixed_v = (heads_first(fixed[:, i * width : (i + 1) * width], size) for i in range(2))
    scale = size ** (-0.5)
    documents = positions >= length
    starts = (positions == 0) | (positions == length)
    allowed = ((positions[None, :] <= positions[:, None]) & (documents[:, None] == documents[None, :]))[None]
    log_keep = jax.nn.log_sigmoid(logits)
    total_log = cumulative(log_keep, positions).T
    keep = jnp.where(starts[:, None], 0.0, jax.nn.sigmoid(logits)).T
    lose = jnp.where(starts[:, None], 1.0, jax.nn.sigmoid(-logits)).T
    inflow = jnp.sqrt(lose * (1.0 + keep))
    scores = batched(q, k, (2, 2)) * scale
    fixed_scores = batched(q, fixed_k, (2, 2)) * scale
    masked = jnp.where(allowed, scores, negative)
    top = jnp.maximum(jnp.max(masked, axis=2), jnp.max(fixed_scores, axis=2))[:, :, None]
    weights, fixed_weights = jnp.exp(masked - top), jnp.exp(fixed_scores - top)
    mass = 1.0 / (jnp.sum(weights, axis=2) + jnp.sum(fixed_weights, axis=2))[:, :, None]
    weights, fixed_weights = weights * mass, fixed_weights * mass
    fall = jnp.exp(jnp.where(allowed, total_log[:, :, None] - total_log[:, None, :], negative))
    reach = scores * fall
    both = (weights + reach * inflow[:, None, :]).astype(half)
    return q, k, v, fixed_k, fixed_v, weights, fixed_weights, fall, reach, both, keep, lose, inflow


def mixer(projected, logits, fixed, length, positions, size):
    parts = mixer_parts(projected, logits, fixed, length, positions, size)
    q, k, v, fixed_k, fixed_v, weights, fixed_weights, fall, reach, both, keep, lose, inflow = parts
    mixed = batched(both, v, (2, 1)) + batched(fixed_weights.astype(half), fixed_v, (2, 1))
    return rows_first(mixed.astype(half))


def mixer_back(projected, logits, fixed, length, positions, size, grad):
    parts = mixer_parts(projected, logits, fixed, length, positions, size)
    q, k, v, fixed_k, fixed_v, weights, fixed_weights, fall, reach, both, keep, lose, inflow = parts
    scale = size ** (-0.5)
    grad = heads_first(grad, size)
    grad_both = batched(grad, v, (2, 2))
    grad_fixed = batched(grad, fixed_v, (2, 2))
    delta = (jnp.sum(weights * grad_both, axis=2) + jnp.sum(fixed_weights * grad_fixed, axis=2))[:, :, None]
    grad_scores = (weights * (grad_both - delta) + grad_both * fall * inflow[:, None, :]).astype(half)
    grad_fixed_scores = (fixed_weights * (grad_fixed - delta)).astype(half)
    grad_q = (batched(grad_scores, k, (2, 1)) + batched(grad_fixed_scores, fixed_k, (2, 1))) * scale
    grad_k = batched(grad_scores, q, (1, 1)) * scale
    grad_v = batched(both, grad, (1, 1))
    grad_fixed_k = batched(grad_fixed_scores, q, (1, 1)) * scale
    grad_fixed_v = batched(fixed_weights.astype(half), grad, (1, 1))
    pull = grad_both * reach
    grad_inflow = jnp.sum(pull, axis=1)
    grad_total = jnp.sum(pull * inflow[:, None, :], axis=2) - inflow * grad_inflow
    later = (positions[None, :] >= positions[:, None]).astype(wide)
    grad_log = jnp.dot(grad_total, later.T, precision=lax.Precision.HIGHEST)
    lose_all = jax.nn.sigmoid(-logits).T
    grad_logits = grad_log * lose_all - grad_inflow * keep * keep * lose / inflow
    grad_projected = jnp.concatenate([rows_first(grad_q), rows_first(grad_k), rows_first(grad_v)], axis=1)
    grad_persistent = jnp.concatenate([rows_first(grad_fixed_k), rows_first(grad_fixed_v)], axis=1)
    return grad_projected.astype(half), grad_logits.T, grad_persistent


def general_device(
    tokens,
    lengths,
    cotangent,
    norm_one,
    qkv_weight,
    decay_weight,
    decay_bias,
    persistent,
    out_weight,
    norm_two,
    gate_up,
    down_weight,
):
    sections, ctx_count, fsdp_count = (lax.axis_size(a) for a in ("section", "ctx", "fsdp"))
    section, ctx, fsdp = (lax.axis_index(a) for a in ("section", "ctx", "fsdp"))
    spread = ctx_count // fsdp_count
    rows, width = tokens.shape[2:]
    heads_here = decay_bias.shape[1]
    size = width // (heads_here * fsdp_count)
    inner = heads_here * size
    first = section == 0

    def own_batch(value):
        return lax.dynamic_index_in_dim(value, section, 0, False)[0]

    pairs = [(c * fsdp_count + f, f * ctx_count + c) for c in range(ctx_count) for f in range(fsdp_count)]

    def to_plane(value):
        return lax.ppermute(value, ("ctx", "fsdp"), pairs)

    def from_plane(value):
        return lax.ppermute(value, ("ctx", "fsdp"), [(b, a) for a, b in pairs])

    x_in = to_plane(own_batch(tokens))
    g_in = to_plane(own_batch(cotangent))
    length = to_plane(own_batch(lengths))[0]

    def both_layers(own):
        other = exchange(own, "section", 1)
        return jnp.where(first, own, other), jnp.where(first, other, own)

    small = jnp.concatenate(
        [
            norm_one[0],
            norm_two[0],
            decay_weight[0].reshape(-1),
            persistent[0].reshape(-1),
        ]
    )
    small = jnp.stack(both_layers(in_order([p[None] for p in gather_parts(small, "fsdp")], fsdp, 0)))
    cut = width // fsdp_count
    sizes = [cut, cut, decay_weight[0].size, persistent[0].size]
    edges = [0]
    for piece in sizes:
        edges.append(edges[-1] + piece)
    gains_one, gains_two, decays, fixeds = (small[:, :, a:b] for a, b in zip(edges[:-1], edges[1:]))
    gains_one = gains_one.reshape(2, width).astype(wide)
    gains_two = gains_two.reshape(2, width).astype(wide)
    head_count = heads_here * fsdp_count
    decays = lax.dynamic_slice_in_dim(decays.reshape(2, width, head_count), fsdp * heads_here, heads_here, 2)
    slots = persistent.shape[1]
    fixeds = fixeds.reshape(2, fsdp_count, slots, 2 * cut).transpose(0, 2, 1, 3).reshape(2, slots, 2, fsdp_count, inner)
    fixeds = lax.dynamic_index_in_dim(fixeds, fsdp, 3, False).reshape(2, slots, 2 * inner)
    biases = jnp.stack(both_layers(decay_bias[0])).astype(wide)
    qkvs = both_layers(columns_here(qkv_weight[0], 3, "fsdp"))
    outs = both_layers(out_weight[0])
    gate_ups = both_layers(columns_here(gate_up[0], 2, "fsdp"))
    downs = both_layers(down_weight[0])
    hidden = downs[0].shape[0]

    pieces = [(k * fsdp_count + (fsdp ^ r)) * rows + jnp.arange(rows) for k in range(spread) for r in range(fsdp_count)]
    all_positions = jnp.concatenate(pieces)
    groups = [[g * spread + k for k in range(spread)] for g in range(ctx_count // spread)]

    def whole(value):
        if spread == 1:
            return value
        return lax.all_gather(value, "ctx", axis_index_groups=groups, axis=0, tiled=True)

    def own_rows(value):
        if spread == 1:
            return value
        count = value.shape[0] // spread
        return lax.dynamic_slice_in_dim(value, (ctx % spread) * count, count, 0)

    def blocks_of(value):
        return list(value.reshape(fsdp_count, rows, value.shape[1]))

    def forward(layer, x, last):
        normed = jnp.concatenate(gather_parts(normalise(x, gains_one[layer]), "fsdp"))
        projected = dot(normed, qkvs[layer]).astype(half)
        logits = dot(normed, decays[layer]) + biases[layer]
        seen, seen_logits = whole(projected), whole(logits)
        combined = own_rows(mixer(seen, seen_logits, fixeds[layer], length, all_positions, size))
        middle = x + scatter_sum(blocks_of(dot(combined, outs[layer])), "fsdp")
        normed_two = jnp.concatenate(gather_parts(normalise(middle, gains_two[layer]), "fsdp"))
        gates = dot(normed_two, gate_ups[layer])
        activated = (jax.nn.silu(gates[:, :hidden]) * gates[:, hidden:]).astype(half)
        out = middle + scatter_sum(blocks_of(dot(activated, downs[layer])), "fsdp")
        return out.astype(half), (x, normed, seen, seen_logits, combined, middle, normed_two, gates, activated)

    def backward(layer, g_out, saved):
        x, normed, seen, seen_logits, combined, middle, normed_two, gates, activated = saved
        g_rows = jnp.concatenate(gather_parts(g_out, "fsdp"))
        grad_down = dot(activated, g_rows, (0, 0))
        g_activated = dot(g_rows, downs[layer], (1, 1))
        gate, up = gates[:, :hidden], gates[:, hidden:]
        sig = jax.nn.sigmoid(gate)
        g_up = g_activated * gate * sig
        g_gate = g_activated * up * sig * (1.0 + gate * (1.0 - sig))
        g_gates = jnp.concatenate([g_gate, g_up], axis=1).astype(half)
        grad_gate_up = dot(normed_two, g_gates, (0, 0))
        g_normed_two = scatter_sum(blocks_of(dot(g_gates, gate_ups[layer], (1, 1))), "fsdp")
        g_middle, grad_norm_two = normalise_back(middle, gains_two[layer], g_normed_two)
        g_middle = g_middle + g_out.astype(wide)
        g_branch = jnp.concatenate(gather_parts(g_middle.astype(half), "fsdp"))
        grad_out = dot(combined, g_branch, (0, 0))
        g_combined = whole(dot(g_branch, outs[layer], (1, 1)).astype(half))
        g_projected, g_logits, grad_fixed = mixer_back(
            seen, seen_logits, fixeds[layer], length, all_positions, size, g_combined
        )
        g_projected, g_logits = own_rows(g_projected), own_rows(g_logits)
        grad_fixed = jnp.where(ctx % spread == 0, grad_fixed, 0.0)
        grad_qkv = dot(normed, g_projected, (0, 0))
        grad_decay = dot(normed.astype(wide), g_logits, (0, 0))
        grad_bias = jnp.sum(g_logits, axis=0)
        g_normed = dot(g_projected, qkvs[layer], (1, 1)) + dot(g_logits, decays[layer].astype(wide), (1, 1))
        g_normed = scatter_sum(blocks_of(g_normed), "fsdp")
        g_x, grad_norm_one = normalise_back(x, gains_one[layer], g_normed)
        g_x = (g_x + g_middle).astype(half)
        large = (grad_qkv, grad_out, grad_gate_up, grad_down)
        return g_x, tuple(g.astype(half) for g in large), (grad_norm_one, grad_norm_two, grad_decay, grad_bias, grad_fixed)

    between, saved_first = forward(0, x_in.astype(wide), False)
    out, saved_second = forward(1, between.astype(wide), True)
    g_between, large_second, small_second = backward(1, g_in, saved_second)
    g_input, large_first, small_first = backward(0, g_between, saved_first)

    def reduced(from_first, from_second):
        received = exchange(jnp.where(first, from_second, from_first), "section", 1)
        own = jnp.where(first, from_first, from_second)
        own = (own.astype(wide) + received.astype(wide)).astype(half)
        return line_sum(own, "ctx")

    grad_qkv, grad_out, grad_gate_up, grad_down = (reduced(a, b) for a, b in zip(large_first, large_second))
    grad_qkv = rows_here(grad_qkv, 3, "fsdp")
    grad_gate_up = rows_here(grad_gate_up, 2, "fsdp")

    def small_whole(pieces):
        n_one, n_two, decay, bias, fixed = pieces
        decay_all = lax.dynamic_update_slice_in_dim(jnp.zeros((width, head_count), wide), decay, fsdp * heads_here, 1)
        bias_all = lax.dynamic_update_slice_in_dim(jnp.zeros((head_count,), wide), bias, fsdp * heads_here, 0)
        fixed_all = jnp.zeros((slots, 2, fsdp_count, inner), wide)
        fixed_all = lax.dynamic_update_slice_in_dim(fixed_all, fixed.reshape(slots, 2, 1, inner), fsdp, 2)
        return jnp.concatenate([n_one, n_two, decay_all.reshape(-1), fixed_all.reshape(-1), bias_all])

    tiny_first, tiny_second = small_whole(small_first), small_whole(small_second)
    tiny = lax.psum(jnp.stack([tiny_first, tiny_second]), ("section", "ctx", "fsdp"))
    tiny = lax.dynamic_index_in_dim(tiny, section, 0, False)
    grad_norm_one = lax.dynamic_slice_in_dim(tiny[:width], fsdp * cut, cut, 0)
    grad_norm_two = lax.dynamic_slice_in_dim(tiny[width : 2 * width], fsdp * cut, cut, 0)
    at = 2 * width
    grad_decay = lax.dynamic_slice_in_dim(tiny[at : at + width * head_count].reshape(width, head_count), fsdp * cut, cut, 0)
    at += width * head_count
    grad_fixed = tiny[at : at + slots * 2 * width].reshape(slots, 2 * width)
    grad_fixed = lax.dynamic_slice_in_dim(grad_fixed, fsdp * 2 * cut, 2 * cut, 1)
    at += slots * 2 * width
    grad_bias = lax.dynamic_slice_in_dim(tiny[at:], fsdp * heads_here, heads_here, 0)

    return (
        from_plane(out)[None, None],
        from_plane(g_input)[None, None],
        grad_norm_one[None],
        grad_qkv.astype(wide)[None],
        grad_decay[None],
        grad_bias[None],
        grad_fixed[None],
        grad_out.astype(wide)[None],
        grad_norm_two[None],
        grad_gate_up.astype(wide)[None],
        grad_down.astype(wide)[None],
    )


def solution(mesh):
    by_row = P("section", "fsdp", None)
    by_gain = P("section", "fsdp")
    by_token = P(None, "fsdp", "ctx", None)
    by_output = P("section", "fsdp", "ctx", None)
    by_slot = P("section", None, "fsdp")
    plane = mesh.shape["ctx"] == mesh.shape["fsdp"] == 4
    return jax.shard_map(
        plane_device if plane else general_device,
        mesh=mesh,
        in_specs=(
            by_token,
            P(None, "fsdp", None),
            by_token,
            by_gain,
            by_row,
            by_row,
            by_gain,
            by_slot,
            by_row,
            by_gain,
            by_row,
            by_row,
        ),
        out_specs=(
            by_output,
            by_output,
            by_gain,
            by_row,
            by_row,
            by_gain,
            by_slot,
            by_row,
            by_gain,
            by_row,
            by_row,
        ),
        check_vma=False,
    )
```

```python
import jax
import jax.numpy as jnp
from jax import lax
from jax.experimental import pallas as pl
from jax.experimental.pallas import tpu as pltpu
from jax.sharding import PartitionSpec as P

epsilon = 1e-05
negative = -1e30
wide = jnp.float32
half = jnp.bfloat16
LANES = 128
PAIR = 64
ROOM = {
    "mix_forward": 20,
    "mix_backward": 24,
    "feed_forward": 20,
    "feed_backward": 24,
    "grad_feed": 20,
    "grad_mix": 16,
    "assemble": 12,
    "pack_gates": 16,
    "spread": 12,
    "collect_feed": 12,
    "unpack_mix": 16,
}
vmem = pl.BlockSpec(memory_space=pltpu.VMEM)
smem = pl.BlockSpec(memory_space=pltpu.SMEM)
anywhere = pl.BlockSpec(memory_space=pl.ANY)


def mm(a, b):
    return lax.dot_general(a, b, (((1,), (0,)), ((), ())), preferred_element_type=wide)


def mm_nt(a, b):
    return lax.dot_general(a, b, (((1,), (1,)), ((), ())), preferred_element_type=wide)


def mm_tn(a, b):
    return lax.dot_general(a, b, (((0,), (0,)), ((), ())), preferred_element_type=wide)


def sig(v):
    return 1.0 / (1.0 + jnp.exp(-v))


def call(body, out_shape, in_specs, scratch, flops, moved, name):
    return pl.pallas_call(
        body,
        out_shape=out_shape,
        in_specs=in_specs,
        out_specs=jax.tree.map(lambda _: vmem, out_shape),
        scratch_shapes=scratch,
        compiler_params=pltpu.CompilerParams(vmem_limit_bytes=ROOM.get(name, 8) * 1024 * 1024),
        cost_estimate=pl.CostEstimate(flops=flops, bytes_accessed=moved, transcendentals=0),
        name=name,
    )


def shape(dims, kind=half):
    return jax.ShapeDtypeStruct(tuple(dims), kind)


def pack_heads(count, shard, place):
    rows, columns = shard.shape
    inner = columns // (3 * count)

    def body(place_ref, shard_ref, *outs):
        for r in range(count):
            target = place_ref[0] ^ r
            for kind in range(3):
                at = pl.multiple_of(kind * count * inner + target * inner, inner)
                outs[r][:, kind * inner : (kind + 1) * inner] = shard_ref[:, pl.ds(at, inner)]

    outs = [shape((rows, 3 * inner))] * count
    return call(body, outs, [smem, vmem], [], 0, 2 * shard.size * 2, "pack_heads")(place, shard)


def pack_gates(count, shard, place):
    rows, columns = shard.shape
    hidden = columns // 2
    mine = columns // count

    def body(place_ref, shard_ref, *rest):
        outs, mixed = rest[:count], rest[count]
        low = lax.broadcasted_iota(jnp.int32, (rows, LANES), 1) < PAIR
        for m in range(hidden // LANES):
            gate = shard_ref[:, m * LANES : (m + 1) * LANES].astype(wide)
            up = shard_ref[:, hidden + m * LANES : hidden + (m + 1) * LANES].astype(wide)
            even = jnp.where(low, gate, pltpu.roll(up, PAIR, 1))
            odd = jnp.where(low, pltpu.roll(gate, PAIR, 1), up)
            mixed[:, 2 * m * LANES : (2 * m + 1) * LANES] = even.astype(half)
            mixed[:, (2 * m + 1) * LANES : (2 * m + 2) * LANES] = odd.astype(half)
        for r in range(count):
            at = pl.multiple_of((place_ref[0] ^ r) * mine, LANES)
            outs[r][...] = mixed[:, pl.ds(at, mine)]

    outs = [shape((rows, mine))] * count
    scratch = [pltpu.VMEM((rows, columns), half)]
    return call(body, outs, [smem, vmem], scratch, 0, 2 * shard.size * 2, "pack_gates")(place, shard)


def assemble(place, parts):
    count = len(parts)
    rows, columns = parts[0].shape

    def body(place_ref, *refs):
        put_rows(refs[:count], refs[count], place_ref)

    outs = [shape((rows * count, columns))]
    moved = 4 * rows * count * columns
    return call(body, outs, [smem] + [vmem] * count, [], 0, moved, "assemble")(place, *parts)[0]


def fetch(place_ref, layer, mine, other, target, sems, span=None):
    rows, columns = mine.shape
    span = columns if span is None else span
    handles = []
    for k, at in enumerate(range(0, columns, span)):
        lanes = pl.ds(at, min(span, columns - at))
        where = target.at[pl.ds(0, rows), lanes]
        for own, source in ((True, mine), (False, other)):

            @pl.when((place_ref[1] == layer) == own)
            def _(source=source, lanes=lanes, where=where, k=k):
                pltpu.make_async_copy(source.at[pl.ds(0, rows), lanes], where, sems.at[k]).start()

        handles.append(pltpu.make_async_copy(mine.at[pl.ds(0, rows), lanes], where, sems.at[k]))
    return handles


def finish(handles):
    for handle in handles:
        handle.wait()


def put_rows(parts, target, place_ref):
    rows = parts[0].shape[0]
    for r, part in enumerate(parts):
        target[pl.ds(pl.multiple_of((place_ref[0] ^ r) * rows, rows), rows), :] = part[...]


def take_rows(source, outs, place_ref):
    rows = outs[0].shape[0]
    for r, out in enumerate(outs):
        out[...] = source[pl.ds(pl.multiple_of((place_ref[0] ^ r) * rows, rows), rows), :].astype(out.dtype)


def three_way(v):
    high = v.astype(half)
    rest = v - high.astype(wide)
    middle = rest.astype(half)
    return high, middle, (rest - middle.astype(wide)).astype(half)


def exact_sum(values, mask):
    return sum(mm(piece, mask) for piece in three_way(values))


def gate_lanes(logits, length):
    rows = logits.shape[1]
    at = lax.broadcasted_iota(jnp.int32, logits.shape, 1)
    starts = (at == 0) | (at == length)
    spill = jnp.log(1.0 + jnp.exp(-jnp.abs(logits)))
    log_keep = jnp.minimum(logits, 0.0) - spill
    keep = jnp.where(starts, 0.0, sig(logits))
    lose = jnp.where(starts, 1.0, sig(-logits))
    before = lax.broadcasted_iota(jnp.int32, (rows, rows), 0) <= lax.broadcasted_iota(jnp.int32, (rows, rows), 1)
    return log_keep, keep, lose, exact_sum(log_keep, before.astype(wide).astype(half))


def turned(values):
    return jnp.concatenate([values, jnp.zeros((LANES - values.shape[0], values.shape[1]), wide)], axis=0).T


def head_scores(head, size, inner, projected, fixed, total, total_t, inflow_t, length, scale):
    rows = projected.shape[0]
    lanes = slice(head * size, (head + 1) * size)
    q = projected[:, lanes]
    k = projected[:, inner + head * size : inner + (head + 1) * size]
    v = projected[:, 2 * inner + head * size : 2 * inner + (head + 1) * size]
    fixed_k = fixed[:, lanes]
    fixed_v = fixed[:, inner + head * size : inner + (head + 1) * size]
    scores = mm_nt(q, k) * scale
    fixed_scores = mm_nt(q, fixed_k) * scale
    at = lax.broadcasted_iota(jnp.int32, (rows, 1), 0)
    begin = jnp.where(at >= length, length, 0)
    column = lax.broadcasted_iota(jnp.int32, (rows, rows), 1)
    allowed = (column <= at) & (column >= begin)
    masked = jnp.where(allowed, scores, negative)
    top = jnp.maximum(jnp.max(masked, axis=1, keepdims=True), jnp.max(fixed_scores, axis=1, keepdims=True))
    weights, fixed_weights = jnp.exp(masked - top), jnp.exp(fixed_scores - top)
    mass = 1.0 / (jnp.sum(weights, axis=1, keepdims=True) + jnp.sum(fixed_weights, axis=1, keepdims=True))
    weights, fixed_weights = weights * mass, fixed_weights * mass
    fall = jnp.exp(jnp.where(allowed, total[:, head : head + 1] - total_t[head : head + 1, :], negative))
    reach = scores * fall
    both = (weights + reach * inflow_t[head : head + 1, :]).astype(half)
    return q, k, v, fixed_k, fixed_v, weights, fixed_weights, fall, reach, both


def mix_forward(layer, heads, size, place, parts, rows, gain, weights, decay, bias, fixed):
    count = len(parts)
    width = parts[0].shape[1]
    total_rows, inner = rows * count, heads * size
    scale = size ** (-0.5)

    def body(place_ref, *refs):
        parts_in, refs = refs[:count], refs[count:]
        (mine, other, o_mine, o_other), refs = refs[:4], refs[4:]
        (gain_ref, decay_ref, bias_ref, fixed_ref), refs = refs[:4], refs[4:]
        terms, refs = refs[:count], refs[count:]
        combined, normed, projected, logits_out, weight, out_weight, whole, sems = refs
        handles = fetch(place_ref, layer, mine, other, weight, sems, inner)
        out_handles = fetch(place_ref, layer, o_mine, o_other, out_weight, sems.at[pl.ds(3, 1)])
        for r, part in enumerate(parts_in):
            values = part[0:rows, :].astype(wide)
            root = lax.rsqrt(jnp.mean(values * values, axis=1, keepdims=True) + epsilon)
            here = pl.ds(pl.multiple_of((place_ref[0] ^ r) * rows, rows), rows)
            normed[here, :] = (values * root * gain_ref[...]).astype(half)
        length = place_ref[2]
        logits = mm_nt(decay_ref[...], normed[...]) + bias_ref[:, 0:1]
        logits_out[...] = logits
        log_keep, keep, lose, total_t = gate_lanes(logits, length)
        total = turned(total_t)
        inflow_t = jnp.sqrt(lose * (1.0 + keep))
        for kind in range(3):
            handles[kind].wait()
            lanes = slice(kind * inner, (kind + 1) * inner)
            projected[:, lanes] = mm(normed[...], weight[:, lanes]).astype(half)
        for head in range(heads):
            q, k, v, fixed_k, fixed_v, soft, fixed_soft, fall, reach, both = head_scores(
                head, size, inner, projected, fixed_ref, total, total_t, inflow_t, length, scale
            )
            mixed = mm(both, v) + mm(fixed_soft.astype(half), fixed_v)
            combined[:, head * size : (head + 1) * size] = mixed.astype(half)
        finish(out_handles)
        whole[...] = mm(combined[...], out_weight[...])
        take_rows(whole, terms, place_ref)

    outs = [shape((rows, width), wide if r == 0 else half) for r in range(count)] + [
        shape((total_rows, inner)),
        shape((total_rows, width)),
        shape((total_rows, 3 * inner)),
        shape((16, total_rows), wide),
    ]
    scratch = [
        pltpu.VMEM((width, 3 * inner), half),
        pltpu.VMEM((inner, width), half),
        pltpu.VMEM((total_rows, width), wide),
        pltpu.SemaphoreType.DMA((4,)),
    ]
    specs = [smem] + [vmem] * count + [anywhere] * 4 + [vmem] * 4
    flops = 2 * total_rows * (width * 4 * inner + inner * total_rows * 2)
    moved = 2 * (width * 3 * inner + total_rows * (2 * width + 4 * inner))
    return call(body, outs, specs, scratch, flops, moved, "mix_forward")(
        place, *parts, *weights, gain, decay, bias, fixed
    )


def mix_backward(layer, heads, size, place, parts, weights, decay, fixed, projected, logits, normed, gain):
    count = len(parts)
    rows, width = parts[0].shape
    total_rows, inner = rows * count, heads * size
    scale = size ** (-0.5)

    def body(place_ref, *refs):
        parts_in, refs = refs[:count], refs[count:]
        (mine, other, o_mine, o_other), refs = refs[:4], refs[4:]
        decay_ref, fixed_ref, projected, logits_ref, normed_ref, gain_ref = refs[:6]
        refs = refs[6:]
        terms, refs = refs[:count], refs[count:]
        branch, g_projected, g_logits_out, g_fixed, g_gain, refs = refs[0], refs[1], refs[2], refs[3], refs[4], refs[5:]
        weight, out_weight, combined, pulled, pushed, whole, sems = refs
        out_handles = fetch(place_ref, layer, o_mine, o_other, out_weight, sems.at[pl.ds(1, 1)])
        handles = fetch(place_ref, layer, mine, other, weight, sems.at[pl.ds(0, 1)])
        put_rows(parts_in, branch, place_ref)
        length = place_ref[2]
        logits = logits_ref[...]
        log_keep, keep, lose, total_t = gate_lanes(logits, length)
        total = turned(total_t)
        inflow_t = jnp.sqrt(lose * (1.0 + keep))
        finish(out_handles)
        combined[...] = mm_nt(branch[...], out_weight[...]).astype(half)
        pulled[...] = jnp.zeros_like(pulled)
        pushed[...] = jnp.zeros_like(pushed)
        for head in range(heads):
            lanes, key_lanes, value_lanes = (
                slice(kind * inner + head * size, kind * inner + (head + 1) * size) for kind in range(3)
            )
            q, k, v, fixed_k, fixed_v, weights, fixed_weights, fall, reach, both = head_scores(
                head, size, inner, projected, fixed_ref, total, total_t, inflow_t, length, scale
            )
            grad = combined[:, lanes]
            g_both = mm_nt(grad, v)
            g_few = mm_nt(grad, fixed_v)
            delta = jnp.sum(weights * g_both, axis=1, keepdims=True) + jnp.sum(
                fixed_weights * g_few, axis=1, keepdims=True
            )
            inflow_row = inflow_t[head : head + 1, :]
            g_scores = (weights * (g_both - delta) + g_both * fall * inflow_row).astype(half)
            g_few_scores = (fixed_weights * (g_few - delta)).astype(half)
            g_projected[:, lanes] = ((mm(g_scores, k) + mm(g_few_scores, fixed_k)) * scale).astype(half)
            g_projected[:, key_lanes] = (mm_tn(g_scores, q) * scale).astype(half)
            g_projected[:, value_lanes] = mm_tn(both, grad).astype(half)
            g_fixed[:, lanes] = mm_tn(g_few_scores, q) * scale
            g_fixed[:, key_lanes] = mm_tn(fixed_weights.astype(half), grad)
            pull = g_both * reach
            pulled[head : head + 1, :] = jnp.sum(pull, axis=0, keepdims=True)
            pushed[:, head : head + 1] = jnp.sum(pull * inflow_row, axis=1, keepdims=True)
        g_inflow = pulled[...]
        g_total = pushed[...].T[0:16] - inflow_t * g_inflow
        after = lax.broadcasted_iota(jnp.int32, (total_rows, total_rows), 0) >= lax.broadcasted_iota(
            jnp.int32, (total_rows, total_rows), 1
        )
        g_log = exact_sum(g_total, after.astype(wide).astype(half))
        g_logits = g_log * sig(-logits) - g_inflow * keep * keep * lose / inflow_t
        row = lax.broadcasted_iota(jnp.int32, g_logits.shape, 0)
        g_logits = jnp.where(row < heads, g_logits, 0.0)
        g_logits_out[...] = g_logits
        finish(handles)
        high, middle, low = three_way(g_logits)
        whole[...] = (
            mm_nt(g_projected[...], weight[...]) + mm_tn(high, decay_ref[...]) + mm_tn(middle, decay_ref[...])
        )
        pulls = jnp.sum(whole[...] * normed_ref[...].astype(wide), axis=0, keepdims=True) / gain_ref[...]
        g_gain[...] = jnp.broadcast_to(pulls, g_gain.shape)
        take_rows(whole, terms, place_ref)

    outs = [shape((rows, width), wide if r == 0 else half) for r in range(count)] + [
        shape((total_rows, width)),
        shape((total_rows, 3 * inner)),
        shape((16, total_rows), wide),
        shape((fixed.shape[0], 2 * inner), wide),
        shape((8, width), wide),
    ]
    scratch = [
        pltpu.VMEM((width, 3 * inner), half),
        pltpu.VMEM((inner, width), half),
        pltpu.VMEM((total_rows, inner), half),
        pltpu.VMEM((16, total_rows), wide),
        pltpu.VMEM((total_rows, LANES), wide),
        pltpu.VMEM((total_rows, width), wide),
        pltpu.SemaphoreType.DMA((2,)),
    ]
    specs = [smem] + [vmem] * count + [anywhere] * 4 + [vmem] * 6
    flops = 2 * total_rows * (width * 4 * inner + inner * total_rows * 5)
    moved = 2 * (width * 4 * inner + total_rows * (5 * width + 6 * inner))
    return call(body, outs, specs, scratch, flops, moved, "mix_backward")(
        place, *parts, *weights, decay, fixed, projected, logits, normed, gain
    )


def gates_of(tile_pair):
    rows, columns = tile_pair.shape
    if columns > 2 * LANES:
        found = [gates_of(tile_pair[:, at : at + size]) for at, size in tile_ranges(columns)]
        return tuple(jnp.concatenate([pair[k] for pair in found], axis=1) for k in range(2))
    if columns == LANES:
        return tile_pair[:, :PAIR], pltpu.roll(tile_pair, PAIR, 1)[:, :PAIR]
    first, second = tile_pair[:, :LANES], tile_pair[:, LANES:]
    low = lax.broadcasted_iota(jnp.int32, (rows, LANES), 1) < PAIR
    gate = jnp.where(low, first, pltpu.roll(second, PAIR, 1))
    up = jnp.where(low, pltpu.roll(first, PAIR, 1), second)
    return gate, up


def tiles_of(gate, up):
    rows, columns = gate.shape
    if columns > LANES:
        steps = [(at, min(LANES, columns - at)) for at in range(0, columns, LANES)]
        return jnp.concatenate([tiles_of(gate[:, at : at + size], up[:, at : at + size]) for at, size in steps], axis=1)
    if columns == PAIR:
        return jnp.concatenate([gate, up], axis=1)
    low = lax.broadcasted_iota(jnp.int32, (rows, LANES), 1) < PAIR
    first = jnp.where(low, gate, pltpu.roll(up, PAIR, 1))
    second = jnp.where(low, pltpu.roll(gate, PAIR, 1), up)
    return jnp.concatenate([first, second], axis=1)


def tile_ranges(columns, tiles=2):
    return [(at, min(tiles * LANES, columns - at)) for at in range(0, columns, tiles * LANES)]


def feed_forward(layer, place, parts, weights):
    count = len(parts)
    rows, width = parts[0].shape
    total_rows = rows * count
    columns, hidden = weights[0].shape[1], weights[2].shape[0]
    padded = -(-hidden // LANES) * LANES

    def body(place_ref, *refs):
        parts_in, refs = refs[:count], refs[count:]
        (mine, other, d_mine, d_other), refs = refs[:4], refs[4:]
        terms, normed, refs = refs[:count], refs[count], refs[count + 1 :]
        weight, down, active, whole, sems = refs
        handles = fetch(place_ref, layer, mine, other, weight, sems.at[pl.ds(0, 1)])
        down_handles = fetch(place_ref, layer, d_mine, d_other, down, sems.at[pl.ds(1, 1)])
        put_rows(parts_in, normed, place_ref)
        if padded != hidden:
            down[hidden:, :] = jnp.zeros((padded - hidden, width), half)
            active[:, padded - LANES :] = jnp.zeros((total_rows, LANES), half)
        finish(handles)
        for at, size in tile_ranges(columns):
            gate, up = gates_of(mm(normed[...], weight[:, at : at + size]))
            active[:, at // 2 : (at + size) // 2] = (gate * sig(gate) * up).astype(half)
        finish(down_handles)
        whole[...] = mm(active[...], down[...])
        take_rows(whole, terms, place_ref)

    outs = [shape((rows, width), wide if r == 0 else half) for r in range(count)] + [shape((total_rows, width))]
    scratch = [
        pltpu.VMEM((width, columns), half),
        pltpu.VMEM((padded, width), half),
        pltpu.VMEM((total_rows, padded), half),
        pltpu.VMEM((total_rows, width), wide),
        pltpu.SemaphoreType.DMA((2,)),
    ]
    specs = [smem] + [vmem] * count + [anywhere] * 4
    flops = 2 * total_rows * width * (columns + hidden)
    moved = 2 * (width * (columns + hidden) + total_rows * 4 * width)
    return call(body, outs, specs, scratch, flops, moved, "feed_forward")(
        place, *parts, *weights
    )


def feed_backward(layer, place, parts, normed_parts, gain, weights, forward):
    count = len(parts)
    rows, width = parts[0].shape
    total_rows = rows * count
    columns, hidden = weights[0].shape[1], weights[2].shape[0]
    padded = -(-hidden // LANES) * LANES

    def body(place_ref, *refs):
        parts_in, refs = refs[:count], refs[count:]
        normed_in, refs = refs[: len(normed_parts)], refs[len(normed_parts) :]
        gain_ref, (mine, other, d_mine, d_other), refs = refs[0], refs[1:5], refs[5:]
        terms, refs = refs[:count], refs[count:]
        g_out, g_gates, active, g_gain, refs = refs[0], refs[1], refs[2], refs[3], refs[4:]
        if forward:
            ahead, normed, refs = refs[:count], refs[count], refs[count + 1 :]
        else:
            normed = normed_in[0]
        weight, down, held, whole, sems = refs
        handles = fetch(place_ref, layer, mine, other, weight, sems.at[pl.ds(0, 1)])
        down_handles = fetch(place_ref, layer, d_mine, d_other, down, sems.at[pl.ds(1, 1)])
        put_rows(parts_in, g_out, place_ref)
        if forward:
            put_rows(normed_in, normed, place_ref)
        if padded != hidden:
            down[hidden:, :] = jnp.zeros((padded - hidden, width), half)
            held[:, padded - LANES :] = jnp.zeros((total_rows, LANES), half)
        finish(handles)
        finish(down_handles)
        for at, size in tile_ranges(columns, 4):
            inside = slice(at // 2, (at + size) // 2)
            gate, up = gates_of(mm(normed[...], weight[:, at : at + size]))
            g_active = mm_nt(g_out[...], down[inside, :])
            open_ = sig(gate)
            lit = gate * open_
            product = (lit * up).astype(half)
            active[:, inside] = product
            if forward:
                held[:, inside] = product
            g_up = g_active * lit
            g_gate = g_active * up * (open_ * (1.0 + gate - lit))
            g_gates[:, at : at + size] = tiles_of(g_gate, g_up).astype(half)
        whole[...] = mm_nt(g_gates[...], weight[...])
        pulls = jnp.sum(whole[...] * normed[...].astype(wide), axis=0, keepdims=True) / gain_ref[...]
        g_gain[...] = jnp.broadcast_to(pulls, g_gain.shape)
        take_rows(whole, terms, place_ref)
        if forward:
            whole[...] = mm(held[...], down[...])
            take_rows(whole, ahead, place_ref)

    term_shapes = [shape((rows, width), wide if r == 0 else half) for r in range(count)]
    outs = term_shapes + [
        shape((total_rows, width)),
        shape((total_rows, columns)),
        shape((total_rows, hidden)),
        shape((8, width), wide),
    ]
    if forward:
        outs = outs + term_shapes + [shape((total_rows, width))]
    scratch = [
        pltpu.VMEM((width, columns), half),
        pltpu.VMEM((padded, width), half),
        pltpu.VMEM((total_rows, padded), half),
        pltpu.VMEM((total_rows, width), wide),
        pltpu.SemaphoreType.DMA((2,)),
    ]
    specs = [smem] + [vmem] * (count + len(normed_parts) + 1) + [anywhere] * 4
    flops = 2 * total_rows * width * (2 * columns + hidden)
    moved = 2 * (width * (columns + hidden) + total_rows * (6 * width + columns + hidden))
    return call(body, outs, specs, scratch, flops, moved, "feed_backward")(
        place, *parts, *normed_parts, gain, *weights
    )


def pack_small(norm_one, norm_two, decay, bias, persistent, lengths):
    cut, heads_all = decay.shape
    slots, columns = persistent.shape
    heads = bias.shape[1]
    lanes = cut // LANES
    total = 16 * (1 + lanes + columns // LANES)

    batches = lengths.shape[0]

    def body(lengths_ref, one_ref, two_ref, decay_ref, bias_ref, fixed_ref, out):
        rows = [ref[0:1, b * LANES : (b + 1) * LANES].astype(wide) for ref in (one_ref, two_ref) for b in range(lanes)]
        rows.append(jnp.concatenate([bias_ref[...].astype(wide), jnp.zeros((1, LANES - heads), wide)], axis=1))
        for m in range(batches):
            for part in (lengths_ref[m] // 64, lengths_ref[m] % 64):
                rows.append(jnp.full((1, LANES), part.astype(wide)))
        rows.append(jnp.zeros((16 - len(rows), LANES), wide))
        out[0:16, :] = jnp.concatenate(rows, axis=0).astype(half)
        padded = jnp.concatenate([decay_ref[...].astype(wide), jnp.zeros((cut, LANES - heads_all), wide)], axis=1).T
        for b in range(lanes):
            out[16 * (1 + b) : 16 * (2 + b), :] = padded[0:16, b * LANES : (b + 1) * LANES].astype(half)
        for c in range(columns // LANES):
            at = 16 * (1 + lanes + c)
            out[at : at + slots, :] = fixed_ref[:, c * LANES : (c + 1) * LANES]

    return call(body, [shape((total, LANES))], [smem] + [vmem] * 5, [], 0, 1 << 17, "pack_small")(
        lengths, norm_one, norm_two, decay, bias, persistent
    )[0]


def beside(rows, mine, other):
    height, width = rows.shape
    groups = 2 * mine.shape[0] // 16
    across = width // LANES
    below = 16 * -(-groups // across)

    def body(rows_ref, mine_ref, other_ref, out):
        out[0:height, :] = rows_ref[...]
        out[height:, :] = jnp.zeros((below, width), half)
        for g in range(groups):
            ref, at = (mine_ref, g) if g < groups // 2 else (other_ref, g - groups // 2)
            spot = (height + 16 * (g // across), LANES * (g % across))
            out[spot[0] : spot[0] + 16, spot[1] : spot[1] + LANES] = ref[16 * at : 16 * at + 16, :]

    outs = [shape((height + below, width))]
    return call(body, outs, [vmem] * 3, [], 0, 1 << 20, "beside")(rows, mine, other)[0]


def turn_bias(row):
    at = lax.broadcasted_iota(jnp.int32, (16, LANES), 0) == lax.broadcasted_iota(jnp.int32, (16, LANES), 1)
    return jnp.broadcast_to(jnp.sum(jnp.where(at, row, 0.0), axis=1, keepdims=True), (16, LANES))


def unpack_small(heads, slots, height, rows, place, parts):
    count = len(parts)
    width = parts[0].shape[1]
    cut = width // count
    lanes = cut // LANES
    across = width // LANES
    inner = heads * LANES

    def body(place_ref, *refs):
        ins, outs, length, held = refs[:count], refs[count:-2], refs[-2], refs[-1]
        f = place_ref[0]
        for r, part in enumerate(ins):
            for k in range(2):
                layer = place_ref[1] if k == 0 else 1 - place_ref[1]
                for g in range(rows // 16):
                    at = k * (rows // 16) + g
                    top, left = height + 16 * (at // across), LANES * (at % across)
                    held[layer, f ^ r, 16 * g : 16 * g + 16, :] = part[top : top + 16, left : left + LANES].astype(wide)
        at = 2 * lanes + 1 + 2 * place_ref[1]
        found = held[place_ref[1], place_ref[2], pl.ds(at, 2), :]
        length[...] = jnp.broadcast_to(found[0:1] * 64.0 + found[1:2], length.shape).astype(jnp.int32)
        for layer in range(2):
            one, two, decay, bias, fixed = outs[5 * layer : 5 * layer + 5]
            for t in range(count):
                for b in range(lanes):
                    at = t * cut + b * LANES
                    one[0:1, at : at + LANES] = held[layer, t, b : b + 1, :]
                    two[0:1, at : at + LANES] = held[layer, t, lanes + b : lanes + b + 1, :]
                    group = held[layer, t, 16 * (1 + b) : 16 * (2 + b), :]
                    row = lax.broadcasted_iota(jnp.int32, (16, LANES), 0)
                    mine = [
                        jnp.sum(jnp.where(row == f * heads + h, group, 0.0), axis=0, keepdims=True) for h in range(heads)
                    ]
                    mine.append(jnp.zeros((16 - heads, LANES), wide))
                    decay[:, at : at + LANES] = jnp.concatenate(mine, axis=0).astype(half)
            bias[...] = turn_bias(held[layer, f, 2 * lanes : 2 * lanes + 1, :])
            for kind in range(2):
                source = kind * (count // 2) + f // 2
                for h in range(heads):
                    at = pl.multiple_of(16 * (1 + lanes + (f % 2) * heads + h), 16)
                    lane = kind * inner + h * LANES
                    fixed[:, lane : lane + LANES] = held[layer, source, pl.ds(at, slots), :].astype(half)

    outs = [
        shape((1, width), wide),
        shape((1, width), wide),
        shape((16, width)),
        shape((16, LANES), wide),
        shape((slots, 2 * inner)),
    ] * 2 + [shape((8, LANES), jnp.int32)]
    scratch = [pltpu.VMEM((2, count, rows, LANES), wide)]
    made = call(body, outs, [smem] + [vmem] * count, scratch, 0, 1 << 20, "unpack_small")(place, *parts)
    return [list(pair) for pair in zip(made[:5], made[5:10])], made[10][0, 0]


def join_forward(rounded, terms, residual, gain):
    dims = terms[0].shape

    def body(*refs):
        count = len(terms)
        residual_ref, refs_in = refs[count], refs[:count]
        total = residual_ref[...].astype(wide)
        for ref in refs_in:
            total = total + ref[...].astype(wide)
        if gain is None:
            refs[count + 1][...] = total.astype(half)
            return
        gain_ref, out, normed = refs[count + 1 :]
        if rounded:
            total = total.astype(half).astype(wide)
        out[...] = total.astype(out.dtype)
        scale = lax.rsqrt(jnp.mean(total * total, axis=1, keepdims=True) + epsilon)
        normed[...] = (total * scale * gain_ref[...]).astype(half)

    outs = [shape(dims, half if rounded else wide), shape(dims)]
    inputs = [*terms, residual, gain]
    if gain is None:
        outs, inputs = [shape(dims)], inputs[:-1]
    return call(body, outs, [vmem] * len(inputs), [], 0, dims[0] * dims[1] * 20, "join_forward")(*inputs)


def join_backward(terms, values, gain, onward):
    dims = terms[0].shape

    def body(*refs):
        count = len(terms)
        values_ref, gain_ref, onward_ref, out, rounded = refs[count:]
        grad = refs[0][...].astype(wide)
        for ref in refs[1:count]:
            grad = grad + ref[...].astype(wide)
        v = values_ref[...].astype(wide)
        scale = lax.rsqrt(jnp.mean(v * v, axis=1, keepdims=True) + epsilon)
        unit = v * scale
        scaled = grad * gain_ref[...]
        through = scale * (scaled - unit * jnp.mean(scaled * unit, axis=1, keepdims=True))
        total = onward_ref[...].astype(wide) + through
        out[...] = total
        rounded[...] = total.astype(half)

    outs = [shape(dims, wide), shape(dims)]
    inputs = [*terms, values, gain, onward]
    return call(body, outs, [vmem] * len(inputs), [], 0, dims[0] * dims[1] * 24, "join_backward")(*inputs)


SMALL = 16


def lane_half(source, target, which, count):
    for t in range(count):
        at = pl.multiple_of(t * 2 * LANES + which * LANES, LANES)
        target[:, t * LANES : (t + 1) * LANES] = source[:, pl.ds(at, LANES)]


STRIPS = 4


def strip_of(columns):
    return SMALL * -(-(columns + SMALL) // (SMALL * STRIPS))


def packer(packed):
    def put(at, value):
        packed[at : at + value.shape[0], :] = value.astype(half)

    return put


def strip_packer(packed, strip, chunk):
    def put(t, at, value):
        done = 0
        while done < value.shape[0]:
            k, row = divmod(at + done, strip)
            size = min(value.shape[0] - done, strip - row)
            where = k * chunk + t * strip + row
            packed[where : where + size, :] = value[done : done + size].astype(half)
            done += size

    return put


def small_rows(rows):
    found = jnp.concatenate(rows, axis=0)
    return jnp.concatenate([found, jnp.zeros((SMALL - found.shape[0], LANES), wide)], axis=0)


def grad_call(body, chunks, total, inputs, scratch, flops, name):
    outs = [shape((total, LANES))] + [shape((b - a, LANES)) for a, b in split_rows(total, chunks)]
    scratch = scratch + [pltpu.VMEM((total, LANES), half)]
    moved = sum(v.size * v.dtype.itemsize for v in inputs) + total * LANES * 4
    return call(body, outs, [smem] + [vmem] * (len(inputs) - 1), scratch, flops, moved, name)(*inputs)


def grad_feed(chunks, count, place, normed, g_gates, active, g_out, g_gain):
    total_rows, width = normed.shape
    columns, hidden = g_gates.shape[1], active.shape[1]
    tiles = columns // LANES
    strip = strip_of(columns)
    chunk = count * strip + hidden
    side = width // 2

    def body(place_ref, normed_ref, gates_ref, active_ref, g_out_ref, gain_ref, *refs):
        sent, outs, left, packed = refs[0], refs[1:-2], refs[-2], refs[-1]
        for turn in range(2):
            which = 1 - place_ref[1] if turn == 0 else place_ref[1]
            packed_here = sent if turn == 0 else packed
            put, put_row = packer(packed_here), strip_packer(packed_here, strip, chunk)
            lane_half(normed_ref, left, which, count)
            turned = left[...].T
            for at in range(0, columns, 2 * LANES):
                size = min(2 * LANES, columns - at)
                tile = mm(turned, gates_ref[:, at : at + size])
                for t in range(count):
                    for c in range(size // LANES):
                        put_row(t, at + c * LANES, tile[t * LANES : (t + 1) * LANES, c * LANES : (c + 1) * LANES])
            for t in range(count):
                at = pl.multiple_of(t * 2 * LANES + which * LANES, LANES)
                rest = STRIPS * strip - columns - SMALL
                put_row(t, columns, small_rows([gain_ref[0:1, pl.ds(at, LANES)]]))
                put_row(t, columns + SMALL, jnp.zeros((rest, LANES), wide))
            active_t = active_ref[...].T
            for c in range(0, side // LANES, 2):
                at = pl.multiple_of(which * side + c * LANES, LANES)
                tile = mm(active_t, g_out_ref[:, pl.ds(at, 2 * LANES)])
                put(c * chunk + count * strip, tile[:, :LANES])
                put((c + 1) * chunk + count * strip, tile[:, LANES:])
        chunk_out(packed, outs)

    inputs = [place, normed, g_gates, active, g_out, g_gain]
    scratch = [pltpu.VMEM((total_rows, side), half)]
    flops = total_rows * width * (columns + hidden)
    return grad_call(body, chunks, STRIPS * chunk, inputs, scratch, flops, "grad_feed")


def grad_mix(chunks, total, count, place, normed, g_projected, combined, branch, g_logits, g_gain, g_fixed):
    total_rows, width = normed.shape
    columns, inner = g_projected.shape[1], combined.shape[1]
    heads = inner // LANES
    slots = g_fixed.shape[0]
    block = columns + SMALL + slots
    side = width // 2

    def body(place_ref, normed_ref, proj_ref, comb_ref, branch_ref, logits_ref, gain_ref, fixed_ref, *refs):
        sent, outs, left, packed = refs[0], refs[1:-2], refs[-2], refs[-1]
        for turn in range(2):
            which = 1 - place_ref[1] if turn == 0 else place_ref[1]
            put = packer(sent if turn == 0 else packed)
            lane_half(normed_ref, left, which, count)
            turned = left[...].T
            for at in range(0, columns, 2 * LANES):
                tile = mm(turned, proj_ref[:, at : at + 2 * LANES])
                for t in range(count):
                    for c in range(2):
                        put(t * block + at + c * LANES, tile[t * LANES : (t + 1) * LANES, c * LANES : (c + 1) * LANES])
            logits = logits_ref[...]
            decay = sum(mm(piece, left[...]) for piece in three_way(logits)[:2])
            near = pl.multiple_of(which * LANES, LANES)
            for t in range(count):
                at = pl.multiple_of(t * 2 * LANES + which * LANES, LANES)
                rows = [decay[0:heads, t * LANES : (t + 1) * LANES], gain_ref[0:1, pl.ds(at, LANES)]]
                put(t * block + columns, small_rows(rows))
                keys_here = (place_ref[0] // 2 == t).astype(wide)
                values_here = (place_ref[0] // 2 + 2 == t).astype(wide)
                fixed = fixed_ref[:, pl.ds(near, LANES)] * keys_here
                fixed = fixed + fixed_ref[:, pl.ds(pl.multiple_of(inner + near, LANES), LANES)] * values_here
                put(t * block + columns + SMALL, fixed)
            comb_t = comb_ref[:, pl.ds(near, LANES)].T
            for c in range(0, width // LANES, 2):
                tile = mm(comb_t, branch_ref[:, c * LANES : (c + 2) * LANES])
                put(count * block + c * LANES, tile[:, :LANES])
                put(count * block + (c + 1) * LANES, tile[:, LANES:])
            put(count * block + width, jnp.broadcast_to(jnp.sum(logits, axis=1, keepdims=True), (SMALL, LANES)))
            (sent if turn == 0 else packed)[count * block + width + SMALL :, :] = jnp.zeros(
                (total - count * block - width - SMALL, LANES), half
            )
        chunk_out(packed, outs)

    inputs = [place, normed, g_projected, combined, branch, g_logits, g_gain, g_fixed]
    scratch = [pltpu.VMEM((total_rows, side), half)]
    flops = total_rows * width * (columns + inner)
    return grad_call(body, chunks, total, inputs, scratch, flops, "grad_mix")


def split_rows(total, chunks):
    units = total // SMALL
    edges = [SMALL * (units * k // chunks) for k in range(chunks)] + [total]
    return list(zip(edges[:-1], edges[1:]))


def chunk_out(whole, outs):
    at = 0
    for out in outs:
        out[...] = whole[at : at + out.shape[0], :]
        at += out.shape[0]


def spread(count, block, place, chunks, add=False):
    total = sum(chunk.shape[0] for chunk, _ in chunks)

    def body(place_ref, *refs):
        ins, outs, whole = refs[: 2 * len(chunks)], refs[2 * len(chunks) : -1], refs[-1]
        at = 0
        if add:
            for one, two in zip(ins[0::2], ins[1::2]):
                whole[at : at + one.shape[0], :] = (one[...].astype(wide) + two[...].astype(wide)).astype(half)
                at += one.shape[0]
        for inner in range(0 if add else 2):

            @pl.when(place_ref[3] == inner)
            def _(inner=inner):
                at = 0
                for chunk in ins[1 - inner :: 2]:
                    whole[at : at + chunk.shape[0], :] = chunk[...]
                    at += chunk.shape[0]

        take_rows(whole, outs[:count], place_ref)
        outs[count][...] = whole[count * block :, :]

    outs = [shape((block, LANES))] * count + [shape((total - count * block, LANES))]
    scratch = [pltpu.VMEM((total, LANES), half)]
    flat = [piece for pair in chunks for piece in pair]
    return call(body, outs, [smem] + [vmem] * len(flat), scratch, 0, total * 768, "spread")(place, *flat)


def spread_strips(count, strip, place, chunks):
    chunk = chunks[0][0].shape[0]
    own = chunk - count * strip
    many = len(chunks)

    def body(place_ref, *refs):
        ins, outs = refs[: 2 * many], refs[2 * many :]
        for inner in range(2):

            @pl.when(place_ref[3] == inner)
            def _(inner=inner):
                for k, ref in enumerate(ins[1 - inner :: 2]):
                    for r in range(count):
                        at = pl.multiple_of((place_ref[0] ^ r) * strip, SMALL)
                        outs[r][k * strip : (k + 1) * strip, :] = ref[pl.ds(at, strip), :]
                    outs[count][k * own : (k + 1) * own, :] = ref[count * strip :, :]

    outs = [shape((many * strip, LANES))] * count + [shape((many * own, LANES))]
    flat = [piece for pair in chunks for piece in pair]
    return call(body, outs, [smem] + [vmem] * len(flat), [], 0, many * chunk * 768, "spread")(place, *flat)


def collect_feed(columns, place, sets):
    count = len(sets[0][0])
    strip = strip_of(columns)
    own = sum(local.shape[0] for _, local in sets)
    total = count * columns + SMALL + own
    flat = [piece for parts, local in sets for piece in (*parts, local)]

    def body(place_ref, *refs):
        ins, whole = refs[: len(flat)], refs[-1]
        first, below = 0, count * columns + SMALL
        small = jnp.zeros((SMALL, LANES), wide)
        for number, (parts, local) in enumerate(sets):
            here = ins[number * (count + 1) : (number + 1) * (count + 1)]
            many = parts[0].shape[0] // strip
            for k in range(many):
                row = (first + k) * strip
                size = min(strip, columns - row)
                for r in range(count):
                    at = pl.multiple_of((place_ref[0] ^ r) * columns + row, SMALL)
                    whole[pl.ds(at, size), :] = here[r][k * strip : k * strip + size, :]
                    if size < strip:
                        small = small + here[r][k * strip + size : k * strip + size + SMALL, :].astype(wide)
            first += many
            whole[below : below + local.shape[0], :] = here[count][...]
            below += local.shape[0]
        whole[count * columns : count * columns + SMALL, :] = small.astype(half)

    outs = [shape((total, LANES))]
    return call(body, outs, [smem] + [vmem] * len(flat), [], 0, total * 512, "collect_feed")(place, *flat)


def collect_mix(chunks, heads, total, place, parts, local):
    count = len(parts)
    slots = parts[0].shape[0] % (3 * heads * LANES) - SMALL
    columns = parts[0].shape[0] - SMALL - slots
    filled = count * columns + SMALL + 2 * slots + local.shape[0]

    def body(place_ref, *refs):
        parts_in, local_ref, outs, whole, few = refs[:count], refs[count], refs[count + 1 : -2], refs[-2], refs[-1]
        for r, part in enumerate(parts_in):
            source = place_ref[0] ^ r
            at = pl.multiple_of(source * columns, columns)
            whole[pl.ds(at, columns), :] = part[0:columns, :]
            few[pl.ds(source, 1)] = part[columns:, :].astype(wide)[None]
        base = count * columns
        decay = [few[t, 0:heads, :] for t in range(count)]
        gain = sum(few[t, heads : heads + 1, :] for t in range(count))
        whole[base : base + SMALL, :] = small_rows(decay + [gain]).astype(half)
        near = (place_ref[0] % 2) * 2
        for k in range(2):
            at = base + SMALL + k * slots
            whole[at : at + slots, :] = few[near + k, SMALL:, :].astype(half)
        whole[base + SMALL + 2 * slots : filled, :] = local_ref[...]
        whole[filled:, :] = jnp.zeros((total - filled, LANES), half)
        chunk_out(whole, outs)

    outs = [shape((b - a, LANES)) for a, b in split_rows(total, chunks)]
    scratch = [pltpu.VMEM((total, LANES), half), pltpu.VMEM((count, SMALL + slots, LANES), wide)]
    return call(body, outs, [smem] + [vmem] * (count + 1), scratch, 0, total * 512, "collect_mix")(place, *parts, local)


def gather_halves(place_ref, ins, halves, sems, edges):
    chunks = len(edges) - 1
    handles = []
    for side in range(2):
        for c in range(chunks):
            spot = place_ref[1] if side == 0 else 1 - place_ref[1]
            where = halves.at[spot, pl.ds(edges[c], edges[c + 1] - edges[c])]
            sem = sems.at[side * chunks + c]
            for layer in range(2):
                source = ins[layer * 2 * chunks + side * chunks + c]

                @pl.when(place_ref[1] == layer)
                def _(source=source, where=where, sem=sem):
                    pltpu.make_async_copy(source, where, sem).start()

            handles.append(pltpu.make_async_copy(ins[side * chunks + c], where, sem))
    finish(handles)


def unpack(body, totals, out_shape, place, name):
    chunks = len(totals[0][0])
    edges = [0]
    for chunk in totals[0][0]:
        edges.append(edges[-1] + chunk.shape[0])

    def whole_body(place_ref, *refs):
        ins, outs, halves, sems = refs[: 4 * chunks], refs[4 * chunks : -2], refs[-2], refs[-1]
        gather_halves(place_ref, ins, halves, sems, edges)
        body(place_ref, halves, *outs)

    inputs = [piece for layer in totals for side in layer for piece in side]
    scratch = [pltpu.VMEM((2, edges[-1], LANES), half), pltpu.SemaphoreType.DMA((2 * chunks,))]
    moved = sum(o.size * 4 for o in out_shape) + 4 * edges[-1] * LANES
    return call(whole_body, out_shape, [smem] + [anywhere] * len(inputs), scratch, 0, moved, name)(place, *inputs)


def unpack_feed(count, columns, hidden, width, totals, place):
    part = width // count
    side = width // 2
    chunks = len(totals[0][0])
    edges = [0]
    for chunk in totals[0][0]:
        edges.append(edges[-1] + chunk.shape[0])
    steps = 4
    span = count * columns // steps
    tiles = span // LANES

    def body(place_ref, *refs):
        ins, (gate_up, down, gain), halves, sems = refs[: 4 * chunks], refs[4 * chunks : -2], refs[-2], refs[-1]
        step = pl.program_id(0)

        @pl.when(step == 0)
        def _():
            gather_halves(place_ref, ins, halves, sems, edges)
            base = count * columns
            for h in range(2):
                gain[0:1, h * LANES : (h + 1) * LANES] = halves[h, base : base + SMALL, :].astype(wide)[0:1]

        low = lax.broadcasted_iota(jnp.int32, (LANES, LANES), 1) < PAIR
        for is_up in range(2):

            @pl.when(step // 2 == is_up)
            def _(is_up=is_up):
                for h in range(2):
                    for m in range(tiles):
                        at = pl.multiple_of((step % 2) * 2 * span + 2 * m * LANES, LANES)
                        even = halves[h, pl.ds(at, LANES), :].astype(wide)
                        odd = halves[h, pl.ds(at + LANES, LANES), :].astype(wide)
                        if is_up:
                            value = jnp.where(low, pltpu.roll(even, PAIR, 1), odd)
                        else:
                            value = jnp.where(low, even, pltpu.roll(odd, PAIR, 1))
                        gate_up[h * LANES : (h + 1) * LANES, m * LANES : (m + 1) * LANES] = value

        base = count * columns + SMALL
        for c in range(2):
            at = pl.multiple_of(base + ((step % 2) * 2 + c) * hidden, SMALL)
            down[:, c * LANES : (c + 1) * LANES] = halves[step // 2, pl.ds(at, hidden), :].astype(wide)

    outs = [shape((part, count * columns), wide), shape((hidden, width), wide), shape((1, part), wide)]
    inputs = [piece for layer in totals for half_side in layer for piece in half_side]
    moved = sum(o.size * 4 for o in outs) + 4 * edges[-1] * LANES
    return pl.pallas_call(
        body,
        grid=(steps,),
        out_shape=outs,
        in_specs=[smem] + [anywhere] * len(inputs),
        out_specs=[
            pl.BlockSpec((part, span), lambda i: (0, i)),
            pl.BlockSpec((hidden, width // steps), lambda i: (0, i)),
            pl.BlockSpec((1, part), lambda i: (0, 0)),
        ],
        scratch_shapes=[pltpu.VMEM((2, edges[-1], LANES), half), pltpu.SemaphoreType.DMA((2 * chunks,))],
        compiler_params=pltpu.CompilerParams(vmem_limit_bytes=16 * 1024 * 1024),
        cost_estimate=pl.CostEstimate(flops=0, bytes_accessed=moved, transcendentals=0),
        name="unpack_feed",
    )(place, *inputs)


def unpack_mix(count, heads, slots, width, totals, place):
    part = width // count
    inner = heads * LANES
    columns = 3 * inner

    def body(place_ref, halves, qkv, out, gain, decay, bias, fixed):
        for h in range(2):
            rows = slice(h * LANES, (h + 1) * LANES)
            for t in range(count):
                for kind in range(3):
                    for head in range(heads):
                        source = t * columns + kind * inner + head * LANES
                        at = kind * count * inner + t * inner + head * LANES
                        qkv[rows, at : at + LANES] = halves[h, source : source + LANES, :].astype(wide)
            base = count * columns
            small = halves[h, base : base + SMALL, :].astype(wide)
            padded = jnp.concatenate([small, jnp.zeros((LANES - SMALL, LANES), wide)], axis=0).T
            decay[rows, :] = padded[:, 0 : count * heads]
            gain[0:1, rows] = small[count * heads : count * heads + 1]
            for k in range(2):
                at = base + SMALL + k * slots
                lanes = slice(k * inner + h * LANES, k * inner + (h + 1) * LANES)
                fixed[:, lanes] = halves[h, at : at + slots, :].astype(wide)
            base += SMALL + 2 * slots
            for c in range(width // LANES):
                source = base + c * LANES
                out[rows, c * LANES : (c + 1) * LANES] = halves[h, source : source + LANES, :].astype(wide)
            if h == 0:
                found = halves[h, base + width : base + width + SMALL, :].astype(wide)
                bias[...] = jnp.concatenate([found[k : k + 1, 0:1] for k in range(heads)], axis=1)

    outs = [
        shape((part, count * columns), wide),
        shape((inner, width), wide),
        shape((1, part), wide),
        shape((part, count * heads), wide),
        shape((1, heads), wide),
        shape((slots, 2 * inner), wide),
    ]
    return unpack(body, totals, outs, place, "unpack_mix")


def tie(*values):
    return lax.optimization_barrier(values)


def exchange(value, axis, distance):
    count = lax.axis_size(axis)
    return lax.ppermute(value, axis, [(i, i ^ distance) for i in range(count)])


def gather_parts(block, axis):
    count = lax.axis_size(axis)
    far = tie(*(exchange(block, axis, r) for r in reversed(range(1, count))))
    return [block, *reversed(far)]


def trade_terms(blocks, axis):
    found = trade_parts(blocks, axis)
    return found


def trade_parts(blocks, axis):
    far = {r: exchange(blocks[r], axis, r) for r in reversed(range(1, len(blocks)))}
    return [blocks[0]] + [far[r] for r in range(1, len(blocks))]


def plane_device(
    tokens,
    lengths,
    cotangent,
    norm_one,
    qkv_weight,
    decay_weight,
    decay_bias,
    persistent,
    out_weight,
    norm_two,
    gate_up,
    down_weight,
):
    ctx_count, count = lax.axis_size("ctx"), lax.axis_size("fsdp")
    section, ctx, fsdp = (lax.axis_index(a) for a in ("section", "ctx", "fsdp"))
    rows, width = tokens.shape[2:]
    heads = decay_bias.shape[1]
    size = width // (heads * count)
    inner = heads * size

    def own_batch(value):
        return lax.dynamic_index_in_dim(value, section, 0, False)[0]

    pairs = []
    for s in range(2):
        flip = s * (count - 1)
        for c in range(ctx_count):
            for f in range(count):
                here, there = c * count + f, (f ^ flip) * count + (c ^ flip)
                pairs.append((s * ctx_count * count + here, s * ctx_count * count + there))

    def turn_plane(value):
        return lax.ppermute(value, ("section", "ctx", "fsdp"), pairs)

    def swap(value):
        return exchange(value, "section", 1)

    slots = persistent.shape[1]
    flip = section * (count - 1)
    spot = jnp.stack([fsdp, section, ctx ^ flip]).astype(jnp.int32)
    x_own, qkv_shard = tie(own_batch(tokens), qkv_weight[0])
    x_in = turn_plane(x_own)
    qkv_packed = pack_heads(count, qkv_shard, spot)
    qkv_parts = trade_parts(qkv_packed, "fsdp")
    small = pack_small(norm_one, norm_two, decay_weight[0], decay_bias, persistent[0], lengths[:, 0, 0])
    x_parts = gather_parts(beside(x_in, small, swap(small)), "fsdp")
    (gains_one, gains_two, decays, biases, fixeds), length = unpack_small(
        heads, slots, rows, small.shape[0], spot, x_parts
    )
    gu_packed = pack_gates(count, gate_up[0], spot)
    qkv_parts, gu_packed, _, g_own = tie(qkv_parts, gu_packed, x_parts, own_batch(cotangent))
    g_in = turn_plane(g_own)
    gu_parts = trade_parts(gu_packed, "fsdp")
    qkv_mine = assemble(spot, qkv_parts)
    qkv_other = swap(qkv_mine)
    out_mine = out_weight[0]
    out_other = swap(out_mine)
    mix_weights = (qkv_mine, qkv_other, out_mine, out_other)
    down_mine = down_weight[0]
    down_other = swap(down_mine)
    length, down_other = tie(length, down_other)
    place = jnp.stack([fsdp, section, length, (ctx == 1) | (ctx == 2)]).astype(jnp.int32)
    seat = jnp.stack([fsdp ^ flip, section, length]).astype(jnp.int32)
    hidden = down_mine.shape[0]
    columns = gu_packed[0].shape[1]

    def mix_first_half(layer, parts):
        *terms, combined, seen, projected, logits = mix_forward(
            layer, heads, size, seat, parts, rows, gains_one[layer], mix_weights, decays[layer], biases[layer], fixeds[layer]
        )
        return terms, (seen, projected, logits, combined)

    def mix_second_half(layer, terms, x):
        middle, normed_two = join_forward(False, trade_terms(terms, "fsdp"), x, gains_two[layer])
        return middle, gather_parts(normed_two, "fsdp")

    def feed_step(layer, parts, saved):
        *terms, g_rows, g_gates, active, g_gain = feed_backward(
            layer, seat, parts, [saved[6]], gains_two[layer], feed_weights, False
        )
        return terms, (saved[6], g_gates, active, g_rows, g_gain)

    def mix_step(layer, parts, saved):
        x, seen, projected, logits, combined, middle, seen_two = saved
        *terms, branch, g_projected, g_logits, g_fixed, g_gain = mix_backward(
            layer, heads, size, seat, parts, mix_weights, decays[layer], fixeds[layer], projected, logits, seen, gains_one[layer]
        )
        return terms, (seen, g_projected, combined, branch, g_logits, g_gain, g_fixed)

    inside = (ctx == 1) | (ctx == 2)
    line = {"queue": [], "inward": None, "across": None, "total": None, "flight": (None, None), "sums": []}

    def begin():
        own = line["queue"].pop(0) if line["queue"] else None
        total = line["total"]
        if own is not None and total is not None:
            sent = jnp.where(inside, total, own)
            route = [(0, 1), (3, 2), (1, 0), (2, 3)]
        else:
            sent = own if total is None else total
            route = [(0, 1), (3, 2)] if total is None else [(1, 0), (2, 3)]
        pair = line["across"]
        line["sent"] = (sent, pair, own, total is not None)
        return [v for v in (sent, pair) if v is not None], route

    def go(values, route):
        values = list(values)
        sent, pair, own, closing = line["sent"]
        sent = values.pop(0) if sent is not None else None
        pair = values.pop(0) if pair is not None else None
        line["sent"] = (sent, pair, own, closing)
        flight = [None, None]
        if sent is not None:
            flight[0] = lax.ppermute(sent, "ctx", route)
        if pair is not None:
            flight[1] = lax.ppermute(pair, "ctx", [(1, 2), (2, 1)])
        line["flight"] = flight

    def plus(a, b):
        return (a.astype(wide) + b.astype(wide)).astype(half)

    def step(*held, more=None):
        landed, crossed = line["flight"]
        waiting = [v for v in (landed, crossed) if v is not None]
        held, waiting = tie(held, waiting)
        if landed is not None:
            landed = waiting.pop(0)
        if crossed is not None:
            crossed = waiting.pop(0)
        sent, pair, own, closing = line.get("sent", (None, None, None, False))
        line["total"] = None if pair is None else plus(pair, crossed)
        line["across"] = None if own is None else plus(own, landed)
        if closing:
            line["sums"].append((sent, landed))
        if more is not None:
            line["queue"].extend(more(*held))
        ready, route = begin()
        held, ready = tie(held, ready)
        go(ready, route)
        return held

    def taken(number, skip=0):
        found = line["sums"][skip : skip + number]
        del line["sums"][skip : skip + number]
        return found

    terms, kept = mix_first_half(0, x_parts)
    terms, gu_parts[1], g_in = tie(terms, gu_parts[1], g_in)
    terms, gu_parts = tie(trade_terms(terms, "fsdp"), gu_parts)
    gu_mine = assemble(spot, gu_parts)
    feed_weights = (gu_mine, swap(gu_mine), down_mine, down_other)
    middle, normed_two = join_forward(False, terms, x_in, gains_two[0])
    parts = gather_parts(normed_two, "fsdp")
    *terms, seen_two = feed_forward(0, seat, parts, feed_weights)
    terms = trade_terms(terms, "fsdp")
    saved_first = (x_in, *kept, middle, seen_two)
    between = join_forward(True, terms, middle, None)[0]
    terms, kept = mix_first_half(1, gather_parts(between, "fsdp"))
    terms, g_three, g_two, g_one = tie(terms, *(exchange(g_in, "fsdp", r) for r in (3, 2, 1)))
    middle, parts = mix_second_half(1, terms, between)
    made = feed_backward(1, seat, [g_in, g_one, g_two, g_three], parts, gains_two[1], feed_weights, True)
    terms, (g_rows, g_gates, active, g_gain), terms_out, seen_two = made[:4], made[4:8], made[8:12], made[12]
    feed = (seen_two, g_gates, active, g_rows, g_gain)
    saved_second = (between, *kept, middle, seen_two)

    def to_owner(layer, chunks):
        return [lax.ppermute(chunk, "section", [(1 - layer, layer)]) for chunk in chunks]

    def trade(block, chunks, add=False):
        *blocks, local = spread(count, block, place, chunks, add)
        return trade_parts(blocks, "fsdp"), local

    def trade_strips(chunks):
        *blocks, local = spread_strips(count, strip, place, chunks)
        return trade_parts(blocks, "fsdp"), local

    strip = strip_of(columns)
    pad = 2 * (count * strip + hidden)
    mix_block = 3 * inner + SMALL + slots

    def summed(own, received):
        at, chunks = 0, []
        for chunk in own:
            chunks.append(plus(chunk, received[at : at + chunk.shape[0]]))
            at += chunk.shape[0]
        return chunks

    sent, *own = grad_feed(4, count, place, *feed)
    terms, sent = tie(trade_terms(terms, "fsdp"), sent)
    g_middle, g_branch = join_backward(terms, saved_second[5], gains_two[1], g_in)
    parts = gather_parts(g_branch, "fsdp")
    parts, received = tie(parts, swap(sent))
    (parts,) = step(parts, more=lambda _: summed(own, received))
    terms, mix = mix_step(1, parts, saved_second)
    terms, terms_out = step(terms, trade_terms(terms_out, "fsdp"))
    out = join_forward(True, terms_out, saved_second[5], None)[0]
    sent, *own = grad_mix(2, pad, count, place, *mix)
    terms, sent = step(trade_terms(terms, "fsdp"), sent)
    g_middle, g_branch = join_backward(terms, between, gains_one[1], g_middle)
    parts, sent = step(gather_parts(g_branch, "fsdp"), sent)
    terms, feed = feed_step(0, parts, saved_first)
    terms, _ = step(terms, swap(sent), more=lambda _, received: summed(own, received))
    sent, *own = grad_feed(4, count, place, *feed)
    terms, sent = step(trade_terms(terms, "fsdp"), sent)
    received = swap(sent)
    g_middle, g_branch = join_backward(terms, saved_first[5], gains_two[0], g_branch)
    g_branch, received = tie(g_branch, received)
    (parts,) = step(gather_parts(g_branch, "fsdp"), more=lambda _: summed(own, received))
    f1 = trade_strips(taken(4))
    terms, mix = mix_step(0, parts, saved_first)
    terms, f1 = step(terms, f1)
    feed_second = collect_feed(columns, place, [f1])
    sent, *own = grad_mix(1, pad, count, place, *mix)
    (terms,) = step(trade_terms(terms, "fsdp"))
    g_input = join_backward(terms, x_in, gains_one[0], g_middle)[1]
    received = swap(sent)
    g_input, received, feed_second = step(g_input, received, feed_second)
    m0 = trade(mix_block, [(own[0], received)], add=True)
    (m0,) = step(m0, more=lambda pieces: collect_mix(2, heads, pad, place, *pieces))
    f0 = trade_strips(taken(2, 2))
    (f0,) = step(f0)
    m1 = trade(mix_block, taken(2))
    (m1,) = step(m1)
    feed_second_other = to_owner(1, feed_second)
    f0_last = trade_strips(taken(2))
    mix_second = collect_mix(2, heads, pad, place, *m1)
    f0_last, mix_second, g_input = step(f0_last, mix_second, g_input)
    feed_first = collect_feed(columns, place, [f0, f0_last])
    feed_first_other = to_owner(0, feed_first)
    m0_first = [jnp.where(inside, *pair) for pair in taken(1)]
    m0_first_other = to_owner(0, m0_first)
    mix_second_other = to_owner(1, mix_second)
    feed_first_other, feed_second_other, m0_first_other, mix_second_other, g_input, out = step(
        feed_first_other, feed_second_other, m0_first_other, mix_second_other, g_input, out
    )
    m0_last = [jnp.where(inside, *pair) for pair in taken(1)]
    m0_last_other = to_owner(0, m0_last)
    turned_both = turn_plane(jnp.stack([out, g_input]))
    grad_gate_up, grad_down, grad_norm_two = unpack_feed(
        count,
        columns,
        hidden,
        width,
        ((feed_first, feed_first_other), (feed_second, feed_second_other)),
        place,
    )
    m0_last_other, grad_down = tie(m0_last_other, grad_down)
    grad_qkv, grad_out, grad_norm_one, grad_decay, grad_bias, grad_fixed = unpack_mix(
        count,
        heads,
        slots,
        width,
        ((m0_first + m0_last, m0_first_other + m0_last_other), (mix_second, mix_second_other)),
        place,
    )
    turned_both, grad_bias = tie(turned_both, grad_bias)
    return (
        turned_both[0][None, None],
        turned_both[1][None, None],
        grad_norm_one,
        grad_qkv[None],
        grad_decay[None],
        grad_bias,
        grad_fixed[None],
        grad_out[None],
        grad_norm_two,
        grad_gate_up[None],
        grad_down[None],
    )


def scatter_sum(blocks, axis):
    total = blocks[0].astype(wide)
    for r in range(1, len(blocks)):
        total = total + exchange(blocks[r].astype(half), axis, r).astype(wide)
    return total


def in_order(parts, index, dim):
    count = len(parts)
    shape = list(parts[0].shape)
    size = shape[dim]
    shape[dim] = size * count
    whole = jnp.zeros(shape, parts[0].dtype)
    for r, part in enumerate(parts):
        whole = lax.dynamic_update_slice_in_dim(whole, part, (index ^ r) * size, dim)
    return whole


def columns_here(shard, kinds, axis):
    count, index = lax.axis_size(axis), lax.axis_index(axis)
    rows, width = shard.shape[0], shard.shape[1] // (kinds * count)
    blocks = shard.reshape(rows, kinds, count, width)
    parts = []
    for r in range(count):
        block = lax.dynamic_index_in_dim(blocks, index ^ r, 2, False).reshape(rows, kinds * width)
        parts.append(block if r == 0 else exchange(block, axis, r))
    return in_order(parts, index, 0)


def rows_here(columns, kinds, axis):
    count, index = lax.axis_size(axis), lax.axis_index(axis)
    rows, width = columns.shape[0] // count, columns.shape[1] // kinds
    parts = []
    for r in range(count):
        block = lax.dynamic_slice_in_dim(columns, (index ^ r) * rows, rows, 0)
        block = block if r == 0 else exchange(block, axis, r)
        parts.append(block.reshape(rows, kinds, 1, width))
    return in_order(parts, index, 2).reshape(rows, kinds * count * width)


def line_sum(value, axis):
    count, index = lax.axis_size(axis), lax.axis_index(axis)
    if count != 4:
        return lax.psum(value, axis)

    def plus(a, b):
        return (a.astype(wide) + b.astype(wide)).astype(value.dtype)

    pair = plus(value, lax.ppermute(value, axis, [(0, 1), (3, 2)]))
    total = plus(pair, lax.ppermute(pair, axis, [(1, 2), (2, 1)]))
    outer = lax.ppermute(total, axis, [(1, 0), (2, 3)])
    return jnp.where((index == 0) | (index == 3), outer, total)


def dot(a, b, contract=(1, 0)):
    return lax.dot_general(a, b, (((contract[0],), (contract[1],)), ((), ())), preferred_element_type=wide)


def normalise(values, gain):
    scale = lax.rsqrt(jnp.mean(values * values, axis=-1, keepdims=True) + epsilon)
    return (values * scale * gain).astype(half)


def normalise_back(values, gain, grad):
    scale = lax.rsqrt(jnp.mean(values * values, axis=-1, keepdims=True) + epsilon)
    unit = values * scale
    grad_gain = jnp.sum(grad * unit, axis=0)
    scaled = grad * gain
    return scale * (scaled - unit * jnp.mean(scaled * unit, axis=-1, keepdims=True)), grad_gain


def heads_first(rows, size):
    return rows.reshape(rows.shape[0], rows.shape[1] // size, size).transpose(1, 0, 2)


def rows_first(heads):
    return heads.transpose(1, 0, 2).reshape(heads.shape[1], heads.shape[0] * heads.shape[2])


def batched(a, b, contract):
    return lax.dot_general(a, b, (((contract[0],), (contract[1],)), ((0,), (0,))), preferred_element_type=wide)


def cumulative(values, positions):
    earlier = (positions[None, :] <= positions[:, None]).astype(wide)
    return jnp.dot(earlier, values, precision=lax.Precision.HIGHEST)


def mixer_parts(projected, logits, fixed, length, positions, size):
    width = projected.shape[1] // 3
    q, k, v = (heads_first(projected[:, i * width : (i + 1) * width], size) for i in range(3))
    fixed_k, fixed_v = (heads_first(fixed[:, i * width : (i + 1) * width], size) for i in range(2))
    scale = size ** (-0.5)
    documents = positions >= length
    starts = (positions == 0) | (positions == length)
    allowed = ((positions[None, :] <= positions[:, None]) & (documents[:, None] == documents[None, :]))[None]
    log_keep = jax.nn.log_sigmoid(logits)
    total_log = cumulative(log_keep, positions).T
    keep = jnp.where(starts[:, None], 0.0, jax.nn.sigmoid(logits)).T
    lose = jnp.where(starts[:, None], 1.0, jax.nn.sigmoid(-logits)).T
    inflow = jnp.sqrt(lose * (1.0 + keep))
    scores = batched(q, k, (2, 2)) * scale
    fixed_scores = batched(q, fixed_k, (2, 2)) * scale
    masked = jnp.where(allowed, scores, negative)
    top = jnp.maximum(jnp.max(masked, axis=2), jnp.max(fixed_scores, axis=2))[:, :, None]
    weights, fixed_weights = jnp.exp(masked - top), jnp.exp(fixed_scores - top)
    mass = 1.0 / (jnp.sum(weights, axis=2) + jnp.sum(fixed_weights, axis=2))[:, :, None]
    weights, fixed_weights = weights * mass, fixed_weights * mass
    fall = jnp.exp(jnp.where(allowed, total_log[:, :, None] - total_log[:, None, :], negative))
    reach = scores * fall
    both = (weights + reach * inflow[:, None, :]).astype(half)
    return q, k, v, fixed_k, fixed_v, weights, fixed_weights, fall, reach, both, keep, lose, inflow


def mixer(projected, logits, fixed, length, positions, size):
    parts = mixer_parts(projected, logits, fixed, length, positions, size)
    q, k, v, fixed_k, fixed_v, weights, fixed_weights, fall, reach, both, keep, lose, inflow = parts
    mixed = batched(both, v, (2, 1)) + batched(fixed_weights.astype(half), fixed_v, (2, 1))
    return rows_first(mixed.astype(half))


def mixer_back(projected, logits, fixed, length, positions, size, grad):
    parts = mixer_parts(projected, logits, fixed, length, positions, size)
    q, k, v, fixed_k, fixed_v, weights, fixed_weights, fall, reach, both, keep, lose, inflow = parts
    scale = size ** (-0.5)
    grad = heads_first(grad, size)
    grad_both = batched(grad, v, (2, 2))
    grad_fixed = batched(grad, fixed_v, (2, 2))
    delta = (jnp.sum(weights * grad_both, axis=2) + jnp.sum(fixed_weights * grad_fixed, axis=2))[:, :, None]
    grad_scores = (weights * (grad_both - delta) + grad_both * fall * inflow[:, None, :]).astype(half)
    grad_fixed_scores = (fixed_weights * (grad_fixed - delta)).astype(half)
    grad_q = (batched(grad_scores, k, (2, 1)) + batched(grad_fixed_scores, fixed_k, (2, 1))) * scale
    grad_k = batched(grad_scores, q, (1, 1)) * scale
    grad_v = batched(both, grad, (1, 1))
    grad_fixed_k = batched(grad_fixed_scores, q, (1, 1)) * scale
    grad_fixed_v = batched(fixed_weights.astype(half), grad, (1, 1))
    pull = grad_both * reach
    grad_inflow = jnp.sum(pull, axis=1)
    grad_total = jnp.sum(pull * inflow[:, None, :], axis=2) - inflow * grad_inflow
    later = (positions[None, :] >= positions[:, None]).astype(wide)
    grad_log = jnp.dot(grad_total, later.T, precision=lax.Precision.HIGHEST)
    lose_all = jax.nn.sigmoid(-logits).T
    grad_logits = grad_log * lose_all - grad_inflow * keep * keep * lose / inflow
    grad_projected = jnp.concatenate([rows_first(grad_q), rows_first(grad_k), rows_first(grad_v)], axis=1)
    grad_persistent = jnp.concatenate([rows_first(grad_fixed_k), rows_first(grad_fixed_v)], axis=1)
    return grad_projected.astype(half), grad_logits.T, grad_persistent


def general_device(
    tokens,
    lengths,
    cotangent,
    norm_one,
    qkv_weight,
    decay_weight,
    decay_bias,
    persistent,
    out_weight,
    norm_two,
    gate_up,
    down_weight,
):
    sections, ctx_count, fsdp_count = (lax.axis_size(a) for a in ("section", "ctx", "fsdp"))
    section, ctx, fsdp = (lax.axis_index(a) for a in ("section", "ctx", "fsdp"))
    spread = ctx_count // fsdp_count
    rows, width = tokens.shape[2:]
    heads_here = decay_bias.shape[1]
    size = width // (heads_here * fsdp_count)
    inner = heads_here * size
    first = section == 0

    def own_batch(value):
        return lax.dynamic_index_in_dim(value, section, 0, False)[0]

    pairs = [(c * fsdp_count + f, f * ctx_count + c) for c in range(ctx_count) for f in range(fsdp_count)]

    def to_plane(value):
        return lax.ppermute(value, ("ctx", "fsdp"), pairs)

    def from_plane(value):
        return lax.ppermute(value, ("ctx", "fsdp"), [(b, a) for a, b in pairs])

    x_in = to_plane(own_batch(tokens))
    g_in = to_plane(own_batch(cotangent))
    length = to_plane(own_batch(lengths))[0]

    def both_layers(own):
        other = exchange(own, "section", 1)
        return jnp.where(first, own, other), jnp.where(first, other, own)

    small = jnp.concatenate(
        [
            norm_one[0],
            norm_two[0],
            decay_weight[0].reshape(-1),
            persistent[0].reshape(-1),
        ]
    )
    small = jnp.stack(both_layers(in_order([p[None] for p in gather_parts(small, "fsdp")], fsdp, 0)))
    cut = width // fsdp_count
    sizes = [cut, cut, decay_weight[0].size, persistent[0].size]
    edges = [0]
    for piece in sizes:
        edges.append(edges[-1] + piece)
    gains_one, gains_two, decays, fixeds = (small[:, :, a:b] for a, b in zip(edges[:-1], edges[1:]))
    gains_one = gains_one.reshape(2, width).astype(wide)
    gains_two = gains_two.reshape(2, width).astype(wide)
    head_count = heads_here * fsdp_count
    decays = lax.dynamic_slice_in_dim(decays.reshape(2, width, head_count), fsdp * heads_here, heads_here, 2)
    slots = persistent.shape[1]
    fixeds = fixeds.reshape(2, fsdp_count, slots, 2 * cut).transpose(0, 2, 1, 3).reshape(2, slots, 2, fsdp_count, inner)
    fixeds = lax.dynamic_index_in_dim(fixeds, fsdp, 3, False).reshape(2, slots, 2 * inner)
    biases = jnp.stack(both_layers(decay_bias[0])).astype(wide)
    qkvs = both_layers(columns_here(qkv_weight[0], 3, "fsdp"))
    outs = both_layers(out_weight[0])
    gate_ups = both_layers(columns_here(gate_up[0], 2, "fsdp"))
    downs = both_layers(down_weight[0])
    hidden = downs[0].shape[0]

    pieces = [(k * fsdp_count + (fsdp ^ r)) * rows + jnp.arange(rows) for k in range(spread) for r in range(fsdp_count)]
    all_positions = jnp.concatenate(pieces)
    groups = [[g * spread + k for k in range(spread)] for g in range(ctx_count // spread)]

    def whole(value):
        if spread == 1:
            return value
        return lax.all_gather(value, "ctx", axis_index_groups=groups, axis=0, tiled=True)

    def own_rows(value):
        if spread == 1:
            return value
        count = value.shape[0] // spread
        return lax.dynamic_slice_in_dim(value, (ctx % spread) * count, count, 0)

    def blocks_of(value):
        return list(value.reshape(fsdp_count, rows, value.shape[1]))

    def forward(layer, x, last):
        normed = jnp.concatenate(gather_parts(normalise(x, gains_one[layer]), "fsdp"))
        projected = dot(normed, qkvs[layer]).astype(half)
        logits = dot(normed, decays[layer]) + biases[layer]
        seen, seen_logits = whole(projected), whole(logits)
        combined = own_rows(mixer(seen, seen_logits, fixeds[layer], length, all_positions, size))
        middle = x + scatter_sum(blocks_of(dot(combined, outs[layer])), "fsdp")
        normed_two = jnp.concatenate(gather_parts(normalise(middle, gains_two[layer]), "fsdp"))
        gates = dot(normed_two, gate_ups[layer])
        activated = (jax.nn.silu(gates[:, :hidden]) * gates[:, hidden:]).astype(half)
        out = middle + scatter_sum(blocks_of(dot(activated, downs[layer])), "fsdp")
        return out.astype(half), (x, normed, seen, seen_logits, combined, middle, normed_two, gates, activated)

    def backward(layer, g_out, saved):
        x, normed, seen, seen_logits, combined, middle, normed_two, gates, activated = saved
        g_rows = jnp.concatenate(gather_parts(g_out, "fsdp"))
        grad_down = dot(activated, g_rows, (0, 0))
        g_activated = dot(g_rows, downs[layer], (1, 1))
        gate, up = gates[:, :hidden], gates[:, hidden:]
        sig = jax.nn.sigmoid(gate)
        g_up = g_activated * gate * sig
        g_gate = g_activated * up * sig * (1.0 + gate * (1.0 - sig))
        g_gates = jnp.concatenate([g_gate, g_up], axis=1).astype(half)
        grad_gate_up = dot(normed_two, g_gates, (0, 0))
        g_normed_two = scatter_sum(blocks_of(dot(g_gates, gate_ups[layer], (1, 1))), "fsdp")
        g_middle, grad_norm_two = normalise_back(middle, gains_two[layer], g_normed_two)
        g_middle = g_middle + g_out.astype(wide)
        g_branch = jnp.concatenate(gather_parts(g_middle.astype(half), "fsdp"))
        grad_out = dot(combined, g_branch, (0, 0))
        g_combined = whole(dot(g_branch, outs[layer], (1, 1)).astype(half))
        g_projected, g_logits, grad_fixed = mixer_back(
            seen, seen_logits, fixeds[layer], length, all_positions, size, g_combined
        )
        g_projected, g_logits = own_rows(g_projected), own_rows(g_logits)
        grad_fixed = jnp.where(ctx % spread == 0, grad_fixed, 0.0)
        grad_qkv = dot(normed, g_projected, (0, 0))
        grad_decay = dot(normed.astype(wide), g_logits, (0, 0))
        grad_bias = jnp.sum(g_logits, axis=0)
        g_normed = dot(g_projected, qkvs[layer], (1, 1)) + dot(g_logits, decays[layer].astype(wide), (1, 1))
        g_normed = scatter_sum(blocks_of(g_normed), "fsdp")
        g_x, grad_norm_one = normalise_back(x, gains_one[layer], g_normed)
        g_x = (g_x + g_middle).astype(half)
        large = (grad_qkv, grad_out, grad_gate_up, grad_down)
        return g_x, tuple(g.astype(half) for g in large), (grad_norm_one, grad_norm_two, grad_decay, grad_bias, grad_fixed)

    between, saved_first = forward(0, x_in.astype(wide), False)
    out, saved_second = forward(1, between.astype(wide), True)
    g_between, large_second, small_second = backward(1, g_in, saved_second)
    g_input, large_first, small_first = backward(0, g_between, saved_first)

    def reduced(from_first, from_second):
        received = exchange(jnp.where(first, from_second, from_first), "section", 1)
        own = jnp.where(first, from_first, from_second)
        own = (own.astype(wide) + received.astype(wide)).astype(half)
        return line_sum(own, "ctx")

    grad_qkv, grad_out, grad_gate_up, grad_down = (reduced(a, b) for a, b in zip(large_first, large_second))
    grad_qkv = rows_here(grad_qkv, 3, "fsdp")
    grad_gate_up = rows_here(grad_gate_up, 2, "fsdp")

    def small_whole(pieces):
        n_one, n_two, decay, bias, fixed = pieces
        decay_all = lax.dynamic_update_slice_in_dim(jnp.zeros((width, head_count), wide), decay, fsdp * heads_here, 1)
        bias_all = lax.dynamic_update_slice_in_dim(jnp.zeros((head_count,), wide), bias, fsdp * heads_here, 0)
        fixed_all = jnp.zeros((slots, 2, fsdp_count, inner), wide)
        fixed_all = lax.dynamic_update_slice_in_dim(fixed_all, fixed.reshape(slots, 2, 1, inner), fsdp, 2)
        return jnp.concatenate([n_one, n_two, decay_all.reshape(-1), fixed_all.reshape(-1), bias_all])

    tiny_first, tiny_second = small_whole(small_first), small_whole(small_second)
    tiny = lax.psum(jnp.stack([tiny_first, tiny_second]), ("section", "ctx", "fsdp"))
    tiny = lax.dynamic_index_in_dim(tiny, section, 0, False)
    grad_norm_one = lax.dynamic_slice_in_dim(tiny[:width], fsdp * cut, cut, 0)
    grad_norm_two = lax.dynamic_slice_in_dim(tiny[width : 2 * width], fsdp * cut, cut, 0)
    at = 2 * width
    grad_decay = lax.dynamic_slice_in_dim(tiny[at : at + width * head_count].reshape(width, head_count), fsdp * cut, cut, 0)
    at += width * head_count
    grad_fixed = tiny[at : at + slots * 2 * width].reshape(slots, 2 * width)
    grad_fixed = lax.dynamic_slice_in_dim(grad_fixed, fsdp * 2 * cut, 2 * cut, 1)
    at += slots * 2 * width
    grad_bias = lax.dynamic_slice_in_dim(tiny[at:], fsdp * heads_here, heads_here, 0)

    return (
        from_plane(out)[None, None],
        from_plane(g_input)[None, None],
        grad_norm_one[None],
        grad_qkv.astype(wide)[None],
        grad_decay[None],
        grad_bias[None],
        grad_fixed[None],
        grad_out.astype(wide)[None],
        grad_norm_two[None],
        grad_gate_up.astype(wide)[None],
        grad_down.astype(wide)[None],
    )


def solution(mesh):
    by_row = P("section", "fsdp", None)
    by_gain = P("section", "fsdp")
    by_token = P(None, "fsdp", "ctx", None)
    by_output = P("section", "fsdp", "ctx", None)
    by_slot = P("section", None, "fsdp")
    plane = mesh.shape["ctx"] == mesh.shape["fsdp"] == 4
    return jax.shard_map(
        plane_device if plane else general_device,
        mesh=mesh,
        in_specs=(
            by_token,
            P(None, "fsdp", None),
            by_token,
            by_gain,
            by_row,
            by_row,
            by_gain,
            by_slot,
            by_row,
            by_gain,
            by_row,
            by_row,
        ),
        out_specs=(
            by_output,
            by_output,
            by_gain,
            by_row,
            by_row,
            by_gain,
            by_slot,
            by_row,
            by_gain,
            by_row,
            by_row,
        ),
        check_vma=False,
    )
```

```python
import jax
import jax.numpy as jnp
from jax import lax
from jax.experimental import pallas as pl
from jax.experimental.pallas import tpu as pltpu
from jax.sharding import PartitionSpec as P

epsilon = 1e-05
negative = -1e30
wide = jnp.float32
half = jnp.bfloat16
LANES = 128
PAIR = 64
ROOM = {
    "mix_forward": 20,
    "mix_backward": 24,
    "feed_forward": 20,
    "feed_backward": 24,
    "grad_feed": 20,
    "grad_mix": 16,
    "assemble": 12,
    "pack_gates": 16,
    "spread": 12,
    "collect_feed": 12,
    "unpack_mix": 16,
}
vmem = pl.BlockSpec(memory_space=pltpu.VMEM)
smem = pl.BlockSpec(memory_space=pltpu.SMEM)
anywhere = pl.BlockSpec(memory_space=pl.ANY)


def mm(a, b):
    return lax.dot_general(a, b, (((1,), (0,)), ((), ())), preferred_element_type=wide)


def mm_nt(a, b):
    return lax.dot_general(a, b, (((1,), (1,)), ((), ())), preferred_element_type=wide)


def mm_tn(a, b):
    return lax.dot_general(a, b, (((0,), (0,)), ((), ())), preferred_element_type=wide)


def sig(v):
    return 1.0 / (1.0 + jnp.exp(-v))


def call(body, out_shape, in_specs, scratch, flops, moved, name):
    return pl.pallas_call(
        body,
        out_shape=out_shape,
        in_specs=in_specs,
        out_specs=jax.tree.map(lambda _: vmem, out_shape),
        scratch_shapes=scratch,
        compiler_params=pltpu.CompilerParams(vmem_limit_bytes=ROOM.get(name, 8) * 1024 * 1024),
        cost_estimate=pl.CostEstimate(flops=flops, bytes_accessed=moved, transcendentals=0),
        name=name,
    )


def shape(dims, kind=half):
    return jax.ShapeDtypeStruct(tuple(dims), kind)


def kept(dims, kind=half):
    return pltpu.HBM(tuple(dims), kind)


def pack_heads(count, shard, place):
    rows, columns = shard.shape
    inner = columns // (3 * count)

    def body(place_ref, shard_ref, *outs):
        for r in range(count):
            target = place_ref[0] ^ r
            for kind in range(3):
                at = pl.multiple_of(kind * count * inner + target * inner, inner)
                outs[r][:, kind * inner : (kind + 1) * inner] = shard_ref[:, pl.ds(at, inner)]

    outs = [shape((rows, 3 * inner))] * count
    return call(body, outs, [smem, vmem], [], 0, 2 * shard.size * 2, "pack_heads")(place, shard)


def pack_gates(count, shard, place):
    rows, columns = shard.shape
    hidden = columns // 2
    mine = columns // count

    def body(place_ref, shard_ref, *rest):
        outs, mixed = rest[:count], rest[count]
        low = lax.broadcasted_iota(jnp.int32, (rows, LANES), 1) < PAIR
        for m in range(hidden // LANES):
            gate = shard_ref[:, m * LANES : (m + 1) * LANES].astype(wide)
            up = shard_ref[:, hidden + m * LANES : hidden + (m + 1) * LANES].astype(wide)
            even = jnp.where(low, gate, pltpu.roll(up, PAIR, 1))
            odd = jnp.where(low, pltpu.roll(gate, PAIR, 1), up)
            mixed[:, 2 * m * LANES : (2 * m + 1) * LANES] = even.astype(half)
            mixed[:, (2 * m + 1) * LANES : (2 * m + 2) * LANES] = odd.astype(half)
        for r in range(count):
            at = pl.multiple_of((place_ref[0] ^ r) * mine, LANES)
            outs[r][...] = mixed[:, pl.ds(at, mine)]

    outs = [shape((rows, mine))] * count
    scratch = [pltpu.VMEM((rows, columns), half)]
    return call(body, outs, [smem, vmem], scratch, 0, 2 * shard.size * 2, "pack_gates")(place, shard)


def assemble(place, parts):
    count = len(parts)
    rows, columns = parts[0].shape

    def body(place_ref, *refs):
        put_rows(refs[:count], refs[count], place_ref)

    outs = [shape((rows * count, columns))]
    moved = 4 * rows * count * columns
    return call(body, outs, [smem] + [vmem] * count, [], 0, moved, "assemble")(place, *parts)[0]


def fetch(place_ref, layer, mine, other, target, sems, span=None):
    rows, columns = mine.shape
    span = columns if span is None else span
    handles = []
    for k, at in enumerate(range(0, columns, span)):
        lanes = pl.ds(at, min(span, columns - at))
        where = target.at[pl.ds(0, rows), lanes]
        for own, source in ((True, mine), (False, other)):

            @pl.when((place_ref[1] == layer) == own)
            def _(source=source, lanes=lanes, where=where, k=k):
                pltpu.make_async_copy(source.at[pl.ds(0, rows), lanes], where, sems.at[k]).start()

        handles.append(pltpu.make_async_copy(mine.at[pl.ds(0, rows), lanes], where, sems.at[k]))
    return handles


def finish(handles):
    for handle in handles:
        handle.wait()


def put_rows(parts, target, place_ref):
    rows = parts[0].shape[0]
    for r, part in enumerate(parts):
        target[pl.ds(pl.multiple_of((place_ref[0] ^ r) * rows, rows), rows), :] = part[...]


def take_rows(source, outs, place_ref):
    rows = outs[0].shape[0]
    for r, out in enumerate(outs):
        out[...] = source[pl.ds(pl.multiple_of((place_ref[0] ^ r) * rows, rows), rows), :].astype(out.dtype)


def three_way(v):
    high = v.astype(half)
    rest = v - high.astype(wide)
    middle = rest.astype(half)
    return high, middle, (rest - middle.astype(wide)).astype(half)


def exact_sum(values, mask):
    return sum(mm(piece, mask) for piece in three_way(values))


def gate_lanes(logits, length):
    rows = logits.shape[1]
    at = lax.broadcasted_iota(jnp.int32, logits.shape, 1)
    starts = (at == 0) | (at == length)
    spill = jnp.log(1.0 + jnp.exp(-jnp.abs(logits)))
    log_keep = jnp.minimum(logits, 0.0) - spill
    keep = jnp.where(starts, 0.0, sig(logits))
    lose = jnp.where(starts, 1.0, sig(-logits))
    before = lax.broadcasted_iota(jnp.int32, (rows, rows), 0) <= lax.broadcasted_iota(jnp.int32, (rows, rows), 1)
    return log_keep, keep, lose, exact_sum(log_keep, before.astype(wide).astype(half))


def turned(values):
    return jnp.concatenate([values, jnp.zeros((LANES - values.shape[0], values.shape[1]), wide)], axis=0).T


def head_scores(head, size, inner, projected, fixed, total, total_t, inflow_t, length, scale):
    rows = projected.shape[0]
    lanes = slice(head * size, (head + 1) * size)
    q = projected[:, lanes]
    k = projected[:, inner + head * size : inner + (head + 1) * size]
    v = projected[:, 2 * inner + head * size : 2 * inner + (head + 1) * size]
    fixed_k = fixed[:, lanes]
    fixed_v = fixed[:, inner + head * size : inner + (head + 1) * size]
    scores = mm_nt(q, k) * scale
    fixed_scores = mm_nt(q, fixed_k) * scale
    at = lax.broadcasted_iota(jnp.int32, (rows, 1), 0)
    begin = jnp.where(at >= length, length, 0)
    column = lax.broadcasted_iota(jnp.int32, (rows, rows), 1)
    allowed = (column <= at) & (column >= begin)
    masked = jnp.where(allowed, scores, negative)
    top = jnp.maximum(jnp.max(masked, axis=1, keepdims=True), jnp.max(fixed_scores, axis=1, keepdims=True))
    weights, fixed_weights = jnp.exp(masked - top), jnp.exp(fixed_scores - top)
    mass = 1.0 / (jnp.sum(weights, axis=1, keepdims=True) + jnp.sum(fixed_weights, axis=1, keepdims=True))
    weights, fixed_weights = weights * mass, fixed_weights * mass
    fall = jnp.exp(jnp.where(allowed, total[:, head : head + 1] - total_t[head : head + 1, :], negative))
    reach = scores * fall
    both = (weights + reach * inflow_t[head : head + 1, :]).astype(half)
    return q, k, v, fixed_k, fixed_v, weights, fixed_weights, fall, reach, both


def mix_forward(layer, heads, size, place, parts, rows, gain, weights, decay, bias, fixed):
    count = len(parts)
    width = parts[0].shape[1]
    total_rows, inner = rows * count, heads * size
    scale = size ** (-0.5)

    def body(place_ref, *refs):
        parts_in, refs = refs[:count], refs[count:]
        (mine, other, o_mine, o_other), refs = refs[:4], refs[4:]
        (gain_ref, decay_ref, bias_ref, fixed_ref), refs = refs[:4], refs[4:]
        terms, refs = refs[:count], refs[count:]
        combined, normed, projected, logits_out, weight, out_weight, whole, sems = refs
        handles = fetch(place_ref, layer, mine, other, weight, sems, inner)
        out_handles = fetch(place_ref, layer, o_mine, o_other, out_weight, sems.at[pl.ds(3, 1)])
        for r, part in enumerate(parts_in):
            values = part[0:rows, :].astype(wide)
            root = lax.rsqrt(jnp.mean(values * values, axis=1, keepdims=True) + epsilon)
            here = pl.ds(pl.multiple_of((place_ref[0] ^ r) * rows, rows), rows)
            normed[here, :] = (values * root * gain_ref[...]).astype(half)
        length = place_ref[2]
        logits = mm_nt(decay_ref[...], normed[...]) + bias_ref[:, 0:1]
        logits_out[...] = logits
        log_keep, keep, lose, total_t = gate_lanes(logits, length)
        total = turned(total_t)
        inflow_t = jnp.sqrt(lose * (1.0 + keep))
        for kind in range(3):
            handles[kind].wait()
            lanes = slice(kind * inner, (kind + 1) * inner)
            projected[:, lanes] = mm(normed[...], weight[:, lanes]).astype(half)
        for head in range(heads):
            q, k, v, fixed_k, fixed_v, soft, fixed_soft, fall, reach, both = head_scores(
                head, size, inner, projected, fixed_ref, total, total_t, inflow_t, length, scale
            )
            mixed = mm(both, v) + mm(fixed_soft.astype(half), fixed_v)
            combined[:, head * size : (head + 1) * size] = mixed.astype(half)
        finish(out_handles)
        whole[...] = mm(combined[...], out_weight[...])
        take_rows(whole, terms, place_ref)

    outs = [shape((rows, width), wide if r == 0 else half) for r in range(count)] + [
        shape((total_rows, inner)),
        (kept if layer else shape)((total_rows, width)),
        shape((total_rows, 3 * inner)),
        shape((16, total_rows), wide),
    ]
    scratch = [
        pltpu.VMEM((width, 3 * inner), half),
        pltpu.VMEM((inner, width), half),
        pltpu.VMEM((total_rows, width), wide),
        pltpu.SemaphoreType.DMA((4,)),
    ]
    specs = [smem] + [vmem] * count + [anywhere] * 4 + [vmem] * 4
    flops = 2 * total_rows * (width * 4 * inner + inner * total_rows * 2)
    moved = 2 * (width * 3 * inner + total_rows * (2 * width + 4 * inner))
    return call(body, outs, specs, scratch, flops, moved, "mix_forward")(
        place, *parts, *weights, gain, decay, bias, fixed
    )


def mix_backward(layer, heads, size, place, parts, weights, decay, fixed, projected, logits, normed, gain):
    count = len(parts)
    rows, width = parts[0].shape
    total_rows, inner = rows * count, heads * size
    scale = size ** (-0.5)

    def body(place_ref, *refs):
        parts_in, refs = refs[:count], refs[count:]
        (mine, other, o_mine, o_other), refs = refs[:4], refs[4:]
        decay_ref, fixed_ref, projected, logits_ref, normed_ref, gain_ref = refs[:6]
        refs = refs[6:]
        terms, refs = refs[:count], refs[count:]
        branch, g_projected, g_logits_out, g_fixed, g_gain, refs = refs[0], refs[1], refs[2], refs[3], refs[4], refs[5:]
        weight, out_weight, combined, pulled, pushed, whole, sems = refs
        out_handles = fetch(place_ref, layer, o_mine, o_other, out_weight, sems.at[pl.ds(1, 1)])
        handles = fetch(place_ref, layer, mine, other, weight, sems.at[pl.ds(0, 1)])
        put_rows(parts_in, branch, place_ref)
        length = place_ref[2]
        logits = logits_ref[...]
        log_keep, keep, lose, total_t = gate_lanes(logits, length)
        total = turned(total_t)
        inflow_t = jnp.sqrt(lose * (1.0 + keep))
        finish(out_handles)
        combined[...] = mm_nt(branch[...], out_weight[...]).astype(half)
        pulled[...] = jnp.zeros_like(pulled)
        pushed[...] = jnp.zeros_like(pushed)
        for head in range(heads):
            lanes, key_lanes, value_lanes = (
                slice(kind * inner + head * size, kind * inner + (head + 1) * size) for kind in range(3)
            )
            q, k, v, fixed_k, fixed_v, weights, fixed_weights, fall, reach, both = head_scores(
                head, size, inner, projected, fixed_ref, total, total_t, inflow_t, length, scale
            )
            grad = combined[:, lanes]
            g_both = mm_nt(grad, v)
            g_few = mm_nt(grad, fixed_v)
            delta = jnp.sum(weights * g_both, axis=1, keepdims=True) + jnp.sum(
                fixed_weights * g_few, axis=1, keepdims=True
            )
            inflow_row = inflow_t[head : head + 1, :]
            g_scores = (weights * (g_both - delta) + g_both * fall * inflow_row).astype(half)
            g_few_scores = (fixed_weights * (g_few - delta)).astype(half)
            g_projected[:, lanes] = ((mm(g_scores, k) + mm(g_few_scores, fixed_k)) * scale).astype(half)
            g_projected[:, key_lanes] = (mm_tn(g_scores, q) * scale).astype(half)
            g_projected[:, value_lanes] = mm_tn(both, grad).astype(half)
            g_fixed[:, lanes] = mm_tn(g_few_scores, q) * scale
            g_fixed[:, key_lanes] = mm_tn(fixed_weights.astype(half), grad)
            pull = g_both * reach
            pulled[head : head + 1, :] = jnp.sum(pull, axis=0, keepdims=True)
            pushed[:, head : head + 1] = jnp.sum(pull * inflow_row, axis=1, keepdims=True)
        g_inflow = pulled[...]
        g_total = pushed[...].T[0:16] - inflow_t * g_inflow
        after = lax.broadcasted_iota(jnp.int32, (total_rows, total_rows), 0) >= lax.broadcasted_iota(
            jnp.int32, (total_rows, total_rows), 1
        )
        g_log = exact_sum(g_total, after.astype(wide).astype(half))
        g_logits = g_log * sig(-logits) - g_inflow * keep * keep * lose / inflow_t
        row = lax.broadcasted_iota(jnp.int32, g_logits.shape, 0)
        g_logits = jnp.where(row < heads, g_logits, 0.0)
        g_logits_out[...] = g_logits
        finish(handles)
        high, middle, low = three_way(g_logits)
        whole[...] = (
            mm_nt(g_projected[...], weight[...]) + mm_tn(high, decay_ref[...]) + mm_tn(middle, decay_ref[...])
        )
        pulls = jnp.sum(whole[...] * normed_ref[...].astype(wide), axis=0, keepdims=True) / gain_ref[...]
        g_gain[...] = jnp.broadcast_to(pulls, g_gain.shape)
        take_rows(whole, terms, place_ref)

    outs = [shape((rows, width), wide if r == 0 else half) for r in range(count)] + [
        shape((total_rows, width)),
        shape((total_rows, 3 * inner)),
        shape((16, total_rows), wide),
        shape((fixed.shape[0], 2 * inner), wide),
        shape((8, width), wide),
    ]
    scratch = [
        pltpu.VMEM((width, 3 * inner), half),
        pltpu.VMEM((inner, width), half),
        pltpu.VMEM((total_rows, inner), half),
        pltpu.VMEM((16, total_rows), wide),
        pltpu.VMEM((total_rows, LANES), wide),
        pltpu.VMEM((total_rows, width), wide),
        pltpu.SemaphoreType.DMA((2,)),
    ]
    specs = [smem] + [vmem] * count + [anywhere] * 4 + [vmem] * 6
    flops = 2 * total_rows * (width * 4 * inner + inner * total_rows * 5)
    moved = 2 * (width * 4 * inner + total_rows * (5 * width + 6 * inner))
    return call(body, outs, specs, scratch, flops, moved, "mix_backward")(
        place, *parts, *weights, decay, fixed, projected, logits, normed, gain
    )


def gates_of(tile_pair):
    rows, columns = tile_pair.shape
    if columns > 2 * LANES:
        found = [gates_of(tile_pair[:, at : at + size]) for at, size in tile_ranges(columns)]
        return tuple(jnp.concatenate([pair[k] for pair in found], axis=1) for k in range(2))
    if columns == LANES:
        return tile_pair[:, :PAIR], pltpu.roll(tile_pair, PAIR, 1)[:, :PAIR]
    first, second = tile_pair[:, :LANES], tile_pair[:, LANES:]
    low = lax.broadcasted_iota(jnp.int32, (rows, LANES), 1) < PAIR
    gate = jnp.where(low, first, pltpu.roll(second, PAIR, 1))
    up = jnp.where(low, pltpu.roll(first, PAIR, 1), second)
    return gate, up


def tiles_of(gate, up):
    rows, columns = gate.shape
    if columns > LANES:
        steps = [(at, min(LANES, columns - at)) for at in range(0, columns, LANES)]
        return jnp.concatenate([tiles_of(gate[:, at : at + size], up[:, at : at + size]) for at, size in steps], axis=1)
    if columns == PAIR:
        return jnp.concatenate([gate, up], axis=1)
    low = lax.broadcasted_iota(jnp.int32, (rows, LANES), 1) < PAIR
    first = jnp.where(low, gate, pltpu.roll(up, PAIR, 1))
    second = jnp.where(low, pltpu.roll(gate, PAIR, 1), up)
    return jnp.concatenate([first, second], axis=1)


def tile_ranges(columns, tiles=2):
    return [(at, min(tiles * LANES, columns - at)) for at in range(0, columns, tiles * LANES)]


def feed_forward(layer, place, parts, weights):
    count = len(parts)
    rows, width = parts[0].shape
    total_rows = rows * count
    columns, hidden = weights[0].shape[1], weights[2].shape[0]
    padded = -(-hidden // LANES) * LANES

    def body(place_ref, *refs):
        parts_in, refs = refs[:count], refs[count:]
        (mine, other, d_mine, d_other), refs = refs[:4], refs[4:]
        terms, normed, refs = refs[:count], refs[count], refs[count + 1 :]
        weight, down, active, whole, sems = refs
        handles = fetch(place_ref, layer, mine, other, weight, sems.at[pl.ds(0, 1)])
        down_handles = fetch(place_ref, layer, d_mine, d_other, down, sems.at[pl.ds(1, 1)])
        put_rows(parts_in, normed, place_ref)
        if padded != hidden:
            down[hidden:, :] = jnp.zeros((padded - hidden, width), half)
            active[:, padded - LANES :] = jnp.zeros((total_rows, LANES), half)
        finish(handles)
        for at, size in tile_ranges(columns):
            gate, up = gates_of(mm(normed[...], weight[:, at : at + size]))
            active[:, at // 2 : (at + size) // 2] = (gate * sig(gate) * up).astype(half)
        finish(down_handles)
        whole[...] = mm(active[...], down[...])
        take_rows(whole, terms, place_ref)

    outs = [shape((rows, width), wide if r == 0 else half) for r in range(count)] + [shape((total_rows, width))]
    scratch = [
        pltpu.VMEM((width, columns), half),
        pltpu.VMEM((padded, width), half),
        pltpu.VMEM((total_rows, padded), half),
        pltpu.VMEM((total_rows, width), wide),
        pltpu.SemaphoreType.DMA((2,)),
    ]
    specs = [smem] + [vmem] * count + [anywhere] * 4
    flops = 2 * total_rows * width * (columns + hidden)
    moved = 2 * (width * (columns + hidden) + total_rows * 4 * width)
    return call(body, outs, specs, scratch, flops, moved, "feed_forward")(
        place, *parts, *weights
    )


def feed_backward(layer, place, parts, normed_parts, gain, weights, forward):
    count = len(parts)
    rows, width = parts[0].shape
    total_rows = rows * count
    columns, hidden = weights[0].shape[1], weights[2].shape[0]
    padded = -(-hidden // LANES) * LANES

    def body(place_ref, *refs):
        parts_in, refs = refs[:count], refs[count:]
        normed_in, refs = refs[: len(normed_parts)], refs[len(normed_parts) :]
        gain_ref, (mine, other, d_mine, d_other), refs = refs[0], refs[1:5], refs[5:]
        terms, refs = refs[:count], refs[count:]
        g_out, g_gates, active, g_gain, refs = refs[0], refs[1], refs[2], refs[3], refs[4:]
        if forward:
            ahead, normed, refs = refs[:count], refs[count], refs[count + 1 :]
        else:
            normed = normed_in[0]
        weight, down, held, whole, sems = refs
        handles = fetch(place_ref, layer, mine, other, weight, sems.at[pl.ds(0, 1)])
        down_handles = fetch(place_ref, layer, d_mine, d_other, down, sems.at[pl.ds(1, 1)])
        put_rows(parts_in, g_out, place_ref)
        if forward:
            put_rows(normed_in, normed, place_ref)
        if padded != hidden:
            down[hidden:, :] = jnp.zeros((padded - hidden, width), half)
            held[:, padded - LANES :] = jnp.zeros((total_rows, LANES), half)
        finish(handles)
        finish(down_handles)
        for at, size in tile_ranges(columns, 4):
            inside = slice(at // 2, (at + size) // 2)
            gate, up = gates_of(mm(normed[...], weight[:, at : at + size]))
            g_active = mm_nt(g_out[...], down[inside, :])
            open_ = sig(gate)
            lit = gate * open_
            product = (lit * up).astype(half)
            active[:, inside] = product
            if forward:
                held[:, inside] = product
            g_up = g_active * lit
            g_gate = g_active * up * (open_ * (1.0 + gate - lit))
            g_gates[:, at : at + size] = tiles_of(g_gate, g_up).astype(half)
        whole[...] = mm_nt(g_gates[...], weight[...])
        pulls = jnp.sum(whole[...] * normed[...].astype(wide), axis=0, keepdims=True) / gain_ref[...]
        g_gain[...] = jnp.broadcast_to(pulls, g_gain.shape)
        take_rows(whole, terms, place_ref)
        if forward:
            whole[...] = mm(held[...], down[...])
            take_rows(whole, ahead, place_ref)

    term_shapes = [shape((rows, width), wide if r == 0 else half) for r in range(count)]
    place_of = kept if forward else shape
    outs = [place_of((rows, width), wide), *term_shapes[1:]] + [
        place_of((total_rows, width)),
        place_of((total_rows, columns)),
        place_of((total_rows, hidden)),
        place_of((8, width), wide),
    ]
    if forward:
        outs = outs + [kept(term.shape, term.dtype) for term in term_shapes] + [kept((total_rows, width))]
    scratch = [
        pltpu.VMEM((width, columns), half),
        pltpu.VMEM((padded, width), half),
        pltpu.VMEM((total_rows, padded), half),
        pltpu.VMEM((total_rows, width), wide),
        pltpu.SemaphoreType.DMA((2,)),
    ]
    specs = [smem] + [vmem] * (count + len(normed_parts) + 1) + [anywhere] * 4
    flops = 2 * total_rows * width * (2 * columns + hidden)
    moved = 2 * (width * (columns + hidden) + total_rows * (6 * width + columns + hidden))
    return call(body, outs, specs, scratch, flops, moved, "feed_backward")(
        place, *parts, *normed_parts, gain, *weights
    )


def pack_small(norm_one, norm_two, decay, bias, persistent, lengths):
    cut, heads_all = decay.shape
    slots, columns = persistent.shape
    heads = bias.shape[1]
    lanes = cut // LANES
    total = 16 * (1 + lanes + columns // LANES)

    batches = lengths.shape[0]

    def body(lengths_ref, one_ref, two_ref, decay_ref, bias_ref, fixed_ref, out):
        rows = [ref[0:1, b * LANES : (b + 1) * LANES].astype(wide) for ref in (one_ref, two_ref) for b in range(lanes)]
        rows.append(jnp.concatenate([bias_ref[...].astype(wide), jnp.zeros((1, LANES - heads), wide)], axis=1))
        for m in range(batches):
            for part in (lengths_ref[m] // 64, lengths_ref[m] % 64):
                rows.append(jnp.full((1, LANES), part.astype(wide)))
        rows.append(jnp.zeros((16 - len(rows), LANES), wide))
        out[0:16, :] = jnp.concatenate(rows, axis=0).astype(half)
        padded = jnp.concatenate([decay_ref[...].astype(wide), jnp.zeros((cut, LANES - heads_all), wide)], axis=1).T
        for b in range(lanes):
            out[16 * (1 + b) : 16 * (2 + b), :] = padded[0:16, b * LANES : (b + 1) * LANES].astype(half)
        for c in range(columns // LANES):
            at = 16 * (1 + lanes + c)
            out[at : at + slots, :] = fixed_ref[:, c * LANES : (c + 1) * LANES]

    return call(body, [shape((total, LANES))], [smem] + [vmem] * 5, [], 0, 1 << 17, "pack_small")(
        lengths, norm_one, norm_two, decay, bias, persistent
    )[0]


def beside(rows, mine, other):
    height, width = rows.shape
    groups = 2 * mine.shape[0] // 16
    across = width // LANES
    below = 16 * -(-groups // across)

    def body(rows_ref, mine_ref, other_ref, out):
        out[0:height, :] = rows_ref[...]
        out[height:, :] = jnp.zeros((below, width), half)
        for g in range(groups):
            ref, at = (mine_ref, g) if g < groups // 2 else (other_ref, g - groups // 2)
            spot = (height + 16 * (g // across), LANES * (g % across))
            out[spot[0] : spot[0] + 16, spot[1] : spot[1] + LANES] = ref[16 * at : 16 * at + 16, :]

    outs = [shape((height + below, width))]
    return call(body, outs, [vmem] * 3, [], 0, 1 << 20, "beside")(rows, mine, other)[0]


def turn_bias(row):
    at = lax.broadcasted_iota(jnp.int32, (16, LANES), 0) == lax.broadcasted_iota(jnp.int32, (16, LANES), 1)
    return jnp.broadcast_to(jnp.sum(jnp.where(at, row, 0.0), axis=1, keepdims=True), (16, LANES))


def unpack_small(heads, slots, height, rows, place, parts):
    count = len(parts)
    width = parts[0].shape[1]
    cut = width // count
    lanes = cut // LANES
    across = width // LANES
    inner = heads * LANES

    def body(place_ref, *refs):
        ins, outs, length, held = refs[:count], refs[count:-2], refs[-2], refs[-1]
        f = place_ref[0]
        for r, part in enumerate(ins):
            for k in range(2):
                layer = place_ref[1] if k == 0 else 1 - place_ref[1]
                for g in range(rows // 16):
                    at = k * (rows // 16) + g
                    top, left = height + 16 * (at // across), LANES * (at % across)
                    held[layer, f ^ r, 16 * g : 16 * g + 16, :] = part[top : top + 16, left : left + LANES].astype(wide)
        at = 2 * lanes + 1 + 2 * place_ref[1]
        found = held[place_ref[1], place_ref[2], pl.ds(at, 2), :]
        length[...] = jnp.broadcast_to(found[0:1] * 64.0 + found[1:2], length.shape).astype(jnp.int32)
        for layer in range(2):
            one, two, decay, bias, fixed = outs[5 * layer : 5 * layer + 5]
            for t in range(count):
                for b in range(lanes):
                    at = t * cut + b * LANES
                    one[0:1, at : at + LANES] = held[layer, t, b : b + 1, :]
                    two[0:1, at : at + LANES] = held[layer, t, lanes + b : lanes + b + 1, :]
                    group = held[layer, t, 16 * (1 + b) : 16 * (2 + b), :]
                    row = lax.broadcasted_iota(jnp.int32, (16, LANES), 0)
                    mine = [
                        jnp.sum(jnp.where(row == f * heads + h, group, 0.0), axis=0, keepdims=True) for h in range(heads)
                    ]
                    mine.append(jnp.zeros((16 - heads, LANES), wide))
                    decay[:, at : at + LANES] = jnp.concatenate(mine, axis=0).astype(half)
            bias[...] = turn_bias(held[layer, f, 2 * lanes : 2 * lanes + 1, :])
            for kind in range(2):
                source = kind * (count // 2) + f // 2
                for h in range(heads):
                    at = pl.multiple_of(16 * (1 + lanes + (f % 2) * heads + h), 16)
                    lane = kind * inner + h * LANES
                    fixed[:, lane : lane + LANES] = held[layer, source, pl.ds(at, slots), :].astype(half)

    outs = [
        shape((1, width), wide),
        shape((1, width), wide),
        shape((16, width)),
        shape((16, LANES), wide),
        shape((slots, 2 * inner)),
    ] * 2 + [shape((8, LANES), jnp.int32)]
    scratch = [pltpu.VMEM((2, count, rows, LANES), wide)]
    made = call(body, outs, [smem] + [vmem] * count, scratch, 0, 1 << 20, "unpack_small")(place, *parts)
    return [list(pair) for pair in zip(made[:5], made[5:10])], made[10][0, 0]


def join_forward(rounded, terms, residual, gain):
    dims = terms[0].shape

    def body(*refs):
        count = len(terms)
        residual_ref, refs_in = refs[count], refs[:count]
        total = residual_ref[...].astype(wide)
        for ref in refs_in:
            total = total + ref[...].astype(wide)
        if gain is None:
            refs[count + 1][...] = total.astype(half)
            return
        gain_ref, out, normed = refs[count + 1 :]
        if rounded:
            total = total.astype(half).astype(wide)
        out[...] = total.astype(out.dtype)
        scale = lax.rsqrt(jnp.mean(total * total, axis=1, keepdims=True) + epsilon)
        normed[...] = (total * scale * gain_ref[...]).astype(half)

    outs = [shape(dims, half if rounded else wide), shape(dims)]
    inputs = [*terms, residual, gain]
    if gain is None:
        outs, inputs = [shape(dims)], inputs[:-1]
    return call(body, outs, [vmem] * len(inputs), [], 0, dims[0] * dims[1] * 20, "join_forward")(*inputs)


def join_backward(terms, values, gain, onward):
    dims = terms[0].shape

    def body(*refs):
        count = len(terms)
        values_ref, gain_ref, onward_ref, out, rounded = refs[count:]
        grad = refs[0][...].astype(wide)
        for ref in refs[1:count]:
            grad = grad + ref[...].astype(wide)
        v = values_ref[...].astype(wide)
        scale = lax.rsqrt(jnp.mean(v * v, axis=1, keepdims=True) + epsilon)
        unit = v * scale
        scaled = grad * gain_ref[...]
        through = scale * (scaled - unit * jnp.mean(scaled * unit, axis=1, keepdims=True))
        total = onward_ref[...].astype(wide) + through
        out[...] = total
        rounded[...] = total.astype(half)

    outs = [shape(dims, wide), shape(dims)]
    inputs = [*terms, values, gain, onward]
    return call(body, outs, [vmem] * len(inputs), [], 0, dims[0] * dims[1] * 24, "join_backward")(*inputs)


SMALL = 16


def lane_half(source, target, which, count):
    for t in range(count):
        at = pl.multiple_of(t * 2 * LANES + which * LANES, LANES)
        target[:, t * LANES : (t + 1) * LANES] = source[:, pl.ds(at, LANES)]


STRIPS = 4


def strip_of(columns):
    return SMALL * -(-(columns + SMALL) // (SMALL * STRIPS))


def packer(packed):
    def put(at, value):
        packed[at : at + value.shape[0], :] = value.astype(half)

    return put


def strip_packer(packed, strip, chunk):
    def put(t, at, value):
        done = 0
        while done < value.shape[0]:
            k, row = divmod(at + done, strip)
            size = min(value.shape[0] - done, strip - row)
            where = k * chunk + t * strip + row
            packed[where : where + size, :] = value[done : done + size].astype(half)
            done += size

    return put


def small_rows(rows):
    found = jnp.concatenate(rows, axis=0)
    return jnp.concatenate([found, jnp.zeros((SMALL - found.shape[0], LANES), wide)], axis=0)


def grad_call(body, chunks, total, inputs, scratch, flops, name):
    outs = [shape((total, LANES))] + [shape((b - a, LANES)) for a, b in split_rows(total, chunks)]
    scratch = scratch + [pltpu.VMEM((total, LANES), half)]
    moved = sum(v.size * v.dtype.itemsize for v in inputs) + total * LANES * 4
    return call(body, outs, [smem] + [vmem] * (len(inputs) - 1), scratch, flops, moved, name)(*inputs)


def grad_feed(chunks, count, place, normed, g_gates, active, g_out, g_gain):
    total_rows, width = normed.shape
    columns, hidden = g_gates.shape[1], active.shape[1]
    tiles = columns // LANES
    strip = strip_of(columns)
    chunk = count * strip + hidden
    side = width // 2

    def body(place_ref, normed_ref, gates_ref, active_ref, g_out_ref, gain_ref, *refs):
        sent, outs, left, packed = refs[0], refs[1:-2], refs[-2], refs[-1]
        for turn in range(2):
            which = 1 - place_ref[1] if turn == 0 else place_ref[1]
            packed_here = sent if turn == 0 else packed
            put, put_row = packer(packed_here), strip_packer(packed_here, strip, chunk)
            lane_half(normed_ref, left, which, count)
            turned = left[...].T
            for at in range(0, columns, 2 * LANES):
                size = min(2 * LANES, columns - at)
                tile = mm(turned, gates_ref[:, at : at + size])
                for t in range(count):
                    for c in range(size // LANES):
                        put_row(t, at + c * LANES, tile[t * LANES : (t + 1) * LANES, c * LANES : (c + 1) * LANES])
            for t in range(count):
                at = pl.multiple_of(t * 2 * LANES + which * LANES, LANES)
                rest = STRIPS * strip - columns - SMALL
                put_row(t, columns, small_rows([gain_ref[0:1, pl.ds(at, LANES)]]))
                put_row(t, columns + SMALL, jnp.zeros((rest, LANES), wide))
            active_t = active_ref[...].T
            for c in range(0, side // LANES, 2):
                at = pl.multiple_of(which * side + c * LANES, LANES)
                tile = mm(active_t, g_out_ref[:, pl.ds(at, 2 * LANES)])
                put(c * chunk + count * strip, tile[:, :LANES])
                put((c + 1) * chunk + count * strip, tile[:, LANES:])
        chunk_out(packed, outs)

    inputs = [place, normed, g_gates, active, g_out, g_gain]
    scratch = [pltpu.VMEM((total_rows, side), half)]
    flops = total_rows * width * (columns + hidden)
    return grad_call(body, chunks, STRIPS * chunk, inputs, scratch, flops, "grad_feed")


def grad_mix(chunks, total, count, place, normed, g_projected, combined, branch, g_logits, g_gain, g_fixed):
    total_rows, width = normed.shape
    columns, inner = g_projected.shape[1], combined.shape[1]
    heads = inner // LANES
    slots = g_fixed.shape[0]
    block = columns + SMALL + slots
    side = width // 2

    def body(place_ref, normed_ref, proj_ref, comb_ref, branch_ref, logits_ref, gain_ref, fixed_ref, *refs):
        sent, outs, left, packed = refs[0], refs[1:-2], refs[-2], refs[-1]
        for turn in range(2):
            which = 1 - place_ref[1] if turn == 0 else place_ref[1]
            put = packer(sent if turn == 0 else packed)
            lane_half(normed_ref, left, which, count)
            turned = left[...].T
            for at in range(0, columns, 2 * LANES):
                tile = mm(turned, proj_ref[:, at : at + 2 * LANES])
                for t in range(count):
                    for c in range(2):
                        put(t * block + at + c * LANES, tile[t * LANES : (t + 1) * LANES, c * LANES : (c + 1) * LANES])
            logits = logits_ref[...]
            decay = sum(mm(piece, left[...]) for piece in three_way(logits)[:2])
            near = pl.multiple_of(which * LANES, LANES)
            for t in range(count):
                at = pl.multiple_of(t * 2 * LANES + which * LANES, LANES)
                rows = [decay[0:heads, t * LANES : (t + 1) * LANES], gain_ref[0:1, pl.ds(at, LANES)]]
                put(t * block + columns, small_rows(rows))
                keys_here = (place_ref[0] // 2 == t).astype(wide)
                values_here = (place_ref[0] // 2 + 2 == t).astype(wide)
                fixed = fixed_ref[:, pl.ds(near, LANES)] * keys_here
                fixed = fixed + fixed_ref[:, pl.ds(pl.multiple_of(inner + near, LANES), LANES)] * values_here
                put(t * block + columns + SMALL, fixed)
            comb_t = comb_ref[:, pl.ds(near, LANES)].T
            for c in range(0, width // LANES, 2):
                tile = mm(comb_t, branch_ref[:, c * LANES : (c + 2) * LANES])
                put(count * block + c * LANES, tile[:, :LANES])
                put(count * block + (c + 1) * LANES, tile[:, LANES:])
            put(count * block + width, jnp.broadcast_to(jnp.sum(logits, axis=1, keepdims=True), (SMALL, LANES)))
            (sent if turn == 0 else packed)[count * block + width + SMALL :, :] = jnp.zeros(
                (total - count * block - width - SMALL, LANES), half
            )
        chunk_out(packed, outs)

    inputs = [place, normed, g_projected, combined, branch, g_logits, g_gain, g_fixed]
    scratch = [pltpu.VMEM((total_rows, side), half)]
    flops = total_rows * width * (columns + inner)
    return grad_call(body, chunks, total, inputs, scratch, flops, "grad_mix")


def split_rows(total, chunks):
    units = total // SMALL
    edges = [SMALL * (units * k // chunks) for k in range(chunks)] + [total]
    return list(zip(edges[:-1], edges[1:]))


def chunk_out(whole, outs):
    at = 0
    for out in outs:
        out[...] = whole[at : at + out.shape[0], :]
        at += out.shape[0]


def spread(count, block, place, chunks, add=False):
    total = sum(chunk.shape[0] for chunk, _ in chunks)

    def body(place_ref, *refs):
        ins, outs, whole = refs[: 2 * len(chunks)], refs[2 * len(chunks) : -1], refs[-1]
        at = 0
        if add:
            for one, two in zip(ins[0::2], ins[1::2]):
                whole[at : at + one.shape[0], :] = (one[...].astype(wide) + two[...].astype(wide)).astype(half)
                at += one.shape[0]
        for inner in range(0 if add else 2):

            @pl.when(place_ref[3] == inner)
            def _(inner=inner):
                at = 0
                for chunk in ins[1 - inner :: 2]:
                    whole[at : at + chunk.shape[0], :] = chunk[...]
                    at += chunk.shape[0]

        take_rows(whole, outs[:count], place_ref)
        outs[count][...] = whole[count * block :, :]

    outs = [shape((block, LANES))] * count + [shape((total - count * block, LANES))]
    scratch = [pltpu.VMEM((total, LANES), half)]
    flat = [piece for pair in chunks for piece in pair]
    return call(body, outs, [smem] + [vmem] * len(flat), scratch, 0, total * 768, "spread")(place, *flat)


def spread_strips(count, strip, place, chunks):
    chunk = chunks[0][0].shape[0]
    own = chunk - count * strip
    many = len(chunks)

    def body(place_ref, *refs):
        ins, outs = refs[: 2 * many], refs[2 * many :]
        for inner in range(2):

            @pl.when(place_ref[3] == inner)
            def _(inner=inner):
                for k, ref in enumerate(ins[1 - inner :: 2]):
                    for r in range(count):
                        at = pl.multiple_of((place_ref[0] ^ r) * strip, SMALL)
                        outs[r][k * strip : (k + 1) * strip, :] = ref[pl.ds(at, strip), :]
                    outs[count][k * own : (k + 1) * own, :] = ref[count * strip :, :]

    outs = [shape((many * strip, LANES))] * count + [shape((many * own, LANES))]
    flat = [piece for pair in chunks for piece in pair]
    return call(body, outs, [smem] + [vmem] * len(flat), [], 0, many * chunk * 768, "spread")(place, *flat)


def collect_feed(columns, place, sets):
    count = len(sets[0][0])
    strip = strip_of(columns)
    own = sum(local.shape[0] for _, local in sets)
    total = count * columns + SMALL + own
    flat = [piece for parts, local in sets for piece in (*parts, local)]

    def body(place_ref, *refs):
        ins, whole = refs[: len(flat)], refs[-1]
        first, below = 0, count * columns + SMALL
        small = jnp.zeros((SMALL, LANES), wide)
        for number, (parts, local) in enumerate(sets):
            here = ins[number * (count + 1) : (number + 1) * (count + 1)]
            many = parts[0].shape[0] // strip
            for k in range(many):
                row = (first + k) * strip
                size = min(strip, columns - row)
                for r in range(count):
                    at = pl.multiple_of((place_ref[0] ^ r) * columns + row, SMALL)
                    whole[pl.ds(at, size), :] = here[r][k * strip : k * strip + size, :]
                    if size < strip:
                        small = small + here[r][k * strip + size : k * strip + size + SMALL, :].astype(wide)
            first += many
            whole[below : below + local.shape[0], :] = here[count][...]
            below += local.shape[0]
        whole[count * columns : count * columns + SMALL, :] = small.astype(half)

    outs = [shape((total, LANES))]
    return call(body, outs, [smem] + [vmem] * len(flat), [], 0, total * 512, "collect_feed")(place, *flat)


def collect_mix(chunks, heads, total, place, parts, local):
    count = len(parts)
    slots = parts[0].shape[0] % (3 * heads * LANES) - SMALL
    columns = parts[0].shape[0] - SMALL - slots
    filled = count * columns + SMALL + 2 * slots + local.shape[0]

    def body(place_ref, *refs):
        parts_in, local_ref, outs, whole, few = refs[:count], refs[count], refs[count + 1 : -2], refs[-2], refs[-1]
        for r, part in enumerate(parts_in):
            source = place_ref[0] ^ r
            at = pl.multiple_of(source * columns, columns)
            whole[pl.ds(at, columns), :] = part[0:columns, :]
            few[pl.ds(source, 1)] = part[columns:, :].astype(wide)[None]
        base = count * columns
        decay = [few[t, 0:heads, :] for t in range(count)]
        gain = sum(few[t, heads : heads + 1, :] for t in range(count))
        whole[base : base + SMALL, :] = small_rows(decay + [gain]).astype(half)
        near = (place_ref[0] % 2) * 2
        for k in range(2):
            at = base + SMALL + k * slots
            whole[at : at + slots, :] = few[near + k, SMALL:, :].astype(half)
        whole[base + SMALL + 2 * slots : filled, :] = local_ref[...]
        whole[filled:, :] = jnp.zeros((total - filled, LANES), half)
        chunk_out(whole, outs)

    outs = [shape((b - a, LANES)) for a, b in split_rows(total, chunks)]
    scratch = [pltpu.VMEM((total, LANES), half), pltpu.VMEM((count, SMALL + slots, LANES), wide)]
    return call(body, outs, [smem] + [vmem] * (count + 1), scratch, 0, total * 512, "collect_mix")(place, *parts, local)


def gather_halves(place_ref, ins, halves, sems, edges):
    chunks = len(edges) - 1
    handles = []
    for side in range(2):
        for c in range(chunks):
            spot = place_ref[1] if side == 0 else 1 - place_ref[1]
            where = halves.at[spot, pl.ds(edges[c], edges[c + 1] - edges[c])]
            sem = sems.at[side * chunks + c]
            for layer in range(2):
                source = ins[layer * 2 * chunks + side * chunks + c]

                @pl.when(place_ref[1] == layer)
                def _(source=source, where=where, sem=sem):
                    pltpu.make_async_copy(source, where, sem).start()

            handles.append(pltpu.make_async_copy(ins[side * chunks + c], where, sem))
    finish(handles)


def unpack(body, totals, out_shape, place, name):
    chunks = len(totals[0][0])
    edges = [0]
    for chunk in totals[0][0]:
        edges.append(edges[-1] + chunk.shape[0])

    def whole_body(place_ref, *refs):
        ins, outs, halves, sems = refs[: 4 * chunks], refs[4 * chunks : -2], refs[-2], refs[-1]
        gather_halves(place_ref, ins, halves, sems, edges)
        body(place_ref, halves, *outs)

    inputs = [piece for layer in totals for side in layer for piece in side]
    scratch = [pltpu.VMEM((2, edges[-1], LANES), half), pltpu.SemaphoreType.DMA((2 * chunks,))]
    moved = sum(o.size * 4 for o in out_shape) + 4 * edges[-1] * LANES
    return call(whole_body, out_shape, [smem] + [anywhere] * len(inputs), scratch, 0, moved, name)(place, *inputs)


def unpack_feed(count, columns, hidden, width, totals, place):
    part = width // count
    side = width // 2
    chunks = len(totals[0][0])
    edges = [0]
    for chunk in totals[0][0]:
        edges.append(edges[-1] + chunk.shape[0])
    steps = 4
    span = count * columns // steps
    tiles = span // LANES

    def body(place_ref, *refs):
        ins, (gate_up, down, gain), halves, sems = refs[: 4 * chunks], refs[4 * chunks : -2], refs[-2], refs[-1]
        step = pl.program_id(0)

        @pl.when(step == 0)
        def _():
            gather_halves(place_ref, ins, halves, sems, edges)
            base = count * columns
            for h in range(2):
                gain[0:1, h * LANES : (h + 1) * LANES] = halves[h, base : base + SMALL, :].astype(wide)[0:1]

        low = lax.broadcasted_iota(jnp.int32, (LANES, LANES), 1) < PAIR
        for is_up in range(2):

            @pl.when(step // 2 == is_up)
            def _(is_up=is_up):
                for h in range(2):
                    for m in range(tiles):
                        at = pl.multiple_of((step % 2) * 2 * span + 2 * m * LANES, LANES)
                        even = halves[h, pl.ds(at, LANES), :].astype(wide)
                        odd = halves[h, pl.ds(at + LANES, LANES), :].astype(wide)
                        if is_up:
                            value = jnp.where(low, pltpu.roll(even, PAIR, 1), odd)
                        else:
                            value = jnp.where(low, even, pltpu.roll(odd, PAIR, 1))
                        gate_up[h * LANES : (h + 1) * LANES, m * LANES : (m + 1) * LANES] = value

        base = count * columns + SMALL
        for c in range(2):
            at = pl.multiple_of(base + ((step % 2) * 2 + c) * hidden, SMALL)
            down[:, c * LANES : (c + 1) * LANES] = halves[step // 2, pl.ds(at, hidden), :].astype(wide)

    outs = [shape((part, count * columns), wide), shape((hidden, width), wide), shape((1, part), wide)]
    inputs = [piece for layer in totals for half_side in layer for piece in half_side]
    moved = sum(o.size * 4 for o in outs) + 4 * edges[-1] * LANES
    return pl.pallas_call(
        body,
        grid=(steps,),
        out_shape=outs,
        in_specs=[smem] + [anywhere] * len(inputs),
        out_specs=[
            pl.BlockSpec((part, span), lambda i: (0, i)),
            pl.BlockSpec((hidden, width // steps), lambda i: (0, i)),
            pl.BlockSpec((1, part), lambda i: (0, 0)),
        ],
        scratch_shapes=[pltpu.VMEM((2, edges[-1], LANES), half), pltpu.SemaphoreType.DMA((2 * chunks,))],
        compiler_params=pltpu.CompilerParams(vmem_limit_bytes=16 * 1024 * 1024),
        cost_estimate=pl.CostEstimate(flops=0, bytes_accessed=moved, transcendentals=0),
        name="unpack_feed",
    )(place, *inputs)


def unpack_mix(count, heads, slots, width, totals, place):
    part = width // count
    inner = heads * LANES
    columns = 3 * inner

    def body(place_ref, halves, qkv, out, gain, decay, bias, fixed):
        for h in range(2):
            rows = slice(h * LANES, (h + 1) * LANES)
            for t in range(count):
                for kind in range(3):
                    for head in range(heads):
                        source = t * columns + kind * inner + head * LANES
                        at = kind * count * inner + t * inner + head * LANES
                        qkv[rows, at : at + LANES] = halves[h, source : source + LANES, :].astype(wide)
            base = count * columns
            small = halves[h, base : base + SMALL, :].astype(wide)
            padded = jnp.concatenate([small, jnp.zeros((LANES - SMALL, LANES), wide)], axis=0).T
            decay[rows, :] = padded[:, 0 : count * heads]
            gain[0:1, rows] = small[count * heads : count * heads + 1]
            for k in range(2):
                at = base + SMALL + k * slots
                lanes = slice(k * inner + h * LANES, k * inner + (h + 1) * LANES)
                fixed[:, lanes] = halves[h, at : at + slots, :].astype(wide)
            base += SMALL + 2 * slots
            for c in range(width // LANES):
                source = base + c * LANES
                out[rows, c * LANES : (c + 1) * LANES] = halves[h, source : source + LANES, :].astype(wide)
            if h == 0:
                found = halves[h, base + width : base + width + SMALL, :].astype(wide)
                bias[...] = jnp.concatenate([found[k : k + 1, 0:1] for k in range(heads)], axis=1)

    outs = [
        shape((part, count * columns), wide),
        shape((inner, width), wide),
        shape((1, part), wide),
        shape((part, count * heads), wide),
        shape((1, heads), wide),
        shape((slots, 2 * inner), wide),
    ]
    return unpack(body, totals, outs, place, "unpack_mix")


def tie(*values):
    return lax.optimization_barrier(values)


def exchange(value, axis, distance):
    count = lax.axis_size(axis)
    return lax.ppermute(value, axis, [(i, i ^ distance) for i in range(count)])


def gather_parts(block, axis):
    count = lax.axis_size(axis)
    far = tie(*(exchange(block, axis, r) for r in reversed(range(1, count))))
    return [block, *reversed(far)]


def trade_terms(blocks, axis):
    found = trade_parts(blocks, axis)
    return found


def trade_parts(blocks, axis):
    far = {r: exchange(blocks[r], axis, r) for r in reversed(range(1, len(blocks)))}
    return [blocks[0]] + [far[r] for r in range(1, len(blocks))]


def plane_device(
    tokens,
    lengths,
    cotangent,
    norm_one,
    qkv_weight,
    decay_weight,
    decay_bias,
    persistent,
    out_weight,
    norm_two,
    gate_up,
    down_weight,
):
    ctx_count, count = lax.axis_size("ctx"), lax.axis_size("fsdp")
    section, ctx, fsdp = (lax.axis_index(a) for a in ("section", "ctx", "fsdp"))
    rows, width = tokens.shape[2:]
    heads = decay_bias.shape[1]
    size = width // (heads * count)
    inner = heads * size

    def own_batch(value):
        return lax.dynamic_index_in_dim(value, section, 0, False)[0]

    pairs = []
    for s in range(2):
        flip = s * (count - 1)
        for c in range(ctx_count):
            for f in range(count):
                here, there = c * count + f, (f ^ flip) * count + (c ^ flip)
                pairs.append((s * ctx_count * count + here, s * ctx_count * count + there))

    def turn_plane(value):
        return lax.ppermute(value, ("section", "ctx", "fsdp"), pairs)

    def swap(value):
        return exchange(value, "section", 1)

    slots = persistent.shape[1]
    flip = section * (count - 1)
    spot = jnp.stack([fsdp, section, ctx ^ flip]).astype(jnp.int32)
    x_own, qkv_shard = tie(own_batch(tokens), qkv_weight[0])
    x_in = turn_plane(x_own)
    qkv_packed = pack_heads(count, qkv_shard, spot)
    qkv_parts = trade_parts(qkv_packed, "fsdp")
    small = pack_small(norm_one, norm_two, decay_weight[0], decay_bias, persistent[0], lengths[:, 0, 0])
    x_parts = gather_parts(beside(x_in, small, swap(small)), "fsdp")
    (gains_one, gains_two, decays, biases, fixeds), length = unpack_small(
        heads, slots, rows, small.shape[0], spot, x_parts
    )
    gu_packed = pack_gates(count, gate_up[0], spot)
    qkv_parts, gu_packed, _, g_own = tie(qkv_parts, gu_packed, x_parts, own_batch(cotangent))
    g_in = turn_plane(g_own)
    gu_parts = trade_parts(gu_packed, "fsdp")
    qkv_mine = assemble(spot, qkv_parts)
    qkv_other = swap(qkv_mine)
    out_mine = out_weight[0]
    out_other = swap(out_mine)
    mix_weights = (qkv_mine, qkv_other, out_mine, out_other)
    down_mine = down_weight[0]
    down_other = swap(down_mine)
    length, down_other = tie(length, down_other)
    place = jnp.stack([fsdp, section, length, (ctx == 1) | (ctx == 2)]).astype(jnp.int32)
    seat = jnp.stack([fsdp ^ flip, section, length]).astype(jnp.int32)
    hidden = down_mine.shape[0]
    columns = gu_packed[0].shape[1]

    def mix_first_half(layer, parts):
        *terms, combined, seen, projected, logits = mix_forward(
            layer, heads, size, seat, parts, rows, gains_one[layer], mix_weights, decays[layer], biases[layer], fixeds[layer]
        )
        return terms, (seen, projected, logits, combined)

    def mix_second_half(layer, terms, x):
        middle, normed_two = join_forward(False, trade_terms(terms, "fsdp"), x, gains_two[layer])
        return middle, gather_parts(normed_two, "fsdp")

    def feed_step(layer, parts, saved):
        *terms, g_rows, g_gates, active, g_gain = feed_backward(
            layer, seat, parts, [saved[6]], gains_two[layer], feed_weights, False
        )
        return terms, (saved[6], g_gates, active, g_rows, g_gain)

    def mix_step(layer, parts, saved):
        x, seen, projected, logits, combined, middle, seen_two = saved
        *terms, branch, g_projected, g_logits, g_fixed, g_gain = mix_backward(
            layer, heads, size, seat, parts, mix_weights, decays[layer], fixeds[layer], projected, logits, seen, gains_one[layer]
        )
        return terms, (seen, g_projected, combined, branch, g_logits, g_gain, g_fixed)

    inside = (ctx == 1) | (ctx == 2)
    line = {"queue": [], "inward": None, "across": None, "total": None, "flight": (None, None), "sums": []}

    def begin():
        own = line["queue"].pop(0) if line["queue"] else None
        total = line["total"]
        if own is not None and total is not None:
            sent = jnp.where(inside, total, own)
            route = [(0, 1), (3, 2), (1, 0), (2, 3)]
        else:
            sent = own if total is None else total
            route = [(0, 1), (3, 2)] if total is None else [(1, 0), (2, 3)]
        pair = line["across"]
        line["sent"] = (sent, pair, own, total is not None)
        return [v for v in (sent, pair) if v is not None], route

    def go(values, route):
        values = list(values)
        sent, pair, own, closing = line["sent"]
        sent = values.pop(0) if sent is not None else None
        pair = values.pop(0) if pair is not None else None
        line["sent"] = (sent, pair, own, closing)
        flight = [None, None]
        if sent is not None:
            flight[0] = lax.ppermute(sent, "ctx", route)
        if pair is not None:
            flight[1] = lax.ppermute(pair, "ctx", [(1, 2), (2, 1)])
        line["flight"] = flight

    def plus(a, b):
        return (a.astype(wide) + b.astype(wide)).astype(half)

    def step(*held, more=None):
        landed, crossed = line["flight"]
        waiting = [v for v in (landed, crossed) if v is not None]
        held, waiting = tie(held, waiting)
        if landed is not None:
            landed = waiting.pop(0)
        if crossed is not None:
            crossed = waiting.pop(0)
        sent, pair, own, closing = line.get("sent", (None, None, None, False))
        line["total"] = None if pair is None else plus(pair, crossed)
        line["across"] = None if own is None else plus(own, landed)
        if closing:
            line["sums"].append((sent, landed))
        if more is not None:
            line["queue"].extend(more(*held))
        ready, route = begin()
        held, ready = tie(held, ready)
        go(ready, route)
        return held

    def taken(number, skip=0):
        found = line["sums"][skip : skip + number]
        del line["sums"][skip : skip + number]
        return found

    terms, kept = mix_first_half(0, x_parts)
    terms, gu_parts[1], g_in = tie(terms, gu_parts[1], g_in)
    terms, gu_parts = tie(trade_terms(terms, "fsdp"), gu_parts)
    gu_mine = assemble(spot, gu_parts)
    feed_weights = (gu_mine, swap(gu_mine), down_mine, down_other)
    middle, normed_two = join_forward(False, terms, x_in, gains_two[0])
    parts = gather_parts(normed_two, "fsdp")
    *terms, seen_two = feed_forward(0, seat, parts, feed_weights)
    terms = trade_terms(terms, "fsdp")
    saved_first = (x_in, *kept, middle, seen_two)
    between = join_forward(True, terms, middle, None)[0]
    terms, kept = mix_first_half(1, gather_parts(between, "fsdp"))
    terms, g_three, g_two, g_one = tie(terms, *(exchange(g_in, "fsdp", r) for r in (3, 2, 1)))
    middle, parts = mix_second_half(1, terms, between)
    made = feed_backward(1, seat, [g_in, g_one, g_two, g_three], parts, gains_two[1], feed_weights, True)
    terms, (g_rows, g_gates, active, g_gain), terms_out, seen_two = made[:4], made[4:8], made[8:12], made[12]
    feed = (seen_two, g_gates, active, g_rows, g_gain)
    saved_second = (between, *kept, middle, seen_two)

    def to_owner(layer, chunks):
        return [lax.ppermute(chunk, "section", [(1 - layer, layer)]) for chunk in chunks]

    def trade(block, chunks, add=False):
        *blocks, local = spread(count, block, place, chunks, add)
        return trade_parts(blocks, "fsdp"), local

    def trade_strips(chunks):
        *blocks, local = spread_strips(count, strip, place, chunks)
        return trade_parts(blocks, "fsdp"), local

    strip = strip_of(columns)
    pad = 2 * (count * strip + hidden)
    mix_block = 3 * inner + SMALL + slots

    def summed(own, received):
        at, chunks = 0, []
        for chunk in own:
            chunks.append(plus(chunk, received[at : at + chunk.shape[0]]))
            at += chunk.shape[0]
        return chunks

    sent, *own = grad_feed(4, count, place, *feed)
    terms, sent = tie(trade_terms(terms, "fsdp"), sent)
    g_middle, g_branch = join_backward(terms, saved_second[5], gains_two[1], g_in)
    parts = gather_parts(g_branch, "fsdp")
    parts, received = tie(parts, swap(sent))
    (parts,) = step(parts, more=lambda _: summed(own, received))
    terms, mix = mix_step(1, parts, saved_second)
    terms, terms_out = step(terms, trade_terms(terms_out, "fsdp"))
    out = join_forward(True, terms_out, saved_second[5], None)[0]
    sent, *own = grad_mix(2, pad, count, place, *mix)
    terms, sent = step(trade_terms(terms, "fsdp"), sent)
    g_middle, g_branch = join_backward(terms, between, gains_one[1], g_middle)
    parts, sent = step(gather_parts(g_branch, "fsdp"), sent)
    terms, feed = feed_step(0, parts, saved_first)
    terms, _ = step(terms, swap(sent), more=lambda _, received: summed(own, received))
    sent, *own = grad_feed(4, count, place, *feed)
    terms, sent = step(trade_terms(terms, "fsdp"), sent)
    received = swap(sent)
    g_middle, g_branch = join_backward(terms, saved_first[5], gains_two[0], g_branch)
    g_branch, received = tie(g_branch, received)
    (parts,) = step(gather_parts(g_branch, "fsdp"), more=lambda _: summed(own, received))
    f1 = trade_strips(taken(4))
    terms, mix = mix_step(0, parts, saved_first)
    terms, f1 = step(terms, f1)
    feed_second = collect_feed(columns, place, [f1])
    sent, *own = grad_mix(1, pad, count, place, *mix)
    (terms,) = step(trade_terms(terms, "fsdp"))
    g_input = join_backward(terms, x_in, gains_one[0], g_middle)[1]
    received = swap(sent)
    g_input, received, feed_second = step(g_input, received, feed_second)
    m0 = trade(mix_block, [(own[0], received)], add=True)
    (m0,) = step(m0, more=lambda pieces: collect_mix(2, heads, pad, place, *pieces))
    f0 = trade_strips(taken(2, 2))
    (f0,) = step(f0)
    m1 = trade(mix_block, taken(2))
    (m1,) = step(m1)
    feed_second_other = to_owner(1, feed_second)
    f0_last = trade_strips(taken(2))
    mix_second = collect_mix(2, heads, pad, place, *m1)
    f0_last, mix_second, g_input = step(f0_last, mix_second, g_input)
    feed_first = collect_feed(columns, place, [f0, f0_last])
    feed_first_other = to_owner(0, feed_first)
    m0_first = [jnp.where(inside, *pair) for pair in taken(1)]
    m0_first_other = to_owner(0, m0_first)
    mix_second_other = to_owner(1, mix_second)
    feed_first_other, feed_second_other, m0_first_other, mix_second_other, g_input, out = step(
        feed_first_other, feed_second_other, m0_first_other, mix_second_other, g_input, out
    )
    m0_last = [jnp.where(inside, *pair) for pair in taken(1)]
    m0_last_other = to_owner(0, m0_last)
    turned_both = turn_plane(jnp.stack([out, g_input]))
    grad_gate_up, grad_down, grad_norm_two = unpack_feed(
        count,
        columns,
        hidden,
        width,
        ((feed_first, feed_first_other), (feed_second, feed_second_other)),
        place,
    )
    m0_last_other, grad_down = tie(m0_last_other, grad_down)
    grad_qkv, grad_out, grad_norm_one, grad_decay, grad_bias, grad_fixed = unpack_mix(
        count,
        heads,
        slots,
        width,
        ((m0_first + m0_last, m0_first_other + m0_last_other), (mix_second, mix_second_other)),
        place,
    )
    turned_both, grad_bias = tie(turned_both, grad_bias)
    return (
        turned_both[0][None, None],
        turned_both[1][None, None],
        grad_norm_one,
        grad_qkv[None],
        grad_decay[None],
        grad_bias,
        grad_fixed[None],
        grad_out[None],
        grad_norm_two,
        grad_gate_up[None],
        grad_down[None],
    )


def scatter_sum(blocks, axis):
    total = blocks[0].astype(wide)
    for r in range(1, len(blocks)):
        total = total + exchange(blocks[r].astype(half), axis, r).astype(wide)
    return total


def in_order(parts, index, dim):
    count = len(parts)
    shape = list(parts[0].shape)
    size = shape[dim]
    shape[dim] = size * count
    whole = jnp.zeros(shape, parts[0].dtype)
    for r, part in enumerate(parts):
        whole = lax.dynamic_update_slice_in_dim(whole, part, (index ^ r) * size, dim)
    return whole


def columns_here(shard, kinds, axis):
    count, index = lax.axis_size(axis), lax.axis_index(axis)
    rows, width = shard.shape[0], shard.shape[1] // (kinds * count)
    blocks = shard.reshape(rows, kinds, count, width)
    parts = []
    for r in range(count):
        block = lax.dynamic_index_in_dim(blocks, index ^ r, 2, False).reshape(rows, kinds * width)
        parts.append(block if r == 0 else exchange(block, axis, r))
    return in_order(parts, index, 0)


def rows_here(columns, kinds, axis):
    count, index = lax.axis_size(axis), lax.axis_index(axis)
    rows, width = columns.shape[0] // count, columns.shape[1] // kinds
    parts = []
    for r in range(count):
        block = lax.dynamic_slice_in_dim(columns, (index ^ r) * rows, rows, 0)
        block = block if r == 0 else exchange(block, axis, r)
        parts.append(block.reshape(rows, kinds, 1, width))
    return in_order(parts, index, 2).reshape(rows, kinds * count * width)


def line_sum(value, axis):
    count, index = lax.axis_size(axis), lax.axis_index(axis)
    if count != 4:
        return lax.psum(value, axis)

    def plus(a, b):
        return (a.astype(wide) + b.astype(wide)).astype(value.dtype)

    pair = plus(value, lax.ppermute(value, axis, [(0, 1), (3, 2)]))
    total = plus(pair, lax.ppermute(pair, axis, [(1, 2), (2, 1)]))
    outer = lax.ppermute(total, axis, [(1, 0), (2, 3)])
    return jnp.where((index == 0) | (index == 3), outer, total)


def dot(a, b, contract=(1, 0)):
    return lax.dot_general(a, b, (((contract[0],), (contract[1],)), ((), ())), preferred_element_type=wide)


def normalise(values, gain):
    scale = lax.rsqrt(jnp.mean(values * values, axis=-1, keepdims=True) + epsilon)
    return (values * scale * gain).astype(half)


def normalise_back(values, gain, grad):
    scale = lax.rsqrt(jnp.mean(values * values, axis=-1, keepdims=True) + epsilon)
    unit = values * scale
    grad_gain = jnp.sum(grad * unit, axis=0)
    scaled = grad * gain
    return scale * (scaled - unit * jnp.mean(scaled * unit, axis=-1, keepdims=True)), grad_gain


def heads_first(rows, size):
    return rows.reshape(rows.shape[0], rows.shape[1] // size, size).transpose(1, 0, 2)


def rows_first(heads):
    return heads.transpose(1, 0, 2).reshape(heads.shape[1], heads.shape[0] * heads.shape[2])


def batched(a, b, contract):
    return lax.dot_general(a, b, (((contract[0],), (contract[1],)), ((0,), (0,))), preferred_element_type=wide)


def cumulative(values, positions):
    earlier = (positions[None, :] <= positions[:, None]).astype(wide)
    return jnp.dot(earlier, values, precision=lax.Precision.HIGHEST)


def mixer_parts(projected, logits, fixed, length, positions, size):
    width = projected.shape[1] // 3
    q, k, v = (heads_first(projected[:, i * width : (i + 1) * width], size) for i in range(3))
    fixed_k, fixed_v = (heads_first(fixed[:, i * width : (i + 1) * width], size) for i in range(2))
    scale = size ** (-0.5)
    documents = positions >= length
    starts = (positions == 0) | (positions == length)
    allowed = ((positions[None, :] <= positions[:, None]) & (documents[:, None] == documents[None, :]))[None]
    log_keep = jax.nn.log_sigmoid(logits)
    total_log = cumulative(log_keep, positions).T
    keep = jnp.where(starts[:, None], 0.0, jax.nn.sigmoid(logits)).T
    lose = jnp.where(starts[:, None], 1.0, jax.nn.sigmoid(-logits)).T
    inflow = jnp.sqrt(lose * (1.0 + keep))
    scores = batched(q, k, (2, 2)) * scale
    fixed_scores = batched(q, fixed_k, (2, 2)) * scale
    masked = jnp.where(allowed, scores, negative)
    top = jnp.maximum(jnp.max(masked, axis=2), jnp.max(fixed_scores, axis=2))[:, :, None]
    weights, fixed_weights = jnp.exp(masked - top), jnp.exp(fixed_scores - top)
    mass = 1.0 / (jnp.sum(weights, axis=2) + jnp.sum(fixed_weights, axis=2))[:, :, None]
    weights, fixed_weights = weights * mass, fixed_weights * mass
    fall = jnp.exp(jnp.where(allowed, total_log[:, :, None] - total_log[:, None, :], negative))
    reach = scores * fall
    both = (weights + reach * inflow[:, None, :]).astype(half)
    return q, k, v, fixed_k, fixed_v, weights, fixed_weights, fall, reach, both, keep, lose, inflow


def mixer(projected, logits, fixed, length, positions, size):
    parts = mixer_parts(projected, logits, fixed, length, positions, size)
    q, k, v, fixed_k, fixed_v, weights, fixed_weights, fall, reach, both, keep, lose, inflow = parts
    mixed = batched(both, v, (2, 1)) + batched(fixed_weights.astype(half), fixed_v, (2, 1))
    return rows_first(mixed.astype(half))


def mixer_back(projected, logits, fixed, length, positions, size, grad):
    parts = mixer_parts(projected, logits, fixed, length, positions, size)
    q, k, v, fixed_k, fixed_v, weights, fixed_weights, fall, reach, both, keep, lose, inflow = parts
    scale = size ** (-0.5)
    grad = heads_first(grad, size)
    grad_both = batched(grad, v, (2, 2))
    grad_fixed = batched(grad, fixed_v, (2, 2))
    delta = (jnp.sum(weights * grad_both, axis=2) + jnp.sum(fixed_weights * grad_fixed, axis=2))[:, :, None]
    grad_scores = (weights * (grad_both - delta) + grad_both * fall * inflow[:, None, :]).astype(half)
    grad_fixed_scores = (fixed_weights * (grad_fixed - delta)).astype(half)
    grad_q = (batched(grad_scores, k, (2, 1)) + batched(grad_fixed_scores, fixed_k, (2, 1))) * scale
    grad_k = batched(grad_scores, q, (1, 1)) * scale
    grad_v = batched(both, grad, (1, 1))
    grad_fixed_k = batched(grad_fixed_scores, q, (1, 1)) * scale
    grad_fixed_v = batched(fixed_weights.astype(half), grad, (1, 1))
    pull = grad_both * reach
    grad_inflow = jnp.sum(pull, axis=1)
    grad_total = jnp.sum(pull * inflow[:, None, :], axis=2) - inflow * grad_inflow
    later = (positions[None, :] >= positions[:, None]).astype(wide)
    grad_log = jnp.dot(grad_total, later.T, precision=lax.Precision.HIGHEST)
    lose_all = jax.nn.sigmoid(-logits).T
    grad_logits = grad_log * lose_all - grad_inflow * keep * keep * lose / inflow
    grad_projected = jnp.concatenate([rows_first(grad_q), rows_first(grad_k), rows_first(grad_v)], axis=1)
    grad_persistent = jnp.concatenate([rows_first(grad_fixed_k), rows_first(grad_fixed_v)], axis=1)
    return grad_projected.astype(half), grad_logits.T, grad_persistent


def general_device(
    tokens,
    lengths,
    cotangent,
    norm_one,
    qkv_weight,
    decay_weight,
    decay_bias,
    persistent,
    out_weight,
    norm_two,
    gate_up,
    down_weight,
):
    sections, ctx_count, fsdp_count = (lax.axis_size(a) for a in ("section", "ctx", "fsdp"))
    section, ctx, fsdp = (lax.axis_index(a) for a in ("section", "ctx", "fsdp"))
    spread = ctx_count // fsdp_count
    rows, width = tokens.shape[2:]
    heads_here = decay_bias.shape[1]
    size = width // (heads_here * fsdp_count)
    inner = heads_here * size
    first = section == 0

    def own_batch(value):
        return lax.dynamic_index_in_dim(value, section, 0, False)[0]

    pairs = [(c * fsdp_count + f, f * ctx_count + c) for c in range(ctx_count) for f in range(fsdp_count)]

    def to_plane(value):
        return lax.ppermute(value, ("ctx", "fsdp"), pairs)

    def from_plane(value):
        return lax.ppermute(value, ("ctx", "fsdp"), [(b, a) for a, b in pairs])

    x_in = to_plane(own_batch(tokens))
    g_in = to_plane(own_batch(cotangent))
    length = to_plane(own_batch(lengths))[0]

    def both_layers(own):
        other = exchange(own, "section", 1)
        return jnp.where(first, own, other), jnp.where(first, other, own)

    small = jnp.concatenate(
        [
            norm_one[0],
            norm_two[0],
            decay_weight[0].reshape(-1),
            persistent[0].reshape(-1),
        ]
    )
    small = jnp.stack(both_layers(in_order([p[None] for p in gather_parts(small, "fsdp")], fsdp, 0)))
    cut = width // fsdp_count
    sizes = [cut, cut, decay_weight[0].size, persistent[0].size]
    edges = [0]
    for piece in sizes:
        edges.append(edges[-1] + piece)
    gains_one, gains_two, decays, fixeds = (small[:, :, a:b] for a, b in zip(edges[:-1], edges[1:]))
    gains_one = gains_one.reshape(2, width).astype(wide)
    gains_two = gains_two.reshape(2, width).astype(wide)
    head_count = heads_here * fsdp_count
    decays = lax.dynamic_slice_in_dim(decays.reshape(2, width, head_count), fsdp * heads_here, heads_here, 2)
    slots = persistent.shape[1]
    fixeds = fixeds.reshape(2, fsdp_count, slots, 2 * cut).transpose(0, 2, 1, 3).reshape(2, slots, 2, fsdp_count, inner)
    fixeds = lax.dynamic_index_in_dim(fixeds, fsdp, 3, False).reshape(2, slots, 2 * inner)
    biases = jnp.stack(both_layers(decay_bias[0])).astype(wide)
    qkvs = both_layers(columns_here(qkv_weight[0], 3, "fsdp"))
    outs = both_layers(out_weight[0])
    gate_ups = both_layers(columns_here(gate_up[0], 2, "fsdp"))
    downs = both_layers(down_weight[0])
    hidden = downs[0].shape[0]

    pieces = [(k * fsdp_count + (fsdp ^ r)) * rows + jnp.arange(rows) for k in range(spread) for r in range(fsdp_count)]
    all_positions = jnp.concatenate(pieces)
    groups = [[g * spread + k for k in range(spread)] for g in range(ctx_count // spread)]

    def whole(value):
        if spread == 1:
            return value
        return lax.all_gather(value, "ctx", axis_index_groups=groups, axis=0, tiled=True)

    def own_rows(value):
        if spread == 1:
            return value
        count = value.shape[0] // spread
        return lax.dynamic_slice_in_dim(value, (ctx % spread) * count, count, 0)

    def blocks_of(value):
        return list(value.reshape(fsdp_count, rows, value.shape[1]))

    def forward(layer, x, last):
        normed = jnp.concatenate(gather_parts(normalise(x, gains_one[layer]), "fsdp"))
        projected = dot(normed, qkvs[layer]).astype(half)
        logits = dot(normed, decays[layer]) + biases[layer]
        seen, seen_logits = whole(projected), whole(logits)
        combined = own_rows(mixer(seen, seen_logits, fixeds[layer], length, all_positions, size))
        middle = x + scatter_sum(blocks_of(dot(combined, outs[layer])), "fsdp")
        normed_two = jnp.concatenate(gather_parts(normalise(middle, gains_two[layer]), "fsdp"))
        gates = dot(normed_two, gate_ups[layer])
        activated = (jax.nn.silu(gates[:, :hidden]) * gates[:, hidden:]).astype(half)
        out = middle + scatter_sum(blocks_of(dot(activated, downs[layer])), "fsdp")
        return out.astype(half), (x, normed, seen, seen_logits, combined, middle, normed_two, gates, activated)

    def backward(layer, g_out, saved):
        x, normed, seen, seen_logits, combined, middle, normed_two, gates, activated = saved
        g_rows = jnp.concatenate(gather_parts(g_out, "fsdp"))
        grad_down = dot(activated, g_rows, (0, 0))
        g_activated = dot(g_rows, downs[layer], (1, 1))
        gate, up = gates[:, :hidden], gates[:, hidden:]
        sig = jax.nn.sigmoid(gate)
        g_up = g_activated * gate * sig
        g_gate = g_activated * up * sig * (1.0 + gate * (1.0 - sig))
        g_gates = jnp.concatenate([g_gate, g_up], axis=1).astype(half)
        grad_gate_up = dot(normed_two, g_gates, (0, 0))
        g_normed_two = scatter_sum(blocks_of(dot(g_gates, gate_ups[layer], (1, 1))), "fsdp")
        g_middle, grad_norm_two = normalise_back(middle, gains_two[layer], g_normed_two)
        g_middle = g_middle + g_out.astype(wide)
        g_branch = jnp.concatenate(gather_parts(g_middle.astype(half), "fsdp"))
        grad_out = dot(combined, g_branch, (0, 0))
        g_combined = whole(dot(g_branch, outs[layer], (1, 1)).astype(half))
        g_projected, g_logits, grad_fixed = mixer_back(
            seen, seen_logits, fixeds[layer], length, all_positions, size, g_combined
        )
        g_projected, g_logits = own_rows(g_projected), own_rows(g_logits)
        grad_fixed = jnp.where(ctx % spread == 0, grad_fixed, 0.0)
        grad_qkv = dot(normed, g_projected, (0, 0))
        grad_decay = dot(normed.astype(wide), g_logits, (0, 0))
        grad_bias = jnp.sum(g_logits, axis=0)
        g_normed = dot(g_projected, qkvs[layer], (1, 1)) + dot(g_logits, decays[layer].astype(wide), (1, 1))
        g_normed = scatter_sum(blocks_of(g_normed), "fsdp")
        g_x, grad_norm_one = normalise_back(x, gains_one[layer], g_normed)
        g_x = (g_x + g_middle).astype(half)
        large = (grad_qkv, grad_out, grad_gate_up, grad_down)
        return g_x, tuple(g.astype(half) for g in large), (grad_norm_one, grad_norm_two, grad_decay, grad_bias, grad_fixed)

    between, saved_first = forward(0, x_in.astype(wide), False)
    out, saved_second = forward(1, between.astype(wide), True)
    g_between, large_second, small_second = backward(1, g_in, saved_second)
    g_input, large_first, small_first = backward(0, g_between, saved_first)

    def reduced(from_first, from_second):
        received = exchange(jnp.where(first, from_second, from_first), "section", 1)
        own = jnp.where(first, from_first, from_second)
        own = (own.astype(wide) + received.astype(wide)).astype(half)
        return line_sum(own, "ctx")

    grad_qkv, grad_out, grad_gate_up, grad_down = (reduced(a, b) for a, b in zip(large_first, large_second))
    grad_qkv = rows_here(grad_qkv, 3, "fsdp")
    grad_gate_up = rows_here(grad_gate_up, 2, "fsdp")

    def small_whole(pieces):
        n_one, n_two, decay, bias, fixed = pieces
        decay_all = lax.dynamic_update_slice_in_dim(jnp.zeros((width, head_count), wide), decay, fsdp * heads_here, 1)
        bias_all = lax.dynamic_update_slice_in_dim(jnp.zeros((head_count,), wide), bias, fsdp * heads_here, 0)
        fixed_all = jnp.zeros((slots, 2, fsdp_count, inner), wide)
        fixed_all = lax.dynamic_update_slice_in_dim(fixed_all, fixed.reshape(slots, 2, 1, inner), fsdp, 2)
        return jnp.concatenate([n_one, n_two, decay_all.reshape(-1), fixed_all.reshape(-1), bias_all])

    tiny_first, tiny_second = small_whole(small_first), small_whole(small_second)
    tiny = lax.psum(jnp.stack([tiny_first, tiny_second]), ("section", "ctx", "fsdp"))
    tiny = lax.dynamic_index_in_dim(tiny, section, 0, False)
    grad_norm_one = lax.dynamic_slice_in_dim(tiny[:width], fsdp * cut, cut, 0)
    grad_norm_two = lax.dynamic_slice_in_dim(tiny[width : 2 * width], fsdp * cut, cut, 0)
    at = 2 * width
    grad_decay = lax.dynamic_slice_in_dim(tiny[at : at + width * head_count].reshape(width, head_count), fsdp * cut, cut, 0)
    at += width * head_count
    grad_fixed = tiny[at : at + slots * 2 * width].reshape(slots, 2 * width)
    grad_fixed = lax.dynamic_slice_in_dim(grad_fixed, fsdp * 2 * cut, 2 * cut, 1)
    at += slots * 2 * width
    grad_bias = lax.dynamic_slice_in_dim(tiny[at:], fsdp * heads_here, heads_here, 0)

    return (
        from_plane(out)[None, None],
        from_plane(g_input)[None, None],
        grad_norm_one[None],
        grad_qkv.astype(wide)[None],
        grad_decay[None],
        grad_bias[None],
        grad_fixed[None],
        grad_out.astype(wide)[None],
        grad_norm_two[None],
        grad_gate_up.astype(wide)[None],
        grad_down.astype(wide)[None],
    )


def solution(mesh):
    by_row = P("section", "fsdp", None)
    by_gain = P("section", "fsdp")
    by_token = P(None, "fsdp", "ctx", None)
    by_output = P("section", "fsdp", "ctx", None)
    by_slot = P("section", None, "fsdp")
    plane = mesh.shape["ctx"] == mesh.shape["fsdp"] == 4
    return jax.shard_map(
        plane_device if plane else general_device,
        mesh=mesh,
        in_specs=(
            by_token,
            P(None, "fsdp", None),
            by_token,
            by_gain,
            by_row,
            by_row,
            by_gain,
            by_slot,
            by_row,
            by_gain,
            by_row,
            by_row,
        ),
        out_specs=(
            by_output,
            by_output,
            by_gain,
            by_row,
            by_row,
            by_gain,
            by_slot,
            by_row,
            by_gain,
            by_row,
            by_row,
        ),
        check_vma=False,
    )
```

```python
import jax
import jax.numpy as jnp
from jax import lax
from jax.experimental import pallas as pl
from jax.experimental.pallas import tpu as pltpu
from jax.sharding import PartitionSpec as P

epsilon = 1e-05
negative = -1e30
wide = jnp.float32
half = jnp.bfloat16
LANES = 128
PAIR = 64
ROOM = {
    "mix_forward": 20,
    "mix_backward": 24,
    "feed_forward": 20,
    "feed_backward": 24,
    "grad_feed": 20,
    "grad_mix": 16,
    "assemble": 12,
    "pack_gates": 16,
    "spread": 12,
    "collect_feed": 12,
    "unpack_mix": 16,
}
vmem = pl.BlockSpec(memory_space=pltpu.VMEM)
smem = pl.BlockSpec(memory_space=pltpu.SMEM)
anywhere = pl.BlockSpec(memory_space=pl.ANY)


def mm(a, b):
    return lax.dot_general(a, b, (((1,), (0,)), ((), ())), preferred_element_type=wide)


def mm_nt(a, b):
    return lax.dot_general(a, b, (((1,), (1,)), ((), ())), preferred_element_type=wide)


def mm_tn(a, b):
    return lax.dot_general(a, b, (((0,), (0,)), ((), ())), preferred_element_type=wide)


def sig(v):
    return 1.0 / (1.0 + jnp.exp(-v))


def call(body, out_shape, in_specs, scratch, flops, moved, name):
    return pl.pallas_call(
        body,
        out_shape=out_shape,
        in_specs=in_specs,
        out_specs=jax.tree.map(lambda _: vmem, out_shape),
        scratch_shapes=scratch,
        compiler_params=pltpu.CompilerParams(vmem_limit_bytes=ROOM.get(name, 8) * 1024 * 1024),
        cost_estimate=pl.CostEstimate(flops=flops, bytes_accessed=moved, transcendentals=0),
        name=name,
    )


def shape(dims, kind=half):
    return jax.ShapeDtypeStruct(tuple(dims), kind)


def kept(dims, kind=half):
    return pltpu.HBM(tuple(dims), kind)


def pack_heads(count, shard, place):
    rows, columns = shard.shape
    inner = columns // (3 * count)

    def body(place_ref, shard_ref, *outs):
        for r in range(count):
            target = place_ref[0] ^ r
            for kind in range(3):
                at = pl.multiple_of(kind * count * inner + target * inner, inner)
                outs[r][:, kind * inner : (kind + 1) * inner] = shard_ref[:, pl.ds(at, inner)]

    outs = [shape((rows, 3 * inner))] * count
    return call(body, outs, [smem, vmem], [], 0, 2 * shard.size * 2, "pack_heads")(place, shard)


def pack_gates(count, shard, place):
    rows, columns = shard.shape
    hidden = columns // 2
    mine = columns // count

    def body(place_ref, shard_ref, *rest):
        outs, mixed = rest[:count], rest[count]
        low = lax.broadcasted_iota(jnp.int32, (rows, LANES), 1) < PAIR
        for m in range(hidden // LANES):
            gate = shard_ref[:, m * LANES : (m + 1) * LANES].astype(wide)
            up = shard_ref[:, hidden + m * LANES : hidden + (m + 1) * LANES].astype(wide)
            even = jnp.where(low, gate, pltpu.roll(up, PAIR, 1))
            odd = jnp.where(low, pltpu.roll(gate, PAIR, 1), up)
            mixed[:, 2 * m * LANES : (2 * m + 1) * LANES] = even.astype(half)
            mixed[:, (2 * m + 1) * LANES : (2 * m + 2) * LANES] = odd.astype(half)
        for r in range(count):
            at = pl.multiple_of((place_ref[0] ^ r) * mine, LANES)
            outs[r][...] = mixed[:, pl.ds(at, mine)]

    outs = [shape((rows, mine))] * count
    scratch = [pltpu.VMEM((rows, columns), half)]
    return call(body, outs, [smem, vmem], scratch, 0, 2 * shard.size * 2, "pack_gates")(place, shard)


def assemble(place, parts):
    count = len(parts)
    rows, columns = parts[0].shape

    def body(place_ref, *refs):
        put_rows(refs[:count], refs[count], place_ref)

    outs = [shape((rows * count, columns))]
    moved = 4 * rows * count * columns
    return call(body, outs, [smem] + [vmem] * count, [], 0, moved, "assemble")(place, *parts)[0]


def fetch(place_ref, layer, mine, other, target, sems, span=None):
    rows, columns = mine.shape
    span = columns if span is None else span
    handles = []
    for k, at in enumerate(range(0, columns, span)):
        lanes = pl.ds(at, min(span, columns - at))
        where = target.at[pl.ds(0, rows), lanes]
        for own, source in ((True, mine), (False, other)):

            @pl.when((place_ref[1] == layer) == own)
            def _(source=source, lanes=lanes, where=where, k=k):
                pltpu.make_async_copy(source.at[pl.ds(0, rows), lanes], where, sems.at[k]).start()

        handles.append(pltpu.make_async_copy(mine.at[pl.ds(0, rows), lanes], where, sems.at[k]))
    return handles


def finish(handles):
    for handle in handles:
        handle.wait()


def put_rows(parts, target, place_ref):
    rows = parts[0].shape[0]
    for r, part in enumerate(parts):
        target[pl.ds(pl.multiple_of((place_ref[0] ^ r) * rows, rows), rows), :] = part[...]


def take_rows(source, outs, place_ref):
    rows = outs[0].shape[0]
    for r, out in enumerate(outs):
        out[...] = source[pl.ds(pl.multiple_of((place_ref[0] ^ r) * rows, rows), rows), :].astype(out.dtype)


def three_way(v):
    high = v.astype(half)
    rest = v - high.astype(wide)
    middle = rest.astype(half)
    return high, middle, (rest - middle.astype(wide)).astype(half)


def exact_sum(values, mask):
    return sum(mm(piece, mask) for piece in three_way(values))


def gate_lanes(logits, length):
    rows = logits.shape[1]
    at = lax.broadcasted_iota(jnp.int32, logits.shape, 1)
    starts = (at == 0) | (at == length)
    spill = jnp.log(1.0 + jnp.exp(-jnp.abs(logits)))
    log_keep = jnp.minimum(logits, 0.0) - spill
    keep = jnp.where(starts, 0.0, sig(logits))
    lose = jnp.where(starts, 1.0, sig(-logits))
    before = lax.broadcasted_iota(jnp.int32, (rows, rows), 0) <= lax.broadcasted_iota(jnp.int32, (rows, rows), 1)
    return log_keep, keep, lose, exact_sum(log_keep, before.astype(wide).astype(half))


def turned(values):
    return jnp.concatenate([values, jnp.zeros((LANES - values.shape[0], values.shape[1]), wide)], axis=0).T


def head_scores(head, size, inner, projected, fixed, total, total_t, inflow_t, length, scale):
    rows = projected.shape[0]
    lanes = slice(head * size, (head + 1) * size)
    q = projected[:, lanes]
    k = projected[:, inner + head * size : inner + (head + 1) * size]
    v = projected[:, 2 * inner + head * size : 2 * inner + (head + 1) * size]
    fixed_k = fixed[:, lanes]
    fixed_v = fixed[:, inner + head * size : inner + (head + 1) * size]
    scores = mm_nt(q, k) * scale
    fixed_scores = mm_nt(q, fixed_k) * scale
    at = lax.broadcasted_iota(jnp.int32, (rows, 1), 0)
    begin = jnp.where(at >= length, length, 0)
    column = lax.broadcasted_iota(jnp.int32, (rows, rows), 1)
    allowed = (column <= at) & (column >= begin)
    masked = jnp.where(allowed, scores, negative)
    top = jnp.maximum(jnp.max(masked, axis=1, keepdims=True), jnp.max(fixed_scores, axis=1, keepdims=True))
    weights, fixed_weights = jnp.exp(masked - top), jnp.exp(fixed_scores - top)
    mass = 1.0 / (jnp.sum(weights, axis=1, keepdims=True) + jnp.sum(fixed_weights, axis=1, keepdims=True))
    weights, fixed_weights = weights * mass, fixed_weights * mass
    fall = jnp.exp(jnp.where(allowed, total[:, head : head + 1] - total_t[head : head + 1, :], negative))
    reach = scores * fall
    both = (weights + reach * inflow_t[head : head + 1, :]).astype(half)
    return q, k, v, fixed_k, fixed_v, weights, fixed_weights, fall, reach, both


def mix_forward(layer, heads, size, place, parts, rows, gain, weights, decay, bias, fixed):
    count = len(parts)
    width = parts[0].shape[1]
    total_rows, inner = rows * count, heads * size
    scale = size ** (-0.5)

    def body(place_ref, *refs):
        parts_in, refs = refs[:count], refs[count:]
        (mine, other, o_mine, o_other), refs = refs[:4], refs[4:]
        (gain_ref, decay_ref, bias_ref, fixed_ref), refs = refs[:4], refs[4:]
        terms, refs = refs[:count], refs[count:]
        combined, normed, projected, logits_out, weight, out_weight, whole, sems = refs
        handles = fetch(place_ref, layer, mine, other, weight, sems, inner)
        out_handles = fetch(place_ref, layer, o_mine, o_other, out_weight, sems.at[pl.ds(3, 1)])
        for r, part in enumerate(parts_in):
            values = part[0:rows, :].astype(wide)
            root = lax.rsqrt(jnp.mean(values * values, axis=1, keepdims=True) + epsilon)
            here = pl.ds(pl.multiple_of((place_ref[0] ^ r) * rows, rows), rows)
            normed[here, :] = (values * root * gain_ref[...]).astype(half)
        length = place_ref[2]
        logits = mm_nt(decay_ref[...], normed[...]) + bias_ref[:, 0:1]
        logits_out[...] = logits
        log_keep, keep, lose, total_t = gate_lanes(logits, length)
        total = turned(total_t)
        inflow_t = jnp.sqrt(lose * (1.0 + keep))
        for kind in range(3):
            handles[kind].wait()
            lanes = slice(kind * inner, (kind + 1) * inner)
            projected[:, lanes] = mm(normed[...], weight[:, lanes]).astype(half)
        for head in range(heads):
            q, k, v, fixed_k, fixed_v, soft, fixed_soft, fall, reach, both = head_scores(
                head, size, inner, projected, fixed_ref, total, total_t, inflow_t, length, scale
            )
            mixed = mm(both, v) + mm(fixed_soft.astype(half), fixed_v)
            combined[:, head * size : (head + 1) * size] = mixed.astype(half)
        finish(out_handles)
        whole[...] = mm(combined[...], out_weight[...])
        take_rows(whole, terms, place_ref)

    outs = [shape((rows, width), wide if r == 0 else half) for r in range(count)] + [
        shape((total_rows, inner)),
        (kept if layer else shape)((total_rows, width)),
        shape((total_rows, 3 * inner)),
        shape((16, total_rows), wide),
    ]
    scratch = [
        pltpu.VMEM((width, 3 * inner), half),
        pltpu.VMEM((inner, width), half),
        pltpu.VMEM((total_rows, width), wide),
        pltpu.SemaphoreType.DMA((4,)),
    ]
    specs = [smem] + [vmem] * count + [anywhere] * 4 + [vmem] * 4
    flops = 2 * total_rows * (width * 4 * inner + inner * total_rows * 2)
    moved = 2 * (width * 3 * inner + total_rows * (2 * width + 4 * inner))
    return call(body, outs, specs, scratch, flops, moved, "mix_forward")(
        place, *parts, *weights, gain, decay, bias, fixed
    )


def mix_backward(layer, heads, size, place, parts, weights, decay, fixed, projected, logits, normed, gain):
    count = len(parts)
    rows, width = parts[0].shape
    total_rows, inner = rows * count, heads * size
    scale = size ** (-0.5)

    def body(place_ref, *refs):
        parts_in, refs = refs[:count], refs[count:]
        (mine, other, o_mine, o_other), refs = refs[:4], refs[4:]
        decay_ref, fixed_ref, projected, logits_ref, normed_ref, gain_ref = refs[:6]
        refs = refs[6:]
        terms, refs = refs[:count], refs[count:]
        branch, g_projected, g_logits_out, g_fixed, g_gain, refs = refs[0], refs[1], refs[2], refs[3], refs[4], refs[5:]
        weight, out_weight, combined, pulled, pushed, whole, sems = refs
        out_handles = fetch(place_ref, layer, o_mine, o_other, out_weight, sems.at[pl.ds(1, 1)])
        handles = fetch(place_ref, layer, mine, other, weight, sems.at[pl.ds(0, 1)])
        put_rows(parts_in, branch, place_ref)
        length = place_ref[2]
        logits = logits_ref[...]
        log_keep, keep, lose, total_t = gate_lanes(logits, length)
        total = turned(total_t)
        inflow_t = jnp.sqrt(lose * (1.0 + keep))
        finish(out_handles)
        combined[...] = mm_nt(branch[...], out_weight[...]).astype(half)
        pulled[...] = jnp.zeros_like(pulled)
        pushed[...] = jnp.zeros_like(pushed)
        for head in range(heads):
            lanes, key_lanes, value_lanes = (
                slice(kind * inner + head * size, kind * inner + (head + 1) * size) for kind in range(3)
            )
            q, k, v, fixed_k, fixed_v, weights, fixed_weights, fall, reach, both = head_scores(
                head, size, inner, projected, fixed_ref, total, total_t, inflow_t, length, scale
            )
            grad = combined[:, lanes]
            g_both = mm_nt(grad, v)
            g_few = mm_nt(grad, fixed_v)
            delta = jnp.sum(weights * g_both, axis=1, keepdims=True) + jnp.sum(
                fixed_weights * g_few, axis=1, keepdims=True
            )
            inflow_row = inflow_t[head : head + 1, :]
            g_scores = (weights * (g_both - delta) + g_both * fall * inflow_row).astype(half)
            g_few_scores = (fixed_weights * (g_few - delta)).astype(half)
            g_projected[:, lanes] = ((mm(g_scores, k) + mm(g_few_scores, fixed_k)) * scale).astype(half)
            g_projected[:, key_lanes] = (mm_tn(g_scores, q) * scale).astype(half)
            g_projected[:, value_lanes] = mm_tn(both, grad).astype(half)
            g_fixed[:, lanes] = mm_tn(g_few_scores, q) * scale
            g_fixed[:, key_lanes] = mm_tn(fixed_weights.astype(half), grad)
            pull = g_both * reach
            pulled[head : head + 1, :] = jnp.sum(pull, axis=0, keepdims=True)
            pushed[:, head : head + 1] = jnp.sum(pull * inflow_row, axis=1, keepdims=True)
        g_inflow = pulled[...]
        g_total = pushed[...].T[0:16] - inflow_t * g_inflow
        after = lax.broadcasted_iota(jnp.int32, (total_rows, total_rows), 0) >= lax.broadcasted_iota(
            jnp.int32, (total_rows, total_rows), 1
        )
        g_log = exact_sum(g_total, after.astype(wide).astype(half))
        g_logits = g_log * sig(-logits) - g_inflow * keep * keep * lose / inflow_t
        row = lax.broadcasted_iota(jnp.int32, g_logits.shape, 0)
        g_logits = jnp.where(row < heads, g_logits, 0.0)
        g_logits_out[...] = g_logits
        finish(handles)
        high, middle, low = three_way(g_logits)
        whole[...] = (
            mm_nt(g_projected[...], weight[...]) + mm_tn(high, decay_ref[...]) + mm_tn(middle, decay_ref[...])
        )
        pulls = jnp.sum(whole[...] * normed_ref[...].astype(wide), axis=0, keepdims=True) / gain_ref[...]
        g_gain[...] = jnp.broadcast_to(pulls, g_gain.shape)
        take_rows(whole, terms, place_ref)

    outs = [shape((rows, width), wide if r == 0 else half) for r in range(count)] + [
        shape((total_rows, width)),
        shape((total_rows, 3 * inner)),
        shape((16, total_rows), wide),
        shape((fixed.shape[0], 2 * inner), wide),
        shape((8, width), wide),
    ]
    scratch = [
        pltpu.VMEM((width, 3 * inner), half),
        pltpu.VMEM((inner, width), half),
        pltpu.VMEM((total_rows, inner), half),
        pltpu.VMEM((16, total_rows), wide),
        pltpu.VMEM((total_rows, LANES), wide),
        pltpu.VMEM((total_rows, width), wide),
        pltpu.SemaphoreType.DMA((2,)),
    ]
    specs = [smem] + [vmem] * count + [anywhere] * 4 + [vmem] * 6
    flops = 2 * total_rows * (width * 4 * inner + inner * total_rows * 5)
    moved = 2 * (width * 4 * inner + total_rows * (5 * width + 6 * inner))
    return call(body, outs, specs, scratch, flops, moved, "mix_backward")(
        place, *parts, *weights, decay, fixed, projected, logits, normed, gain
    )


def gates_of(tile_pair):
    rows, columns = tile_pair.shape
    if columns > 2 * LANES:
        found = [gates_of(tile_pair[:, at : at + size]) for at, size in tile_ranges(columns)]
        return tuple(jnp.concatenate([pair[k] for pair in found], axis=1) for k in range(2))
    if columns == LANES:
        return tile_pair[:, :PAIR], pltpu.roll(tile_pair, PAIR, 1)[:, :PAIR]
    first, second = tile_pair[:, :LANES], tile_pair[:, LANES:]
    low = lax.broadcasted_iota(jnp.int32, (rows, LANES), 1) < PAIR
    gate = jnp.where(low, first, pltpu.roll(second, PAIR, 1))
    up = jnp.where(low, pltpu.roll(first, PAIR, 1), second)
    return gate, up


def tiles_of(gate, up):
    rows, columns = gate.shape
    if columns > LANES:
        steps = [(at, min(LANES, columns - at)) for at in range(0, columns, LANES)]
        return jnp.concatenate([tiles_of(gate[:, at : at + size], up[:, at : at + size]) for at, size in steps], axis=1)
    if columns == PAIR:
        return jnp.concatenate([gate, up], axis=1)
    low = lax.broadcasted_iota(jnp.int32, (rows, LANES), 1) < PAIR
    first = jnp.where(low, gate, pltpu.roll(up, PAIR, 1))
    second = jnp.where(low, pltpu.roll(gate, PAIR, 1), up)
    return jnp.concatenate([first, second], axis=1)


def tile_ranges(columns, tiles=2):
    return [(at, min(tiles * LANES, columns - at)) for at in range(0, columns, tiles * LANES)]


def feed_forward(layer, place, parts, weights):
    count = len(parts)
    rows, width = parts[0].shape
    total_rows = rows * count
    columns, hidden = weights[0].shape[1], weights[2].shape[0]
    padded = -(-hidden // LANES) * LANES

    def body(place_ref, *refs):
        parts_in, refs = refs[:count], refs[count:]
        (mine, other, d_mine, d_other), refs = refs[:4], refs[4:]
        terms, normed, refs = refs[:count], refs[count], refs[count + 1 :]
        weight, down, active, whole, sems = refs
        handles = fetch(place_ref, layer, mine, other, weight, sems.at[pl.ds(0, 1)])
        down_handles = fetch(place_ref, layer, d_mine, d_other, down, sems.at[pl.ds(1, 1)])
        put_rows(parts_in, normed, place_ref)
        if padded != hidden:
            down[hidden:, :] = jnp.zeros((padded - hidden, width), half)
            active[:, padded - LANES :] = jnp.zeros((total_rows, LANES), half)
        finish(handles)
        for at, size in tile_ranges(columns):
            gate, up = gates_of(mm(normed[...], weight[:, at : at + size]))
            active[:, at // 2 : (at + size) // 2] = (gate * sig(gate) * up).astype(half)
        finish(down_handles)
        whole[...] = mm(active[...], down[...])
        take_rows(whole, terms, place_ref)

    outs = [shape((rows, width), wide if r == 0 else half) for r in range(count)] + [shape((total_rows, width))]
    scratch = [
        pltpu.VMEM((width, columns), half),
        pltpu.VMEM((padded, width), half),
        pltpu.VMEM((total_rows, padded), half),
        pltpu.VMEM((total_rows, width), wide),
        pltpu.SemaphoreType.DMA((2,)),
    ]
    specs = [smem] + [vmem] * count + [anywhere] * 4
    flops = 2 * total_rows * width * (columns + hidden)
    moved = 2 * (width * (columns + hidden) + total_rows * 4 * width)
    return call(body, outs, specs, scratch, flops, moved, "feed_forward")(
        place, *parts, *weights
    )


def feed_backward(layer, place, parts, normed_parts, gain, weights, forward):
    count = len(parts)
    rows, width = parts[0].shape
    total_rows = rows * count
    columns, hidden = weights[0].shape[1], weights[2].shape[0]
    padded = -(-hidden // LANES) * LANES

    def body(place_ref, *refs):
        parts_in, refs = refs[:count], refs[count:]
        normed_in, refs = refs[: len(normed_parts)], refs[len(normed_parts) :]
        gain_ref, (mine, other, d_mine, d_other), refs = refs[0], refs[1:5], refs[5:]
        terms, refs = refs[:count], refs[count:]
        g_out, g_gates, active, g_gain, refs = refs[0], refs[1], refs[2], refs[3], refs[4:]
        if forward:
            ahead, normed, refs = refs[:count], refs[count], refs[count + 1 :]
        else:
            normed = normed_in[0]
        weight, down, held, whole, sems = refs
        handles = fetch(place_ref, layer, mine, other, weight, sems.at[pl.ds(0, 1)])
        down_handles = fetch(place_ref, layer, d_mine, d_other, down, sems.at[pl.ds(1, 1)])
        put_rows(parts_in, g_out, place_ref)
        if forward:
            put_rows(normed_in, normed, place_ref)
        if padded != hidden:
            down[hidden:, :] = jnp.zeros((padded - hidden, width), half)
            held[:, padded - LANES :] = jnp.zeros((total_rows, LANES), half)
        finish(handles)
        finish(down_handles)
        for at, size in tile_ranges(columns, 4):
            inside = slice(at // 2, (at + size) // 2)
            gate, up = gates_of(mm(normed[...], weight[:, at : at + size]))
            g_active = mm_nt(g_out[...], down[inside, :])
            open_ = sig(gate)
            lit = gate * open_
            product = (lit * up).astype(half)
            active[:, inside] = product
            if forward:
                held[:, inside] = product
            g_up = g_active * lit
            g_gate = g_active * up * (open_ * (1.0 + gate - lit))
            g_gates[:, at : at + size] = tiles_of(g_gate, g_up).astype(half)
        whole[...] = mm_nt(g_gates[...], weight[...])
        pulls = jnp.sum(whole[...] * normed[...].astype(wide), axis=0, keepdims=True) / gain_ref[...]
        g_gain[...] = jnp.broadcast_to(pulls, g_gain.shape)
        take_rows(whole, terms, place_ref)
        if forward:
            whole[...] = mm(held[...], down[...])
            take_rows(whole, ahead, place_ref)

    term_shapes = [shape((rows, width), wide if r == 0 else half) for r in range(count)]
    place_of = kept if forward else shape
    outs = [place_of((rows, width), wide), *term_shapes[1:]] + [
        place_of((total_rows, width)),
        place_of((total_rows, columns)),
        place_of((total_rows, hidden)),
        place_of((8, width), wide),
    ]
    if forward:
        outs = outs + [kept(term.shape, term.dtype) for term in term_shapes] + [kept((total_rows, width))]
    scratch = [
        pltpu.VMEM((width, columns), half),
        pltpu.VMEM((padded, width), half),
        pltpu.VMEM((total_rows, padded), half),
        pltpu.VMEM((total_rows, width), wide),
        pltpu.SemaphoreType.DMA((2,)),
    ]
    specs = [smem] + [vmem] * (count + len(normed_parts) + 1) + [anywhere] * 4
    flops = 2 * total_rows * width * (2 * columns + hidden)
    moved = 2 * (width * (columns + hidden) + total_rows * (6 * width + columns + hidden))
    return call(body, outs, specs, scratch, flops, moved, "feed_backward")(
        place, *parts, *normed_parts, gain, *weights
    )


def pack_small(norm_one, norm_two, decay, bias, persistent, lengths):
    cut, heads_all = decay.shape
    slots, columns = persistent.shape
    heads = bias.shape[1]
    lanes = cut // LANES
    total = 16 * (1 + lanes + columns // LANES)

    batches = lengths.shape[0]

    def body(lengths_ref, one_ref, two_ref, decay_ref, bias_ref, fixed_ref, out):
        rows = [ref[0:1, b * LANES : (b + 1) * LANES].astype(wide) for ref in (one_ref, two_ref) for b in range(lanes)]
        rows.append(jnp.concatenate([bias_ref[...].astype(wide), jnp.zeros((1, LANES - heads), wide)], axis=1))
        for m in range(batches):
            for part in (lengths_ref[m] // 64, lengths_ref[m] % 64):
                rows.append(jnp.full((1, LANES), part.astype(wide)))
        rows.append(jnp.zeros((16 - len(rows), LANES), wide))
        out[0:16, :] = jnp.concatenate(rows, axis=0).astype(half)
        padded = jnp.concatenate([decay_ref[...].astype(wide), jnp.zeros((cut, LANES - heads_all), wide)], axis=1).T
        for b in range(lanes):
            out[16 * (1 + b) : 16 * (2 + b), :] = padded[0:16, b * LANES : (b + 1) * LANES].astype(half)
        for c in range(columns // LANES):
            at = 16 * (1 + lanes + c)
            out[at : at + slots, :] = fixed_ref[:, c * LANES : (c + 1) * LANES]

    return call(body, [shape((total, LANES))], [smem] + [vmem] * 5, [], 0, 1 << 17, "pack_small")(
        lengths, norm_one, norm_two, decay, bias, persistent
    )[0]


def beside(rows, mine, other):
    height, width = rows.shape
    groups = 2 * mine.shape[0] // 16
    across = width // LANES
    below = 16 * -(-groups // across)

    def body(rows_ref, mine_ref, other_ref, out):
        out[0:height, :] = rows_ref[...]
        out[height:, :] = jnp.zeros((below, width), half)
        for g in range(groups):
            ref, at = (mine_ref, g) if g < groups // 2 else (other_ref, g - groups // 2)
            spot = (height + 16 * (g // across), LANES * (g % across))
            out[spot[0] : spot[0] + 16, spot[1] : spot[1] + LANES] = ref[16 * at : 16 * at + 16, :]

    outs = [shape((height + below, width))]
    return call(body, outs, [vmem] * 3, [], 0, 1 << 20, "beside")(rows, mine, other)[0]


def turn_bias(row):
    at = lax.broadcasted_iota(jnp.int32, (16, LANES), 0) == lax.broadcasted_iota(jnp.int32, (16, LANES), 1)
    return jnp.broadcast_to(jnp.sum(jnp.where(at, row, 0.0), axis=1, keepdims=True), (16, LANES))


def unpack_small(heads, slots, height, rows, place, parts):
    count = len(parts)
    width = parts[0].shape[1]
    cut = width // count
    lanes = cut // LANES
    across = width // LANES
    inner = heads * LANES

    def body(place_ref, *refs):
        ins, outs, length, held = refs[:count], refs[count:-2], refs[-2], refs[-1]
        f = place_ref[0]
        for r, part in enumerate(ins):
            for k in range(2):
                layer = place_ref[1] if k == 0 else 1 - place_ref[1]
                for g in range(rows // 16):
                    at = k * (rows // 16) + g
                    top, left = height + 16 * (at // across), LANES * (at % across)
                    held[layer, f ^ r, 16 * g : 16 * g + 16, :] = part[top : top + 16, left : left + LANES].astype(wide)
        at = 2 * lanes + 1 + 2 * place_ref[1]
        found = held[place_ref[1], place_ref[2], pl.ds(at, 2), :]
        length[...] = jnp.broadcast_to(found[0:1] * 64.0 + found[1:2], length.shape).astype(jnp.int32)
        for layer in range(2):
            one, two, decay, bias, fixed = outs[5 * layer : 5 * layer + 5]
            for t in range(count):
                for b in range(lanes):
                    at = t * cut + b * LANES
                    one[0:1, at : at + LANES] = held[layer, t, b : b + 1, :]
                    two[0:1, at : at + LANES] = held[layer, t, lanes + b : lanes + b + 1, :]
                    group = held[layer, t, 16 * (1 + b) : 16 * (2 + b), :]
                    row = lax.broadcasted_iota(jnp.int32, (16, LANES), 0)
                    mine = [
                        jnp.sum(jnp.where(row == f * heads + h, group, 0.0), axis=0, keepdims=True) for h in range(heads)
                    ]
                    mine.append(jnp.zeros((16 - heads, LANES), wide))
                    decay[:, at : at + LANES] = jnp.concatenate(mine, axis=0).astype(half)
            bias[...] = turn_bias(held[layer, f, 2 * lanes : 2 * lanes + 1, :])
            for kind in range(2):
                source = kind * (count // 2) + f // 2
                for h in range(heads):
                    at = pl.multiple_of(16 * (1 + lanes + (f % 2) * heads + h), 16)
                    lane = kind * inner + h * LANES
                    fixed[:, lane : lane + LANES] = held[layer, source, pl.ds(at, slots), :].astype(half)

    outs = [
        shape((1, width), wide),
        shape((1, width), wide),
        shape((16, width)),
        shape((16, LANES), wide),
        shape((slots, 2 * inner)),
    ] * 2 + [shape((8, LANES), jnp.int32)]
    scratch = [pltpu.VMEM((2, count, rows, LANES), wide)]
    made = call(body, outs, [smem] + [vmem] * count, scratch, 0, 1 << 20, "unpack_small")(place, *parts)
    return [list(pair) for pair in zip(made[:5], made[5:10])], made[10][0, 0]


def join_forward(rounded, terms, residual, gain):
    dims = terms[0].shape

    def body(*refs):
        count = len(terms)
        residual_ref, refs_in = refs[count], refs[:count]
        total = residual_ref[...].astype(wide)
        for ref in refs_in:
            total = total + ref[...].astype(wide)
        if gain is None:
            refs[count + 1][...] = total.astype(half)
            return
        gain_ref, out, normed = refs[count + 1 :]
        if rounded:
            total = total.astype(half).astype(wide)
        out[...] = total.astype(out.dtype)
        scale = lax.rsqrt(jnp.mean(total * total, axis=1, keepdims=True) + epsilon)
        normed[...] = (total * scale * gain_ref[...]).astype(half)

    outs = [shape(dims, half if rounded else wide), shape(dims)]
    inputs = [*terms, residual, gain]
    if gain is None:
        outs, inputs = [shape(dims)], inputs[:-1]
    return call(body, outs, [vmem] * len(inputs), [], 0, dims[0] * dims[1] * 20, "join_forward")(*inputs)


def join_backward(terms, values, gain, onward):
    dims = terms[0].shape

    def body(*refs):
        count = len(terms)
        values_ref, gain_ref, onward_ref, out, rounded = refs[count:]
        grad = refs[0][...].astype(wide)
        for ref in refs[1:count]:
            grad = grad + ref[...].astype(wide)
        v = values_ref[...].astype(wide)
        scale = lax.rsqrt(jnp.mean(v * v, axis=1, keepdims=True) + epsilon)
        unit = v * scale
        scaled = grad * gain_ref[...]
        through = scale * (scaled - unit * jnp.mean(scaled * unit, axis=1, keepdims=True))
        total = onward_ref[...].astype(wide) + through
        out[...] = total
        rounded[...] = total.astype(half)

    outs = [shape(dims, wide), shape(dims)]
    inputs = [*terms, values, gain, onward]
    return call(body, outs, [vmem] * len(inputs), [], 0, dims[0] * dims[1] * 24, "join_backward")(*inputs)


SMALL = 16


def lane_half(source, target, which, count):
    for t in range(count):
        at = pl.multiple_of(t * 2 * LANES + which * LANES, LANES)
        target[:, t * LANES : (t + 1) * LANES] = source[:, pl.ds(at, LANES)]


STRIPS = 4


def strip_of(columns):
    return SMALL * -(-(columns + SMALL) // (SMALL * STRIPS))


def packer(packed):
    def put(at, value):
        packed[at : at + value.shape[0], :] = value.astype(half)

    return put


def strip_packer(packed, strip, chunk):
    def put(t, at, value):
        done = 0
        while done < value.shape[0]:
            k, row = divmod(at + done, strip)
            size = min(value.shape[0] - done, strip - row)
            where = k * chunk + t * strip + row
            packed[where : where + size, :] = value[done : done + size].astype(half)
            done += size

    return put


def small_rows(rows):
    found = jnp.concatenate(rows, axis=0)
    return jnp.concatenate([found, jnp.zeros((SMALL - found.shape[0], LANES), wide)], axis=0)


def grad_call(body, chunks, total, inputs, scratch, flops, name):
    outs = [shape((total, LANES))] + [shape((b - a, LANES)) for a, b in split_rows(total, chunks)]
    scratch = scratch + [pltpu.VMEM((total, LANES), half)]
    moved = sum(v.size * v.dtype.itemsize for v in inputs) + total * LANES * 4
    return call(body, outs, [smem] + [vmem] * (len(inputs) - 1), scratch, flops, moved, name)(*inputs)


def grad_feed(chunks, count, place, normed, g_gates, active, g_out, g_gain):
    total_rows, width = normed.shape
    columns, hidden = g_gates.shape[1], active.shape[1]
    tiles = columns // LANES
    strip = strip_of(columns)
    chunk = count * strip + hidden
    side = width // 2

    def body(place_ref, normed_ref, gates_ref, active_ref, g_out_ref, gain_ref, *refs):
        sent, outs, left, packed = refs[0], refs[1:-2], refs[-2], refs[-1]
        for turn in range(2):
            which = 1 - place_ref[1] if turn == 0 else place_ref[1]
            packed_here = sent if turn == 0 else packed
            put, put_row = packer(packed_here), strip_packer(packed_here, strip, chunk)
            lane_half(normed_ref, left, which, count)
            turned = left[...].T
            for at in range(0, columns, 2 * LANES):
                size = min(2 * LANES, columns - at)
                tile = mm(turned, gates_ref[:, at : at + size])
                for t in range(count):
                    for c in range(size // LANES):
                        put_row(t, at + c * LANES, tile[t * LANES : (t + 1) * LANES, c * LANES : (c + 1) * LANES])
            for t in range(count):
                at = pl.multiple_of(t * 2 * LANES + which * LANES, LANES)
                rest = STRIPS * strip - columns - SMALL
                put_row(t, columns, small_rows([gain_ref[0:1, pl.ds(at, LANES)]]))
                put_row(t, columns + SMALL, jnp.zeros((rest, LANES), wide))
            active_t = active_ref[...].T
            for c in range(0, side // LANES, 2):
                at = pl.multiple_of(which * side + c * LANES, LANES)
                tile = mm(active_t, g_out_ref[:, pl.ds(at, 2 * LANES)])
                put(c * chunk + count * strip, tile[:, :LANES])
                put((c + 1) * chunk + count * strip, tile[:, LANES:])
        chunk_out(packed, outs)

    inputs = [place, normed, g_gates, active, g_out, g_gain]
    scratch = [pltpu.VMEM((total_rows, side), half)]
    flops = total_rows * width * (columns + hidden)
    return grad_call(body, chunks, STRIPS * chunk, inputs, scratch, flops, "grad_feed")


def grad_mix(chunks, total, count, place, normed, g_projected, combined, branch, g_logits, g_gain, g_fixed):
    total_rows, width = normed.shape
    columns, inner = g_projected.shape[1], combined.shape[1]
    heads = inner // LANES
    slots = g_fixed.shape[0]
    block = columns + SMALL + slots
    side = width // 2

    def body(place_ref, normed_ref, proj_ref, comb_ref, branch_ref, logits_ref, gain_ref, fixed_ref, *refs):
        sent, outs, left, packed = refs[0], refs[1:-2], refs[-2], refs[-1]
        for turn in range(2):
            which = 1 - place_ref[1] if turn == 0 else place_ref[1]
            put = packer(sent if turn == 0 else packed)
            lane_half(normed_ref, left, which, count)
            turned = left[...].T
            for at in range(0, columns, 2 * LANES):
                tile = mm(turned, proj_ref[:, at : at + 2 * LANES])
                for t in range(count):
                    for c in range(2):
                        put(t * block + at + c * LANES, tile[t * LANES : (t + 1) * LANES, c * LANES : (c + 1) * LANES])
            logits = logits_ref[...]
            decay = sum(mm(piece, left[...]) for piece in three_way(logits)[:2])
            near = pl.multiple_of(which * LANES, LANES)
            for t in range(count):
                at = pl.multiple_of(t * 2 * LANES + which * LANES, LANES)
                rows = [decay[0:heads, t * LANES : (t + 1) * LANES], gain_ref[0:1, pl.ds(at, LANES)]]
                put(t * block + columns, small_rows(rows))
                keys_here = (place_ref[0] // 2 == t).astype(wide)
                values_here = (place_ref[0] // 2 + 2 == t).astype(wide)
                fixed = fixed_ref[:, pl.ds(near, LANES)] * keys_here
                fixed = fixed + fixed_ref[:, pl.ds(pl.multiple_of(inner + near, LANES), LANES)] * values_here
                put(t * block + columns + SMALL, fixed)
            comb_t = comb_ref[:, pl.ds(near, LANES)].T
            for c in range(0, width // LANES, 2):
                tile = mm(comb_t, branch_ref[:, c * LANES : (c + 2) * LANES])
                put(count * block + c * LANES, tile[:, :LANES])
                put(count * block + (c + 1) * LANES, tile[:, LANES:])
            put(count * block + width, jnp.broadcast_to(jnp.sum(logits, axis=1, keepdims=True), (SMALL, LANES)))
            (sent if turn == 0 else packed)[count * block + width + SMALL :, :] = jnp.zeros(
                (total - count * block - width - SMALL, LANES), half
            )
        chunk_out(packed, outs)

    inputs = [place, normed, g_projected, combined, branch, g_logits, g_gain, g_fixed]
    scratch = [pltpu.VMEM((total_rows, side), half)]
    flops = total_rows * width * (columns + inner)
    return grad_call(body, chunks, total, inputs, scratch, flops, "grad_mix")


def split_rows(total, chunks):
    units = total // SMALL
    edges = [SMALL * (units * k // chunks) for k in range(chunks)] + [total]
    return list(zip(edges[:-1], edges[1:]))


def chunk_out(whole, outs):
    at = 0
    for out in outs:
        out[...] = whole[at : at + out.shape[0], :]
        at += out.shape[0]


def spread(count, block, place, chunks, add=False):
    total = sum(chunk.shape[0] for chunk, _ in chunks)

    def body(place_ref, *refs):
        ins, outs, whole = refs[: 2 * len(chunks)], refs[2 * len(chunks) : -1], refs[-1]
        at = 0
        if add:
            for one, two in zip(ins[0::2], ins[1::2]):
                whole[at : at + one.shape[0], :] = (one[...].astype(wide) + two[...].astype(wide)).astype(half)
                at += one.shape[0]
        for inner in range(0 if add else 2):

            @pl.when(place_ref[3] == inner)
            def _(inner=inner):
                at = 0
                for chunk in ins[1 - inner :: 2]:
                    whole[at : at + chunk.shape[0], :] = chunk[...]
                    at += chunk.shape[0]

        take_rows(whole, outs[:count], place_ref)
        outs[count][...] = whole[count * block :, :]

    outs = [shape((block, LANES))] * count + [shape((total - count * block, LANES))]
    scratch = [pltpu.VMEM((total, LANES), half)]
    flat = [piece for pair in chunks for piece in pair]
    return call(body, outs, [smem] + [vmem] * len(flat), scratch, 0, total * 768, "spread")(place, *flat)


def spread_strips(count, strip, place, chunks):
    chunk = chunks[0][0].shape[0]
    own = chunk - count * strip
    many = len(chunks)

    def body(place_ref, *refs):
        ins, outs = refs[: 2 * many], refs[2 * many :]
        for inner in range(2):

            @pl.when(place_ref[3] == inner)
            def _(inner=inner):
                for k, ref in enumerate(ins[1 - inner :: 2]):
                    for r in range(count):
                        at = pl.multiple_of((place_ref[0] ^ r) * strip, SMALL)
                        outs[r][k * strip : (k + 1) * strip, :] = ref[pl.ds(at, strip), :]
                    outs[count][k * own : (k + 1) * own, :] = ref[count * strip :, :]

    outs = [shape((many * strip, LANES))] * count + [shape((many * own, LANES))]
    flat = [piece for pair in chunks for piece in pair]
    return call(body, outs, [smem] + [vmem] * len(flat), [], 0, many * chunk * 768, "spread")(place, *flat)


def collect_feed(columns, place, sets):
    count = len(sets[0][0])
    strip = strip_of(columns)
    own = sum(local.shape[0] for _, local in sets)
    total = count * columns + SMALL + own
    flat = [piece for parts, local in sets for piece in (*parts, local)]

    def body(place_ref, *refs):
        ins, whole = refs[: len(flat)], refs[-1]
        first, below = 0, count * columns + SMALL
        small = jnp.zeros((SMALL, LANES), wide)
        for number, (parts, local) in enumerate(sets):
            here = ins[number * (count + 1) : (number + 1) * (count + 1)]
            many = parts[0].shape[0] // strip
            for k in range(many):
                row = (first + k) * strip
                size = min(strip, columns - row)
                for r in range(count):
                    at = pl.multiple_of((place_ref[0] ^ r) * columns + row, SMALL)
                    whole[pl.ds(at, size), :] = here[r][k * strip : k * strip + size, :]
                    if size < strip:
                        small = small + here[r][k * strip + size : k * strip + size + SMALL, :].astype(wide)
            first += many
            whole[below : below + local.shape[0], :] = here[count][...]
            below += local.shape[0]
        whole[count * columns : count * columns + SMALL, :] = small.astype(half)

    outs = [shape((total, LANES))]
    return call(body, outs, [smem] + [vmem] * len(flat), [], 0, total * 512, "collect_feed")(place, *flat)


def collect_mix(chunks, heads, total, place, parts, local):
    count = len(parts)
    slots = parts[0].shape[0] % (3 * heads * LANES) - SMALL
    columns = parts[0].shape[0] - SMALL - slots
    filled = count * columns + SMALL + 2 * slots + local.shape[0]

    def body(place_ref, *refs):
        parts_in, local_ref, outs, whole, few = refs[:count], refs[count], refs[count + 1 : -2], refs[-2], refs[-1]
        for r, part in enumerate(parts_in):
            source = place_ref[0] ^ r
            at = pl.multiple_of(source * columns, columns)
            whole[pl.ds(at, columns), :] = part[0:columns, :]
            few[pl.ds(source, 1)] = part[columns:, :].astype(wide)[None]
        base = count * columns
        decay = [few[t, 0:heads, :] for t in range(count)]
        gain = sum(few[t, heads : heads + 1, :] for t in range(count))
        whole[base : base + SMALL, :] = small_rows(decay + [gain]).astype(half)
        near = (place_ref[0] % 2) * 2
        for k in range(2):
            at = base + SMALL + k * slots
            whole[at : at + slots, :] = few[near + k, SMALL:, :].astype(half)
        whole[base + SMALL + 2 * slots : filled, :] = local_ref[...]
        whole[filled:, :] = jnp.zeros((total - filled, LANES), half)
        chunk_out(whole, outs)

    outs = [shape((b - a, LANES)) for a, b in split_rows(total, chunks)]
    scratch = [pltpu.VMEM((total, LANES), half), pltpu.VMEM((count, SMALL + slots, LANES), wide)]
    return call(body, outs, [smem] + [vmem] * (count + 1), scratch, 0, total * 512, "collect_mix")(place, *parts, local)


def gather_halves(place_ref, ins, halves, sems, counts):
    first = 0
    for layer, many in enumerate(counts):
        pieces = [ins[first : first + many], ins[first + many : first + 2 * many]]
        first += 2 * many

        @pl.when(place_ref[1] == layer)
        def _(pieces=pieces, many=many):
            handles = []
            for side in range(2):
                spot = place_ref[1] if side == 0 else 1 - place_ref[1]
                at = 0
                for c, piece in enumerate(pieces[side]):
                    where = halves.at[spot, pl.ds(at, piece.shape[0])]
                    handles.append(pltpu.make_async_copy(piece, where, sems.at[side * many + c]))
                    handles[-1].start()
                    at += piece.shape[0]
            finish(handles)


def unpack(body, totals, out_shape, place, name):
    counts = [len(own) for own, _ in totals]
    rows = sum(chunk.shape[0] for chunk in totals[0][0])
    inputs = [piece for layer in totals for side in layer for piece in side]

    def whole_body(place_ref, *refs):
        ins, outs, halves, sems = refs[: len(inputs)], refs[len(inputs) : -2], refs[-2], refs[-1]
        gather_halves(place_ref, ins, halves, sems, counts)
        body(place_ref, halves, *outs)

    scratch = [pltpu.VMEM((2, rows, LANES), half), pltpu.SemaphoreType.DMA((2 * max(counts),))]
    moved = sum(o.size * 4 for o in out_shape) + 4 * rows * LANES
    return call(whole_body, out_shape, [smem] + [anywhere] * len(inputs), scratch, 0, moved, name)(place, *inputs)


def unpack_feed(count, columns, hidden, width, totals, place):
    part = width // count
    side = width // 2
    counts = [len(own) for own, _ in totals]
    total = sum(chunk.shape[0] for chunk in totals[0][0])
    inputs = [piece for layer in totals for half_side in layer for piece in half_side]
    steps = 4
    span = count * columns // steps
    tiles = span // LANES

    def body(place_ref, *refs):
        ins, (gate_up, down, gain), halves, sems = refs[: len(inputs)], refs[len(inputs) : -2], refs[-2], refs[-1]
        step = pl.program_id(0)

        @pl.when(step == 0)
        def _():
            gather_halves(place_ref, ins, halves, sems, counts)
            base = count * columns
            for h in range(2):
                gain[0:1, h * LANES : (h + 1) * LANES] = halves[h, base : base + SMALL, :].astype(wide)[0:1]

        low = lax.broadcasted_iota(jnp.int32, (LANES, LANES), 1) < PAIR
        for is_up in range(2):

            @pl.when(step // 2 == is_up)
            def _(is_up=is_up):
                for h in range(2):
                    for m in range(tiles):
                        at = pl.multiple_of((step % 2) * 2 * span + 2 * m * LANES, LANES)
                        even = halves[h, pl.ds(at, LANES), :].astype(wide)
                        odd = halves[h, pl.ds(at + LANES, LANES), :].astype(wide)
                        if is_up:
                            value = jnp.where(low, pltpu.roll(even, PAIR, 1), odd)
                        else:
                            value = jnp.where(low, even, pltpu.roll(odd, PAIR, 1))
                        gate_up[h * LANES : (h + 1) * LANES, m * LANES : (m + 1) * LANES] = value

        base = count * columns + SMALL
        for c in range(2):
            at = pl.multiple_of(base + ((step % 2) * 2 + c) * hidden, SMALL)
            down[:, c * LANES : (c + 1) * LANES] = halves[step // 2, pl.ds(at, hidden), :].astype(wide)

    outs = [shape((part, count * columns), wide), shape((hidden, width), wide), shape((1, part), wide)]
    moved = sum(o.size * 4 for o in outs) + 4 * total * LANES
    return pl.pallas_call(
        body,
        grid=(steps,),
        out_shape=outs,
        in_specs=[smem] + [anywhere] * len(inputs),
        out_specs=[
            pl.BlockSpec((part, span), lambda i: (0, i)),
            pl.BlockSpec((hidden, width // steps), lambda i: (0, i)),
            pl.BlockSpec((1, part), lambda i: (0, 0)),
        ],
        scratch_shapes=[pltpu.VMEM((2, total, LANES), half), pltpu.SemaphoreType.DMA((2 * max(counts),))],
        compiler_params=pltpu.CompilerParams(vmem_limit_bytes=16 * 1024 * 1024),
        cost_estimate=pl.CostEstimate(flops=0, bytes_accessed=moved, transcendentals=0),
        name="unpack_feed",
    )(place, *inputs)


def unpack_mix(count, heads, slots, width, totals, place):
    part = width // count
    inner = heads * LANES
    columns = 3 * inner

    def body(place_ref, halves, qkv, out, gain, decay, bias, fixed):
        for h in range(2):
            rows = slice(h * LANES, (h + 1) * LANES)
            for t in range(count):
                for kind in range(3):
                    for head in range(heads):
                        source = t * columns + kind * inner + head * LANES
                        at = kind * count * inner + t * inner + head * LANES
                        qkv[rows, at : at + LANES] = halves[h, source : source + LANES, :].astype(wide)
            base = count * columns
            small = halves[h, base : base + SMALL, :].astype(wide)
            padded = jnp.concatenate([small, jnp.zeros((LANES - SMALL, LANES), wide)], axis=0).T
            decay[rows, :] = padded[:, 0 : count * heads]
            gain[0:1, rows] = small[count * heads : count * heads + 1]
            for k in range(2):
                at = base + SMALL + k * slots
                lanes = slice(k * inner + h * LANES, k * inner + (h + 1) * LANES)
                fixed[:, lanes] = halves[h, at : at + slots, :].astype(wide)
            base += SMALL + 2 * slots
            for c in range(width // LANES):
                source = base + c * LANES
                out[rows, c * LANES : (c + 1) * LANES] = halves[h, source : source + LANES, :].astype(wide)
            if h == 0:
                found = halves[h, base + width : base + width + SMALL, :].astype(wide)
                bias[...] = jnp.concatenate([found[k : k + 1, 0:1] for k in range(heads)], axis=1)

    outs = [
        shape((part, count * columns), wide),
        shape((inner, width), wide),
        shape((1, part), wide),
        shape((part, count * heads), wide),
        shape((1, heads), wide),
        shape((slots, 2 * inner), wide),
    ]
    return unpack(body, totals, outs, place, "unpack_mix")


def tie(*values):
    return lax.optimization_barrier(values)


def exchange(value, axis, distance):
    count = lax.axis_size(axis)
    return lax.ppermute(value, axis, [(i, i ^ distance) for i in range(count)])


def gather_parts(block, axis):
    count = lax.axis_size(axis)
    far = tie(*(exchange(block, axis, r) for r in reversed(range(1, count))))
    return [block, *reversed(far)]


def trade_terms(blocks, axis):
    found = trade_parts(blocks, axis)
    return found


def trade_parts(blocks, axis):
    far = {r: exchange(blocks[r], axis, r) for r in reversed(range(1, len(blocks)))}
    return [blocks[0]] + [far[r] for r in range(1, len(blocks))]


def plane_device(
    tokens,
    lengths,
    cotangent,
    norm_one,
    qkv_weight,
    decay_weight,
    decay_bias,
    persistent,
    out_weight,
    norm_two,
    gate_up,
    down_weight,
):
    ctx_count, count = lax.axis_size("ctx"), lax.axis_size("fsdp")
    section, ctx, fsdp = (lax.axis_index(a) for a in ("section", "ctx", "fsdp"))
    rows, width = tokens.shape[2:]
    heads = decay_bias.shape[1]
    size = width // (heads * count)
    inner = heads * size

    def own_batch(value):
        return lax.dynamic_index_in_dim(value, section, 0, False)[0]

    pairs = []
    for s in range(2):
        flip = s * (count - 1)
        for c in range(ctx_count):
            for f in range(count):
                here, there = c * count + f, (f ^ flip) * count + (c ^ flip)
                pairs.append((s * ctx_count * count + here, s * ctx_count * count + there))

    def turn_plane(value):
        return lax.ppermute(value, ("section", "ctx", "fsdp"), pairs)

    def swap(value):
        return exchange(value, "section", 1)

    slots = persistent.shape[1]
    flip = section * (count - 1)
    spot = jnp.stack([fsdp, section, ctx ^ flip]).astype(jnp.int32)
    x_own, qkv_shard = tie(own_batch(tokens), qkv_weight[0])
    x_in = turn_plane(x_own)
    qkv_packed = pack_heads(count, qkv_shard, spot)
    qkv_parts = trade_parts(qkv_packed, "fsdp")
    small = pack_small(norm_one, norm_two, decay_weight[0], decay_bias, persistent[0], lengths[:, 0, 0])
    x_parts = gather_parts(beside(x_in, small, swap(small)), "fsdp")
    (gains_one, gains_two, decays, biases, fixeds), length = unpack_small(
        heads, slots, rows, small.shape[0], spot, x_parts
    )
    gu_packed = pack_gates(count, gate_up[0], spot)
    qkv_parts, gu_packed, _, g_own = tie(qkv_parts, gu_packed, x_parts, own_batch(cotangent))
    g_in = turn_plane(g_own)
    gu_parts = trade_parts(gu_packed, "fsdp")
    qkv_mine = assemble(spot, qkv_parts)
    qkv_other = swap(qkv_mine)
    out_mine = out_weight[0]
    out_other = swap(out_mine)
    mix_weights = (qkv_mine, qkv_other, out_mine, out_other)
    down_mine = down_weight[0]
    down_other = swap(down_mine)
    length, down_other = tie(length, down_other)
    place = jnp.stack([fsdp, section, length, (ctx == 1) | (ctx == 2)]).astype(jnp.int32)
    seat = jnp.stack([fsdp ^ flip, section, length]).astype(jnp.int32)
    hidden = down_mine.shape[0]
    columns = gu_packed[0].shape[1]

    def mix_first_half(layer, parts):
        *terms, combined, seen, projected, logits = mix_forward(
            layer, heads, size, seat, parts, rows, gains_one[layer], mix_weights, decays[layer], biases[layer], fixeds[layer]
        )
        return terms, (seen, projected, logits, combined)

    def mix_second_half(layer, terms, x):
        middle, normed_two = join_forward(False, trade_terms(terms, "fsdp"), x, gains_two[layer])
        return middle, gather_parts(normed_two, "fsdp")

    def feed_step(layer, parts, saved):
        *terms, g_rows, g_gates, active, g_gain = feed_backward(
            layer, seat, parts, [saved[6]], gains_two[layer], feed_weights, False
        )
        return terms, (saved[6], g_gates, active, g_rows, g_gain)

    def mix_step(layer, parts, saved):
        x, seen, projected, logits, combined, middle, seen_two = saved
        *terms, branch, g_projected, g_logits, g_fixed, g_gain = mix_backward(
            layer, heads, size, seat, parts, mix_weights, decays[layer], fixeds[layer], projected, logits, seen, gains_one[layer]
        )
        return terms, (seen, g_projected, combined, branch, g_logits, g_gain, g_fixed)

    inside = (ctx == 1) | (ctx == 2)
    line = {"queue": [], "inward": None, "across": None, "total": None, "flight": (None, None), "sums": []}

    def begin():
        own = line["queue"].pop(0) if line["queue"] else None
        total = line["total"]
        if own is not None and total is not None:
            sent = jnp.where(inside, total, own)
            route = [(0, 1), (3, 2), (1, 0), (2, 3)]
        else:
            sent = own if total is None else total
            route = [(0, 1), (3, 2)] if total is None else [(1, 0), (2, 3)]
        pair = line["across"]
        line["sent"] = (sent, pair, own, total is not None)
        return [v for v in (sent, pair) if v is not None], route

    def go(values, route):
        values = list(values)
        sent, pair, own, closing = line["sent"]
        sent = values.pop(0) if sent is not None else None
        pair = values.pop(0) if pair is not None else None
        line["sent"] = (sent, pair, own, closing)
        flight = [None, None]
        if sent is not None:
            flight[0] = lax.ppermute(sent, "ctx", route)
        if pair is not None:
            flight[1] = lax.ppermute(pair, "ctx", [(1, 2), (2, 1)])
        line["flight"] = flight

    def plus(a, b):
        return (a.astype(wide) + b.astype(wide)).astype(half)

    def step(*held, more=None):
        landed, crossed = line["flight"]
        waiting = [v for v in (landed, crossed) if v is not None]
        held, waiting = tie(held, waiting)
        if landed is not None:
            landed = waiting.pop(0)
        if crossed is not None:
            crossed = waiting.pop(0)
        sent, pair, own, closing = line.get("sent", (None, None, None, False))
        line["total"] = None if pair is None else plus(pair, crossed)
        line["across"] = None if own is None else plus(own, landed)
        if closing:
            line["sums"].append((sent, landed))
        if more is not None:
            line["queue"].extend(more(*held))
        ready, route = begin()
        held, ready = tie(held, ready)
        go(ready, route)
        return held

    def taken(number, skip=0):
        found = line["sums"][skip : skip + number]
        del line["sums"][skip : skip + number]
        return found

    terms, kept = mix_first_half(0, x_parts)
    terms, gu_parts[1], g_in = tie(terms, gu_parts[1], g_in)
    terms, gu_parts = tie(trade_terms(terms, "fsdp"), gu_parts)
    gu_mine = assemble(spot, gu_parts)
    feed_weights = (gu_mine, swap(gu_mine), down_mine, down_other)
    middle, normed_two = join_forward(False, terms, x_in, gains_two[0])
    parts = gather_parts(normed_two, "fsdp")
    *terms, seen_two = feed_forward(0, seat, parts, feed_weights)
    terms = trade_terms(terms, "fsdp")
    saved_first = (x_in, *kept, middle, seen_two)
    between = join_forward(True, terms, middle, None)[0]
    terms, kept = mix_first_half(1, gather_parts(between, "fsdp"))
    terms, g_three, g_two, g_one = tie(terms, *(exchange(g_in, "fsdp", r) for r in (3, 2, 1)))
    middle, parts = mix_second_half(1, terms, between)
    made = feed_backward(1, seat, [g_in, g_one, g_two, g_three], parts, gains_two[1], feed_weights, True)
    terms, (g_rows, g_gates, active, g_gain), terms_out, seen_two = made[:4], made[4:8], made[8:12], made[12]
    feed = (seen_two, g_gates, active, g_rows, g_gain)
    saved_second = (between, *kept, middle, seen_two)

    def to_owner(layer, chunks):
        return [lax.ppermute(chunk, "section", [(1 - layer, layer)]) for chunk in chunks]

    def trade(block, chunks, add=False):
        *blocks, local = spread(count, block, place, chunks, add)
        return trade_parts(blocks, "fsdp"), local

    def trade_strips(chunks):
        *blocks, local = spread_strips(count, strip, place, chunks)
        return trade_parts(blocks, "fsdp"), local

    strip = strip_of(columns)
    pad = 2 * (count * strip + hidden)
    mix_block = 3 * inner + SMALL + slots

    def summed(own, received):
        at, chunks = 0, []
        for chunk in own:
            chunks.append(plus(chunk, received[at : at + chunk.shape[0]]))
            at += chunk.shape[0]
        return chunks

    sent, *own = grad_feed(4, count, place, *feed)
    terms, sent = tie(trade_terms(terms, "fsdp"), sent)
    g_middle, g_branch = join_backward(terms, saved_second[5], gains_two[1], g_in)
    parts = gather_parts(g_branch, "fsdp")
    parts, received = tie(parts, swap(sent))
    (parts,) = step(parts, more=lambda _: summed(own, received))
    terms, mix = mix_step(1, parts, saved_second)
    terms, terms_out = step(terms, trade_terms(terms_out, "fsdp"))
    out = join_forward(True, terms_out, saved_second[5], None)[0]
    sent, *own = grad_mix(2, pad, count, place, *mix)
    terms, sent = step(trade_terms(terms, "fsdp"), sent)
    g_middle, g_branch = join_backward(terms, between, gains_one[1], g_middle)
    parts, sent = step(gather_parts(g_branch, "fsdp"), sent)
    terms, feed = feed_step(0, parts, saved_first)
    terms, _ = step(terms, swap(sent), more=lambda _, received: summed(own, received))
    sent, *own = grad_feed(4, count, place, *feed)
    terms, sent = step(trade_terms(terms, "fsdp"), sent)
    received = swap(sent)
    g_middle, g_branch = join_backward(terms, saved_first[5], gains_two[0], g_branch)
    g_branch, received = tie(g_branch, received)
    (parts,) = step(gather_parts(g_branch, "fsdp"), more=lambda _: summed(own, received))
    f1 = trade_strips(taken(4))
    terms, mix = mix_step(0, parts, saved_first)
    terms, f1 = step(terms, f1)
    feed_second = collect_feed(columns, place, [f1])
    sent, *own = grad_mix(1, pad, count, place, *mix)
    (terms,) = step(trade_terms(terms, "fsdp"))
    g_input = join_backward(terms, x_in, gains_one[0], g_middle)[1]
    received = swap(sent)
    g_input, received, feed_second = step(g_input, received, feed_second)
    m0 = trade(mix_block, [(own[0], received)], add=True)
    (m0,) = step(m0, more=lambda pieces: collect_mix(2, heads, pad, place, *pieces))
    f0 = trade_strips(taken(2, 2))
    (f0,) = step(f0)
    m1 = trade(mix_block, taken(2))
    (m1,) = step(m1)
    feed_second_other = to_owner(1, feed_second)
    f0_last = trade_strips(taken(2))
    mix_second = collect_mix(1, heads, pad, place, *m1)
    f0_last, mix_second, g_input = step(f0_last, mix_second, g_input)
    feed_first = collect_feed(columns, place, [f0, f0_last])
    feed_first_other = to_owner(0, feed_first)
    m0_first = [jnp.where(inside, *pair) for pair in taken(1)]
    m0_first_other = to_owner(0, m0_first)
    mix_second_other = to_owner(1, mix_second)
    feed_first_other, feed_second_other, m0_first_other, mix_second_other, g_input, out = step(
        feed_first_other, feed_second_other, m0_first_other, mix_second_other, g_input, out
    )
    m0_last = [jnp.where(inside, *pair) for pair in taken(1)]
    m0_last_other = to_owner(0, m0_last)
    turned_both = turn_plane(jnp.stack([out, g_input]))
    grad_gate_up, grad_down, grad_norm_two = unpack_feed(
        count,
        columns,
        hidden,
        width,
        ((feed_first, feed_first_other), (feed_second, feed_second_other)),
        place,
    )
    m0_last_other, grad_down = tie(m0_last_other, grad_down)
    grad_qkv, grad_out, grad_norm_one, grad_decay, grad_bias, grad_fixed = unpack_mix(
        count,
        heads,
        slots,
        width,
        ((m0_first + m0_last, m0_first_other + m0_last_other), (mix_second, mix_second_other)),
        place,
    )
    turned_both, grad_bias = tie(turned_both, grad_bias)
    return (
        turned_both[0][None, None],
        turned_both[1][None, None],
        grad_norm_one,
        grad_qkv[None],
        grad_decay[None],
        grad_bias,
        grad_fixed[None],
        grad_out[None],
        grad_norm_two,
        grad_gate_up[None],
        grad_down[None],
    )


def scatter_sum(blocks, axis):
    total = blocks[0].astype(wide)
    for r in range(1, len(blocks)):
        total = total + exchange(blocks[r].astype(half), axis, r).astype(wide)
    return total


def in_order(parts, index, dim):
    count = len(parts)
    shape = list(parts[0].shape)
    size = shape[dim]
    shape[dim] = size * count
    whole = jnp.zeros(shape, parts[0].dtype)
    for r, part in enumerate(parts):
        whole = lax.dynamic_update_slice_in_dim(whole, part, (index ^ r) * size, dim)
    return whole


def columns_here(shard, kinds, axis):
    count, index = lax.axis_size(axis), lax.axis_index(axis)
    rows, width = shard.shape[0], shard.shape[1] // (kinds * count)
    blocks = shard.reshape(rows, kinds, count, width)
    parts = []
    for r in range(count):
        block = lax.dynamic_index_in_dim(blocks, index ^ r, 2, False).reshape(rows, kinds * width)
        parts.append(block if r == 0 else exchange(block, axis, r))
    return in_order(parts, index, 0)


def rows_here(columns, kinds, axis):
    count, index = lax.axis_size(axis), lax.axis_index(axis)
    rows, width = columns.shape[0] // count, columns.shape[1] // kinds
    parts = []
    for r in range(count):
        block = lax.dynamic_slice_in_dim(columns, (index ^ r) * rows, rows, 0)
        block = block if r == 0 else exchange(block, axis, r)
        parts.append(block.reshape(rows, kinds, 1, width))
    return in_order(parts, index, 2).reshape(rows, kinds * count * width)


def line_sum(value, axis):
    count, index = lax.axis_size(axis), lax.axis_index(axis)
    if count != 4:
        return lax.psum(value, axis)

    def plus(a, b):
        return (a.astype(wide) + b.astype(wide)).astype(value.dtype)

    pair = plus(value, lax.ppermute(value, axis, [(0, 1), (3, 2)]))
    total = plus(pair, lax.ppermute(pair, axis, [(1, 2), (2, 1)]))
    outer = lax.ppermute(total, axis, [(1, 0), (2, 3)])
    return jnp.where((index == 0) | (index == 3), outer, total)


def dot(a, b, contract=(1, 0)):
    return lax.dot_general(a, b, (((contract[0],), (contract[1],)), ((), ())), preferred_element_type=wide)


def normalise(values, gain):
    scale = lax.rsqrt(jnp.mean(values * values, axis=-1, keepdims=True) + epsilon)
    return (values * scale * gain).astype(half)


def normalise_back(values, gain, grad):
    scale = lax.rsqrt(jnp.mean(values * values, axis=-1, keepdims=True) + epsilon)
    unit = values * scale
    grad_gain = jnp.sum(grad * unit, axis=0)
    scaled = grad * gain
    return scale * (scaled - unit * jnp.mean(scaled * unit, axis=-1, keepdims=True)), grad_gain


def heads_first(rows, size):
    return rows.reshape(rows.shape[0], rows.shape[1] // size, size).transpose(1, 0, 2)


def rows_first(heads):
    return heads.transpose(1, 0, 2).reshape(heads.shape[1], heads.shape[0] * heads.shape[2])


def batched(a, b, contract):
    return lax.dot_general(a, b, (((contract[0],), (contract[1],)), ((0,), (0,))), preferred_element_type=wide)


def cumulative(values, positions):
    earlier = (positions[None, :] <= positions[:, None]).astype(wide)
    return jnp.dot(earlier, values, precision=lax.Precision.HIGHEST)


def mixer_parts(projected, logits, fixed, length, positions, size):
    width = projected.shape[1] // 3
    q, k, v = (heads_first(projected[:, i * width : (i + 1) * width], size) for i in range(3))
    fixed_k, fixed_v = (heads_first(fixed[:, i * width : (i + 1) * width], size) for i in range(2))
    scale = size ** (-0.5)
    documents = positions >= length
    starts = (positions == 0) | (positions == length)
    allowed = ((positions[None, :] <= positions[:, None]) & (documents[:, None] == documents[None, :]))[None]
    log_keep = jax.nn.log_sigmoid(logits)
    total_log = cumulative(log_keep, positions).T
    keep = jnp.where(starts[:, None], 0.0, jax.nn.sigmoid(logits)).T
    lose = jnp.where(starts[:, None], 1.0, jax.nn.sigmoid(-logits)).T
    inflow = jnp.sqrt(lose * (1.0 + keep))
    scores = batched(q, k, (2, 2)) * scale
    fixed_scores = batched(q, fixed_k, (2, 2)) * scale
    masked = jnp.where(allowed, scores, negative)
    top = jnp.maximum(jnp.max(masked, axis=2), jnp.max(fixed_scores, axis=2))[:, :, None]
    weights, fixed_weights = jnp.exp(masked - top), jnp.exp(fixed_scores - top)
    mass = 1.0 / (jnp.sum(weights, axis=2) + jnp.sum(fixed_weights, axis=2))[:, :, None]
    weights, fixed_weights = weights * mass, fixed_weights * mass
    fall = jnp.exp(jnp.where(allowed, total_log[:, :, None] - total_log[:, None, :], negative))
    reach = scores * fall
    both = (weights + reach * inflow[:, None, :]).astype(half)
    return q, k, v, fixed_k, fixed_v, weights, fixed_weights, fall, reach, both, keep, lose, inflow


def mixer(projected, logits, fixed, length, positions, size):
    parts = mixer_parts(projected, logits, fixed, length, positions, size)
    q, k, v, fixed_k, fixed_v, weights, fixed_weights, fall, reach, both, keep, lose, inflow = parts
    mixed = batched(both, v, (2, 1)) + batched(fixed_weights.astype(half), fixed_v, (2, 1))
    return rows_first(mixed.astype(half))


def mixer_back(projected, logits, fixed, length, positions, size, grad):
    parts = mixer_parts(projected, logits, fixed, length, positions, size)
    q, k, v, fixed_k, fixed_v, weights, fixed_weights, fall, reach, both, keep, lose, inflow = parts
    scale = size ** (-0.5)
    grad = heads_first(grad, size)
    grad_both = batched(grad, v, (2, 2))
    grad_fixed = batched(grad, fixed_v, (2, 2))
    delta = (jnp.sum(weights * grad_both, axis=2) + jnp.sum(fixed_weights * grad_fixed, axis=2))[:, :, None]
    grad_scores = (weights * (grad_both - delta) + grad_both * fall * inflow[:, None, :]).astype(half)
    grad_fixed_scores = (fixed_weights * (grad_fixed - delta)).astype(half)
    grad_q = (batched(grad_scores, k, (2, 1)) + batched(grad_fixed_scores, fixed_k, (2, 1))) * scale
    grad_k = batched(grad_scores, q, (1, 1)) * scale
    grad_v = batched(both, grad, (1, 1))
    grad_fixed_k = batched(grad_fixed_scores, q, (1, 1)) * scale
    grad_fixed_v = batched(fixed_weights.astype(half), grad, (1, 1))
    pull = grad_both * reach
    grad_inflow = jnp.sum(pull, axis=1)
    grad_total = jnp.sum(pull * inflow[:, None, :], axis=2) - inflow * grad_inflow
    later = (positions[None, :] >= positions[:, None]).astype(wide)
    grad_log = jnp.dot(grad_total, later.T, precision=lax.Precision.HIGHEST)
    lose_all = jax.nn.sigmoid(-logits).T
    grad_logits = grad_log * lose_all - grad_inflow * keep * keep * lose / inflow
    grad_projected = jnp.concatenate([rows_first(grad_q), rows_first(grad_k), rows_first(grad_v)], axis=1)
    grad_persistent = jnp.concatenate([rows_first(grad_fixed_k), rows_first(grad_fixed_v)], axis=1)
    return grad_projected.astype(half), grad_logits.T, grad_persistent


def general_device(
    tokens,
    lengths,
    cotangent,
    norm_one,
    qkv_weight,
    decay_weight,
    decay_bias,
    persistent,
    out_weight,
    norm_two,
    gate_up,
    down_weight,
):
    sections, ctx_count, fsdp_count = (lax.axis_size(a) for a in ("section", "ctx", "fsdp"))
    section, ctx, fsdp = (lax.axis_index(a) for a in ("section", "ctx", "fsdp"))
    spread = ctx_count // fsdp_count
    rows, width = tokens.shape[2:]
    heads_here = decay_bias.shape[1]
    size = width // (heads_here * fsdp_count)
    inner = heads_here * size
    first = section == 0

    def own_batch(value):
        return lax.dynamic_index_in_dim(value, section, 0, False)[0]

    pairs = [(c * fsdp_count + f, f * ctx_count + c) for c in range(ctx_count) for f in range(fsdp_count)]

    def to_plane(value):
        return lax.ppermute(value, ("ctx", "fsdp"), pairs)

    def from_plane(value):
        return lax.ppermute(value, ("ctx", "fsdp"), [(b, a) for a, b in pairs])

    x_in = to_plane(own_batch(tokens))
    g_in = to_plane(own_batch(cotangent))
    length = to_plane(own_batch(lengths))[0]

    def both_layers(own):
        other = exchange(own, "section", 1)
        return jnp.where(first, own, other), jnp.where(first, other, own)

    small = jnp.concatenate(
        [
            norm_one[0],
            norm_two[0],
            decay_weight[0].reshape(-1),
            persistent[0].reshape(-1),
        ]
    )
    small = jnp.stack(both_layers(in_order([p[None] for p in gather_parts(small, "fsdp")], fsdp, 0)))
    cut = width // fsdp_count
    sizes = [cut, cut, decay_weight[0].size, persistent[0].size]
    edges = [0]
    for piece in sizes:
        edges.append(edges[-1] + piece)
    gains_one, gains_two, decays, fixeds = (small[:, :, a:b] for a, b in zip(edges[:-1], edges[1:]))
    gains_one = gains_one.reshape(2, width).astype(wide)
    gains_two = gains_two.reshape(2, width).astype(wide)
    head_count = heads_here * fsdp_count
    decays = lax.dynamic_slice_in_dim(decays.reshape(2, width, head_count), fsdp * heads_here, heads_here, 2)
    slots = persistent.shape[1]
    fixeds = fixeds.reshape(2, fsdp_count, slots, 2 * cut).transpose(0, 2, 1, 3).reshape(2, slots, 2, fsdp_count, inner)
    fixeds = lax.dynamic_index_in_dim(fixeds, fsdp, 3, False).reshape(2, slots, 2 * inner)
    biases = jnp.stack(both_layers(decay_bias[0])).astype(wide)
    qkvs = both_layers(columns_here(qkv_weight[0], 3, "fsdp"))
    outs = both_layers(out_weight[0])
    gate_ups = both_layers(columns_here(gate_up[0], 2, "fsdp"))
    downs = both_layers(down_weight[0])
    hidden = downs[0].shape[0]

    pieces = [(k * fsdp_count + (fsdp ^ r)) * rows + jnp.arange(rows) for k in range(spread) for r in range(fsdp_count)]
    all_positions = jnp.concatenate(pieces)
    groups = [[g * spread + k for k in range(spread)] for g in range(ctx_count // spread)]

    def whole(value):
        if spread == 1:
            return value
        return lax.all_gather(value, "ctx", axis_index_groups=groups, axis=0, tiled=True)

    def own_rows(value):
        if spread == 1:
            return value
        count = value.shape[0] // spread
        return lax.dynamic_slice_in_dim(value, (ctx % spread) * count, count, 0)

    def blocks_of(value):
        return list(value.reshape(fsdp_count, rows, value.shape[1]))

    def forward(layer, x, last):
        normed = jnp.concatenate(gather_parts(normalise(x, gains_one[layer]), "fsdp"))
        projected = dot(normed, qkvs[layer]).astype(half)
        logits = dot(normed, decays[layer]) + biases[layer]
        seen, seen_logits = whole(projected), whole(logits)
        combined = own_rows(mixer(seen, seen_logits, fixeds[layer], length, all_positions, size))
        middle = x + scatter_sum(blocks_of(dot(combined, outs[layer])), "fsdp")
        normed_two = jnp.concatenate(gather_parts(normalise(middle, gains_two[layer]), "fsdp"))
        gates = dot(normed_two, gate_ups[layer])
        activated = (jax.nn.silu(gates[:, :hidden]) * gates[:, hidden:]).astype(half)
        out = middle + scatter_sum(blocks_of(dot(activated, downs[layer])), "fsdp")
        return out.astype(half), (x, normed, seen, seen_logits, combined, middle, normed_two, gates, activated)

    def backward(layer, g_out, saved):
        x, normed, seen, seen_logits, combined, middle, normed_two, gates, activated = saved
        g_rows = jnp.concatenate(gather_parts(g_out, "fsdp"))
        grad_down = dot(activated, g_rows, (0, 0))
        g_activated = dot(g_rows, downs[layer], (1, 1))
        gate, up = gates[:, :hidden], gates[:, hidden:]
        sig = jax.nn.sigmoid(gate)
        g_up = g_activated * gate * sig
        g_gate = g_activated * up * sig * (1.0 + gate * (1.0 - sig))
        g_gates = jnp.concatenate([g_gate, g_up], axis=1).astype(half)
        grad_gate_up = dot(normed_two, g_gates, (0, 0))
        g_normed_two = scatter_sum(blocks_of(dot(g_gates, gate_ups[layer], (1, 1))), "fsdp")
        g_middle, grad_norm_two = normalise_back(middle, gains_two[layer], g_normed_two)
        g_middle = g_middle + g_out.astype(wide)
        g_branch = jnp.concatenate(gather_parts(g_middle.astype(half), "fsdp"))
        grad_out = dot(combined, g_branch, (0, 0))
        g_combined = whole(dot(g_branch, outs[layer], (1, 1)).astype(half))
        g_projected, g_logits, grad_fixed = mixer_back(
            seen, seen_logits, fixeds[layer], length, all_positions, size, g_combined
        )
        g_projected, g_logits = own_rows(g_projected), own_rows(g_logits)
        grad_fixed = jnp.where(ctx % spread == 0, grad_fixed, 0.0)
        grad_qkv = dot(normed, g_projected, (0, 0))
        grad_decay = dot(normed.astype(wide), g_logits, (0, 0))
        grad_bias = jnp.sum(g_logits, axis=0)
        g_normed = dot(g_projected, qkvs[layer], (1, 1)) + dot(g_logits, decays[layer].astype(wide), (1, 1))
        g_normed = scatter_sum(blocks_of(g_normed), "fsdp")
        g_x, grad_norm_one = normalise_back(x, gains_one[layer], g_normed)
        g_x = (g_x + g_middle).astype(half)
        large = (grad_qkv, grad_out, grad_gate_up, grad_down)
        return g_x, tuple(g.astype(half) for g in large), (grad_norm_one, grad_norm_two, grad_decay, grad_bias, grad_fixed)

    between, saved_first = forward(0, x_in.astype(wide), False)
    out, saved_second = forward(1, between.astype(wide), True)
    g_between, large_second, small_second = backward(1, g_in, saved_second)
    g_input, large_first, small_first = backward(0, g_between, saved_first)

    def reduced(from_first, from_second):
        received = exchange(jnp.where(first, from_second, from_first), "section", 1)
        own = jnp.where(first, from_first, from_second)
        own = (own.astype(wide) + received.astype(wide)).astype(half)
        return line_sum(own, "ctx")

    grad_qkv, grad_out, grad_gate_up, grad_down = (reduced(a, b) for a, b in zip(large_first, large_second))
    grad_qkv = rows_here(grad_qkv, 3, "fsdp")
    grad_gate_up = rows_here(grad_gate_up, 2, "fsdp")

    def small_whole(pieces):
        n_one, n_two, decay, bias, fixed = pieces
        decay_all = lax.dynamic_update_slice_in_dim(jnp.zeros((width, head_count), wide), decay, fsdp * heads_here, 1)
        bias_all = lax.dynamic_update_slice_in_dim(jnp.zeros((head_count,), wide), bias, fsdp * heads_here, 0)
        fixed_all = jnp.zeros((slots, 2, fsdp_count, inner), wide)
        fixed_all = lax.dynamic_update_slice_in_dim(fixed_all, fixed.reshape(slots, 2, 1, inner), fsdp, 2)
        return jnp.concatenate([n_one, n_two, decay_all.reshape(-1), fixed_all.reshape(-1), bias_all])

    tiny_first, tiny_second = small_whole(small_first), small_whole(small_second)
    tiny = lax.psum(jnp.stack([tiny_first, tiny_second]), ("section", "ctx", "fsdp"))
    tiny = lax.dynamic_index_in_dim(tiny, section, 0, False)
    grad_norm_one = lax.dynamic_slice_in_dim(tiny[:width], fsdp * cut, cut, 0)
    grad_norm_two = lax.dynamic_slice_in_dim(tiny[width : 2 * width], fsdp * cut, cut, 0)
    at = 2 * width
    grad_decay = lax.dynamic_slice_in_dim(tiny[at : at + width * head_count].reshape(width, head_count), fsdp * cut, cut, 0)
    at += width * head_count
    grad_fixed = tiny[at : at + slots * 2 * width].reshape(slots, 2 * width)
    grad_fixed = lax.dynamic_slice_in_dim(grad_fixed, fsdp * 2 * cut, 2 * cut, 1)
    at += slots * 2 * width
    grad_bias = lax.dynamic_slice_in_dim(tiny[at:], fsdp * heads_here, heads_here, 0)

    return (
        from_plane(out)[None, None],
        from_plane(g_input)[None, None],
        grad_norm_one[None],
        grad_qkv.astype(wide)[None],
        grad_decay[None],
        grad_bias[None],
        grad_fixed[None],
        grad_out.astype(wide)[None],
        grad_norm_two[None],
        grad_gate_up.astype(wide)[None],
        grad_down.astype(wide)[None],
    )


def solution(mesh):
    by_row = P("section", "fsdp", None)
    by_gain = P("section", "fsdp")
    by_token = P(None, "fsdp", "ctx", None)
    by_output = P("section", "fsdp", "ctx", None)
    by_slot = P("section", None, "fsdp")
    plane = mesh.shape["ctx"] == mesh.shape["fsdp"] == 4
    return jax.shard_map(
        plane_device if plane else general_device,
        mesh=mesh,
        in_specs=(
            by_token,
            P(None, "fsdp", None),
            by_token,
            by_gain,
            by_row,
            by_row,
            by_gain,
            by_slot,
            by_row,
            by_gain,
            by_row,
            by_row,
        ),
        out_specs=(
            by_output,
            by_output,
            by_gain,
            by_row,
            by_row,
            by_gain,
            by_slot,
            by_row,
            by_gain,
            by_row,
            by_row,
        ),
        check_vma=False,
    )
```

```python
import jax
import jax.numpy as jnp
from jax import lax
from jax.experimental import pallas as pl
from jax.experimental.pallas import tpu as pltpu
from jax.sharding import PartitionSpec as P

epsilon = 1e-05
negative = -1e30
wide = jnp.float32
half = jnp.bfloat16
LANES = 128
PAIR = 64
ROOM = {
    "mix_forward": 20,
    "mix_backward": 24,
    "feed_forward": 20,
    "feed_backward": 24,
    "grad_feed": 20,
    "grad_mix": 16,
    "assemble": 12,
    "pack_gates": 16,
    "spread": 12,
    "collect_feed": 12,
    "unpack_mix": 16,
}
vmem = pl.BlockSpec(memory_space=pltpu.VMEM)
smem = pl.BlockSpec(memory_space=pltpu.SMEM)
anywhere = pl.BlockSpec(memory_space=pl.ANY)


def mm(a, b):
    return lax.dot_general(a, b, (((1,), (0,)), ((), ())), preferred_element_type=wide)


def mm_nt(a, b):
    return lax.dot_general(a, b, (((1,), (1,)), ((), ())), preferred_element_type=wide)


def mm_tn(a, b):
    return lax.dot_general(a, b, (((0,), (0,)), ((), ())), preferred_element_type=wide)


def sig(v):
    return 1.0 / (1.0 + jnp.exp(-v))


def call(body, out_shape, in_specs, scratch, flops, moved, name):
    return pl.pallas_call(
        body,
        out_shape=out_shape,
        in_specs=in_specs,
        out_specs=jax.tree.map(lambda _: vmem, out_shape),
        scratch_shapes=scratch,
        compiler_params=pltpu.CompilerParams(vmem_limit_bytes=ROOM.get(name, 8) * 1024 * 1024),
        cost_estimate=pl.CostEstimate(flops=flops, bytes_accessed=moved, transcendentals=0),
        name=name,
    )


def shape(dims, kind=half):
    return jax.ShapeDtypeStruct(tuple(dims), kind)


def kept(dims, kind=half):
    return pltpu.HBM(tuple(dims), kind)


def pack_heads(count, shard, place):
    rows, columns = shard.shape
    inner = columns // (3 * count)

    def body(place_ref, shard_ref, *outs):
        for r in range(count):
            target = place_ref[0] ^ r
            for kind in range(3):
                at = pl.multiple_of(kind * count * inner + target * inner, inner)
                outs[r][:, kind * inner : (kind + 1) * inner] = shard_ref[:, pl.ds(at, inner)]

    outs = [shape((rows, 3 * inner))] * count
    return call(body, outs, [smem, vmem], [], 0, 2 * shard.size * 2, "pack_heads")(place, shard)


def pack_gates(count, shard, place):
    rows, columns = shard.shape
    hidden = columns // 2
    mine = columns // count

    def body(place_ref, shard_ref, *rest):
        outs, mixed = rest[:count], rest[count]
        low = lax.broadcasted_iota(jnp.int32, (rows, LANES), 1) < PAIR
        for m in range(hidden // LANES):
            gate = shard_ref[:, m * LANES : (m + 1) * LANES].astype(wide)
            up = shard_ref[:, hidden + m * LANES : hidden + (m + 1) * LANES].astype(wide)
            even = jnp.where(low, gate, pltpu.roll(up, PAIR, 1))
            odd = jnp.where(low, pltpu.roll(gate, PAIR, 1), up)
            mixed[:, 2 * m * LANES : (2 * m + 1) * LANES] = even.astype(half)
            mixed[:, (2 * m + 1) * LANES : (2 * m + 2) * LANES] = odd.astype(half)
        for r in range(count):
            at = pl.multiple_of((place_ref[0] ^ r) * mine, LANES)
            outs[r][...] = mixed[:, pl.ds(at, mine)]

    outs = [shape((rows, mine))] * count
    scratch = [pltpu.VMEM((rows, columns), half)]
    return call(body, outs, [smem, vmem], scratch, 0, 2 * shard.size * 2, "pack_gates")(place, shard)


def assemble(place, parts):
    count = len(parts)
    rows, columns = parts[0].shape

    def body(place_ref, *refs):
        put_rows(refs[:count], refs[count], place_ref)

    outs = [shape((rows * count, columns))]
    moved = 4 * rows * count * columns
    return call(body, outs, [smem] + [vmem] * count, [], 0, moved, "assemble")(place, *parts)[0]


def fetch(place_ref, layer, mine, other, target, sems, span=None):
    rows, columns = mine.shape
    span = columns if span is None else span
    handles = []
    for k, at in enumerate(range(0, columns, span)):
        lanes = pl.ds(at, min(span, columns - at))
        where = target.at[pl.ds(0, rows), lanes]
        for own, source in ((True, mine), (False, other)):

            @pl.when((place_ref[1] == layer) == own)
            def _(source=source, lanes=lanes, where=where, k=k):
                pltpu.make_async_copy(source.at[pl.ds(0, rows), lanes], where, sems.at[k]).start()

        handles.append(pltpu.make_async_copy(mine.at[pl.ds(0, rows), lanes], where, sems.at[k]))
    return handles


def finish(handles):
    for handle in handles:
        handle.wait()


def put_rows(parts, target, place_ref):
    rows = parts[0].shape[0]
    for r, part in enumerate(parts):
        target[pl.ds(pl.multiple_of((place_ref[0] ^ r) * rows, rows), rows), :] = part[...]


def take_rows(source, outs, place_ref):
    rows = outs[0].shape[0]
    for r, out in enumerate(outs):
        out[...] = source[pl.ds(pl.multiple_of((place_ref[0] ^ r) * rows, rows), rows), :].astype(out.dtype)


def three_way(v):
    high = v.astype(half)
    rest = v - high.astype(wide)
    middle = rest.astype(half)
    return high, middle, (rest - middle.astype(wide)).astype(half)


def exact_sum(values, mask):
    return sum(mm(piece, mask) for piece in three_way(values))


def gate_lanes(logits, length):
    rows = logits.shape[1]
    at = lax.broadcasted_iota(jnp.int32, logits.shape, 1)
    starts = (at == 0) | (at == length)
    spill = jnp.log(1.0 + jnp.exp(-jnp.abs(logits)))
    log_keep = jnp.minimum(logits, 0.0) - spill
    keep = jnp.where(starts, 0.0, sig(logits))
    lose = jnp.where(starts, 1.0, sig(-logits))
    before = lax.broadcasted_iota(jnp.int32, (rows, rows), 0) <= lax.broadcasted_iota(jnp.int32, (rows, rows), 1)
    return log_keep, keep, lose, exact_sum(log_keep, before.astype(wide).astype(half))


def turned(values):
    return jnp.concatenate([values, jnp.zeros((LANES - values.shape[0], values.shape[1]), wide)], axis=0).T


def head_scores(head, size, inner, projected, fixed, total, total_t, inflow_t, length, scale):
    rows = projected.shape[0]
    lanes = slice(head * size, (head + 1) * size)
    q = projected[:, lanes]
    k = projected[:, inner + head * size : inner + (head + 1) * size]
    v = projected[:, 2 * inner + head * size : 2 * inner + (head + 1) * size]
    fixed_k = fixed[:, lanes]
    fixed_v = fixed[:, inner + head * size : inner + (head + 1) * size]
    scores = mm_nt(q, k) * scale
    fixed_scores = mm_nt(q, fixed_k) * scale
    at = lax.broadcasted_iota(jnp.int32, (rows, 1), 0)
    begin = jnp.where(at >= length, length, 0)
    column = lax.broadcasted_iota(jnp.int32, (rows, rows), 1)
    allowed = (column <= at) & (column >= begin)
    masked = jnp.where(allowed, scores, negative)
    top = jnp.maximum(jnp.max(masked, axis=1, keepdims=True), jnp.max(fixed_scores, axis=1, keepdims=True))
    weights, fixed_weights = jnp.exp(masked - top), jnp.exp(fixed_scores - top)
    mass = 1.0 / (jnp.sum(weights, axis=1, keepdims=True) + jnp.sum(fixed_weights, axis=1, keepdims=True))
    weights, fixed_weights = weights * mass, fixed_weights * mass
    fall = jnp.exp(jnp.where(allowed, total[:, head : head + 1] - total_t[head : head + 1, :], negative))
    reach = scores * fall
    both = (weights + reach * inflow_t[head : head + 1, :]).astype(half)
    return q, k, v, fixed_k, fixed_v, weights, fixed_weights, fall, reach, both


def mix_forward(layer, heads, size, place, parts, rows, gain, weights, decay, bias, fixed):
    count = len(parts)
    width = parts[0].shape[1]
    total_rows, inner = rows * count, heads * size
    scale = size ** (-0.5)

    def body(place_ref, *refs):
        parts_in, refs = refs[:count], refs[count:]
        (mine, other, o_mine, o_other), refs = refs[:4], refs[4:]
        (gain_ref, decay_ref, bias_ref, fixed_ref), refs = refs[:4], refs[4:]
        terms, refs = refs[:count], refs[count:]
        combined, normed, projected, logits_out, weight, out_weight, whole, sems = refs
        handles = fetch(place_ref, layer, mine, other, weight, sems, inner)
        out_handles = fetch(place_ref, layer, o_mine, o_other, out_weight, sems.at[pl.ds(3, 1)])
        for r, part in enumerate(parts_in):
            values = part[0:rows, :].astype(wide)
            root = lax.rsqrt(jnp.mean(values * values, axis=1, keepdims=True) + epsilon)
            here = pl.ds(pl.multiple_of((place_ref[0] ^ r) * rows, rows), rows)
            normed[here, :] = (values * root * gain_ref[...]).astype(half)
        length = place_ref[2]
        logits = mm_nt(decay_ref[...], normed[...]) + bias_ref[:, 0:1]
        logits_out[...] = logits
        log_keep, keep, lose, total_t = gate_lanes(logits, length)
        total = turned(total_t)
        inflow_t = jnp.sqrt(lose * (1.0 + keep))
        for kind in range(3):
            handles[kind].wait()
            lanes = slice(kind * inner, (kind + 1) * inner)
            projected[:, lanes] = mm(normed[...], weight[:, lanes]).astype(half)
        for head in range(heads):
            q, k, v, fixed_k, fixed_v, soft, fixed_soft, fall, reach, both = head_scores(
                head, size, inner, projected, fixed_ref, total, total_t, inflow_t, length, scale
            )
            mixed = mm(both, v) + mm(fixed_soft.astype(half), fixed_v)
            combined[:, head * size : (head + 1) * size] = mixed.astype(half)
        finish(out_handles)
        whole[...] = mm(combined[...], out_weight[...])
        take_rows(whole, terms, place_ref)

    outs = [shape((rows, width), wide if r == 0 else half) for r in range(count)] + [
        shape((total_rows, inner)),
        (kept if layer else shape)((total_rows, width)),
        shape((total_rows, 3 * inner)),
        shape((16, total_rows), wide),
    ]
    scratch = [
        pltpu.VMEM((width, 3 * inner), half),
        pltpu.VMEM((inner, width), half),
        pltpu.VMEM((total_rows, width), wide),
        pltpu.SemaphoreType.DMA((4,)),
    ]
    specs = [smem] + [vmem] * count + [anywhere] * 4 + [vmem] * 4
    flops = 2 * total_rows * (width * 4 * inner + inner * total_rows * 2)
    moved = 2 * (width * 3 * inner + total_rows * (2 * width + 4 * inner))
    return call(body, outs, specs, scratch, flops, moved, "mix_forward")(
        place, *parts, *weights, gain, decay, bias, fixed
    )


def mix_backward(layer, heads, size, place, parts, weights, decay, fixed, projected, logits, normed, gain):
    count = len(parts)
    rows, width = parts[0].shape
    total_rows, inner = rows * count, heads * size
    scale = size ** (-0.5)

    def body(place_ref, *refs):
        parts_in, refs = refs[:count], refs[count:]
        (mine, other, o_mine, o_other), refs = refs[:4], refs[4:]
        decay_ref, fixed_ref, projected, logits_ref, normed_ref, gain_ref = refs[:6]
        refs = refs[6:]
        terms, refs = refs[:count], refs[count:]
        branch, g_projected, g_logits_out, g_fixed, g_gain, refs = refs[0], refs[1], refs[2], refs[3], refs[4], refs[5:]
        weight, out_weight, combined, pulled, pushed, whole, sems = refs
        out_handles = fetch(place_ref, layer, o_mine, o_other, out_weight, sems.at[pl.ds(1, 1)])
        handles = fetch(place_ref, layer, mine, other, weight, sems.at[pl.ds(0, 1)])
        put_rows(parts_in, branch, place_ref)
        length = place_ref[2]
        logits = logits_ref[...]
        log_keep, keep, lose, total_t = gate_lanes(logits, length)
        total = turned(total_t)
        inflow_t = jnp.sqrt(lose * (1.0 + keep))
        finish(out_handles)
        combined[...] = mm_nt(branch[...], out_weight[...]).astype(half)
        pulled[...] = jnp.zeros_like(pulled)
        pushed[...] = jnp.zeros_like(pushed)
        for head in range(heads):
            lanes, key_lanes, value_lanes = (
                slice(kind * inner + head * size, kind * inner + (head + 1) * size) for kind in range(3)
            )
            q, k, v, fixed_k, fixed_v, weights, fixed_weights, fall, reach, both = head_scores(
                head, size, inner, projected, fixed_ref, total, total_t, inflow_t, length, scale
            )
            grad = combined[:, lanes]
            g_both = mm_nt(grad, v)
            g_few = mm_nt(grad, fixed_v)
            delta = jnp.sum(weights * g_both, axis=1, keepdims=True) + jnp.sum(
                fixed_weights * g_few, axis=1, keepdims=True
            )
            inflow_row = inflow_t[head : head + 1, :]
            g_scores = (weights * (g_both - delta) + g_both * fall * inflow_row).astype(half)
            g_few_scores = (fixed_weights * (g_few - delta)).astype(half)
            g_projected[:, lanes] = ((mm(g_scores, k) + mm(g_few_scores, fixed_k)) * scale).astype(half)
            g_projected[:, key_lanes] = (mm_tn(g_scores, q) * scale).astype(half)
            g_projected[:, value_lanes] = mm_tn(both, grad).astype(half)
            g_fixed[:, lanes] = mm_tn(g_few_scores, q) * scale
            g_fixed[:, key_lanes] = mm_tn(fixed_weights.astype(half), grad)
            pull = g_both * reach
            pulled[head : head + 1, :] = jnp.sum(pull, axis=0, keepdims=True)
            pushed[:, head : head + 1] = jnp.sum(pull * inflow_row, axis=1, keepdims=True)
        g_inflow = pulled[...]
        g_total = pushed[...].T[0:16] - inflow_t * g_inflow
        after = lax.broadcasted_iota(jnp.int32, (total_rows, total_rows), 0) >= lax.broadcasted_iota(
            jnp.int32, (total_rows, total_rows), 1
        )
        g_log = exact_sum(g_total, after.astype(wide).astype(half))
        g_logits = g_log * sig(-logits) - g_inflow * keep * keep * lose / inflow_t
        row = lax.broadcasted_iota(jnp.int32, g_logits.shape, 0)
        g_logits = jnp.where(row < heads, g_logits, 0.0)
        g_logits_out[...] = g_logits
        finish(handles)
        high, middle, low = three_way(g_logits)
        whole[...] = (
            mm_nt(g_projected[...], weight[...]) + mm_tn(high, decay_ref[...]) + mm_tn(middle, decay_ref[...])
        )
        pulls = jnp.sum(whole[...] * normed_ref[...].astype(wide), axis=0, keepdims=True) / gain_ref[...]
        g_gain[...] = jnp.broadcast_to(pulls, g_gain.shape)
        take_rows(whole, terms, place_ref)

    outs = [shape((rows, width), wide if r == 0 else half) for r in range(count)] + [
        shape((total_rows, width)),
        shape((total_rows, 3 * inner)),
        shape((16, total_rows), wide),
        shape((fixed.shape[0], 2 * inner), wide),
        shape((8, width), wide),
    ]
    scratch = [
        pltpu.VMEM((width, 3 * inner), half),
        pltpu.VMEM((inner, width), half),
        pltpu.VMEM((total_rows, inner), half),
        pltpu.VMEM((16, total_rows), wide),
        pltpu.VMEM((total_rows, LANES), wide),
        pltpu.VMEM((total_rows, width), wide),
        pltpu.SemaphoreType.DMA((2,)),
    ]
    specs = [smem] + [vmem] * count + [anywhere] * 4 + [vmem] * 6
    flops = 2 * total_rows * (width * 4 * inner + inner * total_rows * 5)
    moved = 2 * (width * 4 * inner + total_rows * (5 * width + 6 * inner))
    return call(body, outs, specs, scratch, flops, moved, "mix_backward")(
        place, *parts, *weights, decay, fixed, projected, logits, normed, gain
    )


def gates_of(tile_pair):
    rows, columns = tile_pair.shape
    if columns > 2 * LANES:
        found = [gates_of(tile_pair[:, at : at + size]) for at, size in tile_ranges(columns)]
        return tuple(jnp.concatenate([pair[k] for pair in found], axis=1) for k in range(2))
    if columns == LANES:
        return tile_pair[:, :PAIR], pltpu.roll(tile_pair, PAIR, 1)[:, :PAIR]
    first, second = tile_pair[:, :LANES], tile_pair[:, LANES:]
    low = lax.broadcasted_iota(jnp.int32, (rows, LANES), 1) < PAIR
    gate = jnp.where(low, first, pltpu.roll(second, PAIR, 1))
    up = jnp.where(low, pltpu.roll(first, PAIR, 1), second)
    return gate, up


def tiles_of(gate, up):
    rows, columns = gate.shape
    if columns > LANES:
        steps = [(at, min(LANES, columns - at)) for at in range(0, columns, LANES)]
        return jnp.concatenate([tiles_of(gate[:, at : at + size], up[:, at : at + size]) for at, size in steps], axis=1)
    if columns == PAIR:
        return jnp.concatenate([gate, up], axis=1)
    low = lax.broadcasted_iota(jnp.int32, (rows, LANES), 1) < PAIR
    first = jnp.where(low, gate, pltpu.roll(up, PAIR, 1))
    second = jnp.where(low, pltpu.roll(gate, PAIR, 1), up)
    return jnp.concatenate([first, second], axis=1)


def tile_ranges(columns, tiles=2):
    return [(at, min(tiles * LANES, columns - at)) for at in range(0, columns, tiles * LANES)]


def feed_forward(layer, place, parts, weights):
    count = len(parts)
    rows, width = parts[0].shape
    total_rows = rows * count
    columns, hidden = weights[0].shape[1], weights[2].shape[0]
    padded = -(-hidden // LANES) * LANES

    def body(place_ref, *refs):
        parts_in, refs = refs[:count], refs[count:]
        (mine, other, d_mine, d_other), refs = refs[:4], refs[4:]
        terms, normed, refs = refs[:count], refs[count], refs[count + 1 :]
        weight, down, active, whole, sems = refs
        handles = fetch(place_ref, layer, mine, other, weight, sems.at[pl.ds(0, 1)])
        down_handles = fetch(place_ref, layer, d_mine, d_other, down, sems.at[pl.ds(1, 1)])
        put_rows(parts_in, normed, place_ref)
        if padded != hidden:
            down[hidden:, :] = jnp.zeros((padded - hidden, width), half)
            active[:, padded - LANES :] = jnp.zeros((total_rows, LANES), half)
        finish(handles)
        for at, size in tile_ranges(columns):
            gate, up = gates_of(mm(normed[...], weight[:, at : at + size]))
            active[:, at // 2 : (at + size) // 2] = (gate * sig(gate) * up).astype(half)
        finish(down_handles)
        whole[...] = mm(active[...], down[...])
        take_rows(whole, terms, place_ref)

    outs = [shape((rows, width), wide if r == 0 else half) for r in range(count)] + [shape((total_rows, width))]
    scratch = [
        pltpu.VMEM((width, columns), half),
        pltpu.VMEM((padded, width), half),
        pltpu.VMEM((total_rows, padded), half),
        pltpu.VMEM((total_rows, width), wide),
        pltpu.SemaphoreType.DMA((2,)),
    ]
    specs = [smem] + [vmem] * count + [anywhere] * 4
    flops = 2 * total_rows * width * (columns + hidden)
    moved = 2 * (width * (columns + hidden) + total_rows * 4 * width)
    return call(body, outs, specs, scratch, flops, moved, "feed_forward")(
        place, *parts, *weights
    )


def feed_backward(layer, place, parts, normed_parts, gain, weights, forward):
    count = len(parts)
    rows, width = parts[0].shape
    total_rows = rows * count
    columns, hidden = weights[0].shape[1], weights[2].shape[0]
    padded = -(-hidden // LANES) * LANES

    def body(place_ref, *refs):
        parts_in, refs = refs[:count], refs[count:]
        normed_in, refs = refs[: len(normed_parts)], refs[len(normed_parts) :]
        gain_ref, (mine, other, d_mine, d_other), refs = refs[0], refs[1:5], refs[5:]
        terms, refs = refs[:count], refs[count:]
        g_out, g_gates, active, g_gain, refs = refs[0], refs[1], refs[2], refs[3], refs[4:]
        if forward:
            ahead, normed, refs = refs[:count], refs[count], refs[count + 1 :]
        else:
            normed = normed_in[0]
        weight, down, held, whole, sems = refs
        handles = fetch(place_ref, layer, mine, other, weight, sems.at[pl.ds(0, 1)])
        down_handles = fetch(place_ref, layer, d_mine, d_other, down, sems.at[pl.ds(1, 1)])
        put_rows(parts_in, g_out, place_ref)
        if forward:
            put_rows(normed_in, normed, place_ref)
        if padded != hidden:
            down[hidden:, :] = jnp.zeros((padded - hidden, width), half)
            held[:, padded - LANES :] = jnp.zeros((total_rows, LANES), half)
        finish(handles)
        finish(down_handles)
        for at, size in tile_ranges(columns, 4):
            inside = slice(at // 2, (at + size) // 2)
            gate, up = gates_of(mm(normed[...], weight[:, at : at + size]))
            g_active = mm_nt(g_out[...], down[inside, :])
            open_ = sig(gate)
            lit = gate * open_
            product = (lit * up).astype(half)
            active[:, inside] = product
            if forward:
                held[:, inside] = product
            g_up = g_active * lit
            g_gate = g_active * up * (open_ * (1.0 + gate - lit))
            g_gates[:, at : at + size] = tiles_of(g_gate, g_up).astype(half)
        whole[...] = mm_nt(g_gates[...], weight[...])
        pulls = jnp.sum(whole[...] * normed[...].astype(wide), axis=0, keepdims=True) / gain_ref[...]
        g_gain[...] = jnp.broadcast_to(pulls, g_gain.shape)
        take_rows(whole, terms, place_ref)
        if forward:
            whole[...] = mm(held[...], down[...])
            take_rows(whole, ahead, place_ref)

    term_shapes = [shape((rows, width), wide if r == 0 else half) for r in range(count)]
    place_of = kept if forward else shape
    outs = [place_of((rows, width), wide), *term_shapes[1:]] + [
        place_of((total_rows, width)),
        place_of((total_rows, columns)),
        place_of((total_rows, hidden)),
        place_of((8, width), wide),
    ]
    if forward:
        outs = outs + [kept(term.shape, term.dtype) for term in term_shapes] + [kept((total_rows, width))]
    scratch = [
        pltpu.VMEM((width, columns), half),
        pltpu.VMEM((padded, width), half),
        pltpu.VMEM((total_rows, padded), half),
        pltpu.VMEM((total_rows, width), wide),
        pltpu.SemaphoreType.DMA((2,)),
    ]
    specs = [smem] + [vmem] * (count + len(normed_parts) + 1) + [anywhere] * 4
    flops = 2 * total_rows * width * (2 * columns + hidden)
    moved = 2 * (width * (columns + hidden) + total_rows * (6 * width + columns + hidden))
    return call(body, outs, specs, scratch, flops, moved, "feed_backward")(
        place, *parts, *normed_parts, gain, *weights
    )


def pack_small(norm_one, norm_two, decay, bias, persistent, lengths):
    cut, heads_all = decay.shape
    slots, columns = persistent.shape
    heads = bias.shape[1]
    lanes = cut // LANES
    total = 16 * (1 + lanes + columns // LANES)

    batches = lengths.shape[0]

    def body(lengths_ref, one_ref, two_ref, decay_ref, bias_ref, fixed_ref, out):
        rows = [ref[0:1, b * LANES : (b + 1) * LANES].astype(wide) for ref in (one_ref, two_ref) for b in range(lanes)]
        rows.append(jnp.concatenate([bias_ref[...].astype(wide), jnp.zeros((1, LANES - heads), wide)], axis=1))
        for m in range(batches):
            for part in (lengths_ref[m] // 64, lengths_ref[m] % 64):
                rows.append(jnp.full((1, LANES), part.astype(wide)))
        rows.append(jnp.zeros((16 - len(rows), LANES), wide))
        out[0:16, :] = jnp.concatenate(rows, axis=0).astype(half)
        padded = jnp.concatenate([decay_ref[...].astype(wide), jnp.zeros((cut, LANES - heads_all), wide)], axis=1).T
        for b in range(lanes):
            out[16 * (1 + b) : 16 * (2 + b), :] = padded[0:16, b * LANES : (b + 1) * LANES].astype(half)
        for c in range(columns // LANES):
            at = 16 * (1 + lanes + c)
            out[at : at + slots, :] = fixed_ref[:, c * LANES : (c + 1) * LANES]

    return call(body, [shape((total, LANES))], [smem] + [vmem] * 5, [], 0, 1 << 17, "pack_small")(
        lengths, norm_one, norm_two, decay, bias, persistent
    )[0]


def beside(rows, mine, other):
    height, width = rows.shape
    groups = 2 * mine.shape[0] // 16
    across = width // LANES
    below = 16 * -(-groups // across)

    def body(rows_ref, mine_ref, other_ref, out):
        out[0:height, :] = rows_ref[...]
        out[height:, :] = jnp.zeros((below, width), half)
        for g in range(groups):
            ref, at = (mine_ref, g) if g < groups // 2 else (other_ref, g - groups // 2)
            spot = (height + 16 * (g // across), LANES * (g % across))
            out[spot[0] : spot[0] + 16, spot[1] : spot[1] + LANES] = ref[16 * at : 16 * at + 16, :]

    outs = [shape((height + below, width))]
    return call(body, outs, [vmem] * 3, [], 0, 1 << 20, "beside")(rows, mine, other)[0]


def turn_bias(row):
    at = lax.broadcasted_iota(jnp.int32, (16, LANES), 0) == lax.broadcasted_iota(jnp.int32, (16, LANES), 1)
    return jnp.broadcast_to(jnp.sum(jnp.where(at, row, 0.0), axis=1, keepdims=True), (16, LANES))


def unpack_small(heads, slots, height, rows, place, parts):
    count = len(parts)
    width = parts[0].shape[1]
    cut = width // count
    lanes = cut // LANES
    across = width // LANES
    inner = heads * LANES

    def body(place_ref, *refs):
        ins, outs, length, held = refs[:count], refs[count:-2], refs[-2], refs[-1]
        f = place_ref[0]
        for r, part in enumerate(ins):
            for k in range(2):
                layer = place_ref[1] if k == 0 else 1 - place_ref[1]
                for g in range(rows // 16):
                    at = k * (rows // 16) + g
                    top, left = height + 16 * (at // across), LANES * (at % across)
                    held[layer, f ^ r, 16 * g : 16 * g + 16, :] = part[top : top + 16, left : left + LANES].astype(wide)
        at = 2 * lanes + 1 + 2 * place_ref[1]
        found = held[place_ref[1], place_ref[2], pl.ds(at, 2), :]
        length[...] = jnp.broadcast_to(found[0:1] * 64.0 + found[1:2], length.shape).astype(jnp.int32)
        for layer in range(2):
            one, two, decay, bias, fixed = outs[5 * layer : 5 * layer + 5]
            for t in range(count):
                for b in range(lanes):
                    at = t * cut + b * LANES
                    one[0:1, at : at + LANES] = held[layer, t, b : b + 1, :]
                    two[0:1, at : at + LANES] = held[layer, t, lanes + b : lanes + b + 1, :]
                    group = held[layer, t, 16 * (1 + b) : 16 * (2 + b), :]
                    row = lax.broadcasted_iota(jnp.int32, (16, LANES), 0)
                    mine = [
                        jnp.sum(jnp.where(row == f * heads + h, group, 0.0), axis=0, keepdims=True) for h in range(heads)
                    ]
                    mine.append(jnp.zeros((16 - heads, LANES), wide))
                    decay[:, at : at + LANES] = jnp.concatenate(mine, axis=0).astype(half)
            bias[...] = turn_bias(held[layer, f, 2 * lanes : 2 * lanes + 1, :])
            for kind in range(2):
                source = kind * (count // 2) + f // 2
                for h in range(heads):
                    at = pl.multiple_of(16 * (1 + lanes + (f % 2) * heads + h), 16)
                    lane = kind * inner + h * LANES
                    fixed[:, lane : lane + LANES] = held[layer, source, pl.ds(at, slots), :].astype(half)

    outs = [
        shape((1, width), wide),
        shape((1, width), wide),
        shape((16, width)),
        shape((16, LANES), wide),
        shape((slots, 2 * inner)),
    ] * 2 + [shape((8, LANES), jnp.int32)]
    scratch = [pltpu.VMEM((2, count, rows, LANES), wide)]
    made = call(body, outs, [smem] + [vmem] * count, scratch, 0, 1 << 20, "unpack_small")(place, *parts)
    return [list(pair) for pair in zip(made[:5], made[5:10])], made[10][0, 0]


def join_forward(rounded, terms, residual, gain):
    dims = terms[0].shape

    def body(*refs):
        count = len(terms)
        residual_ref, refs_in = refs[count], refs[:count]
        total = residual_ref[...].astype(wide)
        for ref in refs_in:
            total = total + ref[...].astype(wide)
        if gain is None:
            refs[count + 1][...] = total.astype(half)
            return
        gain_ref, out, normed = refs[count + 1 :]
        if rounded:
            total = total.astype(half).astype(wide)
        out[...] = total.astype(out.dtype)
        scale = lax.rsqrt(jnp.mean(total * total, axis=1, keepdims=True) + epsilon)
        normed[...] = (total * scale * gain_ref[...]).astype(half)

    outs = [shape(dims, half if rounded else wide), shape(dims)]
    inputs = [*terms, residual, gain]
    if gain is None:
        outs, inputs = [shape(dims)], inputs[:-1]
    return call(body, outs, [vmem] * len(inputs), [], 0, dims[0] * dims[1] * 20, "join_forward")(*inputs)


def join_backward(terms, values, gain, onward):
    dims = terms[0].shape

    def body(*refs):
        count = len(terms)
        values_ref, gain_ref, onward_ref, out, rounded = refs[count:]
        grad = refs[0][...].astype(wide)
        for ref in refs[1:count]:
            grad = grad + ref[...].astype(wide)
        v = values_ref[...].astype(wide)
        scale = lax.rsqrt(jnp.mean(v * v, axis=1, keepdims=True) + epsilon)
        unit = v * scale
        scaled = grad * gain_ref[...]
        through = scale * (scaled - unit * jnp.mean(scaled * unit, axis=1, keepdims=True))
        total = onward_ref[...].astype(wide) + through
        out[...] = total
        rounded[...] = total.astype(half)

    outs = [shape(dims, wide), shape(dims)]
    inputs = [*terms, values, gain, onward]
    return call(body, outs, [vmem] * len(inputs), [], 0, dims[0] * dims[1] * 24, "join_backward")(*inputs)


SMALL = 16


def lane_half(source, target, which, count):
    for t in range(count):
        at = pl.multiple_of(t * 2 * LANES + which * LANES, LANES)
        target[:, t * LANES : (t + 1) * LANES] = source[:, pl.ds(at, LANES)]


STRIPS = 4


def strip_of(columns):
    return SMALL * -(-(columns + SMALL) // (SMALL * STRIPS))


def packer(packed):
    def put(at, value):
        packed[at : at + value.shape[0], :] = value.astype(half)

    return put


def strip_packer(packed, strip, chunk):
    def put(t, at, value):
        done = 0
        while done < value.shape[0]:
            k, row = divmod(at + done, strip)
            size = min(value.shape[0] - done, strip - row)
            where = k * chunk + t * strip + row
            packed[where : where + size, :] = value[done : done + size].astype(half)
            done += size

    return put


def small_rows(rows):
    found = jnp.concatenate(rows, axis=0)
    return jnp.concatenate([found, jnp.zeros((SMALL - found.shape[0], LANES), wide)], axis=0)


def grad_call(body, chunks, total, inputs, scratch, flops, name):
    outs = [shape((total, LANES))] + [shape((b - a, LANES)) for a, b in split_rows(total, chunks)]
    scratch = scratch + [pltpu.VMEM((total, LANES), half)]
    moved = sum(v.size * v.dtype.itemsize for v in inputs) + total * LANES * 4
    return call(body, outs, [smem] + [vmem] * (len(inputs) - 1), scratch, flops, moved, name)(*inputs)


def grad_feed(chunks, count, place, normed, g_gates, active, g_out, g_gain):
    total_rows, width = normed.shape
    columns, hidden = g_gates.shape[1], active.shape[1]
    tiles = columns // LANES
    strip = strip_of(columns)
    chunk = count * strip + hidden
    side = width // 2

    def body(place_ref, normed_ref, gates_ref, active_ref, g_out_ref, gain_ref, *refs):
        sent, outs, left, packed = refs[0], refs[1:-2], refs[-2], refs[-1]
        for turn in range(2):
            which = 1 - place_ref[1] if turn == 0 else place_ref[1]
            packed_here = sent if turn == 0 else packed
            put, put_row = packer(packed_here), strip_packer(packed_here, strip, chunk)
            lane_half(normed_ref, left, which, count)
            turned = left[...].T
            for at in range(0, columns, 2 * LANES):
                size = min(2 * LANES, columns - at)
                tile = mm(turned, gates_ref[:, at : at + size])
                for t in range(count):
                    for c in range(size // LANES):
                        put_row(t, at + c * LANES, tile[t * LANES : (t + 1) * LANES, c * LANES : (c + 1) * LANES])
            for t in range(count):
                at = pl.multiple_of(t * 2 * LANES + which * LANES, LANES)
                rest = STRIPS * strip - columns - SMALL
                put_row(t, columns, small_rows([gain_ref[0:1, pl.ds(at, LANES)]]))
                put_row(t, columns + SMALL, jnp.zeros((rest, LANES), wide))
            active_t = active_ref[...].T
            for c in range(0, side // LANES, 2):
                at = pl.multiple_of(which * side + c * LANES, LANES)
                tile = mm(active_t, g_out_ref[:, pl.ds(at, 2 * LANES)])
                put(c * chunk + count * strip, tile[:, :LANES])
                put((c + 1) * chunk + count * strip, tile[:, LANES:])
        chunk_out(packed, outs)

    inputs = [place, normed, g_gates, active, g_out, g_gain]
    scratch = [pltpu.VMEM((total_rows, side), half)]
    flops = total_rows * width * (columns + hidden)
    return grad_call(body, chunks, STRIPS * chunk, inputs, scratch, flops, "grad_feed")


def grad_mix(chunks, total, count, place, normed, g_projected, combined, branch, g_logits, g_gain, g_fixed):
    total_rows, width = normed.shape
    columns, inner = g_projected.shape[1], combined.shape[1]
    heads = inner // LANES
    slots = g_fixed.shape[0]
    block = columns + SMALL + slots
    side = width // 2

    def body(place_ref, normed_ref, proj_ref, comb_ref, branch_ref, logits_ref, gain_ref, fixed_ref, *refs):
        sent, outs, left, packed = refs[0], refs[1:-2], refs[-2], refs[-1]
        for turn in range(2):
            which = 1 - place_ref[1] if turn == 0 else place_ref[1]
            put = packer(sent if turn == 0 else packed)
            lane_half(normed_ref, left, which, count)
            turned = left[...].T
            for at in range(0, columns, 2 * LANES):
                tile = mm(turned, proj_ref[:, at : at + 2 * LANES])
                for t in range(count):
                    for c in range(2):
                        put(t * block + at + c * LANES, tile[t * LANES : (t + 1) * LANES, c * LANES : (c + 1) * LANES])
            logits = logits_ref[...]
            decay = sum(mm(piece, left[...]) for piece in three_way(logits)[:2])
            near = pl.multiple_of(which * LANES, LANES)
            for t in range(count):
                at = pl.multiple_of(t * 2 * LANES + which * LANES, LANES)
                rows = [decay[0:heads, t * LANES : (t + 1) * LANES], gain_ref[0:1, pl.ds(at, LANES)]]
                put(t * block + columns, small_rows(rows))
                keys_here = (place_ref[0] // 2 == t).astype(wide)
                values_here = (place_ref[0] // 2 + 2 == t).astype(wide)
                fixed = fixed_ref[:, pl.ds(near, LANES)] * keys_here
                fixed = fixed + fixed_ref[:, pl.ds(pl.multiple_of(inner + near, LANES), LANES)] * values_here
                put(t * block + columns + SMALL, fixed)
            comb_t = comb_ref[:, pl.ds(near, LANES)].T
            for c in range(0, width // LANES, 2):
                tile = mm(comb_t, branch_ref[:, c * LANES : (c + 2) * LANES])
                put(count * block + c * LANES, tile[:, :LANES])
                put(count * block + (c + 1) * LANES, tile[:, LANES:])
            put(count * block + width, jnp.broadcast_to(jnp.sum(logits, axis=1, keepdims=True), (SMALL, LANES)))
            (sent if turn == 0 else packed)[count * block + width + SMALL :, :] = jnp.zeros(
                (total - count * block - width - SMALL, LANES), half
            )
        chunk_out(packed, outs)

    inputs = [place, normed, g_projected, combined, branch, g_logits, g_gain, g_fixed]
    scratch = [pltpu.VMEM((total_rows, side), half)]
    flops = total_rows * width * (columns + inner)
    return grad_call(body, chunks, total, inputs, scratch, flops, "grad_mix")


def split_rows(total, chunks):
    units = total // SMALL
    edges = [SMALL * (units * k // chunks) for k in range(chunks)] + [total]
    return list(zip(edges[:-1], edges[1:]))


def chunk_out(whole, outs):
    at = 0
    for out in outs:
        out[...] = whole[at : at + out.shape[0], :]
        at += out.shape[0]


def spread(count, block, place, chunks, add=False):
    total = sum(chunk.shape[0] for chunk, _ in chunks)

    def body(place_ref, *refs):
        ins, outs, whole = refs[: 2 * len(chunks)], refs[2 * len(chunks) : -1], refs[-1]
        at = 0
        if add:
            for one, two in zip(ins[0::2], ins[1::2]):
                whole[at : at + one.shape[0], :] = (one[...].astype(wide) + two[...].astype(wide)).astype(half)
                at += one.shape[0]
        for inner in range(0 if add else 2):

            @pl.when(place_ref[3] == inner)
            def _(inner=inner):
                at = 0
                for chunk in ins[1 - inner :: 2]:
                    whole[at : at + chunk.shape[0], :] = chunk[...]
                    at += chunk.shape[0]

        take_rows(whole, outs[:count], place_ref)
        outs[count][...] = whole[count * block :, :]

    outs = [shape((block, LANES))] * count + [shape((total - count * block, LANES))]
    scratch = [pltpu.VMEM((total, LANES), half)]
    flat = [piece for pair in chunks for piece in pair]
    return call(body, outs, [smem] + [vmem] * len(flat), scratch, 0, total * 768, "spread")(place, *flat)


def spread_strips(count, strip, place, chunks):
    chunk = chunks[0][0].shape[0]
    own = chunk - count * strip
    many = len(chunks)

    def body(place_ref, *refs):
        ins, outs = refs[: 2 * many], refs[2 * many :]
        for inner in range(2):

            @pl.when(place_ref[3] == inner)
            def _(inner=inner):
                for k, ref in enumerate(ins[1 - inner :: 2]):
                    for r in range(count):
                        at = pl.multiple_of((place_ref[0] ^ r) * strip, SMALL)
                        outs[r][k * strip : (k + 1) * strip, :] = ref[pl.ds(at, strip), :]
                    outs[count][k * own : (k + 1) * own, :] = ref[count * strip :, :]

    outs = [shape((many * strip, LANES))] * count + [shape((many * own, LANES))]
    flat = [piece for pair in chunks for piece in pair]
    return call(body, outs, [smem] + [vmem] * len(flat), [], 0, many * chunk * 768, "spread")(place, *flat)


def collect_feed(columns, place, sets):
    count = len(sets[0][0])
    strip = strip_of(columns)
    own = sum(local.shape[0] for _, local in sets)
    total = count * columns + SMALL + own
    flat = [piece for parts, local in sets for piece in (*parts, local)]

    def body(place_ref, *refs):
        ins, whole = refs[: len(flat)], refs[-1]
        first, below = 0, count * columns + SMALL
        small = jnp.zeros((SMALL, LANES), wide)
        for number, (parts, local) in enumerate(sets):
            here = ins[number * (count + 1) : (number + 1) * (count + 1)]
            many = parts[0].shape[0] // strip
            for k in range(many):
                row = (first + k) * strip
                size = min(strip, columns - row)
                for r in range(count):
                    at = pl.multiple_of((place_ref[0] ^ r) * columns + row, SMALL)
                    whole[pl.ds(at, size), :] = here[r][k * strip : k * strip + size, :]
                    if size < strip:
                        small = small + here[r][k * strip + size : k * strip + size + SMALL, :].astype(wide)
            first += many
            whole[below : below + local.shape[0], :] = here[count][...]
            below += local.shape[0]
        whole[count * columns : count * columns + SMALL, :] = small.astype(half)

    outs = [shape((total, LANES))]
    return call(body, outs, [smem] + [vmem] * len(flat), [], 0, total * 512, "collect_feed")(place, *flat)


def collect_mix(chunks, heads, total, place, parts, local):
    count = len(parts)
    slots = parts[0].shape[0] % (3 * heads * LANES) - SMALL
    columns = parts[0].shape[0] - SMALL - slots
    filled = count * columns + SMALL + 2 * slots + local.shape[0]

    def body(place_ref, *refs):
        parts_in, local_ref, outs, whole, few = refs[:count], refs[count], refs[count + 1 : -2], refs[-2], refs[-1]
        for r, part in enumerate(parts_in):
            source = place_ref[0] ^ r
            at = pl.multiple_of(source * columns, columns)
            whole[pl.ds(at, columns), :] = part[0:columns, :]
            few[pl.ds(source, 1)] = part[columns:, :].astype(wide)[None]
        base = count * columns
        decay = [few[t, 0:heads, :] for t in range(count)]
        gain = sum(few[t, heads : heads + 1, :] for t in range(count))
        whole[base : base + SMALL, :] = small_rows(decay + [gain]).astype(half)
        near = (place_ref[0] % 2) * 2
        for k in range(2):
            at = base + SMALL + k * slots
            whole[at : at + slots, :] = few[near + k, SMALL:, :].astype(half)
        whole[base + SMALL + 2 * slots : filled, :] = local_ref[...]
        whole[filled:, :] = jnp.zeros((total - filled, LANES), half)
        chunk_out(whole, outs)

    outs = [shape((b - a, LANES)) for a, b in split_rows(total, chunks)]
    scratch = [pltpu.VMEM((total, LANES), half), pltpu.VMEM((count, SMALL + slots, LANES), wide)]
    return call(body, outs, [smem] + [vmem] * (count + 1), scratch, 0, total * 512, "collect_mix")(place, *parts, local)


def gather_halves(place_ref, ins, halves, sems, counts):
    first = 0
    for layer, many in enumerate(counts):
        pieces = [ins[first : first + many], ins[first + many : first + 2 * many]]
        first += 2 * many

        @pl.when(place_ref[1] == layer)
        def _(pieces=pieces, many=many):
            handles = []
            for side in range(2):
                spot = place_ref[1] if side == 0 else 1 - place_ref[1]
                at = 0
                for c, piece in enumerate(pieces[side]):
                    where = halves.at[spot, pl.ds(at, piece.shape[0])]
                    handles.append(pltpu.make_async_copy(piece, where, sems.at[side * many + c]))
                    handles[-1].start()
                    at += piece.shape[0]
            finish(handles)


def unpack(body, totals, out_shape, place, name):
    counts = [len(own) for own, _ in totals]
    rows = sum(chunk.shape[0] for chunk in totals[0][0])
    inputs = [piece for layer in totals for side in layer for piece in side]

    def whole_body(place_ref, *refs):
        ins, outs, halves, sems = refs[: len(inputs)], refs[len(inputs) : -2], refs[-2], refs[-1]
        gather_halves(place_ref, ins, halves, sems, counts)
        body(place_ref, halves, *outs)

    scratch = [pltpu.VMEM((2, rows, LANES), half), pltpu.SemaphoreType.DMA((2 * max(counts),))]
    moved = sum(o.size * 4 for o in out_shape) + 4 * rows * LANES
    return call(whole_body, out_shape, [smem] + [anywhere] * len(inputs), scratch, 0, moved, name)(place, *inputs)


def unpack_feed(count, columns, hidden, width, totals, place):
    part = width // count
    side = width // 2
    counts = [len(own) for own, _ in totals]
    total = sum(chunk.shape[0] for chunk in totals[0][0])
    inputs = [piece for layer in totals for half_side in layer for piece in half_side]
    steps = 4
    span = count * columns // steps
    tiles = span // LANES

    def body(place_ref, *refs):
        ins, (gate_up, down, gain), halves, sems = refs[: len(inputs)], refs[len(inputs) : -2], refs[-2], refs[-1]
        step = pl.program_id(0)

        @pl.when(step == 0)
        def _():
            gather_halves(place_ref, ins, halves, sems, counts)
            base = count * columns
            for h in range(2):
                gain[0:1, h * LANES : (h + 1) * LANES] = halves[h, base : base + SMALL, :].astype(wide)[0:1]

        low = lax.broadcasted_iota(jnp.int32, (LANES, LANES), 1) < PAIR
        for is_up in range(2):

            @pl.when(step // 2 == is_up)
            def _(is_up=is_up):
                for h in range(2):
                    for m in range(tiles):
                        at = pl.multiple_of((step % 2) * 2 * span + 2 * m * LANES, LANES)
                        even = halves[h, pl.ds(at, LANES), :].astype(wide)
                        odd = halves[h, pl.ds(at + LANES, LANES), :].astype(wide)
                        if is_up:
                            value = jnp.where(low, pltpu.roll(even, PAIR, 1), odd)
                        else:
                            value = jnp.where(low, even, pltpu.roll(odd, PAIR, 1))
                        gate_up[h * LANES : (h + 1) * LANES, m * LANES : (m + 1) * LANES] = value

        base = count * columns + SMALL
        for c in range(2):
            at = pl.multiple_of(base + ((step % 2) * 2 + c) * hidden, SMALL)
            down[:, c * LANES : (c + 1) * LANES] = halves[step // 2, pl.ds(at, hidden), :].astype(wide)

    outs = [shape((part, count * columns), wide), shape((hidden, width), wide), shape((1, part), wide)]
    moved = sum(o.size * 4 for o in outs) + 4 * total * LANES
    return pl.pallas_call(
        body,
        grid=(steps,),
        out_shape=outs,
        in_specs=[smem] + [anywhere] * len(inputs),
        out_specs=[
            pl.BlockSpec((part, span), lambda i: (0, i)),
            pl.BlockSpec((hidden, width // steps), lambda i: (0, i)),
            pl.BlockSpec((1, part), lambda i: (0, 0)),
        ],
        scratch_shapes=[pltpu.VMEM((2, total, LANES), half), pltpu.SemaphoreType.DMA((2 * max(counts),))],
        compiler_params=pltpu.CompilerParams(vmem_limit_bytes=16 * 1024 * 1024),
        cost_estimate=pl.CostEstimate(flops=0, bytes_accessed=moved, transcendentals=0),
        name="unpack_feed",
    )(place, *inputs)


def unpack_mix(count, heads, slots, width, totals, place):
    part = width // count
    inner = heads * LANES
    columns = 3 * inner

    def body(place_ref, halves, qkv, out, gain, decay, bias, fixed):
        for h in range(2):
            rows = slice(h * LANES, (h + 1) * LANES)
            for t in range(count):
                for kind in range(3):
                    for head in range(heads):
                        source = t * columns + kind * inner + head * LANES
                        at = kind * count * inner + t * inner + head * LANES
                        qkv[rows, at : at + LANES] = halves[h, source : source + LANES, :].astype(wide)
            base = count * columns
            small = halves[h, base : base + SMALL, :].astype(wide)
            padded = jnp.concatenate([small, jnp.zeros((LANES - SMALL, LANES), wide)], axis=0).T
            decay[rows, :] = padded[:, 0 : count * heads]
            gain[0:1, rows] = small[count * heads : count * heads + 1]
            for k in range(2):
                at = base + SMALL + k * slots
                lanes = slice(k * inner + h * LANES, k * inner + (h + 1) * LANES)
                fixed[:, lanes] = halves[h, at : at + slots, :].astype(wide)
            base += SMALL + 2 * slots
            for c in range(width // LANES):
                source = base + c * LANES
                out[rows, c * LANES : (c + 1) * LANES] = halves[h, source : source + LANES, :].astype(wide)
            if h == 0:
                found = halves[h, base + width : base + width + SMALL, :].astype(wide)
                bias[...] = jnp.concatenate([found[k : k + 1, 0:1] for k in range(heads)], axis=1)

    outs = [
        shape((part, count * columns), wide),
        shape((inner, width), wide),
        shape((1, part), wide),
        shape((part, count * heads), wide),
        shape((1, heads), wide),
        shape((slots, 2 * inner), wide),
    ]
    return unpack(body, totals, outs, place, "unpack_mix")


def tie(*values):
    return lax.optimization_barrier(values)


def exchange(value, axis, distance):
    count = lax.axis_size(axis)
    return lax.ppermute(value, axis, [(i, i ^ distance) for i in range(count)])


def gather_parts(block, axis):
    count = lax.axis_size(axis)
    far = tie(*(exchange(block, axis, r) for r in reversed(range(1, count))))
    return [block, *reversed(far)]


def trade_terms(blocks, axis):
    found = trade_parts(blocks, axis)
    return found


def trade_parts(blocks, axis):
    far = {r: exchange(blocks[r], axis, r) for r in reversed(range(1, len(blocks)))}
    return [blocks[0]] + [far[r] for r in range(1, len(blocks))]


def plane_device(
    tokens,
    lengths,
    cotangent,
    norm_one,
    qkv_weight,
    decay_weight,
    decay_bias,
    persistent,
    out_weight,
    norm_two,
    gate_up,
    down_weight,
):
    ctx_count, count = lax.axis_size("ctx"), lax.axis_size("fsdp")
    section, ctx, fsdp = (lax.axis_index(a) for a in ("section", "ctx", "fsdp"))
    rows, width = tokens.shape[2:]
    heads = decay_bias.shape[1]
    size = width // (heads * count)
    inner = heads * size

    def own_batch(value):
        return lax.dynamic_index_in_dim(value, section, 0, False)[0]

    pairs = []
    for s in range(2):
        flip = s * (count - 1)
        for c in range(ctx_count):
            for f in range(count):
                here, there = c * count + f, (f ^ flip) * count + (c ^ flip)
                pairs.append((s * ctx_count * count + here, s * ctx_count * count + there))

    def turn_plane(value):
        return lax.ppermute(value, ("section", "ctx", "fsdp"), pairs)

    def swap(value):
        return exchange(value, "section", 1)

    slots = persistent.shape[1]
    flip = section * (count - 1)
    spot = jnp.stack([fsdp, section, ctx ^ flip]).astype(jnp.int32)
    x_own, qkv_shard = tie(own_batch(tokens), qkv_weight[0])
    x_in = turn_plane(x_own)
    qkv_packed = pack_heads(count, qkv_shard, spot)
    qkv_parts = trade_parts(qkv_packed, "fsdp")
    small = pack_small(norm_one, norm_two, decay_weight[0], decay_bias, persistent[0], lengths[:, 0, 0])
    x_parts = gather_parts(beside(x_in, small, swap(small)), "fsdp")
    (gains_one, gains_two, decays, biases, fixeds), length = unpack_small(
        heads, slots, rows, small.shape[0], spot, x_parts
    )
    gu_packed = pack_gates(count, gate_up[0], spot)
    qkv_parts, gu_packed, _, g_own = tie(qkv_parts, gu_packed, x_parts, own_batch(cotangent))
    g_in = turn_plane(g_own)
    gu_parts = trade_parts(gu_packed, "fsdp")
    qkv_mine = assemble(spot, qkv_parts)
    qkv_other = swap(qkv_mine)
    out_mine = out_weight[0]
    out_other = swap(out_mine)
    mix_weights = (qkv_mine, qkv_other, out_mine, out_other)
    down_mine = down_weight[0]
    down_other = swap(down_mine)
    length, down_other = tie(length, down_other)
    place = jnp.stack([fsdp, section, length, (ctx == 1) | (ctx == 2)]).astype(jnp.int32)
    seat = jnp.stack([fsdp ^ flip, section, length]).astype(jnp.int32)
    hidden = down_mine.shape[0]
    columns = gu_packed[0].shape[1]

    def mix_first_half(layer, parts):
        *terms, combined, seen, projected, logits = mix_forward(
            layer, heads, size, seat, parts, rows, gains_one[layer], mix_weights, decays[layer], biases[layer], fixeds[layer]
        )
        return terms, (seen, projected, logits, combined)

    def mix_second_half(layer, terms, x):
        middle, normed_two = join_forward(False, trade_terms(terms, "fsdp"), x, gains_two[layer])
        return middle, gather_parts(normed_two, "fsdp")

    def feed_step(layer, parts, saved):
        *terms, g_rows, g_gates, active, g_gain = feed_backward(
            layer, seat, parts, [saved[6]], gains_two[layer], feed_weights, False
        )
        return terms, (saved[6], g_gates, active, g_rows, g_gain)

    def mix_step(layer, parts, saved):
        x, seen, projected, logits, combined, middle, seen_two = saved
        *terms, branch, g_projected, g_logits, g_fixed, g_gain = mix_backward(
            layer, heads, size, seat, parts, mix_weights, decays[layer], fixeds[layer], projected, logits, seen, gains_one[layer]
        )
        return terms, (seen, g_projected, combined, branch, g_logits, g_gain, g_fixed)

    inside = (ctx == 1) | (ctx == 2)
    line = {"queue": [], "inward": None, "across": None, "total": None, "flight": (None, None), "sums": []}

    def begin():
        own = line["queue"].pop(0) if line["queue"] else None
        total = line["total"]
        if own is not None and total is not None:
            sent = jnp.where(inside, total, own)
            route = [(0, 1), (3, 2), (1, 0), (2, 3)]
        else:
            sent = own if total is None else total
            route = [(0, 1), (3, 2)] if total is None else [(1, 0), (2, 3)]
        pair = line["across"]
        line["sent"] = (sent, pair, own, total is not None)
        return [v for v in (sent, pair) if v is not None], route

    def go(values, route):
        values = list(values)
        sent, pair, own, closing = line["sent"]
        sent = values.pop(0) if sent is not None else None
        pair = values.pop(0) if pair is not None else None
        line["sent"] = (sent, pair, own, closing)
        flight = [None, None]
        if sent is not None:
            flight[0] = lax.ppermute(sent, "ctx", route)
        if pair is not None:
            flight[1] = lax.ppermute(pair, "ctx", [(1, 2), (2, 1)])
        line["flight"] = flight

    def plus(a, b):
        return (a.astype(wide) + b.astype(wide)).astype(half)

    def step(*held, more=None):
        landed, crossed = line["flight"]
        waiting = [v for v in (landed, crossed) if v is not None]
        waiting, held = tie(waiting, held)
        if landed is not None:
            landed = waiting.pop(0)
        if crossed is not None:
            crossed = waiting.pop(0)
        sent, pair, own, closing = line.get("sent", (None, None, None, False))
        line["total"] = None if pair is None else plus(pair, crossed)
        line["across"] = None if own is None else plus(own, landed)
        if closing:
            line["sums"].append((sent, landed))
        if more is not None:
            line["queue"].extend(more(*held))
        ready, route = begin()
        held, ready = tie(held, ready)
        go(ready, route)
        return held

    def taken(number, skip=0):
        found = line["sums"][skip : skip + number]
        del line["sums"][skip : skip + number]
        return found

    terms, kept = mix_first_half(0, x_parts)
    terms, gu_parts[1], g_in = tie(terms, gu_parts[1], g_in)
    terms, gu_parts = tie(trade_terms(terms, "fsdp"), gu_parts)
    gu_mine = assemble(spot, gu_parts)
    feed_weights = (gu_mine, swap(gu_mine), down_mine, down_other)
    middle, normed_two = join_forward(False, terms, x_in, gains_two[0])
    parts = gather_parts(normed_two, "fsdp")
    *terms, seen_two = feed_forward(0, seat, parts, feed_weights)
    terms = trade_terms(terms, "fsdp")
    saved_first = (x_in, *kept, middle, seen_two)
    between = join_forward(True, terms, middle, None)[0]
    terms, kept = mix_first_half(1, gather_parts(between, "fsdp"))
    terms, g_three, g_two, g_one = tie(terms, *(exchange(g_in, "fsdp", r) for r in (3, 2, 1)))
    middle, parts = mix_second_half(1, terms, between)
    made = feed_backward(1, seat, [g_in, g_one, g_two, g_three], parts, gains_two[1], feed_weights, True)
    terms, (g_rows, g_gates, active, g_gain), terms_out, seen_two = made[:4], made[4:8], made[8:12], made[12]
    feed = (seen_two, g_gates, active, g_rows, g_gain)
    saved_second = (between, *kept, middle, seen_two)

    def to_owner(layer, chunks):
        return [lax.ppermute(chunk, "section", [(1 - layer, layer)]) for chunk in chunks]

    def trade(block, chunks, add=False):
        *blocks, local = spread(count, block, place, chunks, add)
        return trade_parts(blocks, "fsdp"), local

    def trade_strips(chunks):
        *blocks, local = spread_strips(count, strip, place, chunks)
        return trade_parts(blocks, "fsdp"), local

    strip = strip_of(columns)
    pad = 2 * (count * strip + hidden)
    mix_block = 3 * inner + SMALL + slots

    def summed(own, received):
        at, chunks = 0, []
        for chunk in own:
            chunks.append(plus(chunk, received[at : at + chunk.shape[0]]))
            at += chunk.shape[0]
        return chunks

    sent, *own = grad_feed(4, count, place, *feed)
    terms, sent = tie(trade_terms(terms, "fsdp"), sent)
    g_middle, g_branch = join_backward(terms, saved_second[5], gains_two[1], g_in)
    parts = gather_parts(g_branch, "fsdp")
    parts, received = tie(parts, swap(sent))
    (parts,) = step(parts, more=lambda _: summed(own, received))
    terms, mix = mix_step(1, parts, saved_second)
    terms, terms_out = step(terms, trade_terms(terms_out, "fsdp"))
    out = join_forward(True, terms_out, saved_second[5], None)[0]
    sent, *own = grad_mix(2, pad, count, place, *mix)
    terms, sent = step(trade_terms(terms, "fsdp"), sent)
    g_middle, g_branch = join_backward(terms, between, gains_one[1], g_middle)
    parts, sent = step(gather_parts(g_branch, "fsdp"), sent)
    terms, feed = feed_step(0, parts, saved_first)
    terms, _ = step(terms, swap(sent), more=lambda _, received: summed(own, received))
    sent, *own = grad_feed(4, count, place, *feed)
    terms, sent = step(trade_terms(terms, "fsdp"), sent)
    received = swap(sent)
    g_middle, g_branch = join_backward(terms, saved_first[5], gains_two[0], g_branch)
    g_branch, received = tie(g_branch, received)
    (parts,) = step(gather_parts(g_branch, "fsdp"), more=lambda _: summed(own, received))
    f1 = trade_strips(taken(4))
    terms, mix = mix_step(0, parts, saved_first)
    terms, f1 = step(terms, f1)
    feed_second = collect_feed(columns, place, [f1])
    sent, *own = grad_mix(1, pad, count, place, *mix)
    (terms,) = step(trade_terms(terms, "fsdp"))
    g_input = join_backward(terms, x_in, gains_one[0], g_middle)[1]
    received = swap(sent)
    g_input, received, feed_second = step(g_input, received, feed_second)
    m0 = trade(mix_block, [(own[0], received)], add=True)
    (m0,) = step(m0, more=lambda pieces: collect_mix(2, heads, pad, place, *pieces))
    f0 = trade_strips(taken(2, 2))
    (f0,) = step(f0)
    m1 = trade(mix_block, taken(2))
    (m1,) = step(m1)
    feed_second_other = to_owner(1, feed_second)
    f0_last = trade_strips(taken(2))
    mix_second = collect_mix(1, heads, pad, place, *m1)
    f0_last, mix_second, g_input = step(f0_last, mix_second, g_input)
    feed_first = collect_feed(columns, place, [f0, f0_last])
    feed_first_other = to_owner(0, feed_first)
    m0_first = [jnp.where(inside, *pair) for pair in taken(1)]
    m0_first_other = to_owner(0, m0_first)
    mix_second_other = to_owner(1, mix_second)
    feed_first_other, feed_second_other, m0_first_other, mix_second_other, g_input, out = step(
        feed_first_other, feed_second_other, m0_first_other, mix_second_other, g_input, out
    )
    m0_last = [jnp.where(inside, *pair) for pair in taken(1)]
    m0_last_other = to_owner(0, m0_last)
    turned_both = turn_plane(jnp.stack([out, g_input]))
    grad_gate_up, grad_down, grad_norm_two = unpack_feed(
        count,
        columns,
        hidden,
        width,
        ((feed_first, feed_first_other), (feed_second, feed_second_other)),
        place,
    )
    m0_last_other, grad_down = tie(m0_last_other, grad_down)
    grad_qkv, grad_out, grad_norm_one, grad_decay, grad_bias, grad_fixed = unpack_mix(
        count,
        heads,
        slots,
        width,
        ((m0_first + m0_last, m0_first_other + m0_last_other), (mix_second, mix_second_other)),
        place,
    )
    turned_both, grad_bias = tie(turned_both, grad_bias)
    return (
        turned_both[0][None, None],
        turned_both[1][None, None],
        grad_norm_one,
        grad_qkv[None],
        grad_decay[None],
        grad_bias,
        grad_fixed[None],
        grad_out[None],
        grad_norm_two,
        grad_gate_up[None],
        grad_down[None],
    )


def scatter_sum(blocks, axis):
    total = blocks[0].astype(wide)
    for r in range(1, len(blocks)):
        total = total + exchange(blocks[r].astype(half), axis, r).astype(wide)
    return total


def in_order(parts, index, dim):
    count = len(parts)
    shape = list(parts[0].shape)
    size = shape[dim]
    shape[dim] = size * count
    whole = jnp.zeros(shape, parts[0].dtype)
    for r, part in enumerate(parts):
        whole = lax.dynamic_update_slice_in_dim(whole, part, (index ^ r) * size, dim)
    return whole


def columns_here(shard, kinds, axis):
    count, index = lax.axis_size(axis), lax.axis_index(axis)
    rows, width = shard.shape[0], shard.shape[1] // (kinds * count)
    blocks = shard.reshape(rows, kinds, count, width)
    parts = []
    for r in range(count):
        block = lax.dynamic_index_in_dim(blocks, index ^ r, 2, False).reshape(rows, kinds * width)
        parts.append(block if r == 0 else exchange(block, axis, r))
    return in_order(parts, index, 0)


def rows_here(columns, kinds, axis):
    count, index = lax.axis_size(axis), lax.axis_index(axis)
    rows, width = columns.shape[0] // count, columns.shape[1] // kinds
    parts = []
    for r in range(count):
        block = lax.dynamic_slice_in_dim(columns, (index ^ r) * rows, rows, 0)
        block = block if r == 0 else exchange(block, axis, r)
        parts.append(block.reshape(rows, kinds, 1, width))
    return in_order(parts, index, 2).reshape(rows, kinds * count * width)


def line_sum(value, axis):
    count, index = lax.axis_size(axis), lax.axis_index(axis)
    if count != 4:
        return lax.psum(value, axis)

    def plus(a, b):
        return (a.astype(wide) + b.astype(wide)).astype(value.dtype)

    pair = plus(value, lax.ppermute(value, axis, [(0, 1), (3, 2)]))
    total = plus(pair, lax.ppermute(pair, axis, [(1, 2), (2, 1)]))
    outer = lax.ppermute(total, axis, [(1, 0), (2, 3)])
    return jnp.where((index == 0) | (index == 3), outer, total)


def dot(a, b, contract=(1, 0)):
    return lax.dot_general(a, b, (((contract[0],), (contract[1],)), ((), ())), preferred_element_type=wide)


def normalise(values, gain):
    scale = lax.rsqrt(jnp.mean(values * values, axis=-1, keepdims=True) + epsilon)
    return (values * scale * gain).astype(half)


def normalise_back(values, gain, grad):
    scale = lax.rsqrt(jnp.mean(values * values, axis=-1, keepdims=True) + epsilon)
    unit = values * scale
    grad_gain = jnp.sum(grad * unit, axis=0)
    scaled = grad * gain
    return scale * (scaled - unit * jnp.mean(scaled * unit, axis=-1, keepdims=True)), grad_gain


def heads_first(rows, size):
    return rows.reshape(rows.shape[0], rows.shape[1] // size, size).transpose(1, 0, 2)


def rows_first(heads):
    return heads.transpose(1, 0, 2).reshape(heads.shape[1], heads.shape[0] * heads.shape[2])


def batched(a, b, contract):
    return lax.dot_general(a, b, (((contract[0],), (contract[1],)), ((0,), (0,))), preferred_element_type=wide)


def cumulative(values, positions):
    earlier = (positions[None, :] <= positions[:, None]).astype(wide)
    return jnp.dot(earlier, values, precision=lax.Precision.HIGHEST)


def mixer_parts(projected, logits, fixed, length, positions, size):
    width = projected.shape[1] // 3
    q, k, v = (heads_first(projected[:, i * width : (i + 1) * width], size) for i in range(3))
    fixed_k, fixed_v = (heads_first(fixed[:, i * width : (i + 1) * width], size) for i in range(2))
    scale = size ** (-0.5)
    documents = positions >= length
    starts = (positions == 0) | (positions == length)
    allowed = ((positions[None, :] <= positions[:, None]) & (documents[:, None] == documents[None, :]))[None]
    log_keep = jax.nn.log_sigmoid(logits)
    total_log = cumulative(log_keep, positions).T
    keep = jnp.where(starts[:, None], 0.0, jax.nn.sigmoid(logits)).T
    lose = jnp.where(starts[:, None], 1.0, jax.nn.sigmoid(-logits)).T
    inflow = jnp.sqrt(lose * (1.0 + keep))
    scores = batched(q, k, (2, 2)) * scale
    fixed_scores = batched(q, fixed_k, (2, 2)) * scale
    masked = jnp.where(allowed, scores, negative)
    top = jnp.maximum(jnp.max(masked, axis=2), jnp.max(fixed_scores, axis=2))[:, :, None]
    weights, fixed_weights = jnp.exp(masked - top), jnp.exp(fixed_scores - top)
    mass = 1.0 / (jnp.sum(weights, axis=2) + jnp.sum(fixed_weights, axis=2))[:, :, None]
    weights, fixed_weights = weights * mass, fixed_weights * mass
    fall = jnp.exp(jnp.where(allowed, total_log[:, :, None] - total_log[:, None, :], negative))
    reach = scores * fall
    both = (weights + reach * inflow[:, None, :]).astype(half)
    return q, k, v, fixed_k, fixed_v, weights, fixed_weights, fall, reach, both, keep, lose, inflow


def mixer(projected, logits, fixed, length, positions, size):
    parts = mixer_parts(projected, logits, fixed, length, positions, size)
    q, k, v, fixed_k, fixed_v, weights, fixed_weights, fall, reach, both, keep, lose, inflow = parts
    mixed = batched(both, v, (2, 1)) + batched(fixed_weights.astype(half), fixed_v, (2, 1))
    return rows_first(mixed.astype(half))


def mixer_back(projected, logits, fixed, length, positions, size, grad):
    parts = mixer_parts(projected, logits, fixed, length, positions, size)
    q, k, v, fixed_k, fixed_v, weights, fixed_weights, fall, reach, both, keep, lose, inflow = parts
    scale = size ** (-0.5)
    grad = heads_first(grad, size)
    grad_both = batched(grad, v, (2, 2))
    grad_fixed = batched(grad, fixed_v, (2, 2))
    delta = (jnp.sum(weights * grad_both, axis=2) + jnp.sum(fixed_weights * grad_fixed, axis=2))[:, :, None]
    grad_scores = (weights * (grad_both - delta) + grad_both * fall * inflow[:, None, :]).astype(half)
    grad_fixed_scores = (fixed_weights * (grad_fixed - delta)).astype(half)
    grad_q = (batched(grad_scores, k, (2, 1)) + batched(grad_fixed_scores, fixed_k, (2, 1))) * scale
    grad_k = batched(grad_scores, q, (1, 1)) * scale
    grad_v = batched(both, grad, (1, 1))
    grad_fixed_k = batched(grad_fixed_scores, q, (1, 1)) * scale
    grad_fixed_v = batched(fixed_weights.astype(half), grad, (1, 1))
    pull = grad_both * reach
    grad_inflow = jnp.sum(pull, axis=1)
    grad_total = jnp.sum(pull * inflow[:, None, :], axis=2) - inflow * grad_inflow
    later = (positions[None, :] >= positions[:, None]).astype(wide)
    grad_log = jnp.dot(grad_total, later.T, precision=lax.Precision.HIGHEST)
    lose_all = jax.nn.sigmoid(-logits).T
    grad_logits = grad_log * lose_all - grad_inflow * keep * keep * lose / inflow
    grad_projected = jnp.concatenate([rows_first(grad_q), rows_first(grad_k), rows_first(grad_v)], axis=1)
    grad_persistent = jnp.concatenate([rows_first(grad_fixed_k), rows_first(grad_fixed_v)], axis=1)
    return grad_projected.astype(half), grad_logits.T, grad_persistent


def general_device(
    tokens,
    lengths,
    cotangent,
    norm_one,
    qkv_weight,
    decay_weight,
    decay_bias,
    persistent,
    out_weight,
    norm_two,
    gate_up,
    down_weight,
):
    sections, ctx_count, fsdp_count = (lax.axis_size(a) for a in ("section", "ctx", "fsdp"))
    section, ctx, fsdp = (lax.axis_index(a) for a in ("section", "ctx", "fsdp"))
    spread = ctx_count // fsdp_count
    rows, width = tokens.shape[2:]
    heads_here = decay_bias.shape[1]
    size = width // (heads_here * fsdp_count)
    inner = heads_here * size
    first = section == 0

    def own_batch(value):
        return lax.dynamic_index_in_dim(value, section, 0, False)[0]

    pairs = [(c * fsdp_count + f, f * ctx_count + c) for c in range(ctx_count) for f in range(fsdp_count)]

    def to_plane(value):
        return lax.ppermute(value, ("ctx", "fsdp"), pairs)

    def from_plane(value):
        return lax.ppermute(value, ("ctx", "fsdp"), [(b, a) for a, b in pairs])

    x_in = to_plane(own_batch(tokens))
    g_in = to_plane(own_batch(cotangent))
    length = to_plane(own_batch(lengths))[0]

    def both_layers(own):
        other = exchange(own, "section", 1)
        return jnp.where(first, own, other), jnp.where(first, other, own)

    small = jnp.concatenate(
        [
            norm_one[0],
            norm_two[0],
            decay_weight[0].reshape(-1),
            persistent[0].reshape(-1),
        ]
    )
    small = jnp.stack(both_layers(in_order([p[None] for p in gather_parts(small, "fsdp")], fsdp, 0)))
    cut = width // fsdp_count
    sizes = [cut, cut, decay_weight[0].size, persistent[0].size]
    edges = [0]
    for piece in sizes:
        edges.append(edges[-1] + piece)
    gains_one, gains_two, decays, fixeds = (small[:, :, a:b] for a, b in zip(edges[:-1], edges[1:]))
    gains_one = gains_one.reshape(2, width).astype(wide)
    gains_two = gains_two.reshape(2, width).astype(wide)
    head_count = heads_here * fsdp_count
    decays = lax.dynamic_slice_in_dim(decays.reshape(2, width, head_count), fsdp * heads_here, heads_here, 2)
    slots = persistent.shape[1]
    fixeds = fixeds.reshape(2, fsdp_count, slots, 2 * cut).transpose(0, 2, 1, 3).reshape(2, slots, 2, fsdp_count, inner)
    fixeds = lax.dynamic_index_in_dim(fixeds, fsdp, 3, False).reshape(2, slots, 2 * inner)
    biases = jnp.stack(both_layers(decay_bias[0])).astype(wide)
    qkvs = both_layers(columns_here(qkv_weight[0], 3, "fsdp"))
    outs = both_layers(out_weight[0])
    gate_ups = both_layers(columns_here(gate_up[0], 2, "fsdp"))
    downs = both_layers(down_weight[0])
    hidden = downs[0].shape[0]

    pieces = [(k * fsdp_count + (fsdp ^ r)) * rows + jnp.arange(rows) for k in range(spread) for r in range(fsdp_count)]
    all_positions = jnp.concatenate(pieces)
    groups = [[g * spread + k for k in range(spread)] for g in range(ctx_count // spread)]

    def whole(value):
        if spread == 1:
            return value
        return lax.all_gather(value, "ctx", axis_index_groups=groups, axis=0, tiled=True)

    def own_rows(value):
        if spread == 1:
            return value
        count = value.shape[0] // spread
        return lax.dynamic_slice_in_dim(value, (ctx % spread) * count, count, 0)

    def blocks_of(value):
        return list(value.reshape(fsdp_count, rows, value.shape[1]))

    def forward(layer, x, last):
        normed = jnp.concatenate(gather_parts(normalise(x, gains_one[layer]), "fsdp"))
        projected = dot(normed, qkvs[layer]).astype(half)
        logits = dot(normed, decays[layer]) + biases[layer]
        seen, seen_logits = whole(projected), whole(logits)
        combined = own_rows(mixer(seen, seen_logits, fixeds[layer], length, all_positions, size))
        middle = x + scatter_sum(blocks_of(dot(combined, outs[layer])), "fsdp")
        normed_two = jnp.concatenate(gather_parts(normalise(middle, gains_two[layer]), "fsdp"))
        gates = dot(normed_two, gate_ups[layer])
        activated = (jax.nn.silu(gates[:, :hidden]) * gates[:, hidden:]).astype(half)
        out = middle + scatter_sum(blocks_of(dot(activated, downs[layer])), "fsdp")
        return out.astype(half), (x, normed, seen, seen_logits, combined, middle, normed_two, gates, activated)

    def backward(layer, g_out, saved):
        x, normed, seen, seen_logits, combined, middle, normed_two, gates, activated = saved
        g_rows = jnp.concatenate(gather_parts(g_out, "fsdp"))
        grad_down = dot(activated, g_rows, (0, 0))
        g_activated = dot(g_rows, downs[layer], (1, 1))
        gate, up = gates[:, :hidden], gates[:, hidden:]
        sig = jax.nn.sigmoid(gate)
        g_up = g_activated * gate * sig
        g_gate = g_activated * up * sig * (1.0 + gate * (1.0 - sig))
        g_gates = jnp.concatenate([g_gate, g_up], axis=1).astype(half)
        grad_gate_up = dot(normed_two, g_gates, (0, 0))
        g_normed_two = scatter_sum(blocks_of(dot(g_gates, gate_ups[layer], (1, 1))), "fsdp")
        g_middle, grad_norm_two = normalise_back(middle, gains_two[layer], g_normed_two)
        g_middle = g_middle + g_out.astype(wide)
        g_branch = jnp.concatenate(gather_parts(g_middle.astype(half), "fsdp"))
        grad_out = dot(combined, g_branch, (0, 0))
        g_combined = whole(dot(g_branch, outs[layer], (1, 1)).astype(half))
        g_projected, g_logits, grad_fixed = mixer_back(
            seen, seen_logits, fixeds[layer], length, all_positions, size, g_combined
        )
        g_projected, g_logits = own_rows(g_projected), own_rows(g_logits)
        grad_fixed = jnp.where(ctx % spread == 0, grad_fixed, 0.0)
        grad_qkv = dot(normed, g_projected, (0, 0))
        grad_decay = dot(normed.astype(wide), g_logits, (0, 0))
        grad_bias = jnp.sum(g_logits, axis=0)
        g_normed = dot(g_projected, qkvs[layer], (1, 1)) + dot(g_logits, decays[layer].astype(wide), (1, 1))
        g_normed = scatter_sum(blocks_of(g_normed), "fsdp")
        g_x, grad_norm_one = normalise_back(x, gains_one[layer], g_normed)
        g_x = (g_x + g_middle).astype(half)
        large = (grad_qkv, grad_out, grad_gate_up, grad_down)
        return g_x, tuple(g.astype(half) for g in large), (grad_norm_one, grad_norm_two, grad_decay, grad_bias, grad_fixed)

    between, saved_first = forward(0, x_in.astype(wide), False)
    out, saved_second = forward(1, between.astype(wide), True)
    g_between, large_second, small_second = backward(1, g_in, saved_second)
    g_input, large_first, small_first = backward(0, g_between, saved_first)

    def reduced(from_first, from_second):
        received = exchange(jnp.where(first, from_second, from_first), "section", 1)
        own = jnp.where(first, from_first, from_second)
        own = (own.astype(wide) + received.astype(wide)).astype(half)
        return line_sum(own, "ctx")

    grad_qkv, grad_out, grad_gate_up, grad_down = (reduced(a, b) for a, b in zip(large_first, large_second))
    grad_qkv = rows_here(grad_qkv, 3, "fsdp")
    grad_gate_up = rows_here(grad_gate_up, 2, "fsdp")

    def small_whole(pieces):
        n_one, n_two, decay, bias, fixed = pieces
        decay_all = lax.dynamic_update_slice_in_dim(jnp.zeros((width, head_count), wide), decay, fsdp * heads_here, 1)
        bias_all = lax.dynamic_update_slice_in_dim(jnp.zeros((head_count,), wide), bias, fsdp * heads_here, 0)
        fixed_all = jnp.zeros((slots, 2, fsdp_count, inner), wide)
        fixed_all = lax.dynamic_update_slice_in_dim(fixed_all, fixed.reshape(slots, 2, 1, inner), fsdp, 2)
        return jnp.concatenate([n_one, n_two, decay_all.reshape(-1), fixed_all.reshape(-1), bias_all])

    tiny_first, tiny_second = small_whole(small_first), small_whole(small_second)
    tiny = lax.psum(jnp.stack([tiny_first, tiny_second]), ("section", "ctx", "fsdp"))
    tiny = lax.dynamic_index_in_dim(tiny, section, 0, False)
    grad_norm_one = lax.dynamic_slice_in_dim(tiny[:width], fsdp * cut, cut, 0)
    grad_norm_two = lax.dynamic_slice_in_dim(tiny[width : 2 * width], fsdp * cut, cut, 0)
    at = 2 * width
    grad_decay = lax.dynamic_slice_in_dim(tiny[at : at + width * head_count].reshape(width, head_count), fsdp * cut, cut, 0)
    at += width * head_count
    grad_fixed = tiny[at : at + slots * 2 * width].reshape(slots, 2 * width)
    grad_fixed = lax.dynamic_slice_in_dim(grad_fixed, fsdp * 2 * cut, 2 * cut, 1)
    at += slots * 2 * width
    grad_bias = lax.dynamic_slice_in_dim(tiny[at:], fsdp * heads_here, heads_here, 0)

    return (
        from_plane(out)[None, None],
        from_plane(g_input)[None, None],
        grad_norm_one[None],
        grad_qkv.astype(wide)[None],
        grad_decay[None],
        grad_bias[None],
        grad_fixed[None],
        grad_out.astype(wide)[None],
        grad_norm_two[None],
        grad_gate_up.astype(wide)[None],
        grad_down.astype(wide)[None],
    )


def solution(mesh):
    by_row = P("section", "fsdp", None)
    by_gain = P("section", "fsdp")
    by_token = P(None, "fsdp", "ctx", None)
    by_output = P("section", "fsdp", "ctx", None)
    by_slot = P("section", None, "fsdp")
    plane = mesh.shape["ctx"] == mesh.shape["fsdp"] == 4
    return jax.shard_map(
        plane_device if plane else general_device,
        mesh=mesh,
        in_specs=(
            by_token,
            P(None, "fsdp", None),
            by_token,
            by_gain,
            by_row,
            by_row,
            by_gain,
            by_slot,
            by_row,
            by_gain,
            by_row,
            by_row,
        ),
        out_specs=(
            by_output,
            by_output,
            by_gain,
            by_row,
            by_row,
            by_gain,
            by_slot,
            by_row,
            by_gain,
            by_row,
            by_row,
        ),
        check_vma=False,
    )
```
